32 devices in a mesh: dp: 4 (over z), expert: 8 (over y, x, core).
Axes of the slice: x: 2, y: 2, z: 4, core: 2. Of those that a mesh axis runs over, the one named last changes fastest.
Arguments:
- tokens: bfloat16 [8192, 1536], P(('dp', 'expert')), may hold values from -6 to 6
- lengths: int32 [4, 4], P('dp'), may hold values from 1 to 1024, 2048 in all within a row
- seq_order: int32 [4, 4], P('dp'), may hold values from 0 to 3, each once within a row
- routes: int32 [8192, 4], P(('dp', 'expert')), may hold values from 0 to 7, all different within a row; in each aligned block of 256 rows (0 to 255, 256 to 511, ...) at most 256 rows name the same one
- norm_attn: bfloat16 [1536], P(('dp', 'expert')), may hold values from 0.5 to 1.5
- w_query: bfloat16 [1536, 1536], P(('dp', 'expert')), may hold values from -0.15625 to 0.15625
- key_projection: bfloat16 [1536, 256], P(('dp', 'expert')), may hold values from -0.15625 to 0.15625
- value_projection: bfloat16 [1536, 256], P(('dp', 'expert')), may hold values from -0.15625 to 0.15625
- w_out: bfloat16 [1536, 1536], P(('dp', 'expert')), may hold values from -1.25 to 1.25
- norm_moe: bfloat16 [1536], P(('dp', 'expert')), may hold values from 0.5 to 1.5
- w_router: bfloat16 [1536, 8], P(('dp', 'expert')), may hold values from -0.078125 to 0.078125
- w_gate: bfloat16 [8, 1536, 768], P('expert', 'dp'), may hold values from -0.15625 to 0.15625
- w_up: bfloat16 [8, 1536, 768], P('expert', 'dp'), may hold values from -0.15625 to 0.15625
- w_down: bfloat16 [8, 768, 1536], P('expert', 'dp'), may hold values from -0.21875 to 0.21875
- cotangent: bfloat16 [8192, 1536], P(('dp', 'expert')), may hold values from -6 to 6
Outputs:
- output: bfloat16 [8192, 1536], P(('dp', 'expert'))
- tokens_grad: bfloat16 [8192, 1536], P(('dp', 'expert'))
- norm_attn_grad: float32 [1536], P(('dp', 'expert'))
- w_query_grad: float32 [1536, 1536], P(('dp', 'expert'))
- w_key_grad: float32 [1536, 256], P(('dp', 'expert'))
- w_value_grad: float32 [1536, 256], P(('dp', 'expert'))
- w_out_grad: float32 [1536, 1536], P(('dp', 'expert'))
- norm_moe_grad: float32 [1536], P(('dp', 'expert'))
- w_router_grad: float32 [1536, 8], P(('dp', 'expert'))
- w_gate_grad: float32 [8, 1536, 768], P('expert', 'dp')
- w_up_grad: float32 [8, 1536, 768], P('expert', 'dp')
- w_down_grad: float32 [8, 768, 1536], P('expert', 'dp')
The draws below stay inside these ranges and needn't reach their ends.
Inputs may be any that keep to these rules, and one draw needn't show every extreme that they name: In each group the lengths sum to 2048 and the largest is exactly 1024. `seq_order`: each row holds every number below 4 once. `routes`: each row names 4 different experts; among the rows of one device no expert is named more than 256 times, a bound that some block reaches.
All inputs are finite; a program needn't handle non-finite values.
Results may differ from the reference program's by a relative error of at most 0.018.
Values may be sent and summed in bfloat16 or wider, within the bound.
A program may use at most 256 MiB of HBM per device.

```python
import math
import jax
import jax.numpy as jnp
import numpy as np
from jax import lax

MODEL_WIDTH = 1536
QUERY_HEADS = 12
KEY_VALUE_HEADS = 2
HEAD_SIZE = 128
FFE = 768
TOPK = 4
TOK_DEV = 256
NSEQ = 4
EXPERTS = 8
GROUP_TOKENS = 2048
TOKENS = 8192
MAXLEN = 1024
CAP = 256
N_DP = 4
N_EXPERT = 8


def shard_levels(own_key, extent, split, smallest, high):
    loudness, own = 1.0, jax.random.fold_in(own_key, 6)
    for axis_at, blocks in split:
        heights = jnp.exp(jax.random.uniform(jax.random.fold_in(own, axis_at), (blocks,), jnp.float32, smallest / len(split), high / len(split)))
        loudness = loudness * jnp.repeat(heights, extent[axis_at] // blocks).reshape([-1 if axis == axis_at else 1 for axis in range(len(extent))])
    return loudness


def profile(count, total, limit, slope):
    portions = [(1 << 20) // math.isqrt(rank ** slope) + 1 for rank in range(2, count + 1)]
    surplus, counts = total - limit - (count - 1), [1] * (count - 1)
    while surplus > 0:
        movable = [i for i in range(count - 1) if counts[i] < limit]
        whole, budget = sum([portions[i] for i in movable]), surplus
        for i in movable:
            addition = min(limit - counts[i], max(1, budget * portions[i] // whole), surplus)
            counts[i] = counts[i] + addition
            surplus = surplus - addition
    return np.array([limit] + counts)


def ragged_sizes(own_key, amount, total, limit, slope):
    if amount == 2:
        one = jax.random.randint(own_key, (), max(1, total - limit), min(limit, total - 1) + 1)
        return jnp.stack([one, total - one])
    tallies = jnp.asarray(profile(amount, total, limit, slope), jnp.int32)
    couples = (amount - 1) // 2
    giver, sink = tallies[1:1 + 2 * couples:2], tallies[2:2 + 2 * couples:2]
    room = jnp.minimum(giver - 1, limit - sink)
    moved = jax.random.randint(jax.random.fold_in(own_key, 1), (couples,), 0, 1 << 20) % (room + 1)
    tallies = tallies.at[1:1 + 2 * couples:2].set(giver - moved).at[2:2 + 2 * couples:2].set(sink + moved)
    return tallies[jax.random.permutation(jax.random.fold_in(own_key, 2), amount)]


def routed_block(key, own, number, rows, number_of, top, reach, skew):
    sequence = jax.random.permutation(key, number_of)
    crowded, usual = portions_of(number_of, rows * top, reach, skew, True), portions_of(number_of, rows * top, reach, skew, False)
    places = jnp.arange(number_of)

    def named(sizes, turn):
        used = int((sizes > 0).sum())
        fixed = max(1, used // 4)
        moved = fixed + (places - fixed + turn * (used - fixed)) % max(1, number_of - fixed)
        return jnp.zeros((number_of,), jnp.int32).at[sequence[jnp.where(places < fixed, places, moved)]].set(jnp.asarray(sizes, jnp.int32))

    sizes = jnp.where(number % 4 == 0, named(crowded, number // 4), named(usual, number - number // 4 - 1))
    mixed = jax.random.permutation(jax.random.fold_in(own, 3), number_of)
    source_of, receiver = mixed[0:number_of // 2 * 2:2], mixed[1:number_of // 2 * 2:2]
    slack = jnp.minimum(sizes[source_of] - 1, reach - sizes[receiver]) // 2
    slack = jnp.where((source_of == sequence[0]) | (receiver == sequence[0]) | (sizes[receiver] == 0), 0, jnp.maximum(slack, 0))
    moved = jax.random.randint(jax.random.fold_in(own, 4), (number_of // 2,), 0, 1 << 20) % (slack + 1)
    sizes = sizes.at[source_of].add(-moved).at[receiver].add(moved)
    labels = jnp.searchsorted(jnp.cumsum(sizes), jnp.arange(rows * top), side="right").astype(jnp.int32)
    listing = labels.reshape(top, rows).T
    listing = listing[jax.random.permutation(jax.random.fold_in(own, 1), rows)]
    turn = jax.random.randint(jax.random.fold_in(own, 2), (rows, 1), 0, top)
    return jnp.take_along_axis(listing, (jnp.arange(top)[None, :] + turn) % top, axis=1)


def portions_of(amount, total, most, skew, full):
    loads = [(1 << 20) // math.isqrt(grade ** skew) + 1 for grade in range(1, amount + 1)]
    largest = most if full else min(most, max(-(-total // amount), total * loads[0] // sum(loads)))
    least = 1 if total - largest >= amount - 1 else 0
    counts, spare = [largest] + [least] * (amount - 1), total - largest - least * (amount - 1)
    while spare > 0:
        candidates = [i for i in range(1, amount) if counts[i] < largest] or [i for i in range(1, amount) if counts[i] < most]
        whole, budget = sum([loads[i] for i in candidates]), spare
        for i in candidates:
            addition = min(most - counts[i], max(1, budget * loads[i] // whole), spare)
            counts[i] = counts[i] + addition
            spare = spare - addition
    return np.array(counts)


def noise(rng, extent, scale, limit, shards=(), held_as=jnp.bfloat16):
    factor_of = shard_levels(rng, extent, shards, -0.22, 0.18) if shards else 1.0
    array = jax.random.normal(rng, extent, jnp.float32) * scale * factor_of
    return jnp.minimum(jnp.maximum(array, -limit), limit).astype(held_as)


def setup_inputs(seed: int = 0) -> dict:
    seeds = jax.random.split(jax.random.key(seed), 16)
    tokens = noise(seeds[0], (TOKENS, MODEL_WIDTH), 1.0, 6.0, ((0, 32),))
    lengths = jax.vmap(lambda own: ragged_sizes(own, NSEQ, GROUP_TOKENS, MAXLEN, 2))(jax.random.split(seeds[1], N_DP)).reshape((N_DP, NSEQ)).astype(jnp.int32)
    seq_order = jax.vmap(lambda own: jax.random.permutation(own, NSEQ))(jax.random.split(seeds[2], N_DP)).reshape((N_DP, NSEQ)).astype(jnp.int32)
    routes_keys = jax.random.split(jax.random.fold_in(seeds[3], 1), TOKENS // TOK_DEV)
    routes_turns = jax.random.permutation(jax.random.fold_in(seeds[3], 3), TOKENS // TOK_DEV)
    routes = jax.vmap(lambda own, number: routed_block(jax.random.fold_in(seeds[3], 2), own, number, TOK_DEV, EXPERTS, TOPK, CAP, 1))(routes_keys, routes_turns).reshape((TOKENS, TOPK))
    norm_attn = jnp.clip(1.0 + 0.1 * jax.random.normal(seeds[4], (MODEL_WIDTH,), jnp.float32), 0.5, 1.5).astype(jnp.bfloat16)
    w_query = noise(seeds[5], (MODEL_WIDTH, QUERY_HEADS * HEAD_SIZE), MODEL_WIDTH ** -0.5, 0.15625, ((0, 32),))
    key_projection = noise(seeds[6], (MODEL_WIDTH, KEY_VALUE_HEADS * HEAD_SIZE), MODEL_WIDTH ** -0.5, 0.15625, ((0, 32),))
    value_projection = noise(seeds[7], (MODEL_WIDTH, KEY_VALUE_HEADS * HEAD_SIZE), MODEL_WIDTH ** -0.5, 0.15625, ((0, 32),))
    w_out = noise(seeds[8], (QUERY_HEADS * HEAD_SIZE, MODEL_WIDTH), (QUERY_HEADS * HEAD_SIZE // 64) ** -0.5, 1.25, ((0, 32),))
    norm_moe = jnp.clip(1.0 + 0.1 * jax.random.normal(seeds[9], (MODEL_WIDTH,), jnp.float32), 0.5, 1.5).astype(jnp.bfloat16)
    w_router = noise(seeds[10], (MODEL_WIDTH, EXPERTS), (4 * MODEL_WIDTH) ** -0.5, 0.078125, ((0, 32),))
    w_gate = noise(seeds[11], (EXPERTS, MODEL_WIDTH, FFE), MODEL_WIDTH ** -0.5, 0.15625, ((0, 8), (1, 4)))
    w_up = noise(seeds[12], (EXPERTS, MODEL_WIDTH, FFE), MODEL_WIDTH ** -0.5, 0.15625, ((0, 8), (1, 4)))
    w_down = noise(seeds[13], (EXPERTS, FFE, MODEL_WIDTH), FFE ** -0.5, 0.21875, ((0, 8), (1, 4)))
    cotangent = noise(seeds[14], (TOKENS, MODEL_WIDTH), 1.0, 6.0, ((0, 32),))
    return dict(tokens=tokens, lengths=lengths, seq_order=seq_order, routes=routes, norm_attn=norm_attn, w_query=w_query, key_projection=key_projection, value_projection=value_projection, w_out=w_out, norm_moe=norm_moe, w_router=w_router, w_gate=w_gate, w_up=w_up, w_down=w_down, cotangent=cotangent)


EPSILON = 1e-06
ROPE_BASE = 10000.0
MASKED_SCORE = -1e+30
HIGHEST = lax.Precision.HIGHEST

@jax.custom_vjp
def reduced_precision(v):
    return lax.optimization_barrier(v.astype(jnp.bfloat16)).astype(jnp.float32)

@jax.custom_vjp
def low_back(v):
    return v

def low_keep(v):
    return (reduced_precision(v), None)

def low_pass(kept, grad):
    return (grad,)

def back_keep(v):
    return (v, None)

def back_low(kept, grad):
    return (reduced_precision(grad),)
reduced_precision.defvjp(low_keep, low_pass)
low_back.defvjp(back_keep, back_low)

def rms_scale(values):
    return lax.rsqrt(lax.optimization_barrier(jnp.mean(values * values, axis=-1, keepdims=True)) + EPSILON)

def softmax_last(values):
    highest = lax.optimization_barrier(jnp.max(values, axis=-1, keepdims=True))
    spread = jnp.exp(values - highest)
    return spread / lax.optimization_barrier(jnp.sum(spread, axis=-1, keepdims=True))

def rope_tables(positions, half_size):
    angle_steps = jnp.arange(half_size).astype(jnp.float32)
    frequency = jnp.exp(angle_steps * (-math.log(ROPE_BASE) / half_size))
    angles = positions.astype(jnp.float32)[..., None] * frequency
    return (jnp.cos(angles)[..., None, :], jnp.sin(angles)[..., None, :])

def apply_rotation(values, cosine_table, sine_table):
    half_size = values.shape[-1] // 2
    first = values[..., :half_size]
    second = values[..., half_size:]
    return jnp.concatenate([first * cosine_table - second * sine_table, second * cosine_table + first * sine_table], axis=-1)

def block_to_pass(values):
    return values.reshape(N_DP, N_EXPERT, TOK_DEV, -1).transpose(0, 2, 1, 3).reshape(N_DP, GROUP_TOKENS, -1)

def from_stream(values):
    return values.reshape(N_DP, TOK_DEV, N_EXPERT, -1).transpose(0, 2, 1, 3).reshape(N_DP * N_EXPERT * TOK_DEV, -1)

def group_places(lengths, seq_order):
    count_seq = lengths.shape[1]
    picked = seq_order[:, :, None] == jnp.arange(count_seq).astype(jnp.int32)[None, None, :]
    ordered = lax.optimization_barrier(jnp.sum(jnp.where(picked, lengths[:, None, :], 0), axis=2))
    seq_ends = jnp.cumsum(ordered, axis=1)
    positions = jnp.arange(GROUP_TOKENS).astype(jnp.int32)
    passed = seq_ends[:, None, :] <= positions[None, :, None]
    sequence_index = lax.optimization_barrier(jnp.sum(passed.astype(jnp.int32), axis=2))
    starts = lax.optimization_barrier(jnp.sum(jnp.where(passed, ordered[:, None, :], 0), axis=2))
    return (sequence_index, positions[None, :] - starts)

def expert_slots(routes):
    n_devices = N_DP * N_EXPERT
    per_device = routes.reshape(n_devices, TOK_DEV * TOPK)
    one_hot = (per_device[:, :, None] == jnp.arange(EXPERTS).astype(jnp.int32)[None, None, :]).astype(jnp.int32)
    before = jnp.cumsum(one_hot, axis=1) - one_hot
    places = lax.optimization_barrier(jnp.sum(before * one_hot, axis=2))
    device_ids = jnp.arange(n_devices).astype(jnp.int32)[:, None]
    return (device_ids * CAP + places).reshape(-1)

def attend_token_group(inputs):
    query_rows, keys, values, sequence_index = inputs
    block_row_count = math.gcd(GROUP_TOKENS, 512)
    passing_block = jnp.arange(GROUP_TOKENS).astype(jnp.int32)
    score_scale = 1.0 / math.sqrt(HEAD_SIZE)

    def single_block(pieces):
        query_part, query_seq, query_stream = pieces
        raw_scores = low_back(jnp.einsum('tkrd,skd->krts', query_part, keys, precision=HIGHEST) * score_scale)
        allowed = (query_seq[:, None] == sequence_index[None, :]) & (passing_block[None, :] <= query_stream[:, None])
        chances = reduced_precision(softmax_last(jnp.where(allowed, raw_scores, MASKED_SCORE)))
        return jnp.einsum('krts,skd->tkrd', chances, values, precision=HIGHEST)
    block_count = GROUP_TOKENS // block_row_count
    output_rows = lax.map(jax.checkpoint(single_block), (query_rows.reshape(block_count, block_row_count, KEY_VALUE_HEADS, QUERY_HEADS // KEY_VALUE_HEADS, HEAD_SIZE), sequence_index.reshape(block_count, block_row_count), passing_block.reshape(block_count, block_row_count)))
    return output_rows.reshape(GROUP_TOKENS, QUERY_HEADS * HEAD_SIZE)

def run_expert(inputs):
    row_values, gate_w, up_w, down_w = inputs
    gate_pre = low_back(jnp.dot(row_values, gate_w, precision=HIGHEST))
    up_pre = low_back(jnp.dot(row_values, up_w, precision=HIGHEST))
    hidden = reduced_precision(gate_pre * jax.nn.sigmoid(gate_pre) * up_pre)
    return reduced_precision(low_back(jnp.dot(hidden, down_w, precision=HIGHEST)))

def reference(tokens, lengths, seq_order, routes, norm_attn, w_query, key_projection, value_projection, w_out, norm_moe, w_router, w_gate, w_up, w_down, cotangent):
    sequence_index, relative = group_places(lengths, seq_order)
    expert_ids = routes.reshape(-1)
    slot_ids = expert_slots(routes)
    query_per_key_heads = QUERY_HEADS // KEY_VALUE_HEADS
    cosine_table, sine_table = rope_tables(relative, HEAD_SIZE // 2)

    def forward(inputs_float, gain_one, query_w, key_w, value_w, out_w, gain_two, router_w, gate_w, up_w, down_w):
        normed_one = reduced_precision(inputs_float * rms_scale(inputs_float) * gain_one)
        query_pre = low_back(jnp.dot(normed_one, query_w, precision=HIGHEST))
        key_before_rotation = low_back(jnp.dot(normed_one, key_w, precision=HIGHEST))
        value_projected = low_back(jnp.dot(normed_one, value_w, precision=HIGHEST))
        rotated_queries = reduced_precision(apply_rotation(block_to_pass(query_pre).reshape(N_DP, GROUP_TOKENS, QUERY_HEADS, HEAD_SIZE), cosine_table, sine_table))
        rotated_keys = reduced_precision(apply_rotation(block_to_pass(key_before_rotation).reshape(N_DP, GROUP_TOKENS, KEY_VALUE_HEADS, HEAD_SIZE), cosine_table, sine_table))
        value_reduced = reduced_precision(block_to_pass(value_projected).reshape(N_DP, GROUP_TOKENS, KEY_VALUE_HEADS, HEAD_SIZE))
        attention_output = lax.map(attend_token_group, (rotated_queries.reshape(N_DP, GROUP_TOKENS, KEY_VALUE_HEADS, query_per_key_heads, HEAD_SIZE), rotated_keys, value_reduced, sequence_index))
        attended_low = reduced_precision(low_back(from_stream(attention_output)))
        middle = inputs_float + low_back(jnp.dot(attended_low, out_w, precision=HIGHEST))
        normed_two = reduced_precision(middle * rms_scale(middle) * gain_two)
        logits = low_back(jnp.dot(normed_two, router_w, precision=HIGHEST))
        gates = softmax_last(jnp.take_along_axis(logits, routes, axis=1))
        buffer = jnp.zeros((EXPERTS, N_DP * N_EXPERT * CAP, MODEL_WIDTH), jnp.float32)
        buffer = low_back(buffer.at[expert_ids, slot_ids].set(jnp.repeat(normed_two, TOPK, axis=0)))
        produced = lax.map(jax.checkpoint(run_expert), (buffer, gate_w, up_w, down_w))
        picked = produced[expert_ids, slot_ids].reshape(-1, TOPK, MODEL_WIDTH)
        return middle + lax.optimization_barrier(jnp.sum(gates[:, :, None] * picked, axis=1))
    floats = [value.astype(jnp.float32) for value in (tokens, norm_attn, w_query, key_projection, value_projection, w_out, norm_moe, w_router, w_gate, w_up, w_down)]
    result, pullback = jax.vjp(forward, *floats)
    gradients = pullback(cotangent.astype(jnp.float32))
    return (result.astype(jnp.bfloat16), gradients[0].astype(jnp.bfloat16), gradients[1], gradients[2], gradients[3], gradients[4], gradients[5], gradients[6], gradients[7], gradients[8], gradients[9], gradients[10])
```

```python
import math

import jax
import jax.numpy as jnp
from jax import lax
from jax.sharding import PartitionSpec as P

QUERY_HEADS = 12
KEY_VALUE_HEADS = 2
HEAD_SIZE = 128


EPSILON = 1e-06
ROPE_BASE = 10000.0
MASKED_SCORE = -1e30
BF = jnp.bfloat16
F32 = jnp.float32


def rms_scale(values):
    return lax.rsqrt(jnp.mean(values * values, axis=-1, keepdims=True) + EPSILON)


def rope_tables(positions, half_size):
    angle_steps = lax.broadcasted_iota(F32, (half_size,), 0)
    frequency = jnp.exp(angle_steps * (-math.log(ROPE_BASE) / half_size))
    angles = positions.astype(F32)[:, None] * frequency
    return (jnp.cos(angles)[:, None, :], jnp.sin(angles)[:, None, :])


def apply_rotation(values, cosine_table, sine_table):
    half_size = values.shape[-1] // 2
    first = values[..., :half_size]
    second = values[..., half_size:]
    return jnp.concatenate(
        [first * cosine_table - second * sine_table, second * cosine_table + first * sine_table],
        axis=-1,
    )


def reverse_rotation(grads_in, cosine_table, sine_table):
    return apply_rotation(grads_in, cosine_table, -sine_table)


def seq_layout(lengths, seq_order):
    count_seq = lengths.shape[1]
    picked = seq_order[0][:, None] == lax.broadcasted_iota(jnp.int32, (count_seq, count_seq), 1)
    ordered = jnp.sum(jnp.where(picked, lengths[0][None, :], 0), axis=1)
    return (ordered, jnp.cumsum(ordered))


def seq_place(positions, ordered, seq_ends):
    passed = seq_ends[None, :] <= positions[:, None]
    sequence_index = jnp.sum(passed.astype(jnp.int32), axis=1)
    starts = jnp.sum(jnp.where(passed, ordered[None, :], 0), axis=1)
    return (sequence_index, positions - starts)


def block_scores(
    query_rows, key_portion, query_seq, query_stream, key_seq, key_stream, score_scale
):
    raw_scores = (
        jnp.einsum("tkrd,skd->krts", query_rows, key_portion, preferred_element_type=F32)
        * score_scale
    )
    allowed = (query_seq[:, None] == key_seq[None, :]) & (
        key_stream[None, :] <= query_stream[:, None]
    )
    return jnp.where(allowed, raw_scores, MASKED_SCORE)


def norm_backward(grad_normed, unit_values, inv_scale, gain_float):
    scaled = grad_normed * gain_float
    gain_grad = jnp.sum(grad_normed * unit_values, axis=0)
    input_grad = inv_scale * (
        scaled - unit_values * jnp.mean(scaled * unit_values, axis=-1, keepdims=True)
    )
    return (gain_grad, input_grad)


def dot(a, b):
    return jnp.dot(a, b, preferred_element_type=F32)


def dot_nt(a, b):
    return jnp.einsum("ac,bc->ab", a, b, preferred_element_type=F32)


def dot_tn(a, b):
    return jnp.einsum("ta,tb->ab", a, b, preferred_element_type=F32)


def on_device(
    tokens,
    lengths,
    seq_order,
    routes,
    norm_attn,
    w_query,
    key_projection,
    value_projection,
    w_out,
    norm_moe,
    w_router,
    w_gate,
    w_up,
    w_down,
    cotangent,
):
    token_count, width = tokens.shape
    n_experts = w_router.shape[1]
    rows = w_query.shape[0]
    group_size = lax.axis_size("expert")
    my_index = lax.axis_index("expert")
    query_per_key_heads = QUERY_HEADS // KEY_VALUE_HEADS
    kv_width = KEY_VALUE_HEADS * HEAD_SIZE
    q_width = QUERY_HEADS * HEAD_SIZE
    score_scale = 1.0 / math.sqrt(HEAD_SIZE)
    group_tokens = token_count * group_size

    small = jnp.concatenate(
        [
            w_router,
            norm_attn[:, None],
            norm_moe[:, None],
            jnp.zeros((rows, 128 - n_experts - 2), BF),
        ],
        axis=1,
    )
    pack = jnp.concatenate([w_query, key_projection, value_projection, small, w_out], axis=1)
    gate_w = lax.all_gather(w_gate[0], "dp", axis=0, tiled=True)
    up_w = lax.all_gather(w_up[0], "dp", axis=0, tiled=True)
    down_w = lax.all_gather(w_down[0], "dp", axis=0, tiled=True)
    pack = lax.all_gather(pack, ("dp", "expert"), axis=0, tiled=True)
    cot_all = lax.all_gather(cotangent, "expert", axis=0, tiled=True)
    c_k = q_width
    c_v = c_k + kv_width
    c_s = c_v + kv_width
    c_o = c_s + 128
    query_w = pack[:, :c_k]
    key_w = pack[:, c_k:c_v]
    value_w = pack[:, c_v:c_s]
    router_w = pack[:, c_s : c_s + n_experts]
    gain_one = pack[:, c_s + n_experts].astype(F32)
    gain_two = pack[:, c_s + n_experts + 1].astype(F32)
    out_w = pack[:, c_o:]

    seq_lens, seq_ends = seq_layout(lengths, seq_order)
    my_stream = lax.broadcasted_iota(jnp.int32, (token_count,), 0) * group_size + my_index
    query_seq, query_rel = seq_place(my_stream, seq_lens, seq_ends)
    all_rows = lax.broadcasted_iota(jnp.int32, (group_tokens,), 0)
    key_stream = all_rows % token_count * group_size + all_rows // token_count
    key_seq = seq_place(key_stream, seq_lens, seq_ends)[0]
    block_row_count = math.gcd(group_tokens, 512)
    block_count = group_tokens // block_row_count
    cosine_table, sine_table = rope_tables(query_rel, HEAD_SIZE // 2)
    inputs_float = tokens.astype(F32)
    inv_one = rms_scale(inputs_float)
    unit_one = inputs_float * inv_one
    normed_one = (unit_one * gain_one).astype(BF)
    query_pre = dot(normed_one, query_w)
    key_pre = dot(normed_one, key_w)
    value_pre = dot(normed_one, value_w)
    rotated_queries = (
        apply_rotation(
            query_pre.reshape(token_count, QUERY_HEADS, HEAD_SIZE), cosine_table, sine_table
        )
        .astype(BF)
        .reshape(token_count, KEY_VALUE_HEADS, query_per_key_heads, HEAD_SIZE)
    )
    rotated_keys = apply_rotation(
        key_pre.reshape(token_count, KEY_VALUE_HEADS, HEAD_SIZE),
        cosine_table,
        sine_table,
    ).astype(BF)
    key_value = jnp.concatenate(
        [rotated_keys.reshape(token_count, kv_width), value_pre.astype(BF)],
        axis=1,
    )
    gathered = lax.all_gather(key_value, "expert", axis=0, tiled=True)
    key_blocks = (
        gathered.reshape(block_count, block_row_count, 2 * kv_width),
        key_seq.reshape(block_count, block_row_count),
        key_stream.reshape(block_count, block_row_count),
    )

    def stats_step(carry, blocks):
        run_max, run_sum = carry
        key_value_block, seq_block, stream_block = blocks
        key_portion = key_value_block[:, :kv_width].reshape(-1, KEY_VALUE_HEADS, HEAD_SIZE)
        scores = block_scores(
            rotated_queries, key_portion, query_seq, my_stream, seq_block, stream_block, score_scale
        )
        new_max = jnp.maximum(run_max, jnp.max(scores, axis=-1))
        run_sum = run_sum * jnp.exp(run_max - new_max) + jnp.sum(
            jnp.exp(scores - new_max[..., None]), axis=-1
        )
        return ((new_max, run_sum), None)

    initial_maximum = jnp.full(
        (KEY_VALUE_HEADS, query_per_key_heads, token_count), MASKED_SCORE, F32
    )
    (row_max, row_sum), unused = lax.scan(
        stats_step, (initial_maximum, jnp.zeros_like(initial_maximum)), key_blocks
    )
    log_total = row_max + jnp.log(row_sum)

    def value_step(summed, blocks):
        key_value_block, seq_block, stream_block = blocks
        key_portion = key_value_block[:, :kv_width].reshape(-1, KEY_VALUE_HEADS, HEAD_SIZE)
        value_portion = key_value_block[:, kv_width:].reshape(-1, KEY_VALUE_HEADS, HEAD_SIZE)
        scores = block_scores(
            rotated_queries, key_portion, query_seq, my_stream, seq_block, stream_block, score_scale
        )
        low_chances = jnp.exp(scores - log_total[..., None]).astype(BF)
        summed = summed + jnp.einsum(
            "krts,skd->tkrd", low_chances, value_portion, preferred_element_type=F32
        )
        return (summed, None)

    empty_head_state = jnp.zeros(
        (token_count, KEY_VALUE_HEADS, query_per_key_heads, HEAD_SIZE), F32
    )
    attended, unused = lax.scan(value_step, empty_head_state, key_blocks)
    attended_low = attended.reshape(token_count, q_width).astype(BF)
    middle = inputs_float + dot(attended_low, out_w)
    inv_two = rms_scale(middle)
    unit_two = middle * inv_two
    normed_two = (unit_two * gain_two).astype(BF)

    logits = dot(normed_two, router_w)
    choose = jnp.any(
        routes[:, :, None] == lax.broadcasted_iota(jnp.int32, (1, 1, n_experts), 2), axis=1
    )
    top_logit = jnp.max(jnp.where(choose, logits, -jnp.inf), axis=1, keepdims=True)
    spread = jnp.where(choose, jnp.exp(jnp.minimum(logits - top_logit, 0.0)), 0.0)
    gates = spread / jnp.sum(spread, axis=1, keepdims=True)

    normed_all = lax.all_gather(normed_two, "expert", axis=0, tiled=True)
    gates_all = lax.all_to_all(
        gates.T.reshape(n_experts, 1, token_count), "expert", split_axis=0, concat_axis=1, tiled=True
    )
    gate_col = gates_all.reshape(group_tokens, 1)

    gate_pre = dot(normed_all, gate_w)
    up_pre = dot(normed_all, up_w)
    sig = jax.nn.sigmoid(gate_pre)
    silu = gate_pre * sig
    hidden = (silu * up_pre).astype(BF)
    returned = dot(hidden, down_w).astype(BF).astype(F32)
    cot_float = cot_all.astype(F32)
    grad_gates = jnp.sum(cot_float * returned, axis=1)
    weighted = (gate_col * returned).astype(BF)
    grad_returned = (gate_col * cot_float).astype(BF)
    grad_hidden = dot_nt(grad_returned, down_w)
    grad_gate_pre = (grad_hidden * up_pre * sig * (1.0 + gate_pre * (1.0 - sig))).astype(BF)
    grad_up_pre = (grad_hidden * silu).astype(BF)
    grad_row = (dot_nt(grad_gate_pre, gate_w) + dot_nt(grad_up_pre, up_w)).astype(BF)
    down_grad = dot_tn(hidden, grad_returned).astype(BF)
    gate_grad = dot_tn(normed_all, grad_gate_pre).astype(BF)
    up_grad = dot_tn(normed_all, grad_up_pre).astype(BF)

    grad_gates = lax.all_to_all(
        grad_gates.reshape(group_size, 1, token_count), "expert", split_axis=0, concat_axis=1, tiled=True
    ).reshape(n_experts, token_count).T
    row_sum_grad = lax.psum_scatter(grad_row, "expert", scatter_dimension=0, tiled=True)
    output = (
        middle + lax.psum_scatter(weighted, "expert", scatter_dimension=0, tiled=True).astype(F32)
    ).astype(BF)

    grad_out = cotangent.astype(F32)
    grad_logits = (
        gates * (grad_gates - jnp.sum(gates * grad_gates, axis=1, keepdims=True))
    ).astype(BF)
    router_grad = dot_tn(normed_two, grad_logits)
    grad_normed_two = dot_nt(grad_logits, router_w) + row_sum_grad.astype(F32)
    gain_two_grad, grad_middle = norm_backward(grad_normed_two, unit_two, inv_two, gain_two)
    grad_middle = grad_out + grad_middle
    grad_mixed = grad_middle.astype(BF)
    out_grad = dot_tn(attended_low, grad_mixed)
    grad_attended = dot_nt(grad_mixed, out_w).astype(BF)
    head_gradient = grad_attended.reshape(
        token_count, KEY_VALUE_HEADS, query_per_key_heads, HEAD_SIZE
    )
    row_dot = jnp.transpose(jnp.sum(head_gradient.astype(F32) * attended, axis=-1), (1, 2, 0))

    def grad_step(query_grad, blocks):
        key_value_block, seq_block, stream_block = blocks
        key_portion = key_value_block[:, :kv_width].reshape(-1, KEY_VALUE_HEADS, HEAD_SIZE)
        value_portion = key_value_block[:, kv_width:].reshape(-1, KEY_VALUE_HEADS, HEAD_SIZE)
        scores = block_scores(
            rotated_queries, key_portion, query_seq, my_stream, seq_block, stream_block, score_scale
        )
        chances = jnp.exp(scores - log_total[..., None])
        low_chances = chances.astype(BF)
        grad_chances = jnp.einsum(
            "tkrd,skd->krts", head_gradient, value_portion, preferred_element_type=F32
        )
        grad_scores = (chances * (grad_chances - row_dot[..., None])).astype(BF)
        query_grad = query_grad + jnp.einsum(
            "krts,skd->tkrd", grad_scores, key_portion, preferred_element_type=F32
        )
        key_terms = (
            jnp.einsum("krts,tkrd->skd", grad_scores, rotated_queries, preferred_element_type=F32)
            * score_scale
        )
        value_terms = jnp.einsum(
            "krts,tkrd->skd", low_chances, head_gradient, preferred_element_type=F32
        )
        return (query_grad, (key_terms.astype(BF), value_terms.astype(BF)))

    query_grad, (key_terms, value_terms) = lax.scan(grad_step, empty_head_state, key_blocks)
    query_grad = query_grad * score_scale
    kv_terms = jnp.concatenate(
        [key_terms.reshape(group_tokens, kv_width), value_terms.reshape(group_tokens, kv_width)],
        axis=1,
    )
    kv_mine = lax.psum_scatter(kv_terms, "expert", scatter_dimension=0, tiled=True)
    grad_query_pre = (
        reverse_rotation(
            query_grad.reshape(token_count, QUERY_HEADS, HEAD_SIZE), cosine_table, sine_table
        )
        .reshape(token_count, q_width)
        .astype(BF)
    )
    grad_key_pre = (
        reverse_rotation(
            kv_mine[:, :kv_width].astype(F32).reshape(token_count, KEY_VALUE_HEADS, HEAD_SIZE),
            cosine_table,
            sine_table,
        )
        .reshape(token_count, kv_width)
        .astype(BF)
    )
    grad_qkv = jnp.concatenate([grad_query_pre, grad_key_pre, kv_mine[:, kv_width:]], axis=1)
    grad_normed_one = dot_nt(grad_qkv, pack[:, :c_s])
    qkv_grad = dot_tn(normed_one, grad_qkv)
    gain_one_grad, grad_input = norm_backward(grad_normed_one, unit_one, inv_one, gain_one)
    tokens_grad = (grad_middle + grad_input).astype(BF)
    small_grad = jnp.concatenate(
        [
            router_grad,
            gain_one_grad[:, None],
            gain_two_grad[:, None],
            jnp.zeros((width, 128 - n_experts - 2), F32),
        ],
        axis=1,
    )
    pack_grad = jnp.concatenate(
        [qkv_grad.astype(BF), small_grad.astype(BF), out_grad.astype(BF)], axis=1
    )
    mine = lax.psum_scatter(pack_grad, ("dp", "expert"), scatter_dimension=0, tiled=True)
    mine = mine.astype(F32)
    gate_mine, up_mine, down_mine = (
        lax.psum_scatter(grad, "dp", scatter_dimension=0, tiled=True).astype(F32)[None]
        for grad in (gate_grad, up_grad, down_grad)
    )
    return (
        output,
        tokens_grad,
        mine[:, c_s + n_experts],
        mine[:, :c_k],
        mine[:, c_k:c_v],
        mine[:, c_v:c_s],
        mine[:, c_o:],
        mine[:, c_s + n_experts + 1],
        mine[:, c_s : c_s + n_experts],
        gate_mine,
        up_mine,
        down_mine,
    )


def solution(mesh):
    both = ("dp", "expert")
    return jax.shard_map(
        on_device,
        mesh=mesh,
        in_specs=(
            P(both, None),
            P("dp", None),
            P("dp", None),
            P(both, None),
            P(both),
            P(both, None),
            P(both, None),
            P(both, None),
            P(both, None),
            P(both),
            P(both, None),
            P("expert", "dp", None),
            P("expert", "dp", None),
            P("expert", "dp", None),
            P(both, None),
        ),
        out_specs=(
            P(both, None),
            P(both, None),
            P(both),
            P(both, None),
            P(both, None),
            P(both, None),
            P(both, None),
            P(both),
            P(both, None),
            P("expert", "dp", None),
            P("expert", "dp", None),
            P("expert", "dp", None),
        ),
        check_vma=False,
    )
```

```python
import functools
import math

import jax
import jax.numpy as jnp
from jax import lax
from jax.experimental import pallas as pl
from jax.experimental.pallas import tpu as pltpu
from jax.sharding import PartitionSpec as P

QUERY_HEADS = 12
KEY_VALUE_HEADS = 2
HEAD_SIZE = 128


EPSILON = 1e-06
ROPE_BASE = 10000.0
MASKED_SCORE = -1e30
BF = jnp.bfloat16
F32 = jnp.float32


def rms_scale(values):
    return lax.rsqrt(jnp.mean(values * values, axis=-1, keepdims=True) + EPSILON)


def rope_tables(positions, half_size):
    angle_steps = lax.broadcasted_iota(F32, (half_size,), 0)
    frequency = jnp.exp(angle_steps * (-math.log(ROPE_BASE) / half_size))
    angles = positions.astype(F32)[:, None] * frequency
    return (jnp.cos(angles)[:, None, :], jnp.sin(angles)[:, None, :])


def apply_rotation(values, cosine_table, sine_table):
    half_size = values.shape[-1] // 2
    first = values[..., :half_size]
    second = values[..., half_size:]
    return jnp.concatenate(
        [first * cosine_table - second * sine_table, second * cosine_table + first * sine_table],
        axis=-1,
    )


def reverse_rotation(grads_in, cosine_table, sine_table):
    return apply_rotation(grads_in, cosine_table, -sine_table)


def seq_layout(lengths, seq_order):
    count_seq = lengths.shape[1]
    picked = seq_order[0][:, None] == lax.broadcasted_iota(jnp.int32, (count_seq, count_seq), 1)
    ordered = jnp.sum(jnp.where(picked, lengths[0][None, :], 0), axis=1)
    return (ordered, jnp.cumsum(ordered))


def seq_place(positions, ordered, seq_ends):
    passed = seq_ends[None, :] <= positions[:, None]
    sequence_index = jnp.sum(passed.astype(jnp.int32), axis=1)
    starts = jnp.sum(jnp.where(passed, ordered[None, :], 0), axis=1)
    return (sequence_index, positions - starts)


def block_scores(
    query_rows, key_portion, query_seq, query_stream, key_seq, key_stream, score_scale
):
    raw_scores = (
        jnp.einsum("tkrd,skd->krts", query_rows, key_portion, preferred_element_type=F32)
        * score_scale
    )
    allowed = (query_seq[:, None] == key_seq[None, :]) & (
        key_stream[None, :] <= query_stream[:, None]
    )
    return jnp.where(allowed, raw_scores, MASKED_SCORE)


def norm_backward(grad_normed, unit_values, inv_scale, gain_float):
    scaled = grad_normed * gain_float
    gain_grad = jnp.sum(grad_normed * unit_values, axis=0)
    input_grad = inv_scale * (
        scaled - unit_values * jnp.mean(scaled * unit_values, axis=-1, keepdims=True)
    )
    return (gain_grad, input_grad)


def dot(a, b):
    return jnp.dot(a, b, preferred_element_type=F32)


def dot_nt(a, b):
    return jnp.einsum("ac,bc->ab", a, b, preferred_element_type=F32)


def dot_tn(a, b):
    return jnp.einsum("ta,tb->ab", a, b, preferred_element_type=F32)


def on_device(
    tokens,
    lengths,
    seq_order,
    routes,
    norm_attn,
    w_query,
    key_projection,
    value_projection,
    w_out,
    norm_moe,
    w_router,
    w_gate,
    w_up,
    w_down,
    cotangent,
):
    token_count, width = tokens.shape
    n_experts = w_router.shape[1]
    rows = w_query.shape[0]
    group_size = lax.axis_size("expert")
    my_index = lax.axis_index("expert")
    query_per_key_heads = QUERY_HEADS // KEY_VALUE_HEADS
    kv_width = KEY_VALUE_HEADS * HEAD_SIZE
    q_width = QUERY_HEADS * HEAD_SIZE
    score_scale = 1.0 / math.sqrt(HEAD_SIZE)
    group_tokens = token_count * group_size

    small = jnp.concatenate(
        [
            w_router,
            norm_attn[:, None],
            norm_moe[:, None],
            jnp.zeros((rows, 128 - n_experts - 2), BF),
        ],
        axis=1,
    )
    pack = jnp.concatenate([w_query, key_projection, value_projection, small, w_out], axis=1)
    gate_w = lax.all_gather(w_gate[0], "dp", axis=0, tiled=True)
    up_w = lax.all_gather(w_up[0], "dp", axis=0, tiled=True)
    down_w = lax.all_gather(w_down[0], "dp", axis=0, tiled=True)
    pack = lax.all_gather(pack, ("dp", "expert"), axis=0, tiled=True)
    cot_all = lax.all_gather(cotangent, "expert", axis=0, tiled=True)
    c_k = q_width
    c_v = c_k + kv_width
    c_s = c_v + kv_width
    c_o = c_s + 128
    query_w = pack[:, :c_k]
    key_w = pack[:, c_k:c_v]
    value_w = pack[:, c_v:c_s]
    router_w = pack[:, c_s : c_s + n_experts]
    gain_one = pack[:, c_s + n_experts].astype(F32)
    gain_two = pack[:, c_s + n_experts + 1].astype(F32)
    out_w = pack[:, c_o:]

    seq_lens, seq_ends = seq_layout(lengths, seq_order)
    my_stream = lax.broadcasted_iota(jnp.int32, (token_count,), 0) * group_size + my_index
    query_seq, query_rel = seq_place(my_stream, seq_lens, seq_ends)
    all_rows = lax.broadcasted_iota(jnp.int32, (group_tokens,), 0)
    key_stream = all_rows % token_count * group_size + all_rows // token_count
    key_seq = seq_place(key_stream, seq_lens, seq_ends)[0]
    block_row_count = math.gcd(group_tokens, 512)
    block_count = group_tokens // block_row_count
    cosine_table, sine_table = rope_tables(query_rel, HEAD_SIZE // 2)
    inputs_float = tokens.astype(F32)
    inv_one = rms_scale(inputs_float)
    unit_one = inputs_float * inv_one
    normed_one = (unit_one * gain_one).astype(BF)
    query_pre = dot(normed_one, query_w)
    key_pre = dot(normed_one, key_w)
    value_pre = dot(normed_one, value_w)
    rotated_queries = (
        apply_rotation(
            query_pre.reshape(token_count, QUERY_HEADS, HEAD_SIZE), cosine_table, sine_table
        )
        .astype(BF)
        .reshape(token_count, KEY_VALUE_HEADS, query_per_key_heads, HEAD_SIZE)
    )
    rotated_keys = apply_rotation(
        key_pre.reshape(token_count, KEY_VALUE_HEADS, HEAD_SIZE),
        cosine_table,
        sine_table,
    ).astype(BF)
    key_value = jnp.concatenate(
        [rotated_keys.reshape(token_count, kv_width), value_pre.astype(BF)],
        axis=1,
    )
    gathered = lax.all_gather(key_value, "expert", axis=0, tiled=True)
    key_blocks = (
        gathered.reshape(block_count, block_row_count, 2 * kv_width),
        key_seq.reshape(block_count, block_row_count),
        key_stream.reshape(block_count, block_row_count),
    )

    def stats_step(carry, blocks):
        run_max, run_sum = carry
        key_value_block, seq_block, stream_block = blocks
        key_portion = key_value_block[:, :kv_width].reshape(-1, KEY_VALUE_HEADS, HEAD_SIZE)
        scores = block_scores(
            rotated_queries, key_portion, query_seq, my_stream, seq_block, stream_block, score_scale
        )
        new_max = jnp.maximum(run_max, jnp.max(scores, axis=-1))
        run_sum = run_sum * jnp.exp(run_max - new_max) + jnp.sum(
            jnp.exp(scores - new_max[..., None]), axis=-1
        )
        return ((new_max, run_sum), None)

    initial_maximum = jnp.full(
        (KEY_VALUE_HEADS, query_per_key_heads, token_count), MASKED_SCORE, F32
    )
    (row_max, row_sum), unused = lax.scan(
        stats_step, (initial_maximum, jnp.zeros_like(initial_maximum)), key_blocks
    )
    log_total = row_max + jnp.log(row_sum)

    def value_step(summed, blocks):
        key_value_block, seq_block, stream_block = blocks
        key_portion = key_value_block[:, :kv_width].reshape(-1, KEY_VALUE_HEADS, HEAD_SIZE)
        value_portion = key_value_block[:, kv_width:].reshape(-1, KEY_VALUE_HEADS, HEAD_SIZE)
        scores = block_scores(
            rotated_queries, key_portion, query_seq, my_stream, seq_block, stream_block, score_scale
        )
        low_chances = jnp.exp(scores - log_total[..., None]).astype(BF)
        summed = summed + jnp.einsum(
            "krts,skd->tkrd", low_chances, value_portion, preferred_element_type=F32
        )
        return (summed, None)

    empty_head_state = jnp.zeros(
        (token_count, KEY_VALUE_HEADS, query_per_key_heads, HEAD_SIZE), F32
    )
    attended, unused = lax.scan(value_step, empty_head_state, key_blocks)
    attended_low = attended.reshape(token_count, q_width).astype(BF)
    middle = inputs_float + dot(attended_low, out_w)
    inv_two = rms_scale(middle)
    unit_two = middle * inv_two
    normed_two = (unit_two * gain_two).astype(BF)

    logits = dot(normed_two, router_w)
    choose = jnp.any(
        routes[:, :, None] == lax.broadcasted_iota(jnp.int32, (1, 1, n_experts), 2), axis=1
    )
    top_logit = jnp.max(jnp.where(choose, logits, -jnp.inf), axis=1, keepdims=True)
    spread = jnp.where(choose, jnp.exp(jnp.minimum(logits - top_logit, 0.0)), 0.0)
    gates = spread / jnp.sum(spread, axis=1, keepdims=True)

    normed_all = lax.all_gather(normed_two, "expert", axis=0, tiled=True)
    gates_all = lax.all_to_all(
        gates.T.reshape(n_experts, 1, token_count), "expert", split_axis=0, concat_axis=1, tiled=True
    )
    gate_col = gates_all.reshape(group_tokens, 1)

    gate_pre = dot(normed_all, gate_w)
    up_pre = dot(normed_all, up_w)
    sig = jax.nn.sigmoid(gate_pre)
    silu = gate_pre * sig
    hidden = (silu * up_pre).astype(BF)
    returned = dot(hidden, down_w).astype(BF).astype(F32)
    cot_float = cot_all.astype(F32)
    grad_gates = jnp.sum(cot_float * returned, axis=1)
    weighted = (gate_col * returned).astype(BF)
    grad_returned = (gate_col * cot_float).astype(BF)
    grad_hidden = dot_nt(grad_returned, down_w)
    grad_gate_pre = (grad_hidden * up_pre * sig * (1.0 + gate_pre * (1.0 - sig))).astype(BF)
    grad_up_pre = (grad_hidden * silu).astype(BF)
    grad_row = (dot_nt(grad_gate_pre, gate_w) + dot_nt(grad_up_pre, up_w)).astype(BF)
    down_grad = dot_tn(hidden, grad_returned).astype(BF)
    gate_grad = dot_tn(normed_all, grad_gate_pre).astype(BF)
    up_grad = dot_tn(normed_all, grad_up_pre).astype(BF)

    grad_gates = lax.all_to_all(
        grad_gates.reshape(group_size, 1, token_count), "expert", split_axis=0, concat_axis=1, tiled=True
    ).reshape(n_experts, token_count).T
    row_sum_grad = lax.psum_scatter(grad_row, "expert", scatter_dimension=0, tiled=True)
    output = (
        middle + lax.psum_scatter(weighted, "expert", scatter_dimension=0, tiled=True).astype(F32)
    ).astype(BF)

    grad_out = cotangent.astype(F32)
    grad_logits = (
        gates * (grad_gates - jnp.sum(gates * grad_gates, axis=1, keepdims=True))
    ).astype(BF)
    router_grad = dot_tn(normed_two, grad_logits)
    grad_normed_two = dot_nt(grad_logits, router_w) + row_sum_grad.astype(F32)
    gain_two_grad, grad_middle = norm_backward(grad_normed_two, unit_two, inv_two, gain_two)
    grad_middle = grad_out + grad_middle
    grad_mixed = grad_middle.astype(BF)
    out_grad = dot_tn(attended_low, grad_mixed)
    grad_attended = dot_nt(grad_mixed, out_w).astype(BF)
    head_gradient = grad_attended.reshape(
        token_count, KEY_VALUE_HEADS, query_per_key_heads, HEAD_SIZE
    )
    row_dot = jnp.transpose(jnp.sum(head_gradient.astype(F32) * attended, axis=-1), (1, 2, 0))

    def grad_step(query_grad, blocks):
        key_value_block, seq_block, stream_block = blocks
        key_portion = key_value_block[:, :kv_width].reshape(-1, KEY_VALUE_HEADS, HEAD_SIZE)
        value_portion = key_value_block[:, kv_width:].reshape(-1, KEY_VALUE_HEADS, HEAD_SIZE)
        scores = block_scores(
            rotated_queries, key_portion, query_seq, my_stream, seq_block, stream_block, score_scale
        )
        chances = jnp.exp(scores - log_total[..., None])
        low_chances = chances.astype(BF)
        grad_chances = jnp.einsum(
            "tkrd,skd->krts", head_gradient, value_portion, preferred_element_type=F32
        )
        grad_scores = (chances * (grad_chances - row_dot[..., None])).astype(BF)
        query_grad = query_grad + jnp.einsum(
            "krts,skd->tkrd", grad_scores, key_portion, preferred_element_type=F32
        )
        key_terms = (
            jnp.einsum("krts,tkrd->skd", grad_scores, rotated_queries, preferred_element_type=F32)
            * score_scale
        )
        value_terms = jnp.einsum(
            "krts,tkrd->skd", low_chances, head_gradient, preferred_element_type=F32
        )
        return (query_grad, (key_terms.astype(BF), value_terms.astype(BF)))

    query_grad, (key_terms, value_terms) = lax.scan(grad_step, empty_head_state, key_blocks)
    query_grad = query_grad * score_scale
    kv_terms = jnp.concatenate(
        [key_terms.reshape(group_tokens, kv_width), value_terms.reshape(group_tokens, kv_width)],
        axis=1,
    )
    kv_mine = lax.psum_scatter(kv_terms, "expert", scatter_dimension=0, tiled=True)
    grad_query_pre = (
        reverse_rotation(
            query_grad.reshape(token_count, QUERY_HEADS, HEAD_SIZE), cosine_table, sine_table
        )
        .reshape(token_count, q_width)
        .astype(BF)
    )
    grad_key_pre = (
        reverse_rotation(
            kv_mine[:, :kv_width].astype(F32).reshape(token_count, KEY_VALUE_HEADS, HEAD_SIZE),
            cosine_table,
            sine_table,
        )
        .reshape(token_count, kv_width)
        .astype(BF)
    )
    grad_qkv = jnp.concatenate([grad_query_pre, grad_key_pre, kv_mine[:, kv_width:]], axis=1)
    grad_normed_one = dot_nt(grad_qkv, pack[:, :c_s])
    qkv_grad = dot_tn(normed_one, grad_qkv)
    gain_one_grad, grad_input = norm_backward(grad_normed_one, unit_one, inv_one, gain_one)
    tokens_grad = (grad_middle + grad_input).astype(BF)
    small_grad = jnp.concatenate(
        [
            router_grad,
            gain_one_grad[:, None],
            gain_two_grad[:, None],
            jnp.zeros((width, 128 - n_experts - 2), F32),
        ],
        axis=1,
    )
    pack_grad = jnp.concatenate(
        [qkv_grad.astype(BF), small_grad.astype(BF), out_grad.astype(BF)], axis=1
    )
    mine = lax.psum_scatter(pack_grad, ("dp", "expert"), scatter_dimension=0, tiled=True)
    mine = mine.astype(F32)
    gate_mine, up_mine, down_mine = (
        lax.psum_scatter(grad, "dp", scatter_dimension=0, tiled=True).astype(F32)[None]
        for grad in (gate_grad, up_grad, down_grad)
    )
    return (
        output,
        tokens_grad,
        mine[:, c_s + n_experts],
        mine[:, :c_k],
        mine[:, c_k:c_v],
        mine[:, c_v:c_s],
        mine[:, c_o:],
        mine[:, c_s + n_experts + 1],
        mine[:, c_s : c_s + n_experts],
        gate_mine,
        up_mine,
        down_mine,
    )


MESH_ID = pl.DeviceIdType.MESH
ANY = pl.ANY
LOG2E = math.log2(math.e)


class Place:
    def __init__(self):
        d = lax.axis_index("dp")
        e = lax.axis_index("expert")
        core = lax.rem(e, 2)
        x = lax.rem(lax.div(e, 2), 2)
        y = lax.div(e, 4)
        self.d, self.e, self.core = d, e, core
        self.chip = lax.div(e, 2)
        self.e_s = e + 1 - 2 * core
        self.e_x = e + 2 - 4 * x
        self.e_y = e + 4 - 8 * y
        self.e_d = self.e_x + 4 - 8 * y
        self.chip_x = self.chip + 1 - 2 * x
        self.chip_y = self.chip + 2 - 4 * y
        self.chip_d = self.chip_x + 2 - 4 * y
        self.sib = (d, self.e_s)
        self.nx = (d, self.e_x)
        self.ny = (d, self.e_y)
        half = lax.div(d, 2)
        odd = lax.rem(d, 2)
        self.pair = (2 * half + 1 - odd, e)
        self.cross = (3 - d, e)
        self.inner = (d == 1) | (d == 2)
        self.order = (d, 2 * half + 1 - odd, 2 - half, 3 - 3 * half)

    def greet(self):
        barrier = pltpu.get_barrier_semaphore()
        for other in (self.sib, self.nx, self.ny, self.pair):
            pl.semaphore_signal(barrier, inc=1, device_id=other, device_id_type=MESH_ID)

        @pl.when(self.inner)
        def _():
            pl.semaphore_signal(barrier, inc=1, device_id=self.cross, device_id_type=MESH_ID)
            pl.semaphore_wait(barrier, 5)

        @pl.when(jnp.logical_not(self.inner))
        def _():
            pl.semaphore_wait(barrier, 4)


def rcopy(src, dst, send_sem, recv_sem, device):
    return pltpu.make_async_remote_copy(
        src_ref=src,
        dst_ref=dst,
        send_sem=send_sem,
        recv_sem=recv_sem,
        device_id=device,
        device_id_type=MESH_ID,
    )


class PlaneGather:
    def __init__(self, at, blk, half, send, recv):
        self.at, self.blk, self.half, self.send, self.recv = at, blk, half, send, recv

    def push(self, ref, target, slot_send, slot_recv, src=None):
        rcopy(
            ref if src is None else src, ref, self.send(slot_send), self.recv(slot_recv), target
        ).start()

    def await_(self, ref, slot):
        rcopy(ref, ref, self.send(0), self.recv(slot), self.at.sib).wait_recv()

    def sent(self, ref, slot):
        rcopy(ref, ref, self.send(slot), self.recv(0), self.at.sib).wait_send()

    def start(self, src=None):
        at = self.at
        own = self.blk(at.e)
        self.push(own, at.nx, 0, 0, src)
        self.push(own, at.ny, 1, 1, src)
        self.push(own, at.sib, 2, 4, src)

    def on_x(self):
        at = self.at
        got = self.blk(at.e_x)
        self.await_(got, 0)
        self.push(self.half(at.e_x, 0), at.ny, 3, 3)
        self.push(got, at.sib, 4, 5)

    def on_y(self):
        at = self.at
        got = self.blk(at.e_y)
        self.await_(got, 1)
        self.push(self.half(at.e_y, 1), at.nx, 5, 2)
        self.push(got, at.sib, 6, 6)

    def on_d(self):
        at = self.at
        self.await_(self.half(at.e_d, 1), 2)
        self.await_(self.half(at.e_d, 0), 3)
        self.push(self.blk(at.e_d), at.sib, 7, 7)

    def on_s(self):
        at = self.at
        turn = at.e_s - at.e
        self.await_(self.blk(at.e_s), 4)
        self.await_(self.blk(at.e_x + turn), 5)
        self.await_(self.blk(at.e_y + turn), 6)
        self.await_(self.blk(at.e_d + turn), 7)

    def drain(self):
        at = self.at
        whole = self.blk(at.e)
        for slot in (0, 1, 2, 4, 6, 7):
            self.sent(whole, slot)
        self.sent(self.half(at.e, 0), 3)
        self.sent(self.half(at.e, 1), 5)


class LineGather:
    def __init__(self, at, blk, send, recv):
        self.at, self.blk, self.send, self.recv = at, blk, send, recv

    def start(self, src=None):
        at = self.at
        own = self.blk(at.d)
        from_ = own if src is None else src
        rcopy(from_, own, self.send(0), self.recv(1), at.pair).start()

        @pl.when(at.inner)
        def _():
            rcopy(from_, own, self.send(1), self.recv(2), at.cross).start()

    def on(self, k):
        at = self.at
        got = self.blk(at.order[k])
        rcopy(got, got, self.send(0), self.recv(k), at.pair).wait_recv()

        @pl.when(at.inner)
        def _():
            if k == 1:
                rcopy(got, got, self.send(2), self.recv(3), at.cross).start()
            else:
                rcopy(got, got, self.send(k + 1), self.recv(k), at.pair).start()

    def drain(self):
        at = self.at
        own = self.blk(at.d)
        rcopy(own, own, self.send(0), self.recv(0), at.pair).wait_send()

        @pl.when(at.inner)
        def _():
            for slot in (1, 2, 3, 4):
                rcopy(own, own, self.send(slot), self.recv(0), at.pair).wait_send()


def rows_of(ref, start, size):
    return ref.at[pl.ds(pl.multiple_of(start, 16), size)]


def stream_facts(lens_ref, order_ref, token_count, group_size, e):
    count = lens_ref.shape[1]
    stream = lax.broadcasted_iota(jnp.int32, (token_count, 128), 0) * group_size + e
    begin = jnp.zeros_like(stream)
    end = jnp.int32(0)
    for j in range(count):
        size = jnp.int32(0)
        for i in range(count):
            size = size + jnp.where(order_ref[0, j] == i, lens_ref[0, i], 0)
        end = end + size
        begin = begin + jnp.where(stream >= end, size, 0)
    return stream, begin, stream - begin


def rotary(relative):
    lane = lax.rem(lax.broadcasted_iota(jnp.int32, relative.shape, 1), HEAD_SIZE // 2)
    frequency = jnp.exp(lane.astype(F32) * (-math.log(ROPE_BASE) / (HEAD_SIZE // 2)))
    angles = relative.astype(F32) * frequency
    first = lax.broadcasted_iota(jnp.int32, relative.shape, 1) < HEAD_SIZE // 2
    sine = jnp.sin(angles)
    return jnp.cos(angles), jnp.where(first, -sine, sine)


def swap_halves(values):
    return pltpu.roll(values, HEAD_SIZE // 2, 1)


TILE = 64


def tiles_of(i):
    return range(max(0, i - 2), i + 1)


def tile_bias(i, r, stream, begin, group_size):
    wide = TILE * group_size
    j = lax.broadcasted_iota(jnp.int32, (TILE, wide), 1)
    key = (r * TILE + lax.rem(j, TILE)) * group_size + lax.div(j, TILE)
    ok = key >= begin[i * TILE : (i + 1) * TILE, :1]
    if r == i:
        ok = ok & (key <= stream[i * TILE : (i + 1) * TILE, :1])
    return jnp.where(ok, 0.0, MASKED_SCORE)


def dot_nn(a, b):
    return lax.dot_general(a, b, (((1,), (0,)), ((), ())), preferred_element_type=F32)


def dot_bt(a, b):
    return lax.dot_general(a, b, (((1,), (1,)), ((), ())), preferred_element_type=F32)


def dot_at(a, b):
    return lax.dot_general(a, b, (((0,), (0,)), ((), ())), preferred_element_type=F32)


def column_as_row(small, lane):
    pick = (lax.broadcasted_iota(jnp.int32, (8, 128), 1) == lane).astype(F32).astype(BF)
    return dot_bt(pick, small)[:1]


def front_kernel(
    n_experts,
    lens_ref,
    order_ref,
    tok_ref,
    routes_ref,
    pack_ref,
    wo_ref,
    gw_ref,
    uw_ref,
    dw_ref,
    cot_ref,
    x_all,
    c_all,
    gw_all,
    uw_all,
    dw_all,
    pack_out,
    wo_out,
    kv_out,
    q_out,
    att_out,
    lse_out,
    mid_out,
    pack_all,
    wo_all,
    kv_all,
    unit_ref,
    acc_ref,
    pay_ref,
    s_ref,
    ag_send,
    ag_recv,
    z_send,
    z_recv,
    local,
):
    at = Place()
    at.greet()
    tokens, width = tok_ref.shape
    shard = pack_ref.shape[0]
    group = 8
    kv_width = KEY_VALUE_HEADS * HEAD_SIZE
    q_width = QUERY_HEADS * HEAD_SIZE
    qkv = q_width + 2 * kv_width
    per_kv = QUERY_HEADS // KEY_VALUE_HEADS
    chunk = shard * group
    cut_a = 9 * 128
    cut_b = wo_ref.shape[1] // 2
    items = {}

    def add_item(name, blk, half):
        n = len(items)
        items[name] = PlaneGather(
            at, blk, half, lambda k, n=n: ag_send.at[n, k], lambda k, n=n: ag_recv.at[n, k]
        )

    def add_weight(name, ref, z, cut):
        wide = ref.shape[1]

        def place(e):
            return pl.ds(pl.multiple_of(z * chunk + e * shard, 16), shard)

        def half(e, h):
            return ref.at[place(e), pl.ds(0, cut) if h == 0 else pl.ds(cut, wide - cut)]

        add_item(name, lambda e: ref.at[place(e)], half)

    for k in range(4):
        add_weight(("a", k), pack_all, at.order[k], cut_a)
    for k in range(4):
        add_weight(("b", k), wo_all, at.order[k], cut_b)
    add_item("kv", lambda e: kv_all.at[e], lambda e, h: kv_all.at[e, :, pl.ds(h * kv_width, kv_width)])
    part = tokens // 2
    for name, ref, cut in (("x", x_all, 7 * 128), ("c", c_all, width // 2)):
        wide = ref.shape[2]
        for k in range(2):
            rows = pl.ds(k * part, part)

            def half(e, h, ref=ref, rows=rows, cut=cut, wide=wide):
                return ref.at[e, rows, pl.ds(0, cut) if h == 0 else pl.ds(cut, wide - cut)]

            add_item((name, k), lambda e, ref=ref, rows=rows: ref.at[e, rows], half)

    lines = {}

    def add_line(name, ref, size, start):
        n = len(lines)
        lines[name] = LineGather(
            at,
            lambda z: rows_of(ref, start(z), size),
            lambda k, n=n: z_send.at[n, k],
            lambda k, n=n: z_recv.at[n, k],
        )

    add_line("a", pack_all, shard, lambda z: z * chunk + at.e * shard)
    add_line("b", wo_all, shard, lambda z: z * chunk + at.e * shard)
    for name, ref, src in (("g", gw_all, gw_ref), ("u", uw_all, uw_ref), ("d", dw_all, dw_ref)):
        size = src.shape[0]
        add_line(name, ref, size, lambda z, size=size: z * size)

    own_a = rows_of(pack_all, at.d * chunk + at.e * shard, shard)
    own_b = rows_of(wo_all, at.d * chunk + at.e * shard, shard)
    copies = [
        pltpu.make_async_copy(pack_ref, own_a, local.at[0]),
        pltpu.make_async_copy(wo_ref, own_b, local.at[1]),
    ]
    for n, (name, src) in enumerate((("g", gw_ref), ("u", uw_ref), ("d", dw_ref))):
        copies.append(pltpu.make_async_copy(src, lines[name].blk(at.d), local.at[2 + n]))
    for k in range(2):
        rows = pl.ds(k * part, part)
        copies.append(
            pltpu.make_async_copy(cot_ref.at[rows], c_all.at[at.e, rows], local.at[5 + k])
        )

    lines["a"].start(pack_ref)
    items["a", 0].start(pack_ref)
    lines["b"].start(wo_ref)
    for copy in copies:
        copy.start()

    tok = tok_ref[...].astype(F32)
    scale_one = lax.rsqrt(jnp.mean(tok * tok, axis=1, keepdims=True) + EPSILON)
    unit_ref[...] = tok * scale_one
    stream, begin, relative = stream_facts(lens_ref, order_ref, tokens, group, at.e)
    cosine, sine = rotary(relative)
    acc_ref[...] = jnp.zeros_like(acc_ref)
    copies[0].wait()
    copies[1].wait()

    def consume(k):
        z = at.order[k]
        place = pl.ds(pl.multiple_of(z * chunk, 128), chunk)
        gain = column_as_row(pack_all[place, qkv:], n_experts)
        normed = (unit_ref[:, place] * gain).astype(BF)
        acc_ref[...] += dot_nn(normed, pack_all[place, :qkv])

    lines["a"].on(1)
    items["a", 1].start()
    items["a", 0].on_x()
    items["a", 0].on_y()
    lines["g"].start(gw_ref)
    items["a", 0].on_d()
    lines["a"].on(2)
    items["a", 2].start()
    items["a", 1].on_x()
    items["a", 1].on_y()
    items["a", 0].on_s()
    consume(0)
    lines["a"].on(3)
    items["a", 3].start()
    lines["b"].on(1)
    lines["u"].start(uw_ref)
    lines["d"].start(dw_ref)
    items["a", 1].on_d()
    items["a", 2].on_x()
    items["a", 2].on_y()
    items["a", 1].on_s()
    consume(1)
    lines["b"].on(2)
    items["a", 2].on_d()
    items["a", 3].on_x()
    items["a", 3].on_y()
    items["b", 0].start()
    items["a", 2].on_s()
    consume(2)
    lines["b"].on(3)
    items["a", 3].on_d()
    items["a", 3].on_s()
    consume(3)
    keep = [
        pltpu.make_async_copy(pack_all, pack_out, local.at[7]),
    ]
    keep[0].start()

    def turned(col):
        v = acc_ref[:, col : col + HEAD_SIZE]
        return (v * cosine + swap_halves(v) * sine).astype(BF)

    for h in range(KEY_VALUE_HEADS):
        kv_all[at.e, :, h * HEAD_SIZE : (h + 1) * HEAD_SIZE] = turned(q_width + h * HEAD_SIZE)
    kv_all[at.e, :, kv_width:] = acc_ref[:, q_width + kv_width :].astype(BF)
    items["kv"].start()
    for h in range(QUERY_HEADS):
        q_out[h] = turned(h * HEAD_SIZE)
    items["b", 0].on_x()
    items["b", 0].on_y()
    items["b", 1].start()
    items["kv"].on_x()
    items["kv"].on_y()
    items["b", 0].on_d()
    items["b", 2].start()
    items["kv"].on_d()
    items["kv"].on_s()
    keep.append(pltpu.make_async_copy(kv_all, kv_out, local.at[8]))
    keep[1].start()

    def step_b(n):
        if n == 0:
            items["b", 1].on_x()
            items["b", 1].on_y()
            items["b", 3].start()
        elif n == 1:
            items["b", 1].on_d()
            items["b", 2].on_x()
            items["b", 2].on_y()
        elif n == 2:
            items["b", 2].on_d()
            items["b", 3].on_x()
            items["b", 3].on_y()
        elif n == 3:
            items["b", 3].on_d()

    factor = LOG2E / math.sqrt(HEAD_SIZE)
    wide = TILE * group
    for i in range(tokens // TILE):
        step_b(i)
        first = tiles_of(i)[0]
        biases = [tile_bias(i, r, stream, begin, group) for r in tiles_of(i)]
        here = slice(i * TILE, (i + 1) * TILE)
        for g in range(KEY_VALUE_HEADS):
            queries = q_out[g * per_kv : (g + 1) * per_kv, here, :].reshape(per_kv * TILE, HEAD_SIZE)
            top = None
            for r in tiles_of(i):
                keys = kv_all[:, r * TILE : (r + 1) * TILE, g * HEAD_SIZE : (g + 1) * HEAD_SIZE]
                s = dot_bt(queries, keys.reshape(wide, HEAD_SIZE)) * factor
                s = s.reshape(per_kv, TILE, wide) + biases[r - first][None]
                s = s.reshape(per_kv * TILE, wide)
                s_ref[:, (r - first) * wide : (r - first + 1) * wide] = s
                high = jnp.max(s, axis=1, keepdims=True)
                top = high if top is None else jnp.maximum(top, high)
            total = None
            mixed = None
            for r in tiles_of(i):
                p = jnp.exp2(s_ref[:, (r - first) * wide : (r - first + 1) * wide] - top)
                values = kv_all[
                    :, r * TILE : (r + 1) * TILE, kv_width + g * HEAD_SIZE : kv_width + (g + 1) * HEAD_SIZE
                ].reshape(wide, HEAD_SIZE)
                row = jnp.sum(p, axis=1, keepdims=True)
                term = dot_nn(p.astype(BF), values)
                total = row if total is None else total + row
                mixed = term if mixed is None else mixed + term
            mixed = mixed / total
            lse_out[g, i] = jnp.broadcast_to(top + jnp.log2(total), (per_kv * TILE, 128))
            for h in range(per_kv):
                col = (g * per_kv + h) * HEAD_SIZE
                att_out[here, col : col + HEAD_SIZE] = mixed[h * TILE : (h + 1) * TILE]

    for name in ("g", "u", "d"):
        lines[name].on(1)
    for k in range(4):
        items["b", k].on_s()
    keep.append(pltpu.make_async_copy(wo_all, wo_out, local.at[9]))
    keep[2].start()
    items["c", 0].start(cot_ref.at[pl.ds(0, part)])
    attended = att_out[...].astype(BF)
    step = 256
    for n in range(width // step):
        cols = slice(n * step, (n + 1) * step)
        mid_out[:, cols] = tok_ref[:, cols].astype(F32) + dot_nn(attended, wo_all[:, cols])
    middle = mid_out[...]
    scale_two = lax.rsqrt(jnp.mean(middle * middle, axis=1, keepdims=True) + EPSILON)
    small = pack_all[:, qkv:]
    normed_two = (middle * scale_two * column_as_row(small, n_experts + 1)).astype(BF)
    pay_ref[:, :width] = normed_two
    logits = dot_nn(normed_two, small)
    lane = lax.broadcasted_iota(jnp.int32, (tokens, 128), 1)
    choose = lane == routes_ref[:, :1]
    for k in range(1, routes_ref.shape[1]):
        choose = choose | (lane == routes_ref[:, k : k + 1])
    top = jnp.max(jnp.where(choose, logits, MASKED_SCORE), axis=1, keepdims=True)
    spread = jnp.where(choose, jnp.exp(jnp.minimum(logits - top, 0.0)), 0.0)
    gates = spread / jnp.sum(spread, axis=1, keepdims=True)
    pay_ref[:, width:] = split_three(gates)
    own_x = [
        pltpu.make_async_copy(
            pay_ref.at[pl.ds(k * part, part)], x_all.at[at.e, pl.ds(k * part, part)], local.at[10 + k]
        )
        for k in range(2)
    ]
    for k in range(2):
        items["x", k].start(pay_ref.at[pl.ds(k * part, part)])
        own_x[k].start()
    for name in ("g", "u", "d"):
        lines[name].on(2)
    items["c", 0].on_x()
    items["c", 0].on_y()
    for k in range(2):
        items["x", k].on_x()
        items["x", k].on_y()
    items["c", 1].start(cot_ref.at[pl.ds(part, part)])
    items["c", 0].on_d()
    for k in range(2):
        items["x", k].on_d()
    items["c", 1].on_x()
    items["c", 1].on_y()
    items["c", 1].on_d()
    for name in ("g", "u", "d"):
        lines[name].on(3)
    for k in range(2):
        items["c", k].on_s()
        items["x", k].on_s()
    for item in items.values():
        item.drain()
    for line in lines.values():
        line.drain()
    for copy in copies[2:] + keep + own_x:
        copy.wait()


def split_three(values):
    high = values.astype(BF).astype(F32)
    mid = (values - high).astype(BF).astype(F32)
    low = values - high - mid
    return (high + pltpu.roll(mid, 32, 1) + pltpu.roll(low, 64, 1)).astype(BF)


def front(lengths, seq_order, tokens, routes, pack, wo, gw, uw, dw, cot, n_experts):
    count, width = tokens.shape
    group, line = 8, 4
    kv_width = KEY_VALUE_HEADS * HEAD_SIZE
    per_kv = QUERY_HEADS // KEY_VALUE_HEADS
    sds = jax.ShapeDtypeStruct
    smem = pl.BlockSpec(memory_space=pltpu.SMEM)
    vmem = pl.BlockSpec(memory_space=pltpu.VMEM)
    hbm = pl.BlockSpec(memory_space=ANY)
    n_items = 13
    return pl.pallas_call(
        functools.partial(front_kernel, n_experts),
        in_specs=[smem, smem] + [vmem] * 8,
        out_specs=(hbm,) * 8 + (vmem,) * 4,
        out_shape=(
            sds((group, count, width + 128), BF),
            sds((group, count, width), BF),
            sds((line * gw.shape[0], gw.shape[1]), BF),
            sds((line * uw.shape[0], uw.shape[1]), BF),
            sds((line * dw.shape[0], dw.shape[1]), BF),
            sds((width, pack.shape[1]), BF),
            sds((width, wo.shape[1]), BF),
            sds((group, count, 2 * kv_width), BF),
            sds((QUERY_HEADS, count, HEAD_SIZE), BF),
            sds((count, QUERY_HEADS * HEAD_SIZE), F32),
            sds((KEY_VALUE_HEADS, count // TILE, per_kv * TILE, 128), F32),
            sds((count, width), F32),
        ),
        scratch_shapes=[
            pltpu.VMEM((width, pack.shape[1]), BF),
            pltpu.VMEM((width, wo.shape[1]), BF),
            pltpu.VMEM((group, count, 2 * kv_width), BF),
            pltpu.VMEM((count, width), F32),
            pltpu.VMEM((count, pack.shape[1] - 128), F32),
            pltpu.VMEM((count, width + 128), BF),
            pltpu.VMEM((per_kv * TILE, 3 * TILE * group), F32),
            pltpu.SemaphoreType.DMA((n_items, 8)),
            pltpu.SemaphoreType.DMA((n_items, 8)),
            pltpu.SemaphoreType.DMA((5, 5)),
            pltpu.SemaphoreType.DMA((5, 4)),
            pltpu.SemaphoreType.DMA((12,)),
        ],
        compiler_params=pltpu.CompilerParams(
            collective_id=1, has_side_effects=True, vmem_limit_bytes=60 * 2**20
        ),
    )(lengths, seq_order, tokens, routes, pack, wo, gw, uw, dw, cot)


def moe_kernel(
    x_ref, c_ref, gw, uw, dw, row_ref, out_ref, gg_ref, ug_ref, dg_ref, gacc, uacc, dacc, yacc, racc
):
    step = pl.program_id(0)
    block = x_ref.shape[0]
    width = c_ref.shape[1]
    e = lax.axis_index("expert")
    lane = lax.broadcasted_iota(jnp.int32, (block, 128), 1)
    mine = (lane == e) | (lane == e + 32) | (lane == e + 64)
    gate = jnp.sum(jnp.where(mine, x_ref[:, width:].astype(F32), 0.0), axis=1, keepdims=True)

    @pl.when(step == 0)
    def _():
        gacc[...] = jnp.zeros_like(gacc)
        uacc[...] = jnp.zeros_like(uacc)
        dacc[...] = jnp.zeros_like(dacc)

    grad_returned = (gate * c_ref[...].astype(F32)).astype(BF)
    x = x_ref[:, :width]
    part = 256
    for f in range(gw.shape[1] // part):
        cols = slice(f * part, (f + 1) * part)
        gate_pre = dot_nn(x, gw[:, cols])
        up_pre = dot_nn(x, uw[:, cols])
        sig = 1.0 / (1.0 + jnp.exp(-gate_pre))
        silu = gate_pre * sig
        hidden = (silu * up_pre).astype(BF)
        grad_hidden = dot_bt(grad_returned, dw[cols, :])
        grad_up = (grad_hidden * silu).astype(BF)
        grad_gate = (grad_hidden * up_pre * sig * (1.0 + gate_pre * (1.0 - sig))).astype(BF)
        y = dot_nn(hidden, dw[cols, :])
        r = dot_bt(grad_gate, gw[:, cols]) + dot_bt(grad_up, uw[:, cols])
        if f == 0:
            yacc[...] = y
            racc[...] = r
        else:
            yacc[...] += y
            racc[...] += r
        dacc[cols, :] += dot_at(hidden, grad_returned)
        gacc[:, cols] += dot_at(x, grad_gate)
        uacc[:, cols] += dot_at(x, grad_up)
    returned = yacc[...].astype(BF).astype(F32)
    grad_gates = jnp.sum(c_ref[...].astype(F32) * returned, axis=1, keepdims=True)
    out_ref[...] = (gate * returned).astype(BF)
    row_ref[:, :width] = racc[...].astype(BF)
    high = grad_gates.astype(BF).astype(F32)
    row_ref[:, width:] = jnp.where(
        lane == e, high, jnp.where(lane == e + 32, grad_gates - high, 0.0)
    ).astype(BF)

    @pl.when(step == pl.num_programs(0) - 1)
    def _():
        gg_ref[...] = gacc[...].astype(BF)
        ug_ref[...] = uacc[...].astype(BF)
        dg_ref[...] = dacc[...].astype(BF)


def moe(x_all, c_all, gw, uw, dw):
    rows, width = c_all.shape
    hid = gw.shape[1]
    block = 512

    def full(*shape):
        return pl.BlockSpec(shape, lambda i: (0, 0), pipeline_mode=pl.Buffered(1))

    def moving(cols):
        return pl.BlockSpec((block, cols), lambda i: (i, 0))

    sds = jax.ShapeDtypeStruct
    return pl.pallas_call(
        moe_kernel,
        grid=(rows // block,),
        in_specs=[
            moving(width + 128),
            moving(width),
            full(width, hid),
            full(width, hid),
            full(hid, width),
        ],
        out_specs=(
            moving(width + 128),
            moving(width),
            full(width, hid),
            full(width, hid),
            full(hid, width),
        ),
        out_shape=(
            sds((rows, width + 128), BF),
            sds((rows, width), BF),
            sds((width, hid), BF),
            sds((width, hid), BF),
            sds((hid, width), BF),
        ),
        scratch_shapes=[
            pltpu.VMEM((width, hid), F32),
            pltpu.VMEM((width, hid), F32),
            pltpu.VMEM((hid, width), F32),
            pltpu.VMEM((block, width), F32),
            pltpu.VMEM((block, width), F32),
        ],
        compiler_params=pltpu.CompilerParams(vmem_limit_bytes=60 * 2**20),
        cost_estimate=pl.CostEstimate(
            flops=18 * rows * width * hid,
            bytes_accessed=8 * rows * width + 12 * width * hid,
            transcendentals=rows * hid,
        ),
    )(x_all, c_all, gw, uw, dw)


def pack_weights(w_router, norm_attn, norm_moe, w_query, key_projection, value_projection):
    rows, n_experts = w_router.shape
    small = jnp.concatenate(
        [
            w_router,
            norm_attn[:, None],
            norm_moe[:, None],
            jnp.zeros((rows, 128 - n_experts - 2), BF),
        ],
        axis=1,
    )
    return jnp.concatenate([w_query, key_projection, value_projection, small], axis=1)


def on_device_fast(
    tokens,
    lengths,
    seq_order,
    routes,
    norm_attn,
    w_query,
    key_projection,
    value_projection,
    w_out,
    norm_moe,
    w_router,
    w_gate,
    w_up,
    w_down,
    cotangent,
):
    token_count, width = tokens.shape
    n_experts = w_router.shape[1]
    group_size = lax.axis_size("expert")
    my_index = lax.axis_index("expert")
    per_kv = QUERY_HEADS // KEY_VALUE_HEADS
    kv_width = KEY_VALUE_HEADS * HEAD_SIZE
    q_width = QUERY_HEADS * HEAD_SIZE
    score_scale = 1.0 / math.sqrt(HEAD_SIZE)
    group_tokens = token_count * group_size
    pack = pack_weights(w_router, norm_attn, norm_moe, w_query, key_projection, value_projection)
    x_all, c_all, gw, uw, dw, pack, wo, kv_all, q_rot, attended, lse, middle = front(
        lengths,
        seq_order,
        tokens,
        routes,
        pack,
        w_out,
        w_gate[0],
        w_up[0],
        w_down[0],
        cotangent,
        n_experts,
    )
    grad_row, weighted, gate_grad, up_grad, down_grad = moe(
        x_all.reshape(group_tokens, width + 128), c_all.reshape(group_tokens, width), gw, uw, dw
    )
    c_k = q_width
    c_v = c_k + kv_width
    c_s = c_v + kv_width
    router_w = pack[:, c_s : c_s + n_experts]
    gain_one = pack[:, c_s + n_experts].astype(F32)
    gain_two = pack[:, c_s + n_experts + 1].astype(F32)
    seq_lens, seq_ends = seq_layout(lengths, seq_order)
    my_stream = lax.broadcasted_iota(jnp.int32, (token_count,), 0) * group_size + my_index
    query_seq, query_rel = seq_place(my_stream, seq_lens, seq_ends)
    all_rows = lax.broadcasted_iota(jnp.int32, (group_tokens,), 0)
    key_stream = all_rows % token_count * group_size + all_rows // token_count
    key_seq = seq_place(key_stream, seq_lens, seq_ends)[0]
    cosine_table, sine_table = rope_tables(query_rel, HEAD_SIZE // 2)
    inputs_float = tokens.astype(F32)
    inv_one = rms_scale(inputs_float)
    unit_one = inputs_float * inv_one
    normed_one = (unit_one * gain_one).astype(BF)
    rotated_queries = q_rot.transpose(1, 0, 2).reshape(
        token_count, KEY_VALUE_HEADS, per_kv, HEAD_SIZE
    )
    gathered = kv_all.reshape(group_tokens, 2 * kv_width)
    log_total = (
        lse[..., 0]
        .reshape(KEY_VALUE_HEADS, token_count // TILE, per_kv, TILE)
        .transpose(0, 2, 1, 3)
        .reshape(KEY_VALUE_HEADS, per_kv, token_count)
        / LOG2E
    )
    attended_low = attended.astype(BF)
    attended = attended.reshape(token_count, KEY_VALUE_HEADS, per_kv, HEAD_SIZE)
    inv_two = rms_scale(middle)
    unit_two = middle * inv_two
    own = lax.dynamic_slice_in_dim(x_all, my_index, 1, 0)[0]
    normed_two = own[:, :width]
    ext = own[:, width:].astype(F32)
    gates = ext[:, :n_experts] + ext[:, 32 : 32 + n_experts] + ext[:, 64 : 64 + n_experts]

    row_sum = lax.psum_scatter(grad_row, "expert", scatter_dimension=0, tiled=True)
    row_sum_grad = row_sum[:, :width]
    ext = row_sum[:, width:].astype(F32)
    grad_gates = ext[:, :n_experts] + ext[:, 32 : 32 + n_experts]
    output = (
        middle + lax.psum_scatter(weighted, "expert", scatter_dimension=0, tiled=True).astype(F32)
    ).astype(BF)

    grad_out = cotangent.astype(F32)
    grad_logits = (
        gates * (grad_gates - jnp.sum(gates * grad_gates, axis=1, keepdims=True))
    ).astype(BF)
    router_grad = dot_tn(normed_two, grad_logits)
    grad_normed_two = dot_nt(grad_logits, router_w) + row_sum_grad.astype(F32)
    gain_two_grad, grad_middle = norm_backward(grad_normed_two, unit_two, inv_two, gain_two)
    grad_middle = grad_out + grad_middle
    grad_mixed = grad_middle.astype(BF)
    out_grad = dot_tn(attended_low, grad_mixed)
    head_gradient = (
        dot_nt(grad_mixed, wo).astype(BF).reshape(token_count, KEY_VALUE_HEADS, per_kv, HEAD_SIZE)
    )
    row_dot = jnp.transpose(jnp.sum(head_gradient.astype(F32) * attended, axis=-1), (1, 2, 0))
    key_portion = gathered[:, :kv_width].reshape(-1, KEY_VALUE_HEADS, HEAD_SIZE)
    value_portion = gathered[:, kv_width:].reshape(-1, KEY_VALUE_HEADS, HEAD_SIZE)
    scores = block_scores(
        rotated_queries, key_portion, query_seq, my_stream, key_seq, key_stream, score_scale
    )
    chances = jnp.exp(scores - log_total[..., None])
    grad_chances = jnp.einsum(
        "tkrd,skd->krts", head_gradient, value_portion, preferred_element_type=F32
    )
    grad_scores = (chances * (grad_chances - row_dot[..., None])).astype(BF)
    query_grad = (
        jnp.einsum("krts,skd->tkrd", grad_scores, key_portion, preferred_element_type=F32)
        * score_scale
    )
    key_terms = (
        jnp.einsum("krts,tkrd->skd", grad_scores, rotated_queries, preferred_element_type=F32)
        * score_scale
    )
    value_terms = jnp.einsum(
        "krts,tkrd->skd", chances.astype(BF), head_gradient, preferred_element_type=F32
    )
    kv_terms = jnp.concatenate(
        [
            key_terms.reshape(group_tokens, kv_width).astype(BF),
            value_terms.reshape(group_tokens, kv_width).astype(BF),
        ],
        axis=1,
    )
    kv_mine = lax.psum_scatter(kv_terms, "expert", scatter_dimension=0, tiled=True)
    grad_query_pre = (
        reverse_rotation(
            query_grad.reshape(token_count, QUERY_HEADS, HEAD_SIZE), cosine_table, sine_table
        )
        .reshape(token_count, q_width)
        .astype(BF)
    )
    grad_key_pre = (
        reverse_rotation(
            kv_mine[:, :kv_width].astype(F32).reshape(token_count, KEY_VALUE_HEADS, HEAD_SIZE),
            cosine_table,
            sine_table,
        )
        .reshape(token_count, kv_width)
        .astype(BF)
    )
    grad_qkv = jnp.concatenate([grad_query_pre, grad_key_pre, kv_mine[:, kv_width:]], axis=1)
    grad_normed_one = dot_nt(grad_qkv, pack[:, :c_s])
    qkv_grad = dot_tn(normed_one, grad_qkv)
    gain_one_grad, grad_input = norm_backward(grad_normed_one, unit_one, inv_one, gain_one)
    tokens_grad = (grad_middle + grad_input).astype(BF)
    small_grad = jnp.concatenate(
        [
            router_grad,
            gain_one_grad[:, None],
            gain_two_grad[:, None],
            jnp.zeros((width, 128 - n_experts - 2), F32),
        ],
        axis=1,
    )
    pack_grad = jnp.concatenate(
        [qkv_grad.astype(BF), small_grad.astype(BF), out_grad.astype(BF)], axis=1
    )
    mine = lax.psum_scatter(pack_grad, ("dp", "expert"), scatter_dimension=0, tiled=True)
    mine = mine.astype(F32)
    gate_mine, up_mine, down_mine = (
        lax.psum_scatter(grad, "dp", scatter_dimension=0, tiled=True).astype(F32)[None]
        for grad in (gate_grad, up_grad, down_grad)
    )
    return (
        output,
        tokens_grad,
        mine[:, c_s + n_experts],
        mine[:, :c_k],
        mine[:, c_k:c_v],
        mine[:, c_v:c_s],
        mine[:, c_s + 128 :],
        mine[:, c_s + n_experts + 1],
        mine[:, c_s : c_s + n_experts],
        gate_mine,
        up_mine,
        down_mine,
    )


def solution(mesh):
    both = ("dp", "expert")
    small = mesh.shape["dp"] == 4 and mesh.shape["expert"] == 8
    return jax.shard_map(
        on_device_fast if small else on_device,
        mesh=mesh,
        in_specs=(
            P(both, None),
            P("dp", None),
            P("dp", None),
            P(both, None),
            P(both),
            P(both, None),
            P(both, None),
            P(both, None),
            P(both, None),
            P(both),
            P(both, None),
            P("expert", "dp", None),
            P("expert", "dp", None),
            P("expert", "dp", None),
            P(both, None),
        ),
        out_specs=(
            P(both, None),
            P(both, None),
            P(both),
            P(both, None),
            P(both, None),
            P(both, None),
            P(both, None),
            P(both),
            P(both, None),
            P("expert", "dp", None),
            P("expert", "dp", None),
            P("expert", "dp", None),
        ),
        check_vma=False,
    )
```

```python
import functools
import math

import jax
import jax.numpy as jnp
from jax import lax
from jax.experimental import pallas as pl
from jax.experimental.pallas import tpu as pltpu
from jax.sharding import PartitionSpec as P

QUERY_HEADS = 12
KEY_VALUE_HEADS = 2
HEAD_SIZE = 128


EPSILON = 1e-06
ROPE_BASE = 10000.0
MASKED_SCORE = -1e30
BF = jnp.bfloat16
F32 = jnp.float32


def rms_scale(values):
    return lax.rsqrt(jnp.mean(values * values, axis=-1, keepdims=True) + EPSILON)


def rope_tables(positions, half_size):
    angle_steps = lax.broadcasted_iota(F32, (half_size,), 0)
    frequency = jnp.exp(angle_steps * (-math.log(ROPE_BASE) / half_size))
    angles = positions.astype(F32)[:, None] * frequency
    return (jnp.cos(angles)[:, None, :], jnp.sin(angles)[:, None, :])


def apply_rotation(values, cosine_table, sine_table):
    half_size = values.shape[-1] // 2
    first = values[..., :half_size]
    second = values[..., half_size:]
    return jnp.concatenate(
        [first * cosine_table - second * sine_table, second * cosine_table + first * sine_table],
        axis=-1,
    )


def reverse_rotation(grads_in, cosine_table, sine_table):
    return apply_rotation(grads_in, cosine_table, -sine_table)


def seq_layout(lengths, seq_order):
    count_seq = lengths.shape[1]
    picked = seq_order[0][:, None] == lax.broadcasted_iota(jnp.int32, (count_seq, count_seq), 1)
    ordered = jnp.sum(jnp.where(picked, lengths[0][None, :], 0), axis=1)
    return (ordered, jnp.cumsum(ordered))


def seq_place(positions, ordered, seq_ends):
    passed = seq_ends[None, :] <= positions[:, None]
    sequence_index = jnp.sum(passed.astype(jnp.int32), axis=1)
    starts = jnp.sum(jnp.where(passed, ordered[None, :], 0), axis=1)
    return (sequence_index, positions - starts)


def block_scores(
    query_rows, key_portion, query_seq, query_stream, key_seq, key_stream, score_scale
):
    raw_scores = (
        jnp.einsum("tkrd,skd->krts", query_rows, key_portion, preferred_element_type=F32)
        * score_scale
    )
    allowed = (query_seq[:, None] == key_seq[None, :]) & (
        key_stream[None, :] <= query_stream[:, None]
    )
    return jnp.where(allowed, raw_scores, MASKED_SCORE)


def norm_backward(grad_normed, unit_values, inv_scale, gain_float):
    scaled = grad_normed * gain_float
    gain_grad = jnp.sum(grad_normed * unit_values, axis=0)
    input_grad = inv_scale * (
        scaled - unit_values * jnp.mean(scaled * unit_values, axis=-1, keepdims=True)
    )
    return (gain_grad, input_grad)


def dot(a, b):
    return jnp.dot(a, b, preferred_element_type=F32)


def dot_nt(a, b):
    return jnp.einsum("ac,bc->ab", a, b, preferred_element_type=F32)


def dot_tn(a, b):
    return jnp.einsum("ta,tb->ab", a, b, preferred_element_type=F32)


def on_device(
    tokens,
    lengths,
    seq_order,
    routes,
    norm_attn,
    w_query,
    key_projection,
    value_projection,
    w_out,
    norm_moe,
    w_router,
    w_gate,
    w_up,
    w_down,
    cotangent,
):
    token_count, width = tokens.shape
    n_experts = w_router.shape[1]
    rows = w_query.shape[0]
    group_size = lax.axis_size("expert")
    my_index = lax.axis_index("expert")
    query_per_key_heads = QUERY_HEADS // KEY_VALUE_HEADS
    kv_width = KEY_VALUE_HEADS * HEAD_SIZE
    q_width = QUERY_HEADS * HEAD_SIZE
    score_scale = 1.0 / math.sqrt(HEAD_SIZE)
    group_tokens = token_count * group_size

    small = jnp.concatenate(
        [
            w_router,
            norm_attn[:, None],
            norm_moe[:, None],
            jnp.zeros((rows, 128 - n_experts - 2), BF),
        ],
        axis=1,
    )
    pack = jnp.concatenate([w_query, key_projection, value_projection, small, w_out], axis=1)
    gate_w = lax.all_gather(w_gate[0], "dp", axis=0, tiled=True)
    up_w = lax.all_gather(w_up[0], "dp", axis=0, tiled=True)
    down_w = lax.all_gather(w_down[0], "dp", axis=0, tiled=True)
    pack = lax.all_gather(pack, ("dp", "expert"), axis=0, tiled=True)
    cot_all = lax.all_gather(cotangent, "expert", axis=0, tiled=True)
    c_k = q_width
    c_v = c_k + kv_width
    c_s = c_v + kv_width
    c_o = c_s + 128
    query_w = pack[:, :c_k]
    key_w = pack[:, c_k:c_v]
    value_w = pack[:, c_v:c_s]
    router_w = pack[:, c_s : c_s + n_experts]
    gain_one = pack[:, c_s + n_experts].astype(F32)
    gain_two = pack[:, c_s + n_experts + 1].astype(F32)
    out_w = pack[:, c_o:]

    seq_lens, seq_ends = seq_layout(lengths, seq_order)
    my_stream = lax.broadcasted_iota(jnp.int32, (token_count,), 0) * group_size + my_index
    query_seq, query_rel = seq_place(my_stream, seq_lens, seq_ends)
    all_rows = lax.broadcasted_iota(jnp.int32, (group_tokens,), 0)
    key_stream = all_rows % token_count * group_size + all_rows // token_count
    key_seq = seq_place(key_stream, seq_lens, seq_ends)[0]
    block_row_count = math.gcd(group_tokens, 512)
    block_count = group_tokens // block_row_count
    cosine_table, sine_table = rope_tables(query_rel, HEAD_SIZE // 2)
    inputs_float = tokens.astype(F32)
    inv_one = rms_scale(inputs_float)
    unit_one = inputs_float * inv_one
    normed_one = (unit_one * gain_one).astype(BF)
    query_pre = dot(normed_one, query_w)
    key_pre = dot(normed_one, key_w)
    value_pre = dot(normed_one, value_w)
    rotated_queries = (
        apply_rotation(
            query_pre.reshape(token_count, QUERY_HEADS, HEAD_SIZE), cosine_table, sine_table
        )
        .astype(BF)
        .reshape(token_count, KEY_VALUE_HEADS, query_per_key_heads, HEAD_SIZE)
    )
    rotated_keys = apply_rotation(
        key_pre.reshape(token_count, KEY_VALUE_HEADS, HEAD_SIZE),
        cosine_table,
        sine_table,
    ).astype(BF)
    key_value = jnp.concatenate(
        [rotated_keys.reshape(token_count, kv_width), value_pre.astype(BF)],
        axis=1,
    )
    gathered = lax.all_gather(key_value, "expert", axis=0, tiled=True)
    key_blocks = (
        gathered.reshape(block_count, block_row_count, 2 * kv_width),
        key_seq.reshape(block_count, block_row_count),
        key_stream.reshape(block_count, block_row_count),
    )

    def stats_step(carry, blocks):
        run_max, run_sum = carry
        key_value_block, seq_block, stream_block = blocks
        key_portion = key_value_block[:, :kv_width].reshape(-1, KEY_VALUE_HEADS, HEAD_SIZE)
        scores = block_scores(
            rotated_queries, key_portion, query_seq, my_stream, seq_block, stream_block, score_scale
        )
        new_max = jnp.maximum(run_max, jnp.max(scores, axis=-1))
        run_sum = run_sum * jnp.exp(run_max - new_max) + jnp.sum(
            jnp.exp(scores - new_max[..., None]), axis=-1
        )
        return ((new_max, run_sum), None)

    initial_maximum = jnp.full(
        (KEY_VALUE_HEADS, query_per_key_heads, token_count), MASKED_SCORE, F32
    )
    (row_max, row_sum), unused = lax.scan(
        stats_step, (initial_maximum, jnp.zeros_like(initial_maximum)), key_blocks
    )
    log_total = row_max + jnp.log(row_sum)

    def value_step(summed, blocks):
        key_value_block, seq_block, stream_block = blocks
        key_portion = key_value_block[:, :kv_width].reshape(-1, KEY_VALUE_HEADS, HEAD_SIZE)
        value_portion = key_value_block[:, kv_width:].reshape(-1, KEY_VALUE_HEADS, HEAD_SIZE)
        scores = block_scores(
            rotated_queries, key_portion, query_seq, my_stream, seq_block, stream_block, score_scale
        )
        low_chances = jnp.exp(scores - log_total[..., None]).astype(BF)
        summed = summed + jnp.einsum(
            "krts,skd->tkrd", low_chances, value_portion, preferred_element_type=F32
        )
        return (summed, None)

    empty_head_state = jnp.zeros(
        (token_count, KEY_VALUE_HEADS, query_per_key_heads, HEAD_SIZE), F32
    )
    attended, unused = lax.scan(value_step, empty_head_state, key_blocks)
    attended_low = attended.reshape(token_count, q_width).astype(BF)
    middle = inputs_float + dot(attended_low, out_w)
    inv_two = rms_scale(middle)
    unit_two = middle * inv_two
    normed_two = (unit_two * gain_two).astype(BF)

    logits = dot(normed_two, router_w)
    choose = jnp.any(
        routes[:, :, None] == lax.broadcasted_iota(jnp.int32, (1, 1, n_experts), 2), axis=1
    )
    top_logit = jnp.max(jnp.where(choose, logits, -jnp.inf), axis=1, keepdims=True)
    spread = jnp.where(choose, jnp.exp(jnp.minimum(logits - top_logit, 0.0)), 0.0)
    gates = spread / jnp.sum(spread, axis=1, keepdims=True)

    normed_all = lax.all_gather(normed_two, "expert", axis=0, tiled=True)
    gates_all = lax.all_to_all(
        gates.T.reshape(n_experts, 1, token_count), "expert", split_axis=0, concat_axis=1, tiled=True
    )
    gate_col = gates_all.reshape(group_tokens, 1)

    gate_pre = dot(normed_all, gate_w)
    up_pre = dot(normed_all, up_w)
    sig = jax.nn.sigmoid(gate_pre)
    silu = gate_pre * sig
    hidden = (silu * up_pre).astype(BF)
    returned = dot(hidden, down_w).astype(BF).astype(F32)
    cot_float = cot_all.astype(F32)
    grad_gates = jnp.sum(cot_float * returned, axis=1)
    weighted = (gate_col * returned).astype(BF)
    grad_returned = (gate_col * cot_float).astype(BF)
    grad_hidden = dot_nt(grad_returned, down_w)
    grad_gate_pre = (grad_hidden * up_pre * sig * (1.0 + gate_pre * (1.0 - sig))).astype(BF)
    grad_up_pre = (grad_hidden * silu).astype(BF)
    grad_row = (dot_nt(grad_gate_pre, gate_w) + dot_nt(grad_up_pre, up_w)).astype(BF)
    down_grad = dot_tn(hidden, grad_returned).astype(BF)
    gate_grad = dot_tn(normed_all, grad_gate_pre).astype(BF)
    up_grad = dot_tn(normed_all, grad_up_pre).astype(BF)

    grad_gates = lax.all_to_all(
        grad_gates.reshape(group_size, 1, token_count), "expert", split_axis=0, concat_axis=1, tiled=True
    ).reshape(n_experts, token_count).T
    row_sum_grad = lax.psum_scatter(grad_row, "expert", scatter_dimension=0, tiled=True)
    output = (
        middle + lax.psum_scatter(weighted, "expert", scatter_dimension=0, tiled=True).astype(F32)
    ).astype(BF)

    grad_out = cotangent.astype(F32)
    grad_logits = (
        gates * (grad_gates - jnp.sum(gates * grad_gates, axis=1, keepdims=True))
    ).astype(BF)
    router_grad = dot_tn(normed_two, grad_logits)
    grad_normed_two = dot_nt(grad_logits, router_w) + row_sum_grad.astype(F32)
    gain_two_grad, grad_middle = norm_backward(grad_normed_two, unit_two, inv_two, gain_two)
    grad_middle = grad_out + grad_middle
    grad_mixed = grad_middle.astype(BF)
    out_grad = dot_tn(attended_low, grad_mixed)
    grad_attended = dot_nt(grad_mixed, out_w).astype(BF)
    head_gradient = grad_attended.reshape(
        token_count, KEY_VALUE_HEADS, query_per_key_heads, HEAD_SIZE
    )
    row_dot = jnp.transpose(jnp.sum(head_gradient.astype(F32) * attended, axis=-1), (1, 2, 0))

    def grad_step(query_grad, blocks):
        key_value_block, seq_block, stream_block = blocks
        key_portion = key_value_block[:, :kv_width].reshape(-1, KEY_VALUE_HEADS, HEAD_SIZE)
        value_portion = key_value_block[:, kv_width:].reshape(-1, KEY_VALUE_HEADS, HEAD_SIZE)
        scores = block_scores(
            rotated_queries, key_portion, query_seq, my_stream, seq_block, stream_block, score_scale
        )
        chances = jnp.exp(scores - log_total[..., None])
        low_chances = chances.astype(BF)
        grad_chances = jnp.einsum(
            "tkrd,skd->krts", head_gradient, value_portion, preferred_element_type=F32
        )
        grad_scores = (chances * (grad_chances - row_dot[..., None])).astype(BF)
        query_grad = query_grad + jnp.einsum(
            "krts,skd->tkrd", grad_scores, key_portion, preferred_element_type=F32
        )
        key_terms = (
            jnp.einsum("krts,tkrd->skd", grad_scores, rotated_queries, preferred_element_type=F32)
            * score_scale
        )
        value_terms = jnp.einsum(
            "krts,tkrd->skd", low_chances, head_gradient, preferred_element_type=F32
        )
        return (query_grad, (key_terms.astype(BF), value_terms.astype(BF)))

    query_grad, (key_terms, value_terms) = lax.scan(grad_step, empty_head_state, key_blocks)
    query_grad = query_grad * score_scale
    kv_terms = jnp.concatenate(
        [key_terms.reshape(group_tokens, kv_width), value_terms.reshape(group_tokens, kv_width)],
        axis=1,
    )
    kv_mine = lax.psum_scatter(kv_terms, "expert", scatter_dimension=0, tiled=True)
    grad_query_pre = (
        reverse_rotation(
            query_grad.reshape(token_count, QUERY_HEADS, HEAD_SIZE), cosine_table, sine_table
        )
        .reshape(token_count, q_width)
        .astype(BF)
    )
    grad_key_pre = (
        reverse_rotation(
            kv_mine[:, :kv_width].astype(F32).reshape(token_count, KEY_VALUE_HEADS, HEAD_SIZE),
            cosine_table,
            sine_table,
        )
        .reshape(token_count, kv_width)
        .astype(BF)
    )
    grad_qkv = jnp.concatenate([grad_query_pre, grad_key_pre, kv_mine[:, kv_width:]], axis=1)
    grad_normed_one = dot_nt(grad_qkv, pack[:, :c_s])
    qkv_grad = dot_tn(normed_one, grad_qkv)
    gain_one_grad, grad_input = norm_backward(grad_normed_one, unit_one, inv_one, gain_one)
    tokens_grad = (grad_middle + grad_input).astype(BF)
    small_grad = jnp.concatenate(
        [
            router_grad,
            gain_one_grad[:, None],
            gain_two_grad[:, None],
            jnp.zeros((width, 128 - n_experts - 2), F32),
        ],
        axis=1,
    )
    pack_grad = jnp.concatenate(
        [qkv_grad.astype(BF), small_grad.astype(BF), out_grad.astype(BF)], axis=1
    )
    mine = lax.psum_scatter(pack_grad, ("dp", "expert"), scatter_dimension=0, tiled=True)
    mine = mine.astype(F32)
    gate_mine, up_mine, down_mine = (
        lax.psum_scatter(grad, "dp", scatter_dimension=0, tiled=True).astype(F32)[None]
        for grad in (gate_grad, up_grad, down_grad)
    )
    return (
        output,
        tokens_grad,
        mine[:, c_s + n_experts],
        mine[:, :c_k],
        mine[:, c_k:c_v],
        mine[:, c_v:c_s],
        mine[:, c_o:],
        mine[:, c_s + n_experts + 1],
        mine[:, c_s : c_s + n_experts],
        gate_mine,
        up_mine,
        down_mine,
    )


MESH_ID = pl.DeviceIdType.MESH
ANY = pl.ANY
LOG2E = math.log2(math.e)


class Place:
    def __init__(self):
        d = lax.axis_index("dp")
        e = lax.axis_index("expert")
        core = lax.rem(e, 2)
        x = lax.rem(lax.div(e, 2), 2)
        y = lax.div(e, 4)
        self.d, self.e, self.core = d, e, core
        self.chip = lax.div(e, 2)
        self.e_s = e + 1 - 2 * core
        self.e_x = e + 2 - 4 * x
        self.e_y = e + 4 - 8 * y
        self.e_d = self.e_x + 4 - 8 * y
        self.chip_x = self.chip + 1 - 2 * x
        self.chip_y = self.chip + 2 - 4 * y
        self.chip_d = self.chip_x + 2 - 4 * y
        self.sib = (d, self.e_s)
        self.nx = (d, self.e_x)
        self.ny = (d, self.e_y)
        half = lax.div(d, 2)
        odd = lax.rem(d, 2)
        self.pair = (2 * half + 1 - odd, e)
        self.cross = (3 - d, e)
        self.inner = (d == 1) | (d == 2)
        self.order = (d, 2 * half + 1 - odd, 2 - half, 3 - 3 * half)

    def greet(self):
        barrier = pltpu.get_barrier_semaphore()
        for other in (self.sib, self.nx, self.ny, self.pair):
            pl.semaphore_signal(barrier, inc=1, device_id=other, device_id_type=MESH_ID)

        @pl.when(self.inner)
        def _():
            pl.semaphore_signal(barrier, inc=1, device_id=self.cross, device_id_type=MESH_ID)
            pl.semaphore_wait(barrier, 5)

        @pl.when(jnp.logical_not(self.inner))
        def _():
            pl.semaphore_wait(barrier, 4)


def rcopy(src, dst, send_sem, recv_sem, device):
    return pltpu.make_async_remote_copy(
        src_ref=src,
        dst_ref=dst,
        send_sem=send_sem,
        recv_sem=recv_sem,
        device_id=device,
        device_id_type=MESH_ID,
    )


class PlaneGather:
    def __init__(self, at, blk, half, send, recv):
        self.at, self.blk, self.half, self.send, self.recv = at, blk, half, send, recv

    def push(self, ref, target, slot_send, slot_recv, src=None):
        rcopy(
            ref if src is None else src, ref, self.send(slot_send), self.recv(slot_recv), target
        ).start()

    def await_(self, ref, slot):
        rcopy(ref, ref, self.send(0), self.recv(slot), self.at.sib).wait_recv()

    def sent(self, ref, slot):
        rcopy(ref, ref, self.send(slot), self.recv(0), self.at.sib).wait_send()

    def start(self, src=None):
        at = self.at
        own = self.blk(at.e)
        self.push(own, at.nx, 0, 0, src)
        self.push(own, at.ny, 1, 1, src)
        self.push(own, at.sib, 2, 4, src)

    def on_x(self):
        at = self.at
        got = self.blk(at.e_x)
        self.await_(got, 0)
        self.push(self.half(at.e_x, 0), at.ny, 3, 3)
        self.push(got, at.sib, 4, 5)

    def on_y(self):
        at = self.at
        got = self.blk(at.e_y)
        self.await_(got, 1)
        self.push(self.half(at.e_y, 1), at.nx, 5, 2)
        self.push(got, at.sib, 6, 6)

    def on_d(self):
        at = self.at
        self.await_(self.half(at.e_d, 1), 2)
        self.await_(self.half(at.e_d, 0), 3)
        self.push(self.blk(at.e_d), at.sib, 7, 7)

    def on_s(self):
        at = self.at
        turn = at.e_s - at.e
        self.await_(self.blk(at.e_s), 4)
        self.await_(self.blk(at.e_x + turn), 5)
        self.await_(self.blk(at.e_y + turn), 6)
        self.await_(self.blk(at.e_d + turn), 7)

    def drain(self):
        at = self.at
        whole = self.blk(at.e)
        for slot in (0, 1, 2, 4, 6, 7):
            self.sent(whole, slot)
        self.sent(self.half(at.e, 0), 3)
        self.sent(self.half(at.e, 1), 5)


class LineGather:
    def __init__(self, at, blk, send, recv):
        self.at, self.blk, self.send, self.recv = at, blk, send, recv

    def start(self, src=None):
        at = self.at
        own = self.blk(at.d)
        from_ = own if src is None else src
        rcopy(from_, own, self.send(0), self.recv(1), at.pair).start()

        @pl.when(at.inner)
        def _():
            rcopy(from_, own, self.send(1), self.recv(2), at.cross).start()

    def on(self, k):
        at = self.at
        got = self.blk(at.order[k])
        rcopy(got, got, self.send(0), self.recv(k), at.pair).wait_recv()

        @pl.when(at.inner)
        def _():
            if k == 1:
                rcopy(got, got, self.send(2), self.recv(3), at.cross).start()
            else:
                rcopy(got, got, self.send(k + 1), self.recv(k), at.pair).start()

    def drain(self):
        at = self.at
        own = self.blk(at.d)
        rcopy(own, own, self.send(0), self.recv(0), at.pair).wait_send()

        @pl.when(at.inner)
        def _():
            for slot in (1, 2, 3, 4):
                rcopy(own, own, self.send(slot), self.recv(0), at.pair).wait_send()


def rows_of(ref, start, size):
    return ref.at[pl.ds(pl.multiple_of(start, 16), size)]


def stream_facts(lens_ref, order_ref, token_count, group_size, e):
    count = lens_ref.shape[1]
    stream = lax.broadcasted_iota(jnp.int32, (token_count, 128), 0) * group_size + e
    begin = jnp.zeros_like(stream)
    end = jnp.int32(0)
    for j in range(count):
        size = jnp.int32(0)
        for i in range(count):
            size = size + jnp.where(order_ref[0, j] == i, lens_ref[0, i], 0)
        end = end + size
        begin = begin + jnp.where(stream >= end, size, 0)
    return stream, begin, stream - begin


def rotary(relative):
    lane = lax.rem(lax.broadcasted_iota(jnp.int32, relative.shape, 1), HEAD_SIZE // 2)
    frequency = jnp.exp(lane.astype(F32) * (-math.log(ROPE_BASE) / (HEAD_SIZE // 2)))
    angles = relative.astype(F32) * frequency
    first = lax.broadcasted_iota(jnp.int32, relative.shape, 1) < HEAD_SIZE // 2
    sine = jnp.sin(angles)
    return jnp.cos(angles), jnp.where(first, -sine, sine)


def swap_halves(values):
    return pltpu.roll(values, HEAD_SIZE // 2, 1)


TILE = 64


def tiles_of(i):
    return range(max(0, i - 2), i + 1)


def tile_bias(i, r, stream, begin, group_size):
    wide = TILE * group_size
    j = lax.broadcasted_iota(jnp.int32, (TILE, wide), 1)
    key = (r * TILE + lax.rem(j, TILE)) * group_size + lax.div(j, TILE)
    ok = key >= begin[i * TILE : (i + 1) * TILE, :1]
    if r == i:
        ok = ok & (key <= stream[i * TILE : (i + 1) * TILE, :1])
    return jnp.where(ok, 0.0, MASKED_SCORE)


def dot_nn(a, b):
    return lax.dot_general(a, b, (((1,), (0,)), ((), ())), preferred_element_type=F32)


def dot_bt(a, b):
    return lax.dot_general(a, b, (((1,), (1,)), ((), ())), preferred_element_type=F32)


def dot_at(a, b):
    return lax.dot_general(a, b, (((0,), (0,)), ((), ())), preferred_element_type=F32)


def column_as_row(small, lane):
    pick = (lax.broadcasted_iota(jnp.int32, (8, 128), 1) == lane).astype(F32).astype(BF)
    return dot_bt(pick, small)[:1]


def front_kernel(
    n_experts,
    lens_ref,
    order_ref,
    tok_ref,
    routes_ref,
    pack_ref,
    wo_ref,
    gw_ref,
    uw_ref,
    dw_ref,
    cot_ref,
    x_all,
    c_all,
    gw_all,
    uw_all,
    dw_all,
    pack_out,
    wo_out,
    kv_out,
    q_out,
    att_out,
    lse_out,
    mid_out,
    pay_ref,
    pack_all,
    wo_all,
    kv_all,
    unit_ref,
    acc_ref,
    s_ref,
    ag_send,
    ag_recv,
    z_send,
    z_recv,
    local,
):
    at = Place()
    at.greet()
    tokens, width = tok_ref.shape
    shard = pack_ref.shape[0]
    group = 8
    kv_width = KEY_VALUE_HEADS * HEAD_SIZE
    q_width = QUERY_HEADS * HEAD_SIZE
    qkv = q_width + 2 * kv_width
    per_kv = QUERY_HEADS // KEY_VALUE_HEADS
    chunk = shard * group
    cut_a = 9 * 128
    cut_b = wo_ref.shape[1] // 2
    items = {}

    def add_item(name, blk, half):
        n = len(items)
        items[name] = PlaneGather(
            at, blk, half, lambda k, n=n: ag_send.at[n, k], lambda k, n=n: ag_recv.at[n, k]
        )

    def add_weight(name, ref, z, cut):
        wide = ref.shape[1]

        def place(e):
            return pl.ds(pl.multiple_of(z * chunk + e * shard, 16), shard)

        def half(e, h):
            return ref.at[place(e), pl.ds(0, cut) if h == 0 else pl.ds(cut, wide - cut)]

        add_item(name, lambda e: ref.at[place(e)], half)

    for k in range(4):
        add_weight(("a", k), pack_all, at.order[k], cut_a)
    for k in range(4):
        add_weight(("b", k), wo_all, at.order[k], cut_b)
    add_item("kv", lambda e: kv_all.at[e], lambda e, h: kv_all.at[e, :, pl.ds(h * kv_width, kv_width)])
    part = tokens // 2
    for name, ref, cut in (("x", x_all, 7 * 128), ("c", c_all, width // 2)):
        wide = ref.shape[2]
        for k in range(2):
            rows = pl.ds(k * part, part)

            def half(e, h, ref=ref, rows=rows, cut=cut, wide=wide):
                return ref.at[e, rows, pl.ds(0, cut) if h == 0 else pl.ds(cut, wide - cut)]

            add_item((name, k), lambda e, ref=ref, rows=rows: ref.at[e, rows], half)

    lines = {}

    def add_line(name, ref, size, start):
        n = len(lines)
        lines[name] = LineGather(
            at,
            lambda z: rows_of(ref, start(z), size),
            lambda k, n=n: z_send.at[n, k],
            lambda k, n=n: z_recv.at[n, k],
        )

    add_line("a", pack_all, shard, lambda z: z * chunk + at.e * shard)
    add_line("b", wo_all, shard, lambda z: z * chunk + at.e * shard)
    for name, ref, src in (("g", gw_all, gw_ref), ("u", uw_all, uw_ref), ("d", dw_all, dw_ref)):
        size = src.shape[0]
        add_line(name, ref, size, lambda z, size=size: z * size)

    own_a = rows_of(pack_all, at.d * chunk + at.e * shard, shard)
    own_b = rows_of(wo_all, at.d * chunk + at.e * shard, shard)
    copies = [
        pltpu.make_async_copy(pack_ref, own_a, local.at[0]),
        pltpu.make_async_copy(wo_ref, own_b, local.at[1]),
    ]
    for n, (name, src) in enumerate((("g", gw_ref), ("u", uw_ref), ("d", dw_ref))):
        copies.append(pltpu.make_async_copy(src, lines[name].blk(at.d), local.at[2 + n]))
    for k in range(2):
        rows = pl.ds(k * part, part)
        copies.append(
            pltpu.make_async_copy(cot_ref.at[rows], c_all.at[at.e, rows], local.at[5 + k])
        )

    lines["a"].start(pack_ref)
    items["a", 0].start(pack_ref)
    lines["b"].start(wo_ref)
    for copy in copies:
        copy.start()

    tok = tok_ref[...].astype(F32)
    scale_one = lax.rsqrt(jnp.mean(tok * tok, axis=1, keepdims=True) + EPSILON)
    unit_ref[...] = tok * scale_one
    stream, begin, relative = stream_facts(lens_ref, order_ref, tokens, group, at.e)
    cosine, sine = rotary(relative)
    acc_ref[...] = jnp.zeros_like(acc_ref)
    copies[0].wait()
    copies[1].wait()

    def consume(k):
        z = at.order[k]
        place = pl.ds(pl.multiple_of(z * chunk, 128), chunk)
        gain = column_as_row(pack_all[place, qkv:], n_experts)
        normed = (unit_ref[:, place] * gain).astype(BF)
        acc_ref[...] += dot_nn(normed, pack_all[place, :qkv])

    lines["a"].on(1)
    items["a", 1].start()
    items["a", 0].on_x()
    items["a", 0].on_y()
    lines["g"].start(gw_ref)
    items["a", 0].on_d()
    lines["a"].on(2)
    items["a", 2].start()
    items["a", 1].on_x()
    items["a", 1].on_y()
    items["a", 0].on_s()
    consume(0)
    lines["a"].on(3)
    items["a", 3].start()
    lines["b"].on(1)
    lines["u"].start(uw_ref)
    lines["d"].start(dw_ref)
    items["a", 1].on_d()
    items["a", 2].on_x()
    items["a", 2].on_y()
    items["a", 1].on_s()
    consume(1)
    lines["b"].on(2)
    items["a", 2].on_d()
    items["a", 3].on_x()
    items["a", 3].on_y()
    items["b", 0].start()
    items["a", 2].on_s()
    consume(2)
    lines["b"].on(3)
    items["a", 3].on_d()
    items["a", 3].on_s()
    consume(3)
    keep = [
        pltpu.make_async_copy(pack_all, pack_out, local.at[7]),
    ]
    keep[0].start()

    def turned(col):
        v = acc_ref[:, col : col + HEAD_SIZE]
        return (v * cosine + swap_halves(v) * sine).astype(BF)

    for h in range(KEY_VALUE_HEADS):
        kv_all[at.e, :, h * HEAD_SIZE : (h + 1) * HEAD_SIZE] = turned(q_width + h * HEAD_SIZE)
    kv_all[at.e, :, kv_width:] = acc_ref[:, q_width + kv_width :].astype(BF)
    items["kv"].start()
    for h in range(QUERY_HEADS):
        q_out[h] = turned(h * HEAD_SIZE)
    items["b", 0].on_x()
    items["b", 0].on_y()
    items["b", 1].start()
    items["kv"].on_x()
    items["kv"].on_y()
    items["b", 0].on_d()
    items["b", 2].start()
    items["kv"].on_d()
    items["kv"].on_s()
    keep.append(pltpu.make_async_copy(kv_all, kv_out, local.at[8]))
    keep[1].start()

    def step_b(n):
        if n == 0:
            items["b", 1].on_x()
            items["b", 1].on_y()
            items["b", 3].start()
        elif n == 1:
            items["b", 1].on_d()
            items["b", 2].on_x()
            items["b", 2].on_y()
        elif n == 2:
            items["b", 2].on_d()
            items["b", 3].on_x()
            items["b", 3].on_y()
        elif n == 3:
            items["b", 3].on_d()

    factor = LOG2E / math.sqrt(HEAD_SIZE)
    wide = TILE * group
    for i in range(tokens // TILE):
        step_b(i)
        first = tiles_of(i)[0]
        biases = [tile_bias(i, r, stream, begin, group) for r in tiles_of(i)]
        here = slice(i * TILE, (i + 1) * TILE)
        for g in range(KEY_VALUE_HEADS):
            queries = q_out[g * per_kv : (g + 1) * per_kv, here, :].reshape(per_kv * TILE, HEAD_SIZE)
            top = None
            for r in tiles_of(i):
                keys = kv_all[:, r * TILE : (r + 1) * TILE, g * HEAD_SIZE : (g + 1) * HEAD_SIZE]
                s = dot_bt(queries, keys.reshape(wide, HEAD_SIZE)) * factor
                s = s.reshape(per_kv, TILE, wide) + biases[r - first][None]
                s = s.reshape(per_kv * TILE, wide)
                s_ref[:, (r - first) * wide : (r - first + 1) * wide] = s
                high = jnp.max(s, axis=1, keepdims=True)
                top = high if top is None else jnp.maximum(top, high)
            total = None
            mixed = None
            for r in tiles_of(i):
                p = jnp.exp2(s_ref[:, (r - first) * wide : (r - first + 1) * wide] - top)
                values = kv_all[
                    :, r * TILE : (r + 1) * TILE, kv_width + g * HEAD_SIZE : kv_width + (g + 1) * HEAD_SIZE
                ].reshape(wide, HEAD_SIZE)
                row = jnp.sum(p, axis=1, keepdims=True)
                term = dot_nn(p.astype(BF), values)
                total = row if total is None else total + row
                mixed = term if mixed is None else mixed + term
            mixed = mixed / total
            lse_out[g, i] = jnp.broadcast_to(top + jnp.log2(total), (per_kv * TILE, 128))
            for h in range(per_kv):
                col = (g * per_kv + h) * HEAD_SIZE
                att_out[here, col : col + HEAD_SIZE] = mixed[h * TILE : (h + 1) * TILE]

    for name in ("g", "u", "d"):
        lines[name].on(1)
    for k in range(4):
        items["b", k].on_s()
    keep.append(pltpu.make_async_copy(wo_all, wo_out, local.at[9]))
    keep[2].start()
    items["c", 0].start(cot_ref.at[pl.ds(0, part)])
    attended = att_out[...].astype(BF)
    step = 256
    for n in range(width // step):
        cols = slice(n * step, (n + 1) * step)
        mid_out[:, cols] = tok_ref[:, cols].astype(F32) + dot_nn(attended, wo_all[:, cols])
    middle = mid_out[...]
    scale_two = lax.rsqrt(jnp.mean(middle * middle, axis=1, keepdims=True) + EPSILON)
    small = pack_all[:, qkv:]
    normed_two = (middle * scale_two * column_as_row(small, n_experts + 1)).astype(BF)
    pay_ref[:, :width] = normed_two
    logits = dot_nn(normed_two, small)
    lane = lax.broadcasted_iota(jnp.int32, (tokens, 128), 1)
    choose = lane == routes_ref[:, :1]
    for k in range(1, routes_ref.shape[1]):
        choose = choose | (lane == routes_ref[:, k : k + 1])
    top = jnp.max(jnp.where(choose, logits, MASKED_SCORE), axis=1, keepdims=True)
    spread = jnp.where(choose, jnp.exp(jnp.minimum(logits - top, 0.0)), 0.0)
    gates = spread / jnp.sum(spread, axis=1, keepdims=True)
    pay_ref[:, width:] = split_three(gates)
    own_x = [
        pltpu.make_async_copy(
            pay_ref.at[pl.ds(k * part, part)], x_all.at[at.e, pl.ds(k * part, part)], local.at[10 + k]
        )
        for k in range(2)
    ]
    for k in range(2):
        items["x", k].start(pay_ref.at[pl.ds(k * part, part)])
        own_x[k].start()
    for name in ("g", "u", "d"):
        lines[name].on(2)
    items["c", 0].on_x()
    items["c", 0].on_y()
    for k in range(2):
        items["x", k].on_x()
        items["x", k].on_y()
    items["c", 1].start(cot_ref.at[pl.ds(part, part)])
    items["c", 0].on_d()
    for k in range(2):
        items["x", k].on_d()
    items["c", 1].on_x()
    items["c", 1].on_y()
    items["c", 1].on_d()
    for name in ("g", "u", "d"):
        lines[name].on(3)
    for k in range(2):
        items["c", k].on_s()
        items["x", k].on_s()
    for item in items.values():
        item.drain()
    for line in lines.values():
        line.drain()
    for copy in copies[2:] + keep + own_x:
        copy.wait()


def split_three(values):
    high = values.astype(BF).astype(F32)
    mid = (values - high).astype(BF).astype(F32)
    low = values - high - mid
    return (high + pltpu.roll(mid, 32, 1) + pltpu.roll(low, 64, 1)).astype(BF)


def front(lengths, seq_order, tokens, routes, pack, wo, gw, uw, dw, cot, n_experts):
    count, width = tokens.shape
    group, line = 8, 4
    kv_width = KEY_VALUE_HEADS * HEAD_SIZE
    per_kv = QUERY_HEADS // KEY_VALUE_HEADS
    sds = jax.ShapeDtypeStruct
    smem = pl.BlockSpec(memory_space=pltpu.SMEM)
    vmem = pl.BlockSpec(memory_space=pltpu.VMEM)
    hbm = pl.BlockSpec(memory_space=ANY)
    n_items = 13
    return pl.pallas_call(
        functools.partial(front_kernel, n_experts),
        in_specs=[smem, smem] + [vmem] * 8,
        out_specs=(hbm,) * 8 + (vmem,) * 5,
        out_shape=(
            sds((group, count, width + 128), BF),
            sds((group, count, width), BF),
            sds((line * gw.shape[0], gw.shape[1]), BF),
            sds((line * uw.shape[0], uw.shape[1]), BF),
            sds((line * dw.shape[0], dw.shape[1]), BF),
            sds((width, pack.shape[1]), BF),
            sds((width, wo.shape[1]), BF),
            sds((group, count, 2 * kv_width), BF),
            sds((QUERY_HEADS, count, HEAD_SIZE), BF),
            sds((count, QUERY_HEADS * HEAD_SIZE), F32),
            sds((KEY_VALUE_HEADS, count // TILE, per_kv * TILE, 128), F32),
            sds((count, width), F32),
            sds((count, width + 128), BF),
        ),
        scratch_shapes=[
            pltpu.VMEM((width, pack.shape[1]), BF),
            pltpu.VMEM((width, wo.shape[1]), BF),
            pltpu.VMEM((group, count, 2 * kv_width), BF),
            pltpu.VMEM((count, width), F32),
            pltpu.VMEM((count, pack.shape[1] - 128), F32),
            pltpu.VMEM((per_kv * TILE, 3 * TILE * group), F32),
            pltpu.SemaphoreType.DMA((n_items, 8)),
            pltpu.SemaphoreType.DMA((n_items, 8)),
            pltpu.SemaphoreType.DMA((5, 5)),
            pltpu.SemaphoreType.DMA((5, 4)),
            pltpu.SemaphoreType.DMA((12,)),
        ],
        compiler_params=pltpu.CompilerParams(
            collective_id=1, has_side_effects=True, vmem_limit_bytes=60 * 2**20
        ),
    )(lengths, seq_order, tokens, routes, pack, wo, gw, uw, dw, cot)


def moe_kernel(
    x_ref, c_ref, gw, uw, dw, row_ref, out_ref, gg_ref, ug_ref, dg_ref, gacc, uacc, dacc, yacc, racc
):
    step = pl.program_id(0)
    block = x_ref.shape[0]
    width = c_ref.shape[1]
    e = lax.axis_index("expert")
    lane = lax.broadcasted_iota(jnp.int32, (block, 128), 1)
    mine = (lane == e) | (lane == e + 32) | (lane == e + 64)
    gate = jnp.sum(jnp.where(mine, x_ref[:, width:].astype(F32), 0.0), axis=1, keepdims=True)

    @pl.when(step == 0)
    def _():
        gacc[...] = jnp.zeros_like(gacc)
        uacc[...] = jnp.zeros_like(uacc)
        dacc[...] = jnp.zeros_like(dacc)

    grad_returned = (gate * c_ref[...].astype(F32)).astype(BF)
    x = x_ref[:, :width]
    part = 256
    for f in range(gw.shape[1] // part):
        cols = slice(f * part, (f + 1) * part)
        gate_pre = dot_nn(x, gw[:, cols])
        up_pre = dot_nn(x, uw[:, cols])
        sig = 1.0 / (1.0 + jnp.exp(-gate_pre))
        silu = gate_pre * sig
        hidden = (silu * up_pre).astype(BF)
        grad_hidden = dot_bt(grad_returned, dw[cols, :])
        grad_up = (grad_hidden * silu).astype(BF)
        grad_gate = (grad_hidden * up_pre * sig * (1.0 + gate_pre * (1.0 - sig))).astype(BF)
        y = dot_nn(hidden, dw[cols, :])
        r = dot_bt(grad_gate, gw[:, cols]) + dot_bt(grad_up, uw[:, cols])
        if f == 0:
            yacc[...] = y
            racc[...] = r
        else:
            yacc[...] += y
            racc[...] += r
        dacc[cols, :] += dot_at(hidden, grad_returned)
        gacc[:, cols] += dot_at(x, grad_gate)
        uacc[:, cols] += dot_at(x, grad_up)
    returned = yacc[...].astype(BF).astype(F32)
    grad_gates = jnp.sum(c_ref[...].astype(F32) * returned, axis=1, keepdims=True)
    out_ref[...] = (gate * returned).astype(BF)
    row_ref[:, :width] = racc[...].astype(BF)
    high = grad_gates.astype(BF).astype(F32)
    row_ref[:, width:] = jnp.where(
        lane == e, high, jnp.where(lane == e + 32, grad_gates - high, 0.0)
    ).astype(BF)

    @pl.when(step == pl.num_programs(0) - 1)
    def _():
        gg_ref[...] = gacc[...].astype(BF)
        ug_ref[...] = uacc[...].astype(BF)
        dg_ref[...] = dacc[...].astype(BF)


def moe(x_all, c_all, gw, uw, dw):
    rows, width = c_all.shape
    hid = gw.shape[1]
    block = 512

    def full(*shape):
        return pl.BlockSpec(shape, lambda i: (0, 0), pipeline_mode=pl.Buffered(1))

    def moving(cols):
        return pl.BlockSpec((block, cols), lambda i: (i, 0))

    sds = jax.ShapeDtypeStruct
    return pl.pallas_call(
        moe_kernel,
        grid=(rows // block,),
        in_specs=[
            moving(width + 128),
            moving(width),
            full(width, hid),
            full(width, hid),
            full(hid, width),
        ],
        out_specs=(
            moving(width + 128),
            moving(width),
            full(width, hid),
            full(width, hid),
            full(hid, width),
        ),
        out_shape=(
            sds((rows, width + 128), BF),
            sds((rows, width), BF),
            sds((width, hid), BF),
            sds((width, hid), BF),
            sds((hid, width), BF),
        ),
        scratch_shapes=[
            pltpu.VMEM((width, hid), F32),
            pltpu.VMEM((width, hid), F32),
            pltpu.VMEM((hid, width), F32),
            pltpu.VMEM((block, width), F32),
            pltpu.VMEM((block, width), F32),
        ],
        compiler_params=pltpu.CompilerParams(vmem_limit_bytes=60 * 2**20),
        cost_estimate=pl.CostEstimate(
            flops=18 * rows * width * hid,
            bytes_accessed=8 * rows * width + 12 * width * hid,
            transcendentals=rows * hid,
        ),
    )(x_all, c_all, gw, uw, dw)


def pack_weights(w_router, norm_attn, norm_moe, w_query, key_projection, value_projection):
    rows, n_experts = w_router.shape
    small = jnp.concatenate(
        [
            w_router,
            norm_attn[:, None],
            norm_moe[:, None],
            jnp.zeros((rows, 128 - n_experts - 2), BF),
        ],
        axis=1,
    )
    return jnp.concatenate([w_query, key_projection, value_projection, small], axis=1)


class PlaneReduce:
    def __init__(self, at, src, own, loader, seat, xs, ys, x2, y2, cut, send, recv):
        self.at, self.src, self.own, self.loader = at, src, own, loader
        self.seat, self.xs, self.ys, self.x2, self.y2 = seat, xs, ys, x2, y2
        self.cut, self.send, self.recv = cut, send, recv

    def copy(self, slot, src, dst, target):
        return rcopy(src, dst, self.send(slot), self.recv(slot), target)

    def moves(self):
        at, own, cut = self.at, self.own, self.cut
        low, high = pl.ds(0, cut), pl.ds(cut, self.seat.shape[-1] - cut)
        return {
            0: lambda: self.copy(0, self.src.at[:, 1 - at.core], self.seat, at.sib),
            1: lambda: self.copy(1, own.at[at.chip_x, :, low], self.xs.at[0], at.nx),
            2: lambda: self.copy(2, own.at[at.chip_d, :, low], self.xs.at[1], at.nx),
            3: lambda: self.copy(3, own.at[at.chip_y, :, high], self.ys.at[0], at.ny),
            4: lambda: self.copy(4, own.at[at.chip_d, :, high], self.ys.at[1], at.ny),
            5: lambda: self.copy(5, own.at[at.chip_y, :, low], self.y2, at.ny),
            6: lambda: self.copy(6, own.at[at.chip_x, :, high], self.x2, at.nx),
        }

    def begin(self, slot):
        self.moves()[slot]().start()

    def got(self, slot):
        self.moves()[slot]().wait_recv()

    def start(self):
        self.begin(0)
        if self.loader is not None:
            self.loader.start()

    def on_s(self):
        if self.loader is not None:
            self.loader.wait()
        self.got(0)

        def add(q, none):
            self.own[q] = (self.own[q].astype(F32) + self.seat[q].astype(F32)).astype(BF)
            return none

        lax.fori_loop(0, 4, add, 0)
        for slot in (1, 2, 3, 4):
            self.begin(slot)

    def on_xy(self):
        at, own, cut = self.at, self.own, self.cut
        self.got(1)
        self.got(2)
        own[at.chip_y, :, :cut] = (
            own[at.chip_y, :, :cut].astype(F32) + self.xs[1].astype(F32)
        ).astype(BF)
        self.begin(5)
        self.got(3)
        self.got(4)
        own[at.chip_x, :, cut:] = (
            own[at.chip_x, :, cut:].astype(F32) + self.ys[1].astype(F32)
        ).astype(BF)
        self.begin(6)

    def finish(self):
        at, own, cut = self.at, self.own, self.cut
        self.got(5)
        low = own[at.chip, :, :cut].astype(F32) + self.xs[0].astype(F32) + self.y2[...].astype(F32)
        self.got(6)
        high = own[at.chip, :, cut:].astype(F32) + self.ys[0].astype(F32) + self.x2[...].astype(F32)
        return low, high

    def drain(self):
        for slot in range(7):
            self.moves()[slot]().wait_send()


class LineReduce:
    def __init__(self, at, blocks, near, far, send, recv):
        self.at, self.blocks, self.near, self.far = at, blocks, near, far
        self.send, self.recv = send, recv

    def copy(self, slot, src, dst, target):
        return rcopy(src, dst, self.send(slot), self.recv(slot), target)

    def outer_moves(self):
        at = self.at
        return [
            self.copy(n, self.blocks.at[at.order[n + 1]], self.near.at[n], at.pair)
            for n in range(3)
        ]

    def cross_moves(self):
        at = self.at
        return [
            self.copy(3 + n, self.blocks.at[at.order[n + 2]], self.far.at[n], at.cross)
            for n in range(2)
        ]

    def back_move(self):
        at = self.at
        return self.copy(0, self.blocks.at[at.order[1]], self.near.at[0], at.pair)

    def start(self):
        at = self.at

        @pl.when(jnp.logical_not(at.inner))
        def _():
            for move in self.outer_moves():
                move.start()

    def middle(self):
        at, blocks = self.at, self.blocks

        @pl.when(at.inner)
        def _():
            for n in range(2):
                rcopy(
                    self.near.at[n + 1], self.near.at[n + 1], self.send(0), self.recv(n + 1), at.pair
                ).wait_recv()
                blocks[at.order[n + 2]] = (
                    blocks[at.order[n + 2]].astype(F32) + self.near[n + 1].astype(F32)
                ).astype(BF)
                self.cross_moves()[n].start()

    def last(self):
        at, blocks = self.at, self.blocks

        @pl.when(at.inner)
        def _():
            self.cross_moves()[1].wait_recv()
            blocks[at.order[1]] = (
                blocks[at.order[1]].astype(F32) + self.far[1].astype(F32)
            ).astype(BF)
            self.back_move().start()

    def finish(self, out):
        at = self.at
        self.back_move().wait_recv()
        total = self.blocks[at.d].astype(F32) + self.near[0].astype(F32)

        @pl.when(at.inner)
        def _():
            self.cross_moves()[0].wait_recv()
            out[...] = total + self.far[0].astype(F32)
            for move in self.cross_moves():
                move.wait_send()
            self.back_move().wait_send()

        @pl.when(jnp.logical_not(at.inner))
        def _():
            out[...] = total
            for move in self.outer_moves():
                move.wait_send()


def column_sums(values):
    high = values.astype(BF)
    low = (values - high.astype(F32)).astype(BF)
    ones = jnp.ones((values.shape[0], 128), BF)
    return dot_at(high, ones) + dot_at(low, ones)


N_BACK = 18


def back_kernel(
    n_experts,
    lens_ref,
    order_ref,
    row_in,
    wgt_in,
    tok_in,
    q_in,
    att_in,
    lse_in,
    mid_in,
    cot_in,
    kv_in,
    pay_in,
    pack_in,
    wo_in,
    output_ref,
    tokens_grad_ref,
    aq_out,
    ak_out,
    b_out,
    own_ref,
    seat_ref,
    low1_ref,
    high1_ref,
    low2_ref,
    high2_ref,
    row_ref,
    tok_ref,
    q_ref,
    att_ref,
    lse_ref,
    mid_ref,
    cot_ref,
    kv_ref,
    pay_ref,
    pack_ref,
    wo_ref,
    do_ref,
    dkv_ref,
    kseat,
    klow1,
    khigh1,
    klow2,
    khigh2,
    bseat,
    bhalf1,
    bhalf2,
    aseat,
    ahalf1,
    ahalf2,
    cseat,
    clow1,
    chigh1,
    clow2,
    chigh2,
    n1_ref,
    dqkv_ref,
    small_ref,
    grad_middle_ref,
    bz,
    bnear,
    bfar,
    az,
    anear,
    afar,
    cz,
    cnear,
    cfar,
    r_send,
    r_recv,
    l_send,
    l_recv,
    local,
    credit,
):
    at = Place()
    at.greet()
    tokens, width = tok_ref.shape
    group = 8
    kv_width = KEY_VALUE_HEADS * HEAD_SIZE
    q_width = QUERY_HEADS * HEAD_SIZE
    qkv = q_width + 2 * kv_width
    per_kv = QUERY_HEADS // KEY_VALUE_HEADS
    chunk = width // 4
    shard = chunk // group
    part = tokens // 2
    red = {}

    def sems(n):
        return (lambda k: r_send.at[n, k]), (lambda k: r_recv.at[n, k])

    cut_r = 7 * 128
    for name, src, wide, cut in (("r", row_in, width + 128, cut_r), ("w", wgt_in, width, 6 * 128)):
        for k in range(2):
            send, recv = sems(len(red))
            rows = pl.ds(k * part, part)
            cols = pl.ds(0, wide)
            mine = src.at[:, :, rows]
            own = own_ref.at[k, :, :, cols]
            red[name, k] = PlaneReduce(
                at,
                mine,
                own,
                pltpu.make_async_copy(mine.at[:, at.core], own, local.at[len(red)]),
                seat_ref.at[k, :, :, cols],
                low1_ref.at[k, :, :, pl.ds(0, cut)],
                high1_ref.at[k, :, :, pl.ds(0, wide - cut)],
                high2_ref.at[k, :, pl.ds(0, wide - cut)],
                low2_ref.at[k, :, pl.ds(0, cut)],
                cut,
                send,
                recv,
            )
    for k in range(2):
        send, recv = sems(len(red))
        rows = pl.ds(k * part, part)
        mine = dkv_ref.at[:, :, rows]
        red["k", k] = PlaneReduce(
            at, mine, mine.at[:, at.core], None, kseat.at[k], klow1.at[k], khigh1.at[k],
            khigh2.at[k], klow2.at[k], kv_width, send, recv,
        )
    for z in range(4):
        send, recv = sems(len(red))
        red["b", z] = PlaneReduce(
            at, wo_ref.at[z], wo_ref.at[z, :, at.core], None, bseat.at[z], bhalf1.at[z, 0],
            bhalf1.at[z, 1], bhalf2.at[z, 0], bhalf2.at[z, 1], width // 2, send, recv,
        )
    cols_q, cols_k = pl.ds(0, q_width), pl.ds(q_width, 2 * kv_width + 128)
    for z in range(4):
        send, recv = sems(len(red))
        red["q", z] = PlaneReduce(
            at, pack_ref.at[z, :, :, :, cols_q], pack_ref.at[z, :, at.core, :, cols_q], None,
            aseat.at[z], ahalf1.at[z, 0], ahalf1.at[z, 1], ahalf2.at[z, 0], ahalf2.at[z, 1],
            q_width // 2, send, recv,
        )
    for z in range(4):
        send, recv = sems(len(red))
        red["s", z] = PlaneReduce(
            at, pack_ref.at[z, :, :, :, cols_k], pack_ref.at[z, :, at.core, :, cols_k], None,
            cseat.at[z], clow1.at[z], chigh1.at[z], chigh2.at[z], clow2.at[z],
            3 * 128, send, recv,
        )
    lines = {}
    for n, (name, blocks, near, far) in enumerate(
        (("b", bz, bnear, bfar), ("q", az, anear, afar), ("s", cz, cnear, cfar))
    ):
        lines[name] = LineReduce(
            at, blocks, near, far, lambda k, n=n: l_send.at[n, k], lambda k, n=n: l_recv.at[n, k]
        )

    red["r", 0].start()
    red["r", 1].start()
    loads = {}
    for n, (name, src, dst) in enumerate(
        (
            ("pay", pay_in, pay_ref),
            ("mid", mid_in, mid_ref),
            ("cot", cot_in, cot_ref),
            ("pack", pack_in, pack_ref),
            ("wo", wo_in, wo_ref),
            ("att", att_in, att_ref),
            ("lse", lse_in, lse_ref),
            ("q", q_in, q_ref),
            ("kv", kv_in, kv_ref),
            ("tok", tok_in, tok_ref),
        )
    ):
        loads[name] = pltpu.make_async_copy(src, dst, local.at[4 + n])
        loads[name].start()
    stream, begin, relative = stream_facts(lens_ref, order_ref, tokens, group, at.e)
    cosine, sine = rotary(relative)
    red["r", 0].on_s()
    red["r", 1].on_s()
    for name in ("tok", "pack"):
        loads[name].wait()

    def tok_unit():
        tok = tok_ref[...].astype(F32)
        scale = lax.rsqrt(jnp.mean(tok * tok, axis=1, keepdims=True) + EPSILON)
        return tok * scale, scale

    small = pack_ref[..., qkv:].reshape(width, 128)
    gain_one = column_as_row(small, n_experts)
    gain_two = column_as_row(small, n_experts + 1)
    n1_ref[...] = (tok_unit()[0] * gain_one).astype(BF)
    for k in range(2):
        red["r", k].on_xy()
    for name in ("pay", "mid", "cot"):
        loads[name].wait()
    for k in range(2):
        rows = slice(k * part, (k + 1) * part)
        low, high = red["r", k].finish()
        row_ref[rows, :cut_r] = low
        row_ref[rows, cut_r:] = high
    for k in range(2):
        red["r", k].drain()
    for other in (at.sib, at.nx, at.ny):
        pl.semaphore_signal(credit, inc=1, device_id=other, device_id_type=MESH_ID)

    lane = lax.broadcasted_iota(jnp.int32, (tokens, 128), 1)
    ext = pay_ref[:, width:].astype(F32)
    gates = jnp.where(
        lane < n_experts, ext + pltpu.roll(ext, 96, 1) + pltpu.roll(ext, 64, 1), 0.0
    )
    ext = row_ref[:, width:]
    grad_gates = jnp.where(lane < n_experts, ext + pltpu.roll(ext, 96, 1), 0.0)
    weighted_sum = jnp.sum(gates * grad_gates, axis=1, keepdims=True)
    grad_logits = (gates * (grad_gates - weighted_sum)).astype(BF)
    grad_normed = dot_bt(grad_logits, small) + row_ref[:, :width]
    middle = mid_ref[...]
    scale_two = lax.rsqrt(jnp.mean(middle * middle, axis=1, keepdims=True) + EPSILON)
    unit_two = middle * scale_two
    inner_sum = jnp.mean(grad_normed * gain_two * unit_two, axis=1, keepdims=True)
    grad_middle = cot_ref[...].astype(F32) + scale_two * (
        grad_normed * gain_two - unit_two * inner_sum
    )
    products = grad_normed * unit_two
    pl.semaphore_wait(credit, 3)
    red["w", 0].start()
    loads["wo"].wait()
    grad_middle_ref[...] = grad_middle
    mixed = grad_middle.astype(BF)
    for z in range(4):
        heads = dot_bt(mixed, wo_ref[z].reshape(chunk, width)).astype(BF)
        for j in range(chunk // HEAD_SIZE):
            do_ref[z * (chunk // HEAD_SIZE) + j] = heads[:, j * HEAD_SIZE : (j + 1) * HEAD_SIZE]
    loads["att"].wait()
    for z in range(4):
        left = att_ref[:, z * chunk : (z + 1) * chunk].astype(BF)
        wo_ref[z] = dot_at(left, mixed).astype(BF).reshape(4, 2, shard, width)
        red["b", z].start()
    lane_small = lax.broadcasted_iota(jnp.int32, (width, 128), 1)
    small_ref[...] = dot_at(pay_ref[:, :width], grad_logits) + jnp.where(
        lane_small == n_experts + 1, column_sums(products), 0.0
    )
    for name in ("lse", "q", "kv"):
        loads[name].wait()
    row_ref[:, :width] = jnp.zeros((tokens, width), F32)
    n_tiles = tokens // TILE
    wide = TILE * group
    for g in range(KEY_VALUE_HEADS):
        for i in range(n_tiles):
            here = slice(i * TILE, (i + 1) * TILE)
            dots = []
            for h in range(per_kv):
                col = (g * per_kv + h) * HEAD_SIZE
                dots.append(
                    jnp.sum(
                        do_ref[g * per_kv + h, here, :].astype(F32)
                        * att_ref[here, col : col + HEAD_SIZE],
                        axis=1,
                        keepdims=True,
                    )
                )
            dots = jnp.concatenate(dots, axis=0)
            lse_ref[g, i, :, 64:] = jnp.broadcast_to(dots, (per_kv * TILE, 64))
    red["w", 0].on_s()
    for z in range(4):
        red["b", z].on_s()

    factor = LOG2E / math.sqrt(HEAD_SIZE)
    score_scale = 1.0 / math.sqrt(HEAD_SIZE)

    def attend_back(r):
        queries_of = [i for i in range(n_tiles) if r in tiles_of(i)]
        biases = {i: tile_bias(i, r, stream, begin, group) for i in queries_of}
        there = slice(r * TILE, (r + 1) * TILE)
        for g in range(KEY_VALUE_HEADS):
            key_cols = slice(g * HEAD_SIZE, (g + 1) * HEAD_SIZE)
            value_cols = slice(kv_width + g * HEAD_SIZE, kv_width + (g + 1) * HEAD_SIZE)
            heads = slice(g * per_kv, (g + 1) * per_kv)
            keys = kv_ref[:, there, key_cols].reshape(wide, HEAD_SIZE)
            values = kv_ref[:, there, value_cols].reshape(wide, HEAD_SIZE)
            grad_keys = None
            grad_values = None
            for i in queries_of:
                here = slice(i * TILE, (i + 1) * TILE)
                queries = q_ref[heads, here, :].reshape(per_kv * TILE, HEAD_SIZE)
                grads = do_ref[heads, here, :].reshape(per_kv * TILE, HEAD_SIZE)
                s = dot_bt(queries, keys) * factor
                s = (s.reshape(per_kv, TILE, wide) + biases[i][None]).reshape(per_kv * TILE, wide)
                p = jnp.exp2(s - lse_ref[g, i, :, :1])
                ds = (p * (dot_bt(grads, values) - lse_ref[g, i, :, 64:65])).astype(BF)
                term_k = dot_at(ds, queries)
                term_v = dot_at(p.astype(BF), grads)
                grad_keys = term_k if grad_keys is None else grad_keys + term_k
                grad_values = term_v if grad_values is None else grad_values + term_v
                grad_queries = dot_nn(ds, keys)
                for h in range(per_kv):
                    col = (g * per_kv + h) * HEAD_SIZE
                    row_ref[here, col : col + HEAD_SIZE] += grad_queries[
                        h * TILE : (h + 1) * TILE
                    ]
            dkv_ref[:, :, there, key_cols] = (
                (grad_keys * score_scale).astype(BF).reshape(4, 2, TILE, HEAD_SIZE)
            )
            dkv_ref[:, :, there, value_cols] = grad_values.astype(BF).reshape(4, 2, TILE, HEAD_SIZE)

    def settle(name, z, blocks, cut):
        low, high = red[name, z].finish()
        blocks[z, :, :cut] = low.astype(BF)
        blocks[z, :, cut:] = high.astype(BF)

    attend_back(0)
    for z in range(4):
        red["b", z].on_xy()
    attend_back(1)
    red["k", 0].start()
    red["w", 0].on_xy()
    attend_back(2)
    red["k", 0].on_s()
    for z in range(4):
        settle("b", z, bz, width // 2)
    lines["b"].start()
    attend_back(3)
    red["k", 1].start()
    red["k", 0].on_xy()

    def output_part(k):
        rows = slice(k * part, (k + 1) * part)
        low, high = red["w", k].finish()
        output_ref[rows, : 6 * 128] = (mid_ref[rows, : 6 * 128] + low).astype(BF)
        output_ref[rows, 6 * 128 :] = (mid_ref[rows, 6 * 128 :] + high).astype(BF)

    def turned_back(v):
        return (v * cosine - swap_halves(v) * sine).astype(BF)

    for h in range(QUERY_HEADS):
        cols = slice(h * HEAD_SIZE, (h + 1) * HEAD_SIZE)
        dqkv_ref[:, cols] = turned_back(row_ref[:, cols] * score_scale)
    red["k", 1].on_s()
    grad_q = dqkv_ref[:, :q_width]
    for z in range(4):
        cols = slice(z * chunk, (z + 1) * chunk)
        att_ref[:, cols] = dot_bt(grad_q, pack_ref[z, :, :, :, :q_width].reshape(chunk, q_width))
        pack_ref[z, :, :, :, :q_width] = (
            dot_at(n1_ref[:, cols], grad_q).astype(BF).reshape(4, 2, shard, q_width)
        )
        red["q", z].start()
        if z == 0:
            red["k", 1].on_xy()
    for k in range(2):
        rows = slice(k * part, (k + 1) * part)
        low, high = red["k", k].finish()
        row_ref[rows, :kv_width] = low
        row_ref[rows, kv_width : 2 * kv_width] = high
    lines["b"].middle()
    for z in range(4):
        red["q", z].on_s()
    for h in range(KEY_VALUE_HEADS):
        v = row_ref[:, h * HEAD_SIZE : (h + 1) * HEAD_SIZE]
        dqkv_ref[:, q_width + h * HEAD_SIZE : q_width + (h + 1) * HEAD_SIZE] = turned_back(v)
    dqkv_ref[:, q_width + kv_width :] = row_ref[:, kv_width : 2 * kv_width].astype(BF)
    grad_kv = dqkv_ref[:, q_width:]
    for z in range(4):
        cols = slice(z * chunk, (z + 1) * chunk)
        att_ref[:, cols] += dot_bt(
            grad_kv, pack_ref[z, :, :, :, q_width:qkv].reshape(chunk, 2 * kv_width)
        )
        pack_ref[z, :, :, :, q_width:qkv] = (
            dot_at(n1_ref[:, cols], grad_kv).astype(BF).reshape(4, 2, shard, 2 * kv_width)
        )
    unit_one, scale_one = tok_unit()
    grad_one = att_ref[...]
    small_ref[...] += jnp.where(lane_small == n_experts, column_sums(grad_one * unit_one), 0.0)
    pack_ref[..., qkv:] = small_ref[...].astype(BF).reshape(4, 4, 2, shard, 128)
    for z in range(4):
        red["s", z].start()
    lines["b"].last()
    for z in range(4):
        red["q", z].on_xy()
    for z in range(4):
        red["s", z].on_s()
    inner_sum = jnp.mean(grad_one * gain_one * unit_one, axis=1, keepdims=True)
    back_one = scale_one * (grad_one * gain_one - unit_one * inner_sum)
    tokens_grad_ref[...] = (grad_middle_ref[...] + back_one).astype(BF)
    red["w", 1].start()
    for z in range(4):
        settle("q", z, az, q_width // 2)
    lines["q"].start()
    for z in range(4):
        red["s", z].on_xy()
    red["w", 1].on_s()
    for z in range(4):
        settle("s", z, cz, 3 * 128)
    lines["s"].start()
    lines["q"].middle()
    lines["s"].middle()
    output_part(0)
    red["w", 1].on_xy()
    lines["q"].last()
    lines["s"].last()
    lines["b"].finish(b_out)
    output_part(1)
    lines["q"].finish(aq_out)
    lines["s"].finish(ak_out)
    for key, item in red.items():
        if key[0] != "r":
            item.drain()


def back(
    lengths, seq_order, row, weighted, tokens, q_rot, att, lse, middle, cot, kv, pay, pack, wo, n_experts
):
    count, width = tokens.shape
    group = 8
    shard = width // 32
    kv_width = KEY_VALUE_HEADS * HEAD_SIZE
    part = count // 2
    wide_r, cut_r = width + 128, 7 * 128
    wide_s, cut_s = 2 * kv_width + 128, 3 * 128
    half = width // 2
    sds = jax.ShapeDtypeStruct
    smem = pl.BlockSpec(memory_space=pltpu.SMEM)
    vmem = pl.BlockSpec(memory_space=pltpu.VMEM)
    hbm = pl.BlockSpec(memory_space=ANY)
    row = row.reshape(4, 2, count, wide_r)
    weighted = weighted.reshape(4, 2, count, width)
    pack = pack.reshape(4, 4, 2, shard, pack.shape[1])
    wo = wo.reshape(4, 4, 2, shard, width)

    def low(*shape):
        return pltpu.VMEM(shape, BF)

    def like(a):
        return pltpu.VMEM(a.shape, a.dtype)

    return pl.pallas_call(
        functools.partial(back_kernel, n_experts),
        in_specs=[smem, smem] + [hbm] * 12,
        out_specs=(vmem,) * 5,
        out_shape=(
            sds((count, width), BF),
            sds((count, width), BF),
            sds((shard, width), F32),
            sds((shard, wide_s), F32),
            sds((shard, width), F32),
        ),
        scratch_shapes=[
            low(2, 4, part, wide_r),
            low(2, 4, part, wide_r),
            low(2, 2, part, cut_r),
            low(2, 2, part, wide_r - cut_r),
            low(2, part, cut_r),
            low(2, part, wide_r - cut_r),
            pltpu.VMEM((count, wide_r), F32),
            like(tokens),
            like(q_rot),
            like(att),
            like(lse),
            like(middle),
            like(cot),
            like(kv),
            like(pay),
            like(pack),
            like(wo),
            like(q_rot),
            low(4, 2, count, 2 * kv_width),
            low(2, 4, part, 2 * kv_width),
            low(2, 2, part, kv_width),
            low(2, 2, part, kv_width),
            low(2, part, kv_width),
            low(2, part, kv_width),
            low(4, 4, shard, width),
            low(4, 2, 2, shard, half),
            low(4, 2, shard, half),
            low(4, 4, shard, width),
            low(4, 2, 2, shard, half),
            low(4, 2, shard, half),
            low(4, 4, shard, wide_s),
            low(4, 2, shard, cut_s),
            low(4, 2, shard, wide_s - cut_s),
            low(4, shard, cut_s),
            low(4, shard, wide_s - cut_s),
            low(count, width),
            low(count, width + 2 * kv_width),
            pltpu.VMEM((width, 128), F32),
            pltpu.VMEM((count, width), F32),
            low(4, shard, width),
            low(3, shard, width),
            low(2, shard, width),
            low(4, shard, width),
            low(3, shard, width),
            low(2, shard, width),
            low(4, shard, wide_s),
            low(3, shard, wide_s),
            low(2, shard, wide_s),
            pltpu.SemaphoreType.DMA((N_BACK, 7)),
            pltpu.SemaphoreType.DMA((N_BACK, 7)),
            pltpu.SemaphoreType.DMA((3, 5)),
            pltpu.SemaphoreType.DMA((3, 5)),
            pltpu.SemaphoreType.DMA((14,)),
            pltpu.SemaphoreType.REGULAR,
        ],
        compiler_params=pltpu.CompilerParams(
            collective_id=2, has_side_effects=True, vmem_limit_bytes=63 * 2**20
        ),
        cost_estimate=pl.CostEstimate(
            flops=15 * 10**10, bytes_accessed=5 * 10**7, transcendentals=10**7
        ),
    )(lengths, seq_order, row, weighted, tokens, q_rot, att, lse, middle, cot, kv, pay, pack, wo)


def on_device_fast(
    tokens,
    lengths,
    seq_order,
    routes,
    norm_attn,
    w_query,
    key_projection,
    value_projection,
    w_out,
    norm_moe,
    w_router,
    w_gate,
    w_up,
    w_down,
    cotangent,
):
    token_count, width = tokens.shape
    n_experts = w_router.shape[1]
    kv_width = KEY_VALUE_HEADS * HEAD_SIZE
    group_tokens = token_count * lax.axis_size("expert")
    pack = pack_weights(w_router, norm_attn, norm_moe, w_query, key_projection, value_projection)
    x_all, c_all, gw, uw, dw, pack, wo, kv_all, q_rot, attended, lse, middle, pay = front(
        lengths,
        seq_order,
        tokens,
        routes,
        pack,
        w_out,
        w_gate[0],
        w_up[0],
        w_down[0],
        cotangent,
        n_experts,
    )
    grad_row, weighted, gate_grad, up_grad, down_grad = moe(
        x_all.reshape(group_tokens, width + 128), c_all.reshape(group_tokens, width), gw, uw, dw
    )
    gate_mine, up_mine, down_mine = (
        lax.psum_scatter(grad, "dp", scatter_dimension=0, tiled=True).astype(F32)[None]
        for grad in (gate_grad, up_grad, down_grad)
    )
    output, tokens_grad, query_mine, mine, out_mine = back(
        lengths,
        seq_order,
        grad_row,
        weighted,
        tokens,
        q_rot,
        attended,
        lse,
        middle,
        cotangent,
        kv_all,
        pay,
        pack,
        wo,
        n_experts,
    )
    c_s = 2 * kv_width
    return (
        output,
        tokens_grad,
        mine[:, c_s + n_experts],
        query_mine,
        mine[:, :kv_width],
        mine[:, kv_width:c_s],
        out_mine,
        mine[:, c_s + n_experts + 1],
        mine[:, c_s : c_s + n_experts],
        gate_mine,
        up_mine,
        down_mine,
    )


def solution(mesh):
    both = ("dp", "expert")
    small = mesh.shape["dp"] == 4 and mesh.shape["expert"] == 8
    return jax.shard_map(
        on_device_fast if small else on_device,
        mesh=mesh,
        in_specs=(
            P(both, None),
            P("dp", None),
            P("dp", None),
            P(both, None),
            P(both),
            P(both, None),
            P(both, None),
            P(both, None),
            P(both, None),
            P(both),
            P(both, None),
            P("expert", "dp", None),
            P("expert", "dp", None),
            P("expert", "dp", None),
            P(both, None),
        ),
        out_specs=(
            P(both, None),
            P(both, None),
            P(both),
            P(both, None),
            P(both, None),
            P(both, None),
            P(both, None),
            P(both),
            P(both, None),
            P("expert", "dp", None),
            P("expert", "dp", None),
            P("expert", "dp", None),
        ),
        check_vma=False,
    )
```

```python
import functools
import math

import jax
import jax.numpy as jnp
from jax import lax
from jax.experimental import pallas as pl
from jax.experimental.pallas import tpu as pltpu
from jax.sharding import PartitionSpec as P

QUERY_HEADS = 12
KEY_VALUE_HEADS = 2
HEAD_SIZE = 128


EPSILON = 1e-06
ROPE_BASE = 10000.0
MASKED_SCORE = -1e30
BF = jnp.bfloat16
F32 = jnp.float32


def rms_scale(values):
    return lax.rsqrt(jnp.mean(values * values, axis=-1, keepdims=True) + EPSILON)


def rope_tables(positions, half_size):
    angle_steps = lax.broadcasted_iota(F32, (half_size,), 0)
    frequency = jnp.exp(angle_steps * (-math.log(ROPE_BASE) / half_size))
    angles = positions.astype(F32)[:, None] * frequency
    return (jnp.cos(angles)[:, None, :], jnp.sin(angles)[:, None, :])


def apply_rotation(values, cosine_table, sine_table):
    half_size = values.shape[-1] // 2
    first = values[..., :half_size]
    second = values[..., half_size:]
    return jnp.concatenate(
        [first * cosine_table - second * sine_table, second * cosine_table + first * sine_table],
        axis=-1,
    )


def reverse_rotation(grads_in, cosine_table, sine_table):
    return apply_rotation(grads_in, cosine_table, -sine_table)


def seq_layout(lengths, seq_order):
    count_seq = lengths.shape[1]
    picked = seq_order[0][:, None] == lax.broadcasted_iota(jnp.int32, (count_seq, count_seq), 1)
    ordered = jnp.sum(jnp.where(picked, lengths[0][None, :], 0), axis=1)
    return (ordered, jnp.cumsum(ordered))


def seq_place(positions, ordered, seq_ends):
    passed = seq_ends[None, :] <= positions[:, None]
    sequence_index = jnp.sum(passed.astype(jnp.int32), axis=1)
    starts = jnp.sum(jnp.where(passed, ordered[None, :], 0), axis=1)
    return (sequence_index, positions - starts)


def block_scores(
    query_rows, key_portion, query_seq, query_stream, key_seq, key_stream, score_scale
):
    raw_scores = (
        jnp.einsum("tkrd,skd->krts", query_rows, key_portion, preferred_element_type=F32)
        * score_scale
    )
    allowed = (query_seq[:, None] == key_seq[None, :]) & (
        key_stream[None, :] <= query_stream[:, None]
    )
    return jnp.where(allowed, raw_scores, MASKED_SCORE)


def norm_backward(grad_normed, unit_values, inv_scale, gain_float):
    scaled = grad_normed * gain_float
    gain_grad = jnp.sum(grad_normed * unit_values, axis=0)
    input_grad = inv_scale * (
        scaled - unit_values * jnp.mean(scaled * unit_values, axis=-1, keepdims=True)
    )
    return (gain_grad, input_grad)


def dot(a, b):
    return jnp.dot(a, b, preferred_element_type=F32)


def dot_nt(a, b):
    return jnp.einsum("ac,bc->ab", a, b, preferred_element_type=F32)


def dot_tn(a, b):
    return jnp.einsum("ta,tb->ab", a, b, preferred_element_type=F32)


def on_device(
    tokens,
    lengths,
    seq_order,
    routes,
    norm_attn,
    w_query,
    key_projection,
    value_projection,
    w_out,
    norm_moe,
    w_router,
    w_gate,
    w_up,
    w_down,
    cotangent,
):
    token_count, width = tokens.shape
    n_experts = w_router.shape[1]
    rows = w_query.shape[0]
    group_size = lax.axis_size("expert")
    my_index = lax.axis_index("expert")
    query_per_key_heads = QUERY_HEADS // KEY_VALUE_HEADS
    kv_width = KEY_VALUE_HEADS * HEAD_SIZE
    q_width = QUERY_HEADS * HEAD_SIZE
    score_scale = 1.0 / math.sqrt(HEAD_SIZE)
    group_tokens = token_count * group_size

    small = jnp.concatenate(
        [
            w_router,
            norm_attn[:, None],
            norm_moe[:, None],
            jnp.zeros((rows, 128 - n_experts - 2), BF),
        ],
        axis=1,
    )
    pack = jnp.concatenate([w_query, key_projection, value_projection, small, w_out], axis=1)
    gate_w = lax.all_gather(w_gate[0], "dp", axis=0, tiled=True)
    up_w = lax.all_gather(w_up[0], "dp", axis=0, tiled=True)
    down_w = lax.all_gather(w_down[0], "dp", axis=0, tiled=True)
    pack = lax.all_gather(pack, ("dp", "expert"), axis=0, tiled=True)
    cot_all = lax.all_gather(cotangent, "expert", axis=0, tiled=True)
    c_k = q_width
    c_v = c_k + kv_width
    c_s = c_v + kv_width
    c_o = c_s + 128
    query_w = pack[:, :c_k]
    key_w = pack[:, c_k:c_v]
    value_w = pack[:, c_v:c_s]
    router_w = pack[:, c_s : c_s + n_experts]
    gain_one = pack[:, c_s + n_experts].astype(F32)
    gain_two = pack[:, c_s + n_experts + 1].astype(F32)
    out_w = pack[:, c_o:]

    seq_lens, seq_ends = seq_layout(lengths, seq_order)
    my_stream = lax.broadcasted_iota(jnp.int32, (token_count,), 0) * group_size + my_index
    query_seq, query_rel = seq_place(my_stream, seq_lens, seq_ends)
    all_rows = lax.broadcasted_iota(jnp.int32, (group_tokens,), 0)
    key_stream = all_rows % token_count * group_size + all_rows // token_count
    key_seq = seq_place(key_stream, seq_lens, seq_ends)[0]
    block_row_count = math.gcd(group_tokens, 512)
    block_count = group_tokens // block_row_count
    cosine_table, sine_table = rope_tables(query_rel, HEAD_SIZE // 2)
    inputs_float = tokens.astype(F32)
    inv_one = rms_scale(inputs_float)
    unit_one = inputs_float * inv_one
    normed_one = (unit_one * gain_one).astype(BF)
    query_pre = dot(normed_one, query_w)
    key_pre = dot(normed_one, key_w)
    value_pre = dot(normed_one, value_w)
    rotated_queries = (
        apply_rotation(
            query_pre.reshape(token_count, QUERY_HEADS, HEAD_SIZE), cosine_table, sine_table
        )
        .astype(BF)
        .reshape(token_count, KEY_VALUE_HEADS, query_per_key_heads, HEAD_SIZE)
    )
    rotated_keys = apply_rotation(
        key_pre.reshape(token_count, KEY_VALUE_HEADS, HEAD_SIZE),
        cosine_table,
        sine_table,
    ).astype(BF)
    key_value = jnp.concatenate(
        [rotated_keys.reshape(token_count, kv_width), value_pre.astype(BF)],
        axis=1,
    )
    gathered = lax.all_gather(key_value, "expert", axis=0, tiled=True)
    key_blocks = (
        gathered.reshape(block_count, block_row_count, 2 * kv_width),
        key_seq.reshape(block_count, block_row_count),
        key_stream.reshape(block_count, block_row_count),
    )

    def stats_step(carry, blocks):
        run_max, run_sum = carry
        key_value_block, seq_block, stream_block = blocks
        key_portion = key_value_block[:, :kv_width].reshape(-1, KEY_VALUE_HEADS, HEAD_SIZE)
        scores = block_scores(
            rotated_queries, key_portion, query_seq, my_stream, seq_block, stream_block, score_scale
        )
        new_max = jnp.maximum(run_max, jnp.max(scores, axis=-1))
        run_sum = run_sum * jnp.exp(run_max - new_max) + jnp.sum(
            jnp.exp(scores - new_max[..., None]), axis=-1
        )
        return ((new_max, run_sum), None)

    initial_maximum = jnp.full(
        (KEY_VALUE_HEADS, query_per_key_heads, token_count), MASKED_SCORE, F32
    )
    (row_max, row_sum), unused = lax.scan(
        stats_step, (initial_maximum, jnp.zeros_like(initial_maximum)), key_blocks
    )
    log_total = row_max + jnp.log(row_sum)

    def value_step(summed, blocks):
        key_value_block, seq_block, stream_block = blocks
        key_portion = key_value_block[:, :kv_width].reshape(-1, KEY_VALUE_HEADS, HEAD_SIZE)
        value_portion = key_value_block[:, kv_width:].reshape(-1, KEY_VALUE_HEADS, HEAD_SIZE)
        scores = block_scores(
            rotated_queries, key_portion, query_seq, my_stream, seq_block, stream_block, score_scale
        )
        low_chances = jnp.exp(scores - log_total[..., None]).astype(BF)
        summed = summed + jnp.einsum(
            "krts,skd->tkrd", low_chances, value_portion, preferred_element_type=F32
        )
        return (summed, None)

    empty_head_state = jnp.zeros(
        (token_count, KEY_VALUE_HEADS, query_per_key_heads, HEAD_SIZE), F32
    )
    attended, unused = lax.scan(value_step, empty_head_state, key_blocks)
    attended_low = attended.reshape(token_count, q_width).astype(BF)
    middle = inputs_float + dot(attended_low, out_w)
    inv_two = rms_scale(middle)
    unit_two = middle * inv_two
    normed_two = (unit_two * gain_two).astype(BF)

    logits = dot(normed_two, router_w)
    choose = jnp.any(
        routes[:, :, None] == lax.broadcasted_iota(jnp.int32, (1, 1, n_experts), 2), axis=1
    )
    top_logit = jnp.max(jnp.where(choose, logits, -jnp.inf), axis=1, keepdims=True)
    spread = jnp.where(choose, jnp.exp(jnp.minimum(logits - top_logit, 0.0)), 0.0)
    gates = spread / jnp.sum(spread, axis=1, keepdims=True)

    normed_all = lax.all_gather(normed_two, "expert", axis=0, tiled=True)
    gates_all = lax.all_to_all(
        gates.T.reshape(n_experts, 1, token_count), "expert", split_axis=0, concat_axis=1, tiled=True
    )
    gate_col = gates_all.reshape(group_tokens, 1)

    gate_pre = dot(normed_all, gate_w)
    up_pre = dot(normed_all, up_w)
    sig = jax.nn.sigmoid(gate_pre)
    silu = gate_pre * sig
    hidden = (silu * up_pre).astype(BF)
    returned = dot(hidden, down_w).astype(BF).astype(F32)
    cot_float = cot_all.astype(F32)
    grad_gates = jnp.sum(cot_float * returned, axis=1)
    weighted = (gate_col * returned).astype(BF)
    grad_returned = (gate_col * cot_float).astype(BF)
    grad_hidden = dot_nt(grad_returned, down_w)
    grad_gate_pre = (grad_hidden * up_pre * sig * (1.0 + gate_pre * (1.0 - sig))).astype(BF)
    grad_up_pre = (grad_hidden * silu).astype(BF)
    grad_row = (dot_nt(grad_gate_pre, gate_w) + dot_nt(grad_up_pre, up_w)).astype(BF)
    down_grad = dot_tn(hidden, grad_returned).astype(BF)
    gate_grad = dot_tn(normed_all, grad_gate_pre).astype(BF)
    up_grad = dot_tn(normed_all, grad_up_pre).astype(BF)

    grad_gates = lax.all_to_all(
        grad_gates.reshape(group_size, 1, token_count), "expert", split_axis=0, concat_axis=1, tiled=True
    ).reshape(n_experts, token_count).T
    row_sum_grad = lax.psum_scatter(grad_row, "expert", scatter_dimension=0, tiled=True)
    output = (
        middle + lax.psum_scatter(weighted, "expert", scatter_dimension=0, tiled=True).astype(F32)
    ).astype(BF)

    grad_out = cotangent.astype(F32)
    grad_logits = (
        gates * (grad_gates - jnp.sum(gates * grad_gates, axis=1, keepdims=True))
    ).astype(BF)
    router_grad = dot_tn(normed_two, grad_logits)
    grad_normed_two = dot_nt(grad_logits, router_w) + row_sum_grad.astype(F32)
    gain_two_grad, grad_middle = norm_backward(grad_normed_two, unit_two, inv_two, gain_two)
    grad_middle = grad_out + grad_middle
    grad_mixed = grad_middle.astype(BF)
    out_grad = dot_tn(attended_low, grad_mixed)
    grad_attended = dot_nt(grad_mixed, out_w).astype(BF)
    head_gradient = grad_attended.reshape(
        token_count, KEY_VALUE_HEADS, query_per_key_heads, HEAD_SIZE
    )
    row_dot = jnp.transpose(jnp.sum(head_gradient.astype(F32) * attended, axis=-1), (1, 2, 0))

    def grad_step(query_grad, blocks):
        key_value_block, seq_block, stream_block = blocks
        key_portion = key_value_block[:, :kv_width].reshape(-1, KEY_VALUE_HEADS, HEAD_SIZE)
        value_portion = key_value_block[:, kv_width:].reshape(-1, KEY_VALUE_HEADS, HEAD_SIZE)
        scores = block_scores(
            rotated_queries, key_portion, query_seq, my_stream, seq_block, stream_block, score_scale
        )
        chances = jnp.exp(scores - log_total[..., None])
        low_chances = chances.astype(BF)
        grad_chances = jnp.einsum(
            "tkrd,skd->krts", head_gradient, value_portion, preferred_element_type=F32
        )
        grad_scores = (chances * (grad_chances - row_dot[..., None])).astype(BF)
        query_grad = query_grad + jnp.einsum(
            "krts,skd->tkrd", grad_scores, key_portion, preferred_element_type=F32
        )
        key_terms = (
            jnp.einsum("krts,tkrd->skd", grad_scores, rotated_queries, preferred_element_type=F32)
            * score_scale
        )
        value_terms = jnp.einsum(
            "krts,tkrd->skd", low_chances, head_gradient, preferred_element_type=F32
        )
        return (query_grad, (key_terms.astype(BF), value_terms.astype(BF)))

    query_grad, (key_terms, value_terms) = lax.scan(grad_step, empty_head_state, key_blocks)
    query_grad = query_grad * score_scale
    kv_terms = jnp.concatenate(
        [key_terms.reshape(group_tokens, kv_width), value_terms.reshape(group_tokens, kv_width)],
        axis=1,
    )
    kv_mine = lax.psum_scatter(kv_terms, "expert", scatter_dimension=0, tiled=True)
    grad_query_pre = (
        reverse_rotation(
            query_grad.reshape(token_count, QUERY_HEADS, HEAD_SIZE), cosine_table, sine_table
        )
        .reshape(token_count, q_width)
        .astype(BF)
    )
    grad_key_pre = (
        reverse_rotation(
            kv_mine[:, :kv_width].astype(F32).reshape(token_count, KEY_VALUE_HEADS, HEAD_SIZE),
            cosine_table,
            sine_table,
        )
        .reshape(token_count, kv_width)
        .astype(BF)
    )
    grad_qkv = jnp.concatenate([grad_query_pre, grad_key_pre, kv_mine[:, kv_width:]], axis=1)
    grad_normed_one = dot_nt(grad_qkv, pack[:, :c_s])
    qkv_grad = dot_tn(normed_one, grad_qkv)
    gain_one_grad, grad_input = norm_backward(grad_normed_one, unit_one, inv_one, gain_one)
    tokens_grad = (grad_middle + grad_input).astype(BF)
    small_grad = jnp.concatenate(
        [
            router_grad,
            gain_one_grad[:, None],
            gain_two_grad[:, None],
            jnp.zeros((width, 128 - n_experts - 2), F32),
        ],
        axis=1,
    )
    pack_grad = jnp.concatenate(
        [qkv_grad.astype(BF), small_grad.astype(BF), out_grad.astype(BF)], axis=1
    )
    mine = lax.psum_scatter(pack_grad, ("dp", "expert"), scatter_dimension=0, tiled=True)
    mine = mine.astype(F32)
    gate_mine, up_mine, down_mine = (
        lax.psum_scatter(grad, "dp", scatter_dimension=0, tiled=True).astype(F32)[None]
        for grad in (gate_grad, up_grad, down_grad)
    )
    return (
        output,
        tokens_grad,
        mine[:, c_s + n_experts],
        mine[:, :c_k],
        mine[:, c_k:c_v],
        mine[:, c_v:c_s],
        mine[:, c_o:],
        mine[:, c_s + n_experts + 1],
        mine[:, c_s : c_s + n_experts],
        gate_mine,
        up_mine,
        down_mine,
    )


MESH_ID = pl.DeviceIdType.MESH
ANY = pl.ANY
LOG2E = math.log2(math.e)


class Place:
    def __init__(self):
        d = lax.axis_index("dp")
        e = lax.axis_index("expert")
        core = lax.rem(e, 2)
        x = lax.rem(lax.div(e, 2), 2)
        y = lax.div(e, 4)
        self.d, self.e, self.core = d, e, core
        self.chip = lax.div(e, 2)
        self.e_s = e + 1 - 2 * core
        self.e_x = e + 2 - 4 * x
        self.e_y = e + 4 - 8 * y
        self.e_d = self.e_x + 4 - 8 * y
        self.chip_x = self.chip + 1 - 2 * x
        self.chip_y = self.chip + 2 - 4 * y
        self.chip_d = self.chip_x + 2 - 4 * y
        self.sib = (d, self.e_s)
        self.nx = (d, self.e_x)
        self.ny = (d, self.e_y)
        half = lax.div(d, 2)
        odd = lax.rem(d, 2)
        self.pair = (2 * half + 1 - odd, e)
        self.cross = (3 - d, e)
        self.inner = (d == 1) | (d == 2)
        self.order = (d, 2 * half + 1 - odd, 2 - half, 3 - 3 * half)

    def greet(self):
        barrier = pltpu.get_barrier_semaphore()
        for other in (self.sib, self.nx, self.ny, self.pair):
            pl.semaphore_signal(barrier, inc=1, device_id=other, device_id_type=MESH_ID)

        @pl.when(self.inner)
        def _():
            pl.semaphore_signal(barrier, inc=1, device_id=self.cross, device_id_type=MESH_ID)
            pl.semaphore_wait(barrier, 5)

        @pl.when(jnp.logical_not(self.inner))
        def _():
            pl.semaphore_wait(barrier, 4)


def rcopy(src, dst, send_sem, recv_sem, device):
    return pltpu.make_async_remote_copy(
        src_ref=src,
        dst_ref=dst,
        send_sem=send_sem,
        recv_sem=recv_sem,
        device_id=device,
        device_id_type=MESH_ID,
    )


class PlaneGather:
    def __init__(self, at, blk, half, send, recv):
        self.at, self.blk, self.half, self.send, self.recv = at, blk, half, send, recv

    def push(self, ref, target, slot_send, slot_recv, src=None):
        rcopy(
            ref if src is None else src, ref, self.send(slot_send), self.recv(slot_recv), target
        ).start()

    def await_(self, ref, slot):
        rcopy(ref, ref, self.send(0), self.recv(slot), self.at.sib).wait_recv()

    def sent(self, ref, slot):
        rcopy(ref, ref, self.send(slot), self.recv(0), self.at.sib).wait_send()

    def start(self, src=None):
        at = self.at
        own = self.blk(at.e)
        self.push(own, at.nx, 0, 0, src)
        self.push(own, at.ny, 1, 1, src)
        self.push(own, at.sib, 2, 4, src)

    def on_x(self):
        at = self.at
        got = self.blk(at.e_x)
        self.await_(got, 0)
        self.push(self.half(at.e_x, 0), at.ny, 3, 3)
        self.push(got, at.sib, 4, 5)

    def on_y(self):
        at = self.at
        got = self.blk(at.e_y)
        self.await_(got, 1)
        self.push(self.half(at.e_y, 1), at.nx, 5, 2)
        self.push(got, at.sib, 6, 6)

    def on_d(self):
        at = self.at
        self.await_(self.half(at.e_d, 1), 2)
        self.await_(self.half(at.e_d, 0), 3)
        self.push(self.blk(at.e_d), at.sib, 7, 7)

    def on_s(self):
        at = self.at
        turn = at.e_s - at.e
        self.await_(self.blk(at.e_s), 4)
        self.await_(self.blk(at.e_x + turn), 5)
        self.await_(self.blk(at.e_y + turn), 6)
        self.await_(self.blk(at.e_d + turn), 7)

    def drain(self):
        at = self.at
        whole = self.blk(at.e)
        for slot in (0, 1, 2, 4, 6, 7):
            self.sent(whole, slot)
        self.sent(self.half(at.e, 0), 3)
        self.sent(self.half(at.e, 1), 5)


class LineGather:
    def __init__(self, at, blk, send, recv):
        self.at, self.blk, self.send, self.recv = at, blk, send, recv

    def start(self, src=None):
        at = self.at
        own = self.blk(at.d)
        from_ = own if src is None else src
        rcopy(from_, own, self.send(0), self.recv(1), at.pair).start()

        @pl.when(at.inner)
        def _():
            rcopy(from_, own, self.send(1), self.recv(2), at.cross).start()

    def on(self, k):
        at = self.at
        got = self.blk(at.order[k])
        rcopy(got, got, self.send(0), self.recv(k), at.pair).wait_recv()

        @pl.when(at.inner)
        def _():
            if k == 1:
                rcopy(got, got, self.send(2), self.recv(3), at.cross).start()
            else:
                rcopy(got, got, self.send(k + 1), self.recv(k), at.pair).start()

    def relay(self, k):
        @pl.when(self.at.inner)
        def _():
            self.on(k)

    def land(self):
        at = self.at

        @pl.when(jnp.logical_not(at.inner))
        def _():
            for k in (1, 2, 3):
                got = self.blk(at.order[k])
                rcopy(got, got, self.send(0), self.recv(k), at.pair).wait_recv()

    def drain(self):
        at = self.at
        own = self.blk(at.d)
        rcopy(own, own, self.send(0), self.recv(0), at.pair).wait_send()

        @pl.when(at.inner)
        def _():
            for slot in (1, 2, 3, 4):
                rcopy(own, own, self.send(slot), self.recv(0), at.pair).wait_send()


def rows_of(ref, start, size):
    return ref.at[pl.ds(pl.multiple_of(start, 16), size)]


def stream_facts(lens_ref, order_ref, token_count, group_size, e):
    count = lens_ref.shape[1]
    stream = lax.broadcasted_iota(jnp.int32, (token_count, 128), 0) * group_size + e
    begin = jnp.zeros_like(stream)
    end = jnp.int32(0)
    for j in range(count):
        size = jnp.int32(0)
        for i in range(count):
            size = size + jnp.where(order_ref[0, j] == i, lens_ref[0, i], 0)
        end = end + size
        begin = begin + jnp.where(stream >= end, size, 0)
    return stream, begin, stream - begin


def rotary(relative):
    lane = lax.rem(lax.broadcasted_iota(jnp.int32, relative.shape, 1), HEAD_SIZE // 2)
    frequency = jnp.exp(lane.astype(F32) * (-math.log(ROPE_BASE) / (HEAD_SIZE // 2)))
    angles = relative.astype(F32) * frequency
    first = lax.broadcasted_iota(jnp.int32, relative.shape, 1) < HEAD_SIZE // 2
    sine = jnp.sin(angles)
    return jnp.cos(angles), jnp.where(first, -sine, sine)


def swap_halves(values):
    return pltpu.roll(values, HEAD_SIZE // 2, 1)


TILE = 64


def tiles_of(i):
    return range(max(0, i - 2), i + 1)


def tile_bias(i, r, stream, begin, group_size):
    wide = TILE * group_size
    j = lax.broadcasted_iota(jnp.int32, (TILE, wide), 1)
    key = (r * TILE + lax.rem(j, TILE)) * group_size + lax.div(j, TILE)
    ok = key >= begin[i * TILE : (i + 1) * TILE, :1]
    if r == i:
        ok = ok & (key <= stream[i * TILE : (i + 1) * TILE, :1])
    return jnp.where(ok, 0.0, MASKED_SCORE)


def dot_nn(a, b):
    return lax.dot_general(a, b, (((1,), (0,)), ((), ())), preferred_element_type=F32)


def dot_bt(a, b):
    return lax.dot_general(a, b, (((1,), (1,)), ((), ())), preferred_element_type=F32)


def dot_at(a, b):
    return lax.dot_general(a, b, (((0,), (0,)), ((), ())), preferred_element_type=F32)


def column_as_row(small, lane):
    pick = (lax.broadcasted_iota(jnp.int32, (8, 128), 1) == lane).astype(F32).astype(BF)
    return dot_bt(pick, small)[:1]


def front_kernel(
    n_experts,
    lens_ref,
    order_ref,
    tok_ref,
    routes_ref,
    pack_ref,
    wo_ref,
    gw_ref,
    uw_ref,
    x_all,
    gw_all,
    uw_all,
    pack_out,
    wo_out,
    kv_out,
    q_out,
    att_out,
    lse_out,
    mid_out,
    pay_ref,
    pack_all,
    wo_all,
    kv_all,
    unit_ref,
    acc_ref,
    s_ref,
    ag_send,
    ag_recv,
    z_send,
    z_recv,
    local,
):
    at = Place()
    at.greet()
    tokens, width = tok_ref.shape
    shard = pack_ref.shape[0]
    group = 8
    kv_width = KEY_VALUE_HEADS * HEAD_SIZE
    q_width = QUERY_HEADS * HEAD_SIZE
    qkv = q_width + 2 * kv_width
    per_kv = QUERY_HEADS // KEY_VALUE_HEADS
    chunk = shard * group
    cut_a = 9 * 128
    cut_b = wo_ref.shape[1] // 2
    items = {}

    def add_item(name, blk, half):
        n = len(items)
        items[name] = PlaneGather(
            at, blk, half, lambda k, n=n: ag_send.at[n, k], lambda k, n=n: ag_recv.at[n, k]
        )

    def add_weight(name, ref, z, cut):
        wide = ref.shape[1]

        def place(e):
            return pl.ds(pl.multiple_of(z * chunk + e * shard, 16), shard)

        def half(e, h):
            return ref.at[place(e), pl.ds(0, cut) if h == 0 else pl.ds(cut, wide - cut)]

        add_item(name, lambda e: ref.at[place(e)], half)

    for k in range(4):
        add_weight(("a", k), pack_all, at.order[k], cut_a)
    for k in range(4):
        add_weight(("b", k), wo_all, at.order[k], cut_b)
    add_item("kv", lambda e: kv_all.at[e], lambda e, h: kv_all.at[e, :, pl.ds(h * kv_width, kv_width)])
    part = tokens // 2
    for name, ref, cut in (("x", x_all, 7 * 128),):
        wide = ref.shape[2]
        for k in range(2):
            rows = pl.ds(k * part, part)

            def half(e, h, ref=ref, rows=rows, cut=cut, wide=wide):
                return ref.at[e, rows, pl.ds(0, cut) if h == 0 else pl.ds(cut, wide - cut)]

            add_item((name, k), lambda e, ref=ref, rows=rows: ref.at[e, rows], half)

    lines = {}

    def add_line(name, ref, size, start):
        n = len(lines)
        lines[name] = LineGather(
            at,
            lambda z: rows_of(ref, start(z), size),
            lambda k, n=n: z_send.at[n, k],
            lambda k, n=n: z_recv.at[n, k],
        )

    add_line("a", pack_all, shard, lambda z: z * chunk + at.e * shard)
    add_line("b", wo_all, shard, lambda z: z * chunk + at.e * shard)
    for name, ref, src in (("g", gw_all, gw_ref), ("u", uw_all, uw_ref)):
        size = src.shape[0]
        add_line(name, ref, size, lambda z, size=size: z * size)

    own_a = rows_of(pack_all, at.d * chunk + at.e * shard, shard)
    own_b = rows_of(wo_all, at.d * chunk + at.e * shard, shard)
    copies = [
        pltpu.make_async_copy(pack_ref, own_a, local.at[0]),
        pltpu.make_async_copy(wo_ref, own_b, local.at[1]),
    ]
    for n, (name, src) in enumerate((("g", gw_ref), ("u", uw_ref))):
        copies.append(pltpu.make_async_copy(src, lines[name].blk(at.d), local.at[2 + n]))

    lines["a"].start(pack_ref)
    items["a", 0].start(pack_ref)
    lines["b"].start(wo_ref)
    for copy in copies:
        copy.start()

    tok = tok_ref[...].astype(F32)
    scale_one = lax.rsqrt(jnp.mean(tok * tok, axis=1, keepdims=True) + EPSILON)
    unit_ref[...] = tok * scale_one
    stream, begin, relative = stream_facts(lens_ref, order_ref, tokens, group, at.e)
    cosine, sine = rotary(relative)
    acc_ref[...] = jnp.zeros_like(acc_ref)
    copies[0].wait()
    copies[1].wait()

    def consume(k):
        z = at.order[k]
        place = pl.ds(pl.multiple_of(z * chunk, 128), chunk)
        gain = column_as_row(pack_all[place, qkv:], n_experts)
        normed = (unit_ref[:, place] * gain).astype(BF)
        acc_ref[...] += dot_nn(normed, pack_all[place, :qkv])

    lines["a"].on(1)
    items["a", 1].start()
    items["a", 0].on_x()
    items["a", 0].on_y()
    lines["g"].start(gw_ref)
    items["a", 0].on_d()
    lines["a"].on(2)
    items["a", 2].start()
    items["a", 1].on_x()
    items["a", 1].on_y()
    items["a", 0].on_s()
    consume(0)
    lines["a"].on(3)
    items["a", 3].start()
    lines["b"].on(1)
    lines["u"].start(uw_ref)
    items["a", 1].on_d()
    items["a", 2].on_x()
    items["a", 2].on_y()
    items["a", 1].on_s()
    consume(1)
    lines["b"].on(2)
    items["a", 2].on_d()
    items["a", 3].on_x()
    items["a", 3].on_y()
    items["b", 0].start()
    items["a", 2].on_s()
    consume(2)
    lines["b"].on(3)
    items["a", 3].on_d()
    items["a", 3].on_s()
    consume(3)
    lines["g"].relay(1)
    keep = [
        pltpu.make_async_copy(pack_all, pack_out, local.at[7]),
    ]
    keep[0].start()

    def turned(col):
        v = acc_ref[:, col : col + HEAD_SIZE]
        return (v * cosine + swap_halves(v) * sine).astype(BF)

    for h in range(KEY_VALUE_HEADS):
        kv_all[at.e, :, h * HEAD_SIZE : (h + 1) * HEAD_SIZE] = turned(q_width + h * HEAD_SIZE)
    kv_all[at.e, :, kv_width:] = acc_ref[:, q_width + kv_width :].astype(BF)
    items["kv"].start()
    for h in range(QUERY_HEADS):
        q_out[h] = turned(h * HEAD_SIZE)
    items["b", 0].on_x()
    items["b", 0].on_y()
    items["b", 1].start()
    items["kv"].on_x()
    items["kv"].on_y()
    items["b", 0].on_d()
    items["b", 2].start()
    items["kv"].on_d()
    items["kv"].on_s()
    keep.append(pltpu.make_async_copy(kv_all, kv_out, local.at[8]))
    keep[1].start()

    def step_b(n):
        if n == 0:
            items["b", 1].on_x()
            items["b", 1].on_y()
            items["b", 3].start()
        elif n == 1:
            lines["g"].relay(2)
            items["b", 1].on_d()
            items["b", 2].on_x()
            items["b", 2].on_y()
        elif n == 2:
            lines["u"].relay(1)
            items["b", 2].on_d()
            items["b", 3].on_x()
            items["b", 3].on_y()
        elif n == 3:
            items["b", 3].on_d()
            lines["u"].relay(2)

    factor = LOG2E / math.sqrt(HEAD_SIZE)
    wide = TILE * group
    for i in range(tokens // TILE):
        step_b(i)
        first = tiles_of(i)[0]
        biases = [tile_bias(i, r, stream, begin, group) for r in tiles_of(i)]
        here = slice(i * TILE, (i + 1) * TILE)
        for g in range(KEY_VALUE_HEADS):
            queries = q_out[g * per_kv : (g + 1) * per_kv, here, :].reshape(per_kv * TILE, HEAD_SIZE)
            top = None
            for r in tiles_of(i):
                keys = kv_all[:, r * TILE : (r + 1) * TILE, g * HEAD_SIZE : (g + 1) * HEAD_SIZE]
                s = dot_bt(queries, keys.reshape(wide, HEAD_SIZE)) * factor
                s = s.reshape(per_kv, TILE, wide) + biases[r - first][None]
                s = s.reshape(per_kv * TILE, wide)
                s_ref[:, (r - first) * wide : (r - first + 1) * wide] = s
                high = jnp.max(s, axis=1, keepdims=True)
                top = high if top is None else jnp.maximum(top, high)
            total = None
            mixed = None
            for r in tiles_of(i):
                p = jnp.exp2(s_ref[:, (r - first) * wide : (r - first + 1) * wide] - top)
                values = kv_all[
                    :, r * TILE : (r + 1) * TILE, kv_width + g * HEAD_SIZE : kv_width + (g + 1) * HEAD_SIZE
                ].reshape(wide, HEAD_SIZE)
                row = jnp.sum(p, axis=1, keepdims=True)
                term = dot_nn(p.astype(BF), values)
                total = row if total is None else total + row
                mixed = term if mixed is None else mixed + term
            mixed = mixed / total
            lse_out[g, i] = jnp.broadcast_to(top + jnp.log2(total), (per_kv * TILE, 128))
            for h in range(per_kv):
                col = (g * per_kv + h) * HEAD_SIZE
                att_out[here, col : col + HEAD_SIZE] = mixed[h * TILE : (h + 1) * TILE]

    for k in range(4):
        items["b", k].on_s()
    keep.append(pltpu.make_async_copy(wo_all, wo_out, local.at[9]))
    keep[2].start()
    lines["g"].relay(3)
    attended = att_out[...].astype(BF)
    step = 256
    for n in range(width // step):
        cols = slice(n * step, (n + 1) * step)
        mid_out[:, cols] = tok_ref[:, cols].astype(F32) + dot_nn(attended, wo_all[:, cols])
    middle = mid_out[...]
    scale_two = lax.rsqrt(jnp.mean(middle * middle, axis=1, keepdims=True) + EPSILON)
    small = pack_all[:, qkv:]
    normed_two = (middle * scale_two * column_as_row(small, n_experts + 1)).astype(BF)
    pay_ref[:, :width] = normed_two
    logits = dot_nn(normed_two, small)
    lane = lax.broadcasted_iota(jnp.int32, (tokens, 128), 1)
    choose = lane == routes_ref[:, :1]
    for k in range(1, routes_ref.shape[1]):
        choose = choose | (lane == routes_ref[:, k : k + 1])
    top = jnp.max(jnp.where(choose, logits, MASKED_SCORE), axis=1, keepdims=True)
    spread = jnp.where(choose, jnp.exp(jnp.minimum(logits - top, 0.0)), 0.0)
    gates = spread / jnp.sum(spread, axis=1, keepdims=True)
    pay_ref[:, width:] = split_three(gates)
    own_x = [
        pltpu.make_async_copy(
            pay_ref.at[pl.ds(k * part, part)], x_all.at[at.e, pl.ds(k * part, part)], local.at[10 + k]
        )
        for k in range(2)
    ]
    for k in range(2):
        items["x", k].start(pay_ref.at[pl.ds(k * part, part)])
        own_x[k].start()
    lines["u"].relay(3)
    for k in range(2):
        items["x", k].on_x()
        items["x", k].on_y()
    for k in range(2):
        items["x", k].on_d()
    for k in range(2):
        items["x", k].on_s()
    lines["g"].land()
    lines["u"].land()
    for item in items.values():
        item.drain()
    for line in lines.values():
        line.drain()
    for copy in copies[2:] + keep + own_x:
        copy.wait()


def split_three(values):
    high = values.astype(BF).astype(F32)
    mid = (values - high).astype(BF).astype(F32)
    low = values - high - mid
    return (high + pltpu.roll(mid, 32, 1) + pltpu.roll(low, 64, 1)).astype(BF)


def front(lengths, seq_order, tokens, routes, pack, wo, gw, uw, n_experts):
    count, width = tokens.shape
    group, line = 8, 4
    kv_width = KEY_VALUE_HEADS * HEAD_SIZE
    per_kv = QUERY_HEADS // KEY_VALUE_HEADS
    sds = jax.ShapeDtypeStruct
    smem = pl.BlockSpec(memory_space=pltpu.SMEM)
    vmem = pl.BlockSpec(memory_space=pltpu.VMEM)
    hbm = pl.BlockSpec(memory_space=ANY)
    n_items = 11
    return pl.pallas_call(
        functools.partial(front_kernel, n_experts),
        in_specs=[smem, smem] + [vmem] * 6,
        out_specs=(hbm,) * 6 + (vmem,) * 5,
        out_shape=(
            sds((group, count, width + 128), BF),
            sds((line * gw.shape[0], gw.shape[1]), BF),
            sds((line * uw.shape[0], uw.shape[1]), BF),
            sds((width, pack.shape[1]), BF),
            sds((width, wo.shape[1]), BF),
            sds((group, count, 2 * kv_width), BF),
            sds((QUERY_HEADS, count, HEAD_SIZE), BF),
            sds((count, QUERY_HEADS * HEAD_SIZE), F32),
            sds((KEY_VALUE_HEADS, count // TILE, per_kv * TILE, 128), F32),
            sds((count, width), F32),
            sds((count, width + 128), BF),
        ),
        scratch_shapes=[
            pltpu.VMEM((width, pack.shape[1]), BF),
            pltpu.VMEM((width, wo.shape[1]), BF),
            pltpu.VMEM((group, count, 2 * kv_width), BF),
            pltpu.VMEM((count, width), F32),
            pltpu.VMEM((count, pack.shape[1] - 128), F32),
            pltpu.VMEM((per_kv * TILE, 3 * TILE * group), F32),
            pltpu.SemaphoreType.DMA((n_items, 8)),
            pltpu.SemaphoreType.DMA((n_items, 8)),
            pltpu.SemaphoreType.DMA((4, 5)),
            pltpu.SemaphoreType.DMA((4, 4)),
            pltpu.SemaphoreType.DMA((12,)),
        ],
        compiler_params=pltpu.CompilerParams(
            collective_id=1, has_side_effects=True, vmem_limit_bytes=60 * 2**20
        ),
    )(lengths, seq_order, tokens, routes, pack, wo, gw, uw)


class PlaneReduce:
    def __init__(self, at, first, own, seat, xs, ys, x2, y2, cut, send, recv):
        self.at, self.first, self.own = at, first, own
        self.seat, self.xs, self.ys, self.x2, self.y2 = seat, xs, ys, x2, y2
        self.cut, self.send, self.recv = cut, send, recv

    def copy(self, slot, src, dst, target):
        return rcopy(src, dst, self.send(slot), self.recv(slot), target)

    def moves(self):
        at, own, cut = self.at, self.own, self.cut
        low, high = pl.ds(0, cut), pl.ds(cut, self.seat.shape[-1] - cut)
        return {
            0: lambda: self.copy(0, self.first, self.seat, at.sib),
            1: lambda: self.copy(1, own.at[at.chip_x, :, low], self.xs.at[0], at.nx),
            2: lambda: self.copy(2, own.at[at.chip_d, :, low], self.xs.at[1], at.nx),
            3: lambda: self.copy(3, own.at[at.chip_y, :, high], self.ys.at[0], at.ny),
            4: lambda: self.copy(4, own.at[at.chip_d, :, high], self.ys.at[1], at.ny),
            5: lambda: self.copy(5, own.at[at.chip_y, :, low], self.y2, at.ny),
            6: lambda: self.copy(6, own.at[at.chip_x, :, high], self.x2, at.nx),
        }

    def begin(self, slot):
        self.moves()[slot]().start()

    def got(self, slot):
        self.moves()[slot]().wait_recv()

    def start(self):
        self.begin(0)

    def on_s(self):
        self.got(0)

        def add(q, none):
            self.own[q] = (self.own[q].astype(F32) + self.seat[q].astype(F32)).astype(BF)
            return none

        lax.fori_loop(0, 4, add, 0)
        for slot in (1, 2, 3, 4):
            self.begin(slot)

    def on_xy(self):
        at, own, cut = self.at, self.own, self.cut
        self.got(1)
        self.got(2)
        own[at.chip_y, :, :cut] = (
            own[at.chip_y, :, :cut].astype(F32) + self.xs[1].astype(F32)
        ).astype(BF)
        self.begin(5)
        self.got(3)
        self.got(4)
        own[at.chip_x, :, cut:] = (
            own[at.chip_x, :, cut:].astype(F32) + self.ys[1].astype(F32)
        ).astype(BF)
        self.begin(6)

    def finish(self):
        at, own, cut = self.at, self.own, self.cut
        self.got(5)
        low = own[at.chip, :, :cut].astype(F32) + self.xs[0].astype(F32) + self.y2[...].astype(F32)
        self.got(6)
        high = own[at.chip, :, cut:].astype(F32) + self.ys[0].astype(F32) + self.x2[...].astype(F32)
        return low, high

    def sent(self, slot):
        self.moves()[slot]().wait_send()

    def drain(self, slots=range(7)):
        for slot in slots:
            self.sent(slot)


class LineReduce:
    def __init__(self, at, blocks, near, far, send, recv):
        self.at, self.blocks, self.near, self.far = at, blocks, near, far
        self.send, self.recv = send, recv

    def copy(self, slot, src, dst, target):
        return rcopy(src, dst, self.send(slot), self.recv(slot), target)

    def outer_moves(self):
        at = self.at
        return [
            self.copy(n, self.blocks.at[at.order[n + 1]], self.near.at[n], at.pair)
            for n in range(3)
        ]

    def cross_moves(self):
        at = self.at
        return [
            self.copy(3 + n, self.blocks.at[at.order[n + 2]], self.far.at[n], at.cross)
            for n in range(2)
        ]

    def back_move(self):
        at = self.at
        return self.copy(0, self.blocks.at[at.order[1]], self.near.at[0], at.pair)

    def start(self):
        at = self.at

        @pl.when(jnp.logical_not(at.inner))
        def _():
            for move in self.outer_moves():
                move.start()

    def middle(self):
        at, blocks = self.at, self.blocks

        @pl.when(at.inner)
        def _():
            for n in range(2):
                rcopy(
                    self.near.at[n + 1], self.near.at[n + 1], self.send(0), self.recv(n + 1), at.pair
                ).wait_recv()
                blocks[at.order[n + 2]] = (
                    blocks[at.order[n + 2]].astype(F32) + self.near[n + 1].astype(F32)
                ).astype(BF)
                self.cross_moves()[n].start()

    def last(self):
        at, blocks = self.at, self.blocks

        @pl.when(at.inner)
        def _():
            self.cross_moves()[1].wait_recv()
            blocks[at.order[1]] = (
                blocks[at.order[1]].astype(F32) + self.far[1].astype(F32)
            ).astype(BF)
            self.back_move().start()

    def finish(self, out):
        at = self.at
        self.back_move().wait_recv()
        total = self.blocks[at.d].astype(F32) + self.near[0].astype(F32)

        @pl.when(at.inner)
        def _():
            self.cross_moves()[0].wait_recv()
            out[...] = total + self.far[0].astype(F32)
            for move in self.cross_moves():
                move.wait_send()
            self.back_move().wait_send()

        @pl.when(jnp.logical_not(at.inner))
        def _():
            out[...] = total
            for move in self.outer_moves():
                move.wait_send()


def column_sums(values):
    high = values.astype(BF)
    low = (values - high.astype(F32)).astype(BF)
    ones = jnp.ones((values.shape[0], 128), BF)
    return dot_at(high, ones) + dot_at(low, ones)


def expert_lanes(rows):
    e = lax.axis_index("expert")
    lane = lax.broadcasted_iota(jnp.int32, (rows, 128), 1)
    return e, lane, (lane == e) | (lane == e + 32) | (lane == e + 64)


def gate_of(ext):
    mine = expert_lanes(ext.shape[0])[2]
    return jnp.sum(jnp.where(mine, ext.astype(F32), 0.0), axis=1, keepdims=True)


EXPERT_ROWS = 512


def up_kernel(
    x_in, cot_ref, gw_in, uw_in, dw_in, c_out, dw_all, hid_out, slope_out, grad_ref,
    x_ref, c_ref, gu_ref, dw_ref, hid_ref, slope_ref, back_ref, g_send, g_recv, z_send, z_recv, local,
):
    at = Place()
    at.greet()
    rows = x_ref.shape[0]
    tokens, width = cot_ref.shape
    hid = hid_ref.shape[1]
    part = tokens // 2
    copy = pltpu.make_async_copy
    tall = dw_in.shape[0]
    line = LineGather(
        at, lambda z: rows_of(dw_all, z * tall, tall), lambda k: z_send.at[k], lambda k: z_recv.at[k]
    )
    cots = []
    for k in range(2):
        span = pl.ds(k * part, part)

        def half(e, h, span=span):
            return c_ref.at[e, span, pl.ds(h * (width // 2), width // 2)]

        cots.append(
            PlaneGather(
                at,
                lambda e, span=span: c_ref.at[e, span],
                half,
                lambda s, k=k: g_send.at[k, s],
                lambda s, k=k: g_recv.at[k, s],
            )
        )
    line.start(dw_in)
    for k in range(2):
        cots[k].start(cot_ref.at[pl.ds(k * part, part)])
    gates_w = copy(gw_in, gu_ref.at[:, pl.ds(0, hid)], local.at[0])
    ups_w = copy(uw_in, gu_ref.at[:, pl.ds(hid, hid)], local.at[1])
    own_c = copy(cot_ref, c_ref.at[at.e], local.at[2])
    own_d = copy(dw_in, line.blk(at.d), local.at[3])
    count = rows // EXPERT_ROWS
    spans = [pl.ds(b * EXPERT_ROWS, EXPERT_ROWS) for b in range(count)]
    loads = [copy(x_in.at[spans[b]], x_ref.at[spans[b]], local.at[4 + b]) for b in range(count)]
    saves = []
    gates_w.start()
    loads[0].start()
    ups_w.start()
    for b in range(1, count):
        loads[b].start()
    own_c.start()
    own_d.start()
    gates_w.wait()
    ups_w.wait()
    step = 256
    for b in range(count):
        loads[b].wait()

        def work(h, none, b=b):
            here = pl.ds(pl.multiple_of(b * EXPERT_ROWS + h * step, step), step)
            x = x_ref[here, :width]
            for f in range(hid // 256):
                cols = slice(f * 256, (f + 1) * 256)
                after = slice(hid + f * 256, hid + (f + 1) * 256)
                gate_pre = dot_nn(x, gu_ref[:, cols])
                up_pre = dot_nn(x, gu_ref[:, after])
                sig = 1.0 / (1.0 + jnp.exp(-gate_pre))
                silu = gate_pre * sig
                hid_ref[here, cols] = (silu * up_pre).astype(BF)
                slope_ref[here, after] = silu.astype(BF)
                slope_ref[here, cols] = (up_pre * sig * (1.0 + gate_pre * (1.0 - sig))).astype(BF)
            return none

        lax.fori_loop(0, EXPERT_ROWS // step, work, 0)
        saves.append(copy(hid_ref.at[spans[b]], hid_out.at[spans[b]], local.at[8 + b]))
        saves[-1].start()
        if b == 1:
            line.relay(1)
            line.relay(2)
            for cot in cots:
                cot.on_x()
                cot.on_y()
        if b == 3:
            line.relay(3)
    for cot in cots:
        cot.on_d()
    own_c.wait()
    for cot in cots:
        cot.on_s()
    saves.append(copy(c_ref, c_out, local.at[16]))
    saves[-1].start()

    def weigh(e, none):
        here = pl.ds(pl.multiple_of(e * tokens, tokens), tokens)
        back_ref[here, :] = (gate_of(x_ref[here, width:]) * c_ref[e].astype(F32)).astype(BF)
        return none

    lax.fori_loop(0, c_ref.shape[0], weigh, 0)
    deep = gw_in.shape[0] // 4
    for t in range(2):
        down = dot_at(hid_ref[:, 2 * t * tall : 2 * (t + 1) * tall], back_ref[...]).astype(BF)
        for j in range(2):
            piece = down[j * tall : (j + 1) * tall]
            grad_ref[2 * t + j, 2 * deep : 2 * deep + tall] = piece[:, : width // 2]
            grad_ref[2 * t + j, 2 * deep + tall :] = piece[:, width // 2 :]
    line.land()
    own_d.wait()
    load_d = copy(dw_all, dw_ref, local.at[17])
    load_d.start()
    load_d.wait()

    def slopes(h, none):
        here = pl.ds(pl.multiple_of(h * step, step), step)
        rows_back = back_ref[here, :]
        for f in range(hid // 256):
            cols = slice(f * 256, (f + 1) * 256)
            after = slice(hid + f * 256, hid + (f + 1) * 256)
            grad_hidden = dot_bt(rows_back, dw_ref[cols, :])
            for span in (cols, after):
                slope_ref[here, span] = (grad_hidden * slope_ref[here, span].astype(F32)).astype(BF)
        return none

    lax.fori_loop(0, rows // step, slopes, 0)
    saves.append(copy(slope_ref, slope_out, local.at[12]))
    saves[-1].start()
    for z in range(4):
        both = dot_at(x_ref[:, z * deep : (z + 1) * deep], slope_ref[...]).astype(BF)
        grad_ref[z, :deep] = both[:, :hid]
        grad_ref[z, deep : 2 * deep] = both[:, hid:]
    for cot in cots:
        cot.drain()
    line.drain()
    for save in saves:
        save.wait()


def expert_up(x_all, cot, gw, uw, dw):
    rows = x_all.shape[0]
    tokens, width = cot.shape
    hid = gw.shape[1]
    sds = jax.ShapeDtypeStruct
    vmem = pl.BlockSpec(memory_space=pltpu.VMEM)
    hbm = pl.BlockSpec(memory_space=ANY)

    def low(*shape):
        return pltpu.VMEM(shape, BF)

    return pl.pallas_call(
        up_kernel,
        in_specs=[hbm, vmem, hbm, hbm, vmem],
        out_specs=(hbm, hbm, hbm, hbm, vmem),
        out_shape=(
            sds((rows // tokens, tokens, width), BF),
            sds((hid, width), BF),
            sds((rows, hid), BF),
            sds((rows, 2 * hid), BF),
            sds((4, 3 * width // 4, hid), BF),
        ),
        scratch_shapes=[
            low(rows, width + 128),
            low(rows // tokens, tokens, width),
            low(width, 2 * hid),
            low(hid, width),
            low(rows, hid),
            low(rows, 2 * hid),
            low(rows, width),
            pltpu.SemaphoreType.DMA((2, 8)),
            pltpu.SemaphoreType.DMA((2, 8)),
            pltpu.SemaphoreType.DMA((5,)),
            pltpu.SemaphoreType.DMA((4,)),
            pltpu.SemaphoreType.DMA((18,)),
        ],
        compiler_params=pltpu.CompilerParams(
            collective_id=3, has_side_effects=True, vmem_limit_bytes=62 * 2**20
        ),
        cost_estimate=pl.CostEstimate(
            flops=8 * 10**10, bytes_accessed=5 * 10**7, transcendentals=10**6
        ),
    )(x_all, cot, gw, uw, dw)


PARTS = 4


def down_kernel(
    x_in, c_in, hid_in, slope_in, gw_in, uw_in, dw_in, row_out, wgt_out,
    ext_ref, c_ref, hid_ref, slope_ref, gu_ref, dw_ref, wgt_ref,
    slot, own, seat, low1, high1, low2, high2, send, recv, local,
):
    at = Place()
    at.greet()
    tokens = x_in.shape[2]
    width = c_ref.shape[3]
    hid = dw_ref.shape[0]
    part = tokens // PARTS
    rows = 4 * part
    copy = pltpu.make_async_copy
    cut = 7 * 128
    red = []
    for k in range(PARTS):
        red.append(
            PlaneReduce(
                at, slot.at[k], own.at[k], seat.at[k], low1.at[k], high1.at[k], high2.at[k],
                low2.at[k], cut, lambda s, k=k: send.at[k, s], lambda s, k=k: recv.at[k, s],
            )
        )

    def place(j):
        core = 1 - at.core if j % 2 == 0 else at.core
        return (slice(None), core, pl.ds(j // 2 * part, part))

    count = 2 * PARTS
    ext = (pl.ds(width, 128),)
    loads = [
        [
            copy(hid_in.at[place(j)], hid_ref.at[j], local.at[0, j]),
            copy(c_in.at[place(j)], c_ref.at[j], local.at[1, j]),
            copy(x_in.at[place(j) + ext], ext_ref.at[j], local.at[2, j]),
            copy(slope_in.at[place(j)], slope_ref.at[j], local.at[3, j]),
        ]
        for j in range(count)
    ]
    saves = [copy(wgt_ref.at[j], wgt_out.at[place(j)], local.at[4, j]) for j in range(count)]
    gates_w = copy(gw_in, gu_ref.at[:, pl.ds(0, hid)], local.at[5, 0])
    ups_w = copy(uw_in, gu_ref.at[:, pl.ds(hid, hid)], local.at[5, 1])
    downs_w = copy(dw_in, dw_ref, local.at[5, 2])
    for load in loads[0]:
        load.start()
    gates_w.start()
    ups_w.start()
    downs_w.start()
    for j in range(1, count):
        for load in loads[j]:
            load.start()
    e, lane, mine = expert_lanes(rows)

    def block(j, row_dst):
        for load in loads[j]:
            load.wait()
        if j == 0:
            gates_w.wait()
            ups_w.wait()
        pair = slope_ref[j].reshape(rows, 2 * hid)
        row_dst[:, :, :width] = dot_bt(pair, gu_ref[...]).astype(BF).reshape(4, part, width)
        if j == 0:
            downs_w.wait()
        gate = gate_of(ext_ref[j].reshape(rows, 128))
        returned = dot_nn(hid_ref[j].reshape(rows, hid), dw_ref[...]).astype(BF).astype(F32)
        cot = c_ref[j].reshape(rows, width).astype(F32)
        grad_gates = jnp.sum(cot * returned, axis=1, keepdims=True)
        wgt_ref[j] = (gate * returned).astype(BF).reshape(4, part, width)
        saves[j].start()
        high = grad_gates.astype(BF).astype(F32)
        row_dst[:, :, width:] = (
            jnp.where(lane == e, high, jnp.where(lane == e + 32, grad_gates - high, 0.0))
            .astype(BF)
            .reshape(4, part, 128)
        )

    def settle(k):
        low, high = red[k].finish()
        row_out[k * part : (k + 1) * part, :cut] = low
        row_out[k * part : (k + 1) * part, cut:] = high

    for k in range(PARTS):
        block(2 * k, slot.at[k])
        red[k].start()
        if k >= 1:
            red[k - 1].on_xy()
        if k >= 2:
            settle(k - 2)
        block(2 * k + 1, own.at[k])
        red[k].on_s()
    red[PARTS - 1].on_xy()
    settle(PARTS - 2)
    settle(PARTS - 1)
    for item in red:
        item.drain()
    for save in saves:
        save.wait()


def expert_down(x_all, c_all, hidden, slope, gw, uw, dw):
    group, tokens, width = c_all.shape
    hid = gw.shape[1]
    part = tokens // PARTS
    cut = 7 * 128
    wide = width + 128
    sds = jax.ShapeDtypeStruct
    hbm = pl.BlockSpec(memory_space=ANY)

    def low(*shape):
        return pltpu.VMEM(shape, BF)

    return pl.pallas_call(
        down_kernel,
        in_specs=[hbm] * 7,
        out_specs=(pl.BlockSpec(memory_space=pltpu.VMEM), hbm),
        out_shape=(sds((tokens, wide), F32), sds((4, 2, tokens, width), BF)),
        scratch_shapes=[
            low(2 * PARTS, 4, part, 128),
            low(2 * PARTS, 4, part, width),
            low(2 * PARTS, 4, part, hid),
            low(2 * PARTS, 4, part, 2 * hid),
            low(width, 2 * hid),
            low(hid, width),
            low(2 * PARTS, 4, part, width),
            low(PARTS, 4, part, wide),
            low(PARTS, 4, part, wide),
            low(PARTS, 4, part, wide),
            low(PARTS, 2, part, cut),
            low(PARTS, 2, part, wide - cut),
            low(PARTS, part, cut),
            low(PARTS, part, wide - cut),
            pltpu.SemaphoreType.DMA((PARTS, 7)),
            pltpu.SemaphoreType.DMA((PARTS, 7)),
            pltpu.SemaphoreType.DMA((6, 2 * PARTS)),
        ],
        compiler_params=pltpu.CompilerParams(
            collective_id=4, has_side_effects=True, vmem_limit_bytes=63 * 2**20
        ),
        cost_estimate=pl.CostEstimate(
            flops=5 * 10**10, bytes_accessed=5 * 10**7, transcendentals=10**6
        ),
    )(
        x_all.reshape(4, 2, tokens, wide),
        c_all.reshape(4, 2, tokens, width),
        hidden.reshape(4, 2, tokens, hid),
        slope.reshape(4, 2, tokens, 2 * hid),
        gw,
        uw,
        dw,
    )


def pack_weights(w_router, norm_attn, norm_moe, w_query, key_projection, value_projection):
    rows, n_experts = w_router.shape
    small = jnp.concatenate(
        [
            w_router,
            norm_attn[:, None],
            norm_moe[:, None],
            jnp.zeros((rows, 128 - n_experts - 2), BF),
        ],
        axis=1,
    )
    return jnp.concatenate([w_query, key_projection, value_projection, small], axis=1)


N_BACK = 16


def back_kernel(
    n_experts,
    lens_ref,
    order_ref,
    row_in,
    wgt_in,
    tok_in,
    q_in,
    att_in,
    lse_in,
    mid_in,
    cot_in,
    kv_in,
    pay_in,
    pack_in,
    wo_in,
    output_ref,
    tokens_grad_ref,
    aq_out,
    ak_out,
    b_out,
    w_own,
    w_seat,
    w_half1,
    w_half2,
    row_ref,
    tok_ref,
    q_ref,
    att_ref,
    lse_ref,
    mid_ref,
    cot_ref,
    kv_ref,
    pay_ref,
    pack_ref,
    wo_ref,
    do_ref,
    dkv_ref,
    kseat,
    klow1,
    khigh1,
    klow2,
    khigh2,
    bseat,
    bhalf1,
    bhalf2,
    aseat,
    ahalf1,
    ahalf2,
    cseat,
    clow1,
    chigh1,
    clow2,
    chigh2,
    n1_ref,
    dqkv_ref,
    small_ref,
    grad_middle_ref,
    bz,
    bnear,
    bfar,
    az,
    anear,
    afar,
    cz,
    cnear,
    cfar,
    r_send,
    r_recv,
    l_send,
    l_recv,
    local,
):
    at = Place()
    at.greet()
    tokens, width = tok_ref.shape
    group = 8
    kv_width = KEY_VALUE_HEADS * HEAD_SIZE
    q_width = QUERY_HEADS * HEAD_SIZE
    qkv = q_width + 2 * kv_width
    per_kv = QUERY_HEADS // KEY_VALUE_HEADS
    chunk = width // 4
    shard = chunk // group
    part = tokens // 2
    red = {}

    def sems(n):
        return (lambda k: r_send.at[n, k]), (lambda k: r_recv.at[n, k])

    own_loads = []
    for k in range(2):
        send, recv = sems(len(red))
        mine = wgt_in.at[:, :, pl.ds(k * part, part)]
        own_loads.append(
            pltpu.make_async_copy(mine.at[:, at.core], w_own.at[k], local.at[11 + k])
        )
        red["w", k] = PlaneReduce(
            at, mine.at[:, 1 - at.core], w_own.at[k], w_seat.at[k], w_half1.at[k, 0],
            w_half1.at[k, 1], w_half2.at[k, 0], w_half2.at[k, 1], width // 2, send, recv,
        )
    for k in range(2):
        send, recv = sems(len(red))
        rows = pl.ds(k * part, part)
        mine = dkv_ref.at[:, :, rows]
        red["k", k] = PlaneReduce(
            at, mine.at[:, 1 - at.core], mine.at[:, at.core], kseat.at[k], klow1.at[k], khigh1.at[k],
            khigh2.at[k], klow2.at[k], kv_width, send, recv,
        )
    for z in range(4):
        send, recv = sems(len(red))
        red["b", z] = PlaneReduce(
            at, wo_ref.at[z, :, 1 - at.core], wo_ref.at[z, :, at.core], bseat.at[z], bhalf1.at[z, 0],
            bhalf1.at[z, 1], bhalf2.at[z, 0], bhalf2.at[z, 1], width // 2, send, recv,
        )
    cols_q, cols_k = pl.ds(0, q_width), pl.ds(q_width, 2 * kv_width + 128)
    for z in range(4):
        send, recv = sems(len(red))
        red["q", z] = PlaneReduce(
            at, pack_ref.at[z, :, 1 - at.core, :, cols_q], pack_ref.at[z, :, at.core, :, cols_q],
            aseat.at[z], ahalf1.at[z, 0], ahalf1.at[z, 1], ahalf2.at[z, 0], ahalf2.at[z, 1],
            q_width // 2, send, recv,
        )
    for z in range(4):
        send, recv = sems(len(red))
        red["s", z] = PlaneReduce(
            at, pack_ref.at[z, :, 1 - at.core, :, cols_k], pack_ref.at[z, :, at.core, :, cols_k],
            cseat.at[z], clow1.at[z], chigh1.at[z], chigh2.at[z], clow2.at[z],
            3 * 128, send, recv,
        )
    lines = {}
    for n, (name, blocks, near, far) in enumerate(
        (("b", bz, bnear, bfar), ("q", az, anear, afar), ("s", cz, cnear, cfar))
    ):
        lines[name] = LineReduce(
            at, blocks, near, far, lambda k, n=n: l_send.at[n, k], lambda k, n=n: l_recv.at[n, k]
        )

    loads = {}
    for n, (name, src, dst) in enumerate(
        (
            ("row", row_in, row_ref),
            ("pay", pay_in, pay_ref),
            ("mid", mid_in, mid_ref),
            ("cot", cot_in, cot_ref),
            ("pack", pack_in, pack_ref),
            ("wo", wo_in, wo_ref),
            ("att", att_in, att_ref),
            ("lse", lse_in, lse_ref),
            ("q", q_in, q_ref),
            ("kv", kv_in, kv_ref),
            ("tok", tok_in, tok_ref),
        )
    ):
        loads[name] = pltpu.make_async_copy(src, dst, local.at[n])
        loads[name].start()
    for k in range(2):
        red["w", k].start()
        own_loads[k].start()
    stream, begin, relative = stream_facts(lens_ref, order_ref, tokens, group, at.e)
    cosine, sine = rotary(relative)
    own_loads[0].wait()
    red["w", 0].on_s()
    for name in ("tok", "pack"):
        loads[name].wait()

    def tok_unit():
        tok = tok_ref[...].astype(F32)
        scale = lax.rsqrt(jnp.mean(tok * tok, axis=1, keepdims=True) + EPSILON)
        return tok * scale, scale

    small = pack_ref[..., qkv:].reshape(width, 128)
    gain_one = column_as_row(small, n_experts)
    gain_two = column_as_row(small, n_experts + 1)
    n1_ref[...] = (tok_unit()[0] * gain_one).astype(BF)
    for name in ("pay", "mid", "cot", "row"):
        loads[name].wait()
    lane = lax.broadcasted_iota(jnp.int32, (tokens, 128), 1)
    ext = pay_ref[:, width:].astype(F32)
    gates = jnp.where(
        lane < n_experts, ext + pltpu.roll(ext, 96, 1) + pltpu.roll(ext, 64, 1), 0.0
    )
    ext = row_ref[:, width:]
    grad_gates = jnp.where(lane < n_experts, ext + pltpu.roll(ext, 96, 1), 0.0)
    weighted_sum = jnp.sum(gates * grad_gates, axis=1, keepdims=True)
    grad_logits = (gates * (grad_gates - weighted_sum)).astype(BF)
    grad_normed = dot_bt(grad_logits, small) + row_ref[:, :width]
    middle = mid_ref[...]
    scale_two = lax.rsqrt(jnp.mean(middle * middle, axis=1, keepdims=True) + EPSILON)
    unit_two = middle * scale_two
    inner_sum = jnp.mean(grad_normed * gain_two * unit_two, axis=1, keepdims=True)
    grad_middle = cot_ref[...].astype(F32) + scale_two * (
        grad_normed * gain_two - unit_two * inner_sum
    )
    products = grad_normed * unit_two
    loads["wo"].wait()
    grad_middle_ref[...] = grad_middle
    mixed = grad_middle.astype(BF)
    for z in range(4):
        heads = dot_bt(mixed, wo_ref[z].reshape(chunk, width)).astype(BF)
        for j in range(chunk // HEAD_SIZE):
            do_ref[z * (chunk // HEAD_SIZE) + j] = heads[:, j * HEAD_SIZE : (j + 1) * HEAD_SIZE]
    loads["att"].wait()
    for z in range(4):
        left = att_ref[:, z * chunk : (z + 1) * chunk].astype(BF)
        wo_ref[z] = dot_at(left, mixed).astype(BF).reshape(4, 2, shard, width)
        red["b", z].start()
    lane_small = lax.broadcasted_iota(jnp.int32, (width, 128), 1)
    small_ref[...] = dot_at(pay_ref[:, :width], grad_logits) + jnp.where(
        lane_small == n_experts + 1, column_sums(products), 0.0
    )
    for name in ("lse", "q", "kv"):
        loads[name].wait()
    row_ref[:, :width] = jnp.zeros((tokens, width), F32)
    n_tiles = tokens // TILE
    wide = TILE * group
    for g in range(KEY_VALUE_HEADS):
        for i in range(n_tiles):
            here = slice(i * TILE, (i + 1) * TILE)
            dots = []
            for h in range(per_kv):
                col = (g * per_kv + h) * HEAD_SIZE
                dots.append(
                    jnp.sum(
                        do_ref[g * per_kv + h, here, :].astype(F32)
                        * att_ref[here, col : col + HEAD_SIZE],
                        axis=1,
                        keepdims=True,
                    )
                )
            dots = jnp.concatenate(dots, axis=0)
            lse_ref[g, i, :, 64:] = jnp.broadcast_to(dots, (per_kv * TILE, 64))
    for z in range(4):
        red["b", z].on_s()

    factor = LOG2E / math.sqrt(HEAD_SIZE)
    score_scale = 1.0 / math.sqrt(HEAD_SIZE)

    def attend_back(r):
        queries_of = [i for i in range(n_tiles) if r in tiles_of(i)]
        biases = {i: tile_bias(i, r, stream, begin, group) for i in queries_of}
        there = slice(r * TILE, (r + 1) * TILE)
        for g in range(KEY_VALUE_HEADS):
            key_cols = slice(g * HEAD_SIZE, (g + 1) * HEAD_SIZE)
            value_cols = slice(kv_width + g * HEAD_SIZE, kv_width + (g + 1) * HEAD_SIZE)
            heads = slice(g * per_kv, (g + 1) * per_kv)
            keys = kv_ref[:, there, key_cols].reshape(wide, HEAD_SIZE)
            values = kv_ref[:, there, value_cols].reshape(wide, HEAD_SIZE)
            grad_keys = None
            grad_values = None
            for i in queries_of:
                here = slice(i * TILE, (i + 1) * TILE)
                queries = q_ref[heads, here, :].reshape(per_kv * TILE, HEAD_SIZE)
                grads = do_ref[heads, here, :].reshape(per_kv * TILE, HEAD_SIZE)
                s = dot_bt(queries, keys) * factor
                s = (s.reshape(per_kv, TILE, wide) + biases[i][None]).reshape(per_kv * TILE, wide)
                p = jnp.exp2(s - lse_ref[g, i, :, :1])
                ds = (p * (dot_bt(grads, values) - lse_ref[g, i, :, 64:65])).astype(BF)
                term_k = dot_at(ds, queries)
                term_v = dot_at(p.astype(BF), grads)
                grad_keys = term_k if grad_keys is None else grad_keys + term_k
                grad_values = term_v if grad_values is None else grad_values + term_v
                grad_queries = dot_nn(ds, keys)
                for h in range(per_kv):
                    col = (g * per_kv + h) * HEAD_SIZE
                    row_ref[here, col : col + HEAD_SIZE] += grad_queries[
                        h * TILE : (h + 1) * TILE
                    ]
            dkv_ref[:, :, there, key_cols] = (
                (grad_keys * score_scale).astype(BF).reshape(4, 2, TILE, HEAD_SIZE)
            )
            dkv_ref[:, :, there, value_cols] = grad_values.astype(BF).reshape(4, 2, TILE, HEAD_SIZE)

    def settle(name, z, blocks, cut):
        low, high = red[name, z].finish()
        blocks[z, :, :cut] = low.astype(BF)
        blocks[z, :, cut:] = high.astype(BF)

    red["w", 0].on_xy()
    attend_back(0)
    for z in range(4):
        red["b", z].on_xy()
    attend_back(1)
    red["k", 0].start()
    attend_back(2)
    red["k", 0].on_s()
    for z in range(4):
        settle("b", z, bz, width // 2)
    lines["b"].start()
    attend_back(3)
    red["k", 1].start()
    red["k", 0].on_xy()

    def output_part(k):
        rows = slice(k * part, (k + 1) * part)
        low, high = red["w", k].finish()
        output_ref[rows, : width // 2] = (mid_ref[rows, : width // 2] + low).astype(BF)
        output_ref[rows, width // 2 :] = (mid_ref[rows, width // 2 :] + high).astype(BF)

    def turned_back(v):
        return (v * cosine - swap_halves(v) * sine).astype(BF)

    for h in range(QUERY_HEADS):
        cols = slice(h * HEAD_SIZE, (h + 1) * HEAD_SIZE)
        dqkv_ref[:, cols] = turned_back(row_ref[:, cols] * score_scale)
    red["k", 1].on_s()
    grad_q = dqkv_ref[:, :q_width]
    for z in range(4):
        cols = slice(z * chunk, (z + 1) * chunk)
        att_ref[:, cols] = dot_bt(grad_q, pack_ref[z, :, :, :, :q_width].reshape(chunk, q_width))
        pack_ref[z, :, :, :, :q_width] = (
            dot_at(n1_ref[:, cols], grad_q).astype(BF).reshape(4, 2, shard, q_width)
        )
        red["q", z].start()
        if z == 0:
            red["k", 1].on_xy()
    for k in range(2):
        rows = slice(k * part, (k + 1) * part)
        low, high = red["k", k].finish()
        row_ref[rows, :kv_width] = low
        row_ref[rows, kv_width : 2 * kv_width] = high
    lines["b"].middle()
    for z in range(4):
        red["q", z].on_s()
    for h in range(KEY_VALUE_HEADS):
        v = row_ref[:, h * HEAD_SIZE : (h + 1) * HEAD_SIZE]
        dqkv_ref[:, q_width + h * HEAD_SIZE : q_width + (h + 1) * HEAD_SIZE] = turned_back(v)
    dqkv_ref[:, q_width + kv_width :] = row_ref[:, kv_width : 2 * kv_width].astype(BF)
    grad_kv = dqkv_ref[:, q_width:]
    for z in range(4):
        cols = slice(z * chunk, (z + 1) * chunk)
        att_ref[:, cols] += dot_bt(
            grad_kv, pack_ref[z, :, :, :, q_width:qkv].reshape(chunk, 2 * kv_width)
        )
        pack_ref[z, :, :, :, q_width:qkv] = (
            dot_at(n1_ref[:, cols], grad_kv).astype(BF).reshape(4, 2, shard, 2 * kv_width)
        )
    unit_one, scale_one = tok_unit()
    grad_one = att_ref[...]
    small_ref[...] += jnp.where(lane_small == n_experts, column_sums(grad_one * unit_one), 0.0)
    pack_ref[..., qkv:] = small_ref[...].astype(BF).reshape(4, 4, 2, shard, 128)
    for z in range(4):
        red["s", z].start()
    lines["b"].last()
    for z in range(4):
        red["q", z].on_xy()
    for z in range(4):
        red["s", z].on_s()
    inner_sum = jnp.mean(grad_one * gain_one * unit_one, axis=1, keepdims=True)
    back_one = scale_one * (grad_one * gain_one - unit_one * inner_sum)
    tokens_grad_ref[...] = (grad_middle_ref[...] + back_one).astype(BF)
    for z in range(4):
        settle("q", z, az, q_width // 2)
    lines["q"].start()
    for z in range(4):
        red["s", z].on_xy()
    own_loads[1].wait()
    red["w", 1].on_s()
    output_part(0)
    for z in range(4):
        settle("s", z, cz, 3 * 128)
    lines["s"].start()
    lines["q"].middle()
    lines["s"].middle()
    red["w", 1].on_xy()
    lines["q"].last()
    lines["s"].last()
    lines["b"].finish(b_out)
    output_part(1)
    lines["q"].finish(aq_out)
    lines["s"].finish(ak_out)
    for item in red.values():
        item.drain()


def back(
    lengths, seq_order, row, weighted, tokens, q_rot, att, lse, middle, cot, kv, pay, pack, wo, n_experts
):
    count, width = tokens.shape
    group = 8
    shard = width // 32
    kv_width = KEY_VALUE_HEADS * HEAD_SIZE
    part = count // 2
    wide_r = width + 128
    wide_s, cut_s = 2 * kv_width + 128, 3 * 128
    half = width // 2
    sds = jax.ShapeDtypeStruct
    smem = pl.BlockSpec(memory_space=pltpu.SMEM)
    vmem = pl.BlockSpec(memory_space=pltpu.VMEM)
    hbm = pl.BlockSpec(memory_space=ANY)
    pack = pack.reshape(4, 4, 2, shard, pack.shape[1])
    wo = wo.reshape(4, 4, 2, shard, width)

    def low(*shape):
        return pltpu.VMEM(shape, BF)

    def like(a):
        return pltpu.VMEM(a.shape, a.dtype)

    return pl.pallas_call(
        functools.partial(back_kernel, n_experts),
        in_specs=[smem, smem] + [hbm] * 12,
        out_specs=(vmem,) * 5,
        out_shape=(
            sds((count, width), BF),
            sds((count, width), BF),
            sds((shard, width), F32),
            sds((shard, wide_s), F32),
            sds((shard, width), F32),
        ),
        scratch_shapes=[
            low(2, 4, part, width),
            low(2, 4, part, width),
            low(2, 2, 2, part, half),
            low(2, 2, part, half),
            pltpu.VMEM((count, wide_r), F32),
            like(tokens),
            like(q_rot),
            like(att),
            like(lse),
            like(middle),
            like(cot),
            like(kv),
            like(pay),
            like(pack),
            like(wo),
            like(q_rot),
            low(4, 2, count, 2 * kv_width),
            low(2, 4, part, 2 * kv_width),
            low(2, 2, part, kv_width),
            low(2, 2, part, kv_width),
            low(2, part, kv_width),
            low(2, part, kv_width),
            low(4, 4, shard, width),
            low(4, 2, 2, shard, half),
            low(4, 2, shard, half),
            low(4, 4, shard, width),
            low(4, 2, 2, shard, half),
            low(4, 2, shard, half),
            low(4, 4, shard, wide_s),
            low(4, 2, shard, cut_s),
            low(4, 2, shard, wide_s - cut_s),
            low(4, shard, cut_s),
            low(4, shard, wide_s - cut_s),
            low(count, width),
            low(count, width + 2 * kv_width),
            pltpu.VMEM((width, 128), F32),
            pltpu.VMEM((count, width), F32),
            low(4, shard, width),
            low(3, shard, width),
            low(2, shard, width),
            low(4, shard, width),
            low(3, shard, width),
            low(2, shard, width),
            low(4, shard, wide_s),
            low(3, shard, wide_s),
            low(2, shard, wide_s),
            pltpu.SemaphoreType.DMA((N_BACK, 7)),
            pltpu.SemaphoreType.DMA((N_BACK, 7)),
            pltpu.SemaphoreType.DMA((3, 5)),
            pltpu.SemaphoreType.DMA((3, 5)),
            pltpu.SemaphoreType.DMA((13,)),
        ],
        compiler_params=pltpu.CompilerParams(
            collective_id=2, has_side_effects=True, vmem_limit_bytes=63 * 2**20
        ),
        cost_estimate=pl.CostEstimate(
            flops=15 * 10**10, bytes_accessed=5 * 10**7, transcendentals=10**7
        ),
    )(lengths, seq_order, row, weighted, tokens, q_rot, att, lse, middle, cot, kv, pay, pack, wo)


def on_device_fast(
    tokens,
    lengths,
    seq_order,
    routes,
    norm_attn,
    w_query,
    key_projection,
    value_projection,
    w_out,
    norm_moe,
    w_router,
    w_gate,
    w_up,
    w_down,
    cotangent,
):
    token_count, width = tokens.shape
    n_experts = w_router.shape[1]
    kv_width = KEY_VALUE_HEADS * HEAD_SIZE
    group_tokens = token_count * lax.axis_size("expert")
    pack = pack_weights(w_router, norm_attn, norm_moe, w_query, key_projection, value_projection)
    x_all, gw, uw, pack, wo, kv_all, q_rot, attended, lse, middle, pay = front(
        lengths, seq_order, tokens, routes, pack, w_out, w_gate[0], w_up[0], n_experts
    )
    x_all = x_all.reshape(group_tokens, width + 128)
    c_all, dw, hidden, slope, expert_grads = expert_up(x_all, cotangent, gw, uw, w_down[0])
    grad_row, weighted = expert_down(x_all, c_all, hidden, slope, gw, uw, dw)
    depth, tall = w_gate.shape[1], w_down.shape[1]
    expert_mine = lax.psum_scatter(
        expert_grads.reshape(-1, expert_grads.shape[2]), "dp", scatter_dimension=0, tiled=True
    ).astype(F32)
    gate_mine = expert_mine[None, :depth]
    up_mine = expert_mine[None, depth : 2 * depth]
    down_mine = jnp.concatenate(
        [expert_mine[2 * depth : 2 * depth + tall], expert_mine[2 * depth + tall :]], axis=1
    )[None]
    output, tokens_grad, query_mine, mine, out_mine = back(
        lengths,
        seq_order,
        grad_row,
        weighted,
        tokens,
        q_rot,
        attended,
        lse,
        middle,
        cotangent,
        kv_all,
        pay,
        pack,
        wo,
        n_experts,
    )
    c_s = 2 * kv_width
    return (
        output,
        tokens_grad,
        mine[:, c_s + n_experts],
        query_mine,
        mine[:, :kv_width],
        mine[:, kv_width:c_s],
        out_mine,
        mine[:, c_s + n_experts + 1],
        mine[:, c_s : c_s + n_experts],
        gate_mine,
        up_mine,
        down_mine,
    )


def solution(mesh):
    both = ("dp", "expert")
    small = mesh.shape["dp"] == 4 and mesh.shape["expert"] == 8
    return jax.shard_map(
        on_device_fast if small else on_device,
        mesh=mesh,
        in_specs=(
            P(both, None),
            P("dp", None),
            P("dp", None),
            P(both, None),
            P(both),
            P(both, None),
            P(both, None),
            P(both, None),
            P(both, None),
            P(both),
            P(both, None),
            P("expert", "dp", None),
            P("expert", "dp", None),
            P("expert", "dp", None),
            P(both, None),
        ),
        out_specs=(
            P(both, None),
            P(both, None),
            P(both),
            P(both, None),
            P(both, None),
            P(both, None),
            P(both, None),
            P(both),
            P(both, None),
            P("expert", "dp", None),
            P("expert", "dp", None),
            P("expert", "dp", None),
        ),
        check_vma=False,
    )
```

```python
import functools
import math

import jax
import jax.numpy as jnp
from jax import lax
from jax.experimental import pallas as pl
from jax.experimental.pallas import tpu as pltpu
from jax.sharding import PartitionSpec as P

QUERY_HEADS = 12
KEY_VALUE_HEADS = 2
HEAD_SIZE = 128


EPSILON = 1e-06
ROPE_BASE = 10000.0
MASKED_SCORE = -1e30
BF = jnp.bfloat16
F32 = jnp.float32


def rms_scale(values):
    return lax.rsqrt(jnp.mean(values * values, axis=-1, keepdims=True) + EPSILON)


def rope_tables(positions, half_size):
    angle_steps = lax.broadcasted_iota(F32, (half_size,), 0)
    frequency = jnp.exp(angle_steps * (-math.log(ROPE_BASE) / half_size))
    angles = positions.astype(F32)[:, None] * frequency
    return (jnp.cos(angles)[:, None, :], jnp.sin(angles)[:, None, :])


def apply_rotation(values, cosine_table, sine_table):
    half_size = values.shape[-1] // 2
    first = values[..., :half_size]
    second = values[..., half_size:]
    return jnp.concatenate(
        [first * cosine_table - second * sine_table, second * cosine_table + first * sine_table],
        axis=-1,
    )


def reverse_rotation(grads_in, cosine_table, sine_table):
    return apply_rotation(grads_in, cosine_table, -sine_table)


def seq_layout(lengths, seq_order):
    count_seq = lengths.shape[1]
    picked = seq_order[0][:, None] == lax.broadcasted_iota(jnp.int32, (count_seq, count_seq), 1)
    ordered = jnp.sum(jnp.where(picked, lengths[0][None, :], 0), axis=1)
    return (ordered, jnp.cumsum(ordered))


def seq_place(positions, ordered, seq_ends):
    passed = seq_ends[None, :] <= positions[:, None]
    sequence_index = jnp.sum(passed.astype(jnp.int32), axis=1)
    starts = jnp.sum(jnp.where(passed, ordered[None, :], 0), axis=1)
    return (sequence_index, positions - starts)


def block_scores(
    query_rows, key_portion, query_seq, query_stream, key_seq, key_stream, score_scale
):
    raw_scores = (
        jnp.einsum("tkrd,skd->krts", query_rows, key_portion, preferred_element_type=F32)
        * score_scale
    )
    allowed = (query_seq[:, None] == key_seq[None, :]) & (
        key_stream[None, :] <= query_stream[:, None]
    )
    return jnp.where(allowed, raw_scores, MASKED_SCORE)


def norm_backward(grad_normed, unit_values, inv_scale, gain_float):
    scaled = grad_normed * gain_float
    gain_grad = jnp.sum(grad_normed * unit_values, axis=0)
    input_grad = inv_scale * (
        scaled - unit_values * jnp.mean(scaled * unit_values, axis=-1, keepdims=True)
    )
    return (gain_grad, input_grad)


def dot(a, b):
    return jnp.dot(a, b, preferred_element_type=F32)


def dot_nt(a, b):
    return jnp.einsum("ac,bc->ab", a, b, preferred_element_type=F32)


def dot_tn(a, b):
    return jnp.einsum("ta,tb->ab", a, b, preferred_element_type=F32)


def on_device(
    tokens,
    lengths,
    seq_order,
    routes,
    norm_attn,
    w_query,
    key_projection,
    value_projection,
    w_out,
    norm_moe,
    w_router,
    w_gate,
    w_up,
    w_down,
    cotangent,
):
    token_count, width = tokens.shape
    n_experts = w_router.shape[1]
    rows = w_query.shape[0]
    group_size = lax.axis_size("expert")
    my_index = lax.axis_index("expert")
    query_per_key_heads = QUERY_HEADS // KEY_VALUE_HEADS
    kv_width = KEY_VALUE_HEADS * HEAD_SIZE
    q_width = QUERY_HEADS * HEAD_SIZE
    score_scale = 1.0 / math.sqrt(HEAD_SIZE)
    group_tokens = token_count * group_size

    small = jnp.concatenate(
        [
            w_router,
            norm_attn[:, None],
            norm_moe[:, None],
            jnp.zeros((rows, 128 - n_experts - 2), BF),
        ],
        axis=1,
    )
    pack = jnp.concatenate([w_query, key_projection, value_projection, small, w_out], axis=1)
    gate_w = lax.all_gather(w_gate[0], "dp", axis=0, tiled=True)
    up_w = lax.all_gather(w_up[0], "dp", axis=0, tiled=True)
    down_w = lax.all_gather(w_down[0], "dp", axis=0, tiled=True)
    pack = lax.all_gather(pack, ("dp", "expert"), axis=0, tiled=True)
    cot_all = lax.all_gather(cotangent, "expert", axis=0, tiled=True)
    c_k = q_width
    c_v = c_k + kv_width
    c_s = c_v + kv_width
    c_o = c_s + 128
    query_w = pack[:, :c_k]
    key_w = pack[:, c_k:c_v]
    value_w = pack[:, c_v:c_s]
    router_w = pack[:, c_s : c_s + n_experts]
    gain_one = pack[:, c_s + n_experts].astype(F32)
    gain_two = pack[:, c_s + n_experts + 1].astype(F32)
    out_w = pack[:, c_o:]

    seq_lens, seq_ends = seq_layout(lengths, seq_order)
    my_stream = lax.broadcasted_iota(jnp.int32, (token_count,), 0) * group_size + my_index
    query_seq, query_rel = seq_place(my_stream, seq_lens, seq_ends)
    all_rows = lax.broadcasted_iota(jnp.int32, (group_tokens,), 0)
    key_stream = all_rows % token_count * group_size + all_rows // token_count
    key_seq = seq_place(key_stream, seq_lens, seq_ends)[0]
    block_row_count = math.gcd(group_tokens, 512)
    block_count = group_tokens // block_row_count
    cosine_table, sine_table = rope_tables(query_rel, HEAD_SIZE // 2)
    inputs_float = tokens.astype(F32)
    inv_one = rms_scale(inputs_float)
    unit_one = inputs_float * inv_one
    normed_one = (unit_one * gain_one).astype(BF)
    query_pre = dot(normed_one, query_w)
    key_pre = dot(normed_one, key_w)
    value_pre = dot(normed_one, value_w)
    rotated_queries = (
        apply_rotation(
            query_pre.reshape(token_count, QUERY_HEADS, HEAD_SIZE), cosine_table, sine_table
        )
        .astype(BF)
        .reshape(token_count, KEY_VALUE_HEADS, query_per_key_heads, HEAD_SIZE)
    )
    rotated_keys = apply_rotation(
        key_pre.reshape(token_count, KEY_VALUE_HEADS, HEAD_SIZE),
        cosine_table,
        sine_table,
    ).astype(BF)
    key_value = jnp.concatenate(
        [rotated_keys.reshape(token_count, kv_width), value_pre.astype(BF)],
        axis=1,
    )
    gathered = lax.all_gather(key_value, "expert", axis=0, tiled=True)
    key_blocks = (
        gathered.reshape(block_count, block_row_count, 2 * kv_width),
        key_seq.reshape(block_count, block_row_count),
        key_stream.reshape(block_count, block_row_count),
    )

    def stats_step(carry, blocks):
        run_max, run_sum = carry
        key_value_block, seq_block, stream_block = blocks
        key_portion = key_value_block[:, :kv_width].reshape(-1, KEY_VALUE_HEADS, HEAD_SIZE)
        scores = block_scores(
            rotated_queries, key_portion, query_seq, my_stream, seq_block, stream_block, score_scale
        )
        new_max = jnp.maximum(run_max, jnp.max(scores, axis=-1))
        run_sum = run_sum * jnp.exp(run_max - new_max) + jnp.sum(
            jnp.exp(scores - new_max[..., None]), axis=-1
        )
        return ((new_max, run_sum), None)

    initial_maximum = jnp.full(
        (KEY_VALUE_HEADS, query_per_key_heads, token_count), MASKED_SCORE, F32
    )
    (row_max, row_sum), unused = lax.scan(
        stats_step, (initial_maximum, jnp.zeros_like(initial_maximum)), key_blocks
    )
    log_total = row_max + jnp.log(row_sum)

    def value_step(summed, blocks):
        key_value_block, seq_block, stream_block = blocks
        key_portion = key_value_block[:, :kv_width].reshape(-1, KEY_VALUE_HEADS, HEAD_SIZE)
        value_portion = key_value_block[:, kv_width:].reshape(-1, KEY_VALUE_HEADS, HEAD_SIZE)
        scores = block_scores(
            rotated_queries, key_portion, query_seq, my_stream, seq_block, stream_block, score_scale
        )
        low_chances = jnp.exp(scores - log_total[..., None]).astype(BF)
        summed = summed + jnp.einsum(
            "krts,skd->tkrd", low_chances, value_portion, preferred_element_type=F32
        )
        return (summed, None)

    empty_head_state = jnp.zeros(
        (token_count, KEY_VALUE_HEADS, query_per_key_heads, HEAD_SIZE), F32
    )
    attended, unused = lax.scan(value_step, empty_head_state, key_blocks)
    attended_low = attended.reshape(token_count, q_width).astype(BF)
    middle = inputs_float + dot(attended_low, out_w)
    inv_two = rms_scale(middle)
    unit_two = middle * inv_two
    normed_two = (unit_two * gain_two).astype(BF)

    logits = dot(normed_two, router_w)
    choose = jnp.any(
        routes[:, :, None] == lax.broadcasted_iota(jnp.int32, (1, 1, n_experts), 2), axis=1
    )
    top_logit = jnp.max(jnp.where(choose, logits, -jnp.inf), axis=1, keepdims=True)
    spread = jnp.where(choose, jnp.exp(jnp.minimum(logits - top_logit, 0.0)), 0.0)
    gates = spread / jnp.sum(spread, axis=1, keepdims=True)

    normed_all = lax.all_gather(normed_two, "expert", axis=0, tiled=True)
    gates_all = lax.all_to_all(
        gates.T.reshape(n_experts, 1, token_count), "expert", split_axis=0, concat_axis=1, tiled=True
    )
    gate_col = gates_all.reshape(group_tokens, 1)

    gate_pre = dot(normed_all, gate_w)
    up_pre = dot(normed_all, up_w)
    sig = jax.nn.sigmoid(gate_pre)
    silu = gate_pre * sig
    hidden = (silu * up_pre).astype(BF)
    returned = dot(hidden, down_w).astype(BF).astype(F32)
    cot_float = cot_all.astype(F32)
    grad_gates = jnp.sum(cot_float * returned, axis=1)
    weighted = (gate_col * returned).astype(BF)
    grad_returned = (gate_col * cot_float).astype(BF)
    grad_hidden = dot_nt(grad_returned, down_w)
    grad_gate_pre = (grad_hidden * up_pre * sig * (1.0 + gate_pre * (1.0 - sig))).astype(BF)
    grad_up_pre = (grad_hidden * silu).astype(BF)
    grad_row = (dot_nt(grad_gate_pre, gate_w) + dot_nt(grad_up_pre, up_w)).astype(BF)
    down_grad = dot_tn(hidden, grad_returned).astype(BF)
    gate_grad = dot_tn(normed_all, grad_gate_pre).astype(BF)
    up_grad = dot_tn(normed_all, grad_up_pre).astype(BF)

    grad_gates = lax.all_to_all(
        grad_gates.reshape(group_size, 1, token_count), "expert", split_axis=0, concat_axis=1, tiled=True
    ).reshape(n_experts, token_count).T
    row_sum_grad = lax.psum_scatter(grad_row, "expert", scatter_dimension=0, tiled=True)
    output = (
        middle + lax.psum_scatter(weighted, "expert", scatter_dimension=0, tiled=True).astype(F32)
    ).astype(BF)

    grad_out = cotangent.astype(F32)
    grad_logits = (
        gates * (grad_gates - jnp.sum(gates * grad_gates, axis=1, keepdims=True))
    ).astype(BF)
    router_grad = dot_tn(normed_two, grad_logits)
    grad_normed_two = dot_nt(grad_logits, router_w) + row_sum_grad.astype(F32)
    gain_two_grad, grad_middle = norm_backward(grad_normed_two, unit_two, inv_two, gain_two)
    grad_middle = grad_out + grad_middle
    grad_mixed = grad_middle.astype(BF)
    out_grad = dot_tn(attended_low, grad_mixed)
    grad_attended = dot_nt(grad_mixed, out_w).astype(BF)
    head_gradient = grad_attended.reshape(
        token_count, KEY_VALUE_HEADS, query_per_key_heads, HEAD_SIZE
    )
    row_dot = jnp.transpose(jnp.sum(head_gradient.astype(F32) * attended, axis=-1), (1, 2, 0))

    def grad_step(query_grad, blocks):
        key_value_block, seq_block, stream_block = blocks
        key_portion = key_value_block[:, :kv_width].reshape(-1, KEY_VALUE_HEADS, HEAD_SIZE)
        value_portion = key_value_block[:, kv_width:].reshape(-1, KEY_VALUE_HEADS, HEAD_SIZE)
        scores = block_scores(
            rotated_queries, key_portion, query_seq, my_stream, seq_block, stream_block, score_scale
        )
        chances = jnp.exp(scores - log_total[..., None])
        low_chances = chances.astype(BF)
        grad_chances = jnp.einsum(
            "tkrd,skd->krts", head_gradient, value_portion, preferred_element_type=F32
        )
        grad_scores = (chances * (grad_chances - row_dot[..., None])).astype(BF)
        query_grad = query_grad + jnp.einsum(
            "krts,skd->tkrd", grad_scores, key_portion, preferred_element_type=F32
        )
        key_terms = (
            jnp.einsum("krts,tkrd->skd", grad_scores, rotated_queries, preferred_element_type=F32)
            * score_scale
        )
        value_terms = jnp.einsum(
            "krts,tkrd->skd", low_chances, head_gradient, preferred_element_type=F32
        )
        return (query_grad, (key_terms.astype(BF), value_terms.astype(BF)))

    query_grad, (key_terms, value_terms) = lax.scan(grad_step, empty_head_state, key_blocks)
    query_grad = query_grad * score_scale
    kv_terms = jnp.concatenate(
        [key_terms.reshape(group_tokens, kv_width), value_terms.reshape(group_tokens, kv_width)],
        axis=1,
    )
    kv_mine = lax.psum_scatter(kv_terms, "expert", scatter_dimension=0, tiled=True)
    grad_query_pre = (
        reverse_rotation(
            query_grad.reshape(token_count, QUERY_HEADS, HEAD_SIZE), cosine_table, sine_table
        )
        .reshape(token_count, q_width)
        .astype(BF)
    )
    grad_key_pre = (
        reverse_rotation(
            kv_mine[:, :kv_width].astype(F32).reshape(token_count, KEY_VALUE_HEADS, HEAD_SIZE),
            cosine_table,
            sine_table,
        )
        .reshape(token_count, kv_width)
        .astype(BF)
    )
    grad_qkv = jnp.concatenate([grad_query_pre, grad_key_pre, kv_mine[:, kv_width:]], axis=1)
    grad_normed_one = dot_nt(grad_qkv, pack[:, :c_s])
    qkv_grad = dot_tn(normed_one, grad_qkv)
    gain_one_grad, grad_input = norm_backward(grad_normed_one, unit_one, inv_one, gain_one)
    tokens_grad = (grad_middle + grad_input).astype(BF)
    small_grad = jnp.concatenate(
        [
            router_grad,
            gain_one_grad[:, None],
            gain_two_grad[:, None],
            jnp.zeros((width, 128 - n_experts - 2), F32),
        ],
        axis=1,
    )
    pack_grad = jnp.concatenate(
        [qkv_grad.astype(BF), small_grad.astype(BF), out_grad.astype(BF)], axis=1
    )
    mine = lax.psum_scatter(pack_grad, ("dp", "expert"), scatter_dimension=0, tiled=True)
    mine = mine.astype(F32)
    gate_mine, up_mine, down_mine = (
        lax.psum_scatter(grad, "dp", scatter_dimension=0, tiled=True).astype(F32)[None]
        for grad in (gate_grad, up_grad, down_grad)
    )
    return (
        output,
        tokens_grad,
        mine[:, c_s + n_experts],
        mine[:, :c_k],
        mine[:, c_k:c_v],
        mine[:, c_v:c_s],
        mine[:, c_o:],
        mine[:, c_s + n_experts + 1],
        mine[:, c_s : c_s + n_experts],
        gate_mine,
        up_mine,
        down_mine,
    )


MESH_ID = pl.DeviceIdType.MESH
ANY = pl.ANY
LOG2E = math.log2(math.e)


class Place:
    def __init__(self):
        d = lax.axis_index("dp")
        e = lax.axis_index("expert")
        core = lax.rem(e, 2)
        x = lax.rem(lax.div(e, 2), 2)
        y = lax.div(e, 4)
        self.d, self.e, self.core = d, e, core
        self.chip = lax.div(e, 2)
        self.e_s = e + 1 - 2 * core
        self.e_x = e + 2 - 4 * x
        self.e_y = e + 4 - 8 * y
        self.e_d = self.e_x + 4 - 8 * y
        self.chip_x = self.chip + 1 - 2 * x
        self.chip_y = self.chip + 2 - 4 * y
        self.chip_d = self.chip_x + 2 - 4 * y
        self.sib = (d, self.e_s)
        self.nx = (d, self.e_x)
        self.ny = (d, self.e_y)
        half = lax.div(d, 2)
        odd = lax.rem(d, 2)
        self.pair = (2 * half + 1 - odd, e)
        self.cross = (3 - d, e)
        self.inner = (d == 1) | (d == 2)
        self.order = (d, 2 * half + 1 - odd, 2 - half, 3 - 3 * half)

    def greet(self):
        barrier = pltpu.get_barrier_semaphore()
        for other in (self.sib, self.nx, self.ny, self.pair):
            pl.semaphore_signal(barrier, inc=1, device_id=other, device_id_type=MESH_ID)

        @pl.when(self.inner)
        def _():
            pl.semaphore_signal(barrier, inc=1, device_id=self.cross, device_id_type=MESH_ID)
            pl.semaphore_wait(barrier, 5)

        @pl.when(jnp.logical_not(self.inner))
        def _():
            pl.semaphore_wait(barrier, 4)


def rcopy(src, dst, send_sem, recv_sem, device):
    return pltpu.make_async_remote_copy(
        src_ref=src,
        dst_ref=dst,
        send_sem=send_sem,
        recv_sem=recv_sem,
        device_id=device,
        device_id_type=MESH_ID,
    )


class PlaneGather:
    def __init__(self, at, blk, half, send, recv):
        self.at, self.blk, self.half, self.send, self.recv = at, blk, half, send, recv

    def push(self, ref, target, slot_send, slot_recv, src=None):
        rcopy(
            ref if src is None else src, ref, self.send(slot_send), self.recv(slot_recv), target
        ).start()

    def await_(self, ref, slot):
        rcopy(ref, ref, self.send(0), self.recv(slot), self.at.sib).wait_recv()

    def sent(self, ref, slot):
        rcopy(ref, ref, self.send(slot), self.recv(0), self.at.sib).wait_send()

    def start(self, src=None):
        at = self.at
        own = self.blk(at.e)
        self.push(own, at.nx, 0, 0, src)
        self.push(own, at.ny, 1, 1, src)
        self.push(own, at.sib, 2, 4, src)

    def on_x(self):
        at = self.at
        got = self.blk(at.e_x)
        self.await_(got, 0)
        self.push(self.half(at.e_x, 0), at.ny, 3, 3)
        self.push(got, at.sib, 4, 5)

    def on_y(self):
        at = self.at
        got = self.blk(at.e_y)
        self.await_(got, 1)
        self.push(self.half(at.e_y, 1), at.nx, 5, 2)
        self.push(got, at.sib, 6, 6)

    def on_d(self):
        at = self.at
        self.await_(self.half(at.e_d, 1), 2)
        self.await_(self.half(at.e_d, 0), 3)
        self.push(self.blk(at.e_d), at.sib, 7, 7)

    def on_s(self):
        at = self.at
        turn = at.e_s - at.e
        self.await_(self.blk(at.e_s), 4)
        self.await_(self.blk(at.e_x + turn), 5)
        self.await_(self.blk(at.e_y + turn), 6)
        self.await_(self.blk(at.e_d + turn), 7)

    def drain(self):
        at = self.at
        whole = self.blk(at.e)
        for slot in (0, 1, 2, 4, 6, 7):
            self.sent(whole, slot)
        self.sent(self.half(at.e, 0), 3)
        self.sent(self.half(at.e, 1), 5)


class LineGather:
    def __init__(self, at, blk, send, recv):
        self.at, self.blk, self.send, self.recv = at, blk, send, recv

    def start(self, src=None):
        at = self.at
        own = self.blk(at.d)
        from_ = own if src is None else src
        rcopy(from_, own, self.send(0), self.recv(1), at.pair).start()

        @pl.when(at.inner)
        def _():
            rcopy(from_, own, self.send(1), self.recv(2), at.cross).start()

    def on(self, k):
        at = self.at
        got = self.blk(at.order[k])
        rcopy(got, got, self.send(0), self.recv(k), at.pair).wait_recv()

        @pl.when(at.inner)
        def _():
            if k == 1:
                rcopy(got, got, self.send(2), self.recv(3), at.cross).start()
            else:
                rcopy(got, got, self.send(k + 1), self.recv(k), at.pair).start()

    def relay(self, k):
        @pl.when(self.at.inner)
        def _():
            self.on(k)

    def land(self):
        at = self.at

        @pl.when(jnp.logical_not(at.inner))
        def _():
            for k in (1, 2, 3):
                got = self.blk(at.order[k])
                rcopy(got, got, self.send(0), self.recv(k), at.pair).wait_recv()

    def drain(self):
        at = self.at
        own = self.blk(at.d)
        rcopy(own, own, self.send(0), self.recv(0), at.pair).wait_send()

        @pl.when(at.inner)
        def _():
            for slot in (1, 2, 3, 4):
                rcopy(own, own, self.send(slot), self.recv(0), at.pair).wait_send()


def rows_of(ref, start, size):
    return ref.at[pl.ds(pl.multiple_of(start, 16), size)]


def stream_facts(lens_ref, order_ref, token_count, group_size, e):
    count = lens_ref.shape[1]
    stream = lax.broadcasted_iota(jnp.int32, (token_count, 128), 0) * group_size + e
    begin = jnp.zeros_like(stream)
    end = jnp.int32(0)
    for j in range(count):
        size = jnp.int32(0)
        for i in range(count):
            size = size + jnp.where(order_ref[0, j] == i, lens_ref[0, i], 0)
        end = end + size
        begin = begin + jnp.where(stream >= end, size, 0)
    return stream, begin, stream - begin


def rotary(relative):
    lane = lax.rem(lax.broadcasted_iota(jnp.int32, relative.shape, 1), HEAD_SIZE // 2)
    frequency = jnp.exp(lane.astype(F32) * (-math.log(ROPE_BASE) / (HEAD_SIZE // 2)))
    angles = relative.astype(F32) * frequency
    first = lax.broadcasted_iota(jnp.int32, relative.shape, 1) < HEAD_SIZE // 2
    sine = jnp.sin(angles)
    return jnp.cos(angles), jnp.where(first, -sine, sine)


def swap_halves(values):
    return pltpu.roll(values, HEAD_SIZE // 2, 1)


TILE = 64


def tiles_of(i):
    return range(max(0, i - 2), i + 1)


def tile_bias(i, r, stream, begin, group_size):
    wide = TILE * group_size
    j = lax.broadcasted_iota(jnp.int32, (TILE, wide), 1)
    key = (r * TILE + lax.rem(j, TILE)) * group_size + lax.div(j, TILE)
    ok = key >= begin[i * TILE : (i + 1) * TILE, :1]
    if r == i:
        ok = ok & (key <= stream[i * TILE : (i + 1) * TILE, :1])
    return jnp.where(ok, 0.0, MASKED_SCORE)


def dot_nn(a, b):
    return lax.dot_general(a, b, (((1,), (0,)), ((), ())), preferred_element_type=F32)


def dot_bt(a, b):
    return lax.dot_general(a, b, (((1,), (1,)), ((), ())), preferred_element_type=F32)


def dot_at(a, b):
    return lax.dot_general(a, b, (((0,), (0,)), ((), ())), preferred_element_type=F32)


def column_as_row(small, lane):
    pick = (lax.broadcasted_iota(jnp.int32, (8, 128), 1) == lane).astype(F32).astype(BF)
    return dot_bt(pick, small)[:1]


def front_kernel(
    n_experts,
    lens_ref,
    order_ref,
    tok_ref,
    routes_ref,
    pack_ref,
    wo_ref,
    gw_ref,
    uw_ref,
    x_all,
    gw_all,
    uw_all,
    pack_out,
    wo_out,
    kv_out,
    q_out,
    att_out,
    lse_out,
    mid_out,
    pay_ref,
    pack_all,
    wo_all,
    kv_all,
    unit_ref,
    acc_ref,
    s_ref,
    ag_send,
    ag_recv,
    z_send,
    z_recv,
    local,
):
    at = Place()
    at.greet()
    tokens, width = tok_ref.shape
    shard = pack_ref.shape[0]
    group = 8
    kv_width = KEY_VALUE_HEADS * HEAD_SIZE
    q_width = QUERY_HEADS * HEAD_SIZE
    qkv = q_width + 2 * kv_width
    per_kv = QUERY_HEADS // KEY_VALUE_HEADS
    chunk = shard * group
    cut_a = 9 * 128
    cut_b = wo_ref.shape[1] // 2
    items = {}

    def add_item(name, blk, half):
        n = len(items)
        items[name] = PlaneGather(
            at, blk, half, lambda k, n=n: ag_send.at[n, k], lambda k, n=n: ag_recv.at[n, k]
        )

    def add_weight(name, ref, z, cut):
        wide = ref.shape[1]

        def place(e):
            return pl.ds(pl.multiple_of(z * chunk + e * shard, 16), shard)

        def half(e, h):
            return ref.at[place(e), pl.ds(0, cut) if h == 0 else pl.ds(cut, wide - cut)]

        add_item(name, lambda e: ref.at[place(e)], half)

    for k in range(4):
        add_weight(("a", k), pack_all, at.order[k], cut_a)
    for k in range(4):
        add_weight(("b", k), wo_all, at.order[k], cut_b)
    add_item("kv", lambda e: kv_all.at[e], lambda e, h: kv_all.at[e, :, pl.ds(h * kv_width, kv_width)])
    part = tokens // 2
    for name, ref, cut in (("x", x_all, 7 * 128),):
        wide = ref.shape[2]
        for k in range(2):
            rows = pl.ds(k * part, part)

            def half(e, h, ref=ref, rows=rows, cut=cut, wide=wide):
                return ref.at[e, rows, pl.ds(0, cut) if h == 0 else pl.ds(cut, wide - cut)]

            add_item((name, k), lambda e, ref=ref, rows=rows: ref.at[e, rows], half)

    lines = {}

    def add_line(name, ref, size, start):
        n = len(lines)
        lines[name] = LineGather(
            at,
            lambda z: rows_of(ref, start(z), size),
            lambda k, n=n: z_send.at[n, k],
            lambda k, n=n: z_recv.at[n, k],
        )

    add_line("a", pack_all, shard, lambda z: z * chunk + at.e * shard)
    add_line("b", wo_all, shard, lambda z: z * chunk + at.e * shard)
    for name, ref, src in (("g", gw_all, gw_ref), ("u", uw_all, uw_ref)):
        size = src.shape[0]
        add_line(name, ref, size, lambda z, size=size: z * size)

    own_a = rows_of(pack_all, at.d * chunk + at.e * shard, shard)
    own_b = rows_of(wo_all, at.d * chunk + at.e * shard, shard)
    copies = [
        pltpu.make_async_copy(pack_ref, own_a, local.at[0]),
        pltpu.make_async_copy(wo_ref, own_b, local.at[1]),
    ]
    for n, (name, src) in enumerate((("g", gw_ref), ("u", uw_ref))):
        copies.append(pltpu.make_async_copy(src, lines[name].blk(at.d), local.at[2 + n]))

    lines["a"].start(pack_ref)
    items["a", 0].start(pack_ref)
    lines["b"].start(wo_ref)
    for copy in copies:
        copy.start()

    tok = tok_ref[...].astype(F32)
    scale_one = lax.rsqrt(jnp.mean(tok * tok, axis=1, keepdims=True) + EPSILON)
    unit_ref[...] = tok * scale_one
    stream, begin, relative = stream_facts(lens_ref, order_ref, tokens, group, at.e)
    cosine, sine = rotary(relative)
    acc_ref[...] = jnp.zeros_like(acc_ref)
    copies[0].wait()
    copies[1].wait()

    def consume(k):
        z = at.order[k]
        place = pl.ds(pl.multiple_of(z * chunk, 128), chunk)
        gain = column_as_row(pack_all[place, qkv:], n_experts)
        normed = (unit_ref[:, place] * gain).astype(BF)
        acc_ref[...] += dot_nn(normed, pack_all[place, :qkv])

    lines["a"].on(1)
    items["a", 1].start()
    items["a", 0].on_x()
    items["a", 0].on_y()
    lines["g"].start(gw_ref)
    items["a", 0].on_d()
    lines["a"].on(2)
    items["a", 2].start()
    items["a", 1].on_x()
    items["a", 1].on_y()
    items["a", 0].on_s()
    consume(0)
    lines["a"].on(3)
    items["a", 3].start()
    lines["b"].on(1)
    lines["u"].start(uw_ref)
    items["a", 1].on_d()
    items["a", 2].on_x()
    items["a", 2].on_y()
    items["a", 1].on_s()
    consume(1)
    lines["b"].on(2)
    items["a", 2].on_d()
    items["a", 3].on_x()
    items["a", 3].on_y()
    items["b", 0].start()
    items["a", 2].on_s()
    consume(2)
    lines["b"].on(3)
    items["a", 3].on_d()
    items["a", 3].on_s()
    consume(3)
    lines["g"].relay(1)
    keep = [
        pltpu.make_async_copy(pack_all, pack_out, local.at[7]),
    ]
    keep[0].start()

    def turned(col):
        v = acc_ref[:, col : col + HEAD_SIZE]
        return (v * cosine + swap_halves(v) * sine).astype(BF)

    for h in range(KEY_VALUE_HEADS):
        kv_all[at.e, :, h * HEAD_SIZE : (h + 1) * HEAD_SIZE] = turned(q_width + h * HEAD_SIZE)
    kv_all[at.e, :, kv_width:] = acc_ref[:, q_width + kv_width :].astype(BF)
    items["kv"].start()
    for h in range(QUERY_HEADS):
        q_out[h] = turned(h * HEAD_SIZE)
    items["b", 0].on_x()
    items["b", 0].on_y()
    items["b", 1].start()
    items["kv"].on_x()
    items["kv"].on_y()
    items["b", 0].on_d()
    items["b", 2].start()
    items["kv"].on_d()
    items["kv"].on_s()
    keep.append(pltpu.make_async_copy(kv_all, kv_out, local.at[8]))
    keep[1].start()

    def step_b(n):
        if n == 0:
            items["b", 1].on_x()
            items["b", 1].on_y()
            items["b", 3].start()
        elif n == 1:
            lines["g"].relay(2)
            items["b", 1].on_d()
            items["b", 2].on_x()
            items["b", 2].on_y()
        elif n == 2:
            lines["u"].relay(1)
            items["b", 2].on_d()
            items["b", 3].on_x()
            items["b", 3].on_y()
        elif n == 3:
            items["b", 3].on_d()
            lines["u"].relay(2)

    factor = LOG2E / math.sqrt(HEAD_SIZE)
    wide = TILE * group
    for i in range(tokens // TILE):
        step_b(i)
        first = tiles_of(i)[0]
        biases = [tile_bias(i, r, stream, begin, group) for r in tiles_of(i)]
        here = slice(i * TILE, (i + 1) * TILE)
        for g in range(KEY_VALUE_HEADS):
            queries = q_out[g * per_kv : (g + 1) * per_kv, here, :].reshape(per_kv * TILE, HEAD_SIZE)
            top = None
            for r in tiles_of(i):
                keys = kv_all[:, r * TILE : (r + 1) * TILE, g * HEAD_SIZE : (g + 1) * HEAD_SIZE]
                s = dot_bt(queries, keys.reshape(wide, HEAD_SIZE)) * factor
                s = s.reshape(per_kv, TILE, wide) + biases[r - first][None]
                s = s.reshape(per_kv * TILE, wide)
                s_ref[:, (r - first) * wide : (r - first + 1) * wide] = s
                high = jnp.max(s, axis=1, keepdims=True)
                top = high if top is None else jnp.maximum(top, high)
            total = None
            mixed = None
            for r in tiles_of(i):
                p = jnp.exp2(s_ref[:, (r - first) * wide : (r - first + 1) * wide] - top)
                values = kv_all[
                    :, r * TILE : (r + 1) * TILE, kv_width + g * HEAD_SIZE : kv_width + (g + 1) * HEAD_SIZE
                ].reshape(wide, HEAD_SIZE)
                row = jnp.sum(p, axis=1, keepdims=True)
                term = dot_nn(p.astype(BF), values)
                total = row if total is None else total + row
                mixed = term if mixed is None else mixed + term
            mixed = mixed / total
            lse_out[g, i] = jnp.broadcast_to(top + jnp.log2(total), (per_kv * TILE, 128))
            for h in range(per_kv):
                col = (g * per_kv + h) * HEAD_SIZE
                att_out[here, col : col + HEAD_SIZE] = mixed[h * TILE : (h + 1) * TILE]

    for k in range(4):
        items["b", k].on_s()
    keep.append(pltpu.make_async_copy(wo_all, wo_out, local.at[9]))
    keep[2].start()
    lines["g"].relay(3)
    attended = att_out[...].astype(BF)
    step = 256
    for n in range(width // step):
        cols = slice(n * step, (n + 1) * step)
        mid_out[:, cols] = tok_ref[:, cols].astype(F32) + dot_nn(attended, wo_all[:, cols])
    middle = mid_out[...]
    scale_two = lax.rsqrt(jnp.mean(middle * middle, axis=1, keepdims=True) + EPSILON)
    small = pack_all[:, qkv:]
    normed_two = (middle * scale_two * column_as_row(small, n_experts + 1)).astype(BF)
    pay_ref[:, :width] = normed_two
    logits = dot_nn(normed_two, small)
    lane = lax.broadcasted_iota(jnp.int32, (tokens, 128), 1)
    choose = lane == routes_ref[:, :1]
    for k in range(1, routes_ref.shape[1]):
        choose = choose | (lane == routes_ref[:, k : k + 1])
    top = jnp.max(jnp.where(choose, logits, MASKED_SCORE), axis=1, keepdims=True)
    spread = jnp.where(choose, jnp.exp(jnp.minimum(logits - top, 0.0)), 0.0)
    gates = spread / jnp.sum(spread, axis=1, keepdims=True)
    pay_ref[:, width:] = split_three(gates)
    own_x = [
        pltpu.make_async_copy(
            pay_ref.at[pl.ds(k * part, part)], x_all.at[at.e, pl.ds(k * part, part)], local.at[10 + k]
        )
        for k in range(2)
    ]
    for k in range(2):
        items["x", k].start(pay_ref.at[pl.ds(k * part, part)])
        own_x[k].start()
    lines["u"].relay(3)
    for k in range(2):
        items["x", k].on_x()
        items["x", k].on_y()
    for k in range(2):
        items["x", k].on_d()
    for k in range(2):
        items["x", k].on_s()
    lines["g"].land()
    lines["u"].land()
    for item in items.values():
        item.drain()
    for line in lines.values():
        line.drain()
    for copy in copies[2:] + keep + own_x:
        copy.wait()


def split_three(values):
    high = values.astype(BF).astype(F32)
    mid = (values - high).astype(BF).astype(F32)
    low = values - high - mid
    return (high + pltpu.roll(mid, 32, 1) + pltpu.roll(low, 64, 1)).astype(BF)


def front(lengths, seq_order, tokens, routes, pack, wo, gw, uw, n_experts):
    count, width = tokens.shape
    group, line = 8, 4
    kv_width = KEY_VALUE_HEADS * HEAD_SIZE
    per_kv = QUERY_HEADS // KEY_VALUE_HEADS
    sds = jax.ShapeDtypeStruct
    smem = pl.BlockSpec(memory_space=pltpu.SMEM)
    vmem = pl.BlockSpec(memory_space=pltpu.VMEM)
    hbm = pl.BlockSpec(memory_space=ANY)
    n_items = 11
    return pl.pallas_call(
        functools.partial(front_kernel, n_experts),
        in_specs=[smem, smem] + [vmem] * 6,
        out_specs=(hbm,) * 6 + (vmem,) * 5,
        out_shape=(
            sds((group, count, width + 128), BF),
            sds((line * gw.shape[0], gw.shape[1]), BF),
            sds((line * uw.shape[0], uw.shape[1]), BF),
            sds((width, pack.shape[1]), BF),
            sds((width, wo.shape[1]), BF),
            sds((group, count, 2 * kv_width), BF),
            sds((QUERY_HEADS, count, HEAD_SIZE), BF),
            sds((count, QUERY_HEADS * HEAD_SIZE), F32),
            sds((KEY_VALUE_HEADS, count // TILE, per_kv * TILE, 128), F32),
            sds((count, width), F32),
            sds((count, width + 128), BF),
        ),
        scratch_shapes=[
            pltpu.VMEM((width, pack.shape[1]), BF),
            pltpu.VMEM((width, wo.shape[1]), BF),
            pltpu.VMEM((group, count, 2 * kv_width), BF),
            pltpu.VMEM((count, width), F32),
            pltpu.VMEM((count, pack.shape[1] - 128), F32),
            pltpu.VMEM((per_kv * TILE, 3 * TILE * group), F32),
            pltpu.SemaphoreType.DMA((n_items, 8)),
            pltpu.SemaphoreType.DMA((n_items, 8)),
            pltpu.SemaphoreType.DMA((4, 5)),
            pltpu.SemaphoreType.DMA((4, 4)),
            pltpu.SemaphoreType.DMA((12,)),
        ],
        compiler_params=pltpu.CompilerParams(
            collective_id=1, has_side_effects=True, vmem_limit_bytes=60 * 2**20
        ),
    )(lengths, seq_order, tokens, routes, pack, wo, gw, uw)


class PlaneReduce:
    def __init__(self, at, first, own, seat, xs, ys, x2, y2, cut, send, recv):
        self.at, self.first, self.own = at, first, own
        self.seat, self.xs, self.ys, self.x2, self.y2 = seat, xs, ys, x2, y2
        self.cut, self.send, self.recv = cut, send, recv

    def copy(self, slot, src, dst, target):
        return rcopy(src, dst, self.send(slot), self.recv(slot), target)

    def moves(self):
        at, own, cut = self.at, self.own, self.cut
        low, high = pl.ds(0, cut), pl.ds(cut, self.seat.shape[-1] - cut)
        return {
            0: lambda: self.copy(0, self.first, self.seat, at.sib),
            1: lambda: self.copy(1, own.at[at.chip_x, :, low], self.xs.at[0], at.nx),
            2: lambda: self.copy(2, own.at[at.chip_d, :, low], self.xs.at[1], at.nx),
            3: lambda: self.copy(3, own.at[at.chip_y, :, high], self.ys.at[0], at.ny),
            4: lambda: self.copy(4, own.at[at.chip_d, :, high], self.ys.at[1], at.ny),
            5: lambda: self.copy(5, own.at[at.chip_y, :, low], self.y2, at.ny),
            6: lambda: self.copy(6, own.at[at.chip_x, :, high], self.x2, at.nx),
        }

    def begin(self, slot):
        self.moves()[slot]().start()

    def got(self, slot):
        self.moves()[slot]().wait_recv()

    def start(self):
        self.begin(0)

    def on_s(self):
        self.got(0)

        def add(q, none):
            self.own[q] = (self.own[q].astype(F32) + self.seat[q].astype(F32)).astype(BF)
            return none

        lax.fori_loop(0, 4, add, 0)
        for slot in (1, 2, 3, 4):
            self.begin(slot)

    def on_xy(self):
        at, own, cut = self.at, self.own, self.cut
        self.got(1)
        self.got(2)
        own[at.chip_y, :, :cut] = (
            own[at.chip_y, :, :cut].astype(F32) + self.xs[1].astype(F32)
        ).astype(BF)
        self.begin(5)
        self.got(3)
        self.got(4)
        own[at.chip_x, :, cut:] = (
            own[at.chip_x, :, cut:].astype(F32) + self.ys[1].astype(F32)
        ).astype(BF)
        self.begin(6)

    def finish(self):
        at, own, cut = self.at, self.own, self.cut
        self.got(5)
        low = own[at.chip, :, :cut].astype(F32) + self.xs[0].astype(F32) + self.y2[...].astype(F32)
        self.got(6)
        high = own[at.chip, :, cut:].astype(F32) + self.ys[0].astype(F32) + self.x2[...].astype(F32)
        return low, high

    def sent(self, slot):
        self.moves()[slot]().wait_send()

    def drain(self, slots=range(7)):
        for slot in slots:
            self.sent(slot)


class LineReduce:
    def __init__(self, at, blocks, near, far, send, recv):
        self.at, self.blocks, self.near, self.far = at, blocks, near, far
        self.send, self.recv = send, recv

    def copy(self, slot, src, dst, target):
        return rcopy(src, dst, self.send(slot), self.recv(slot), target)

    def outer_moves(self):
        at = self.at
        return [
            self.copy(n, self.blocks.at[at.order[n + 1]], self.near.at[n], at.pair)
            for n in range(3)
        ]

    def cross_moves(self):
        at = self.at
        return [
            self.copy(3 + n, self.blocks.at[at.order[n + 2]], self.far.at[n], at.cross)
            for n in range(2)
        ]

    def back_move(self):
        at = self.at
        return self.copy(0, self.blocks.at[at.order[1]], self.near.at[0], at.pair)

    def start(self):
        at = self.at

        @pl.when(jnp.logical_not(at.inner))
        def _():
            for move in self.outer_moves():
                move.start()

    def middle(self):
        at, blocks = self.at, self.blocks

        @pl.when(at.inner)
        def _():
            for n in range(2):
                rcopy(
                    self.near.at[n + 1], self.near.at[n + 1], self.send(0), self.recv(n + 1), at.pair
                ).wait_recv()
                blocks[at.order[n + 2]] = (
                    blocks[at.order[n + 2]].astype(F32) + self.near[n + 1].astype(F32)
                ).astype(BF)
                self.cross_moves()[n].start()

    def last(self):
        at, blocks = self.at, self.blocks

        @pl.when(at.inner)
        def _():
            self.cross_moves()[1].wait_recv()
            blocks[at.order[1]] = (
                blocks[at.order[1]].astype(F32) + self.far[1].astype(F32)
            ).astype(BF)
            self.back_move().start()

    def leave(self, k):
        @pl.when(jnp.logical_not(self.at.inner))
        def _():
            self.outer_moves()[k - 1].start()

    def hand(self, k):
        at, blocks = self.at, self.blocks

        @pl.when(at.inner)
        def _():
            if k == 1:
                self.cross_moves()[1].wait_recv()
                come = self.far[1]
            else:
                rcopy(
                    self.near.at[k - 1], self.near.at[k - 1], self.send(0), self.recv(k - 1), at.pair
                ).wait_recv()
                come = self.near[k - 1]
            blocks[at.order[k]] = (blocks[at.order[k]].astype(F32) + come.astype(F32)).astype(BF)
            if k == 1:
                self.back_move().start()
            else:
                self.cross_moves()[k - 2].start()

    def finish(self, out):
        at = self.at
        self.back_move().wait_recv()
        total = self.blocks[at.d].astype(F32) + self.near[0].astype(F32)

        @pl.when(at.inner)
        def _():
            self.cross_moves()[0].wait_recv()
            out[...] = total + self.far[0].astype(F32)
            for move in self.cross_moves():
                move.wait_send()
            self.back_move().wait_send()

        @pl.when(jnp.logical_not(at.inner))
        def _():
            out[...] = total
            for move in self.outer_moves():
                move.wait_send()


def column_sums(values):
    high = values.astype(BF)
    low = (values - high.astype(F32)).astype(BF)
    ones = jnp.ones((values.shape[0], 128), BF)
    return dot_at(high, ones) + dot_at(low, ones)


def expert_lanes(rows):
    e = lax.axis_index("expert")
    lane = lax.broadcasted_iota(jnp.int32, (rows, 128), 1)
    return e, lane, (lane == e) | (lane == e + 32) | (lane == e + 64)


def gate_of(ext):
    mine = expert_lanes(ext.shape[0])[2]
    return jnp.sum(jnp.where(mine, ext.astype(F32), 0.0), axis=1, keepdims=True)


EXPERT_ROWS = 512


def up_kernel(
    x_in, cot_ref, gw_in, uw_in, dw_in, c_out, dw_all, hid_out, slope_out, grad_ref,
    x_ref, c_ref, gu_ref, dw_ref, hid_ref, slope_ref, back_ref, g_send, g_recv, z_send, z_recv, local,
):
    at = Place()
    at.greet()
    rows = x_ref.shape[0]
    tokens, width = cot_ref.shape
    hid = hid_ref.shape[1]
    part = tokens // 2
    copy = pltpu.make_async_copy
    tall = dw_in.shape[0]
    line = LineGather(
        at, lambda z: rows_of(dw_all, z * tall, tall), lambda k: z_send.at[k], lambda k: z_recv.at[k]
    )
    cots = []
    for k in range(2):
        span = pl.ds(k * part, part)

        def half(e, h, span=span):
            return c_ref.at[e, span, pl.ds(h * (width // 2), width // 2)]

        cots.append(
            PlaneGather(
                at,
                lambda e, span=span: c_ref.at[e, span],
                half,
                lambda s, k=k: g_send.at[k, s],
                lambda s, k=k: g_recv.at[k, s],
            )
        )
    line.start(dw_in)
    for k in range(2):
        cots[k].start(cot_ref.at[pl.ds(k * part, part)])
    gates_w = copy(gw_in, gu_ref.at[:, pl.ds(0, hid)], local.at[0])
    ups_w = copy(uw_in, gu_ref.at[:, pl.ds(hid, hid)], local.at[1])
    own_c = copy(cot_ref, c_ref.at[at.e], local.at[2])
    own_d = copy(dw_in, line.blk(at.d), local.at[3])
    count = rows // EXPERT_ROWS
    spans = [pl.ds(b * EXPERT_ROWS, EXPERT_ROWS) for b in range(count)]
    loads = [copy(x_in.at[spans[b]], x_ref.at[spans[b]], local.at[4 + b]) for b in range(count)]
    saves = []
    gates_w.start()
    loads[0].start()
    ups_w.start()
    for b in range(1, count):
        loads[b].start()
    own_c.start()
    own_d.start()
    gates_w.wait()
    ups_w.wait()
    step = 256
    for b in range(count):
        loads[b].wait()

        def work(h, none, b=b):
            here = pl.ds(pl.multiple_of(b * EXPERT_ROWS + h * step, step), step)
            x = x_ref[here, :width]
            for f in range(hid // 256):
                cols = slice(f * 256, (f + 1) * 256)
                after = slice(hid + f * 256, hid + (f + 1) * 256)
                gate_pre = dot_nn(x, gu_ref[:, cols])
                up_pre = dot_nn(x, gu_ref[:, after])
                sig = 1.0 / (1.0 + jnp.exp(-gate_pre))
                silu = gate_pre * sig
                hid_ref[here, cols] = (silu * up_pre).astype(BF)
                slope_ref[here, after] = silu.astype(BF)
                slope_ref[here, cols] = (up_pre * sig * (1.0 + gate_pre * (1.0 - sig))).astype(BF)
            return none

        lax.fori_loop(0, EXPERT_ROWS // step, work, 0)
        saves.append(copy(hid_ref.at[spans[b]], hid_out.at[spans[b]], local.at[8 + b]))
        saves[-1].start()
        if b == 1:
            line.relay(1)
            line.relay(2)
            for cot in cots:
                cot.on_x()
                cot.on_y()
        if b == 3:
            line.relay(3)
    for cot in cots:
        cot.on_d()
    own_c.wait()
    for cot in cots:
        cot.on_s()
    saves.append(copy(c_ref, c_out, local.at[16]))
    saves[-1].start()

    def weigh(e, none):
        here = pl.ds(pl.multiple_of(e * tokens, tokens), tokens)
        back_ref[here, :] = (gate_of(x_ref[here, width:]) * c_ref[e].astype(F32)).astype(BF)
        return none

    lax.fori_loop(0, c_ref.shape[0], weigh, 0)
    deep = gw_in.shape[0] // 4
    for t in range(2):
        down = dot_at(hid_ref[:, 2 * t * tall : 2 * (t + 1) * tall], back_ref[...]).astype(BF)
        for j in range(2):
            piece = down[j * tall : (j + 1) * tall]
            grad_ref[2 * t + j, 2 * deep : 2 * deep + tall] = piece[:, : width // 2]
            grad_ref[2 * t + j, 2 * deep + tall :] = piece[:, width // 2 :]
    line.land()
    own_d.wait()
    load_d = copy(dw_all, dw_ref, local.at[17])
    load_d.start()
    load_d.wait()

    def slopes(h, none):
        here = pl.ds(pl.multiple_of(h * step, step), step)
        rows_back = back_ref[here, :]
        for f in range(hid // 256):
            cols = slice(f * 256, (f + 1) * 256)
            after = slice(hid + f * 256, hid + (f + 1) * 256)
            grad_hidden = dot_bt(rows_back, dw_ref[cols, :])
            for span in (cols, after):
                slope_ref[here, span] = (grad_hidden * slope_ref[here, span].astype(F32)).astype(BF)
        return none

    lax.fori_loop(0, rows // step, slopes, 0)
    saves.append(copy(slope_ref, slope_out, local.at[12]))
    saves[-1].start()
    for z in range(4):
        both = dot_at(x_ref[:, z * deep : (z + 1) * deep], slope_ref[...]).astype(BF)
        grad_ref[z, :deep] = both[:, :hid]
        grad_ref[z, deep : 2 * deep] = both[:, hid:]
    for cot in cots:
        cot.drain()
    line.drain()
    for save in saves:
        save.wait()


def expert_up(x_all, cot, gw, uw, dw):
    rows = x_all.shape[0]
    tokens, width = cot.shape
    hid = gw.shape[1]
    sds = jax.ShapeDtypeStruct
    vmem = pl.BlockSpec(memory_space=pltpu.VMEM)
    hbm = pl.BlockSpec(memory_space=ANY)

    def low(*shape):
        return pltpu.VMEM(shape, BF)

    return pl.pallas_call(
        up_kernel,
        in_specs=[hbm, vmem, hbm, hbm, vmem],
        out_specs=(hbm, hbm, hbm, hbm, vmem),
        out_shape=(
            sds((rows // tokens, tokens, width), BF),
            sds((hid, width), BF),
            sds((rows, hid), BF),
            sds((rows, 2 * hid), BF),
            sds((4, 3 * width // 4, hid), BF),
        ),
        scratch_shapes=[
            low(rows, width + 128),
            low(rows // tokens, tokens, width),
            low(width, 2 * hid),
            low(hid, width),
            low(rows, hid),
            low(rows, 2 * hid),
            low(rows, width),
            pltpu.SemaphoreType.DMA((2, 8)),
            pltpu.SemaphoreType.DMA((2, 8)),
            pltpu.SemaphoreType.DMA((5,)),
            pltpu.SemaphoreType.DMA((4,)),
            pltpu.SemaphoreType.DMA((18,)),
        ],
        compiler_params=pltpu.CompilerParams(
            collective_id=3, has_side_effects=True, vmem_limit_bytes=62 * 2**20
        ),
        cost_estimate=pl.CostEstimate(
            flops=8 * 10**10, bytes_accessed=5 * 10**7, transcendentals=10**6
        ),
    )(x_all, cot, gw, uw, dw)


PARTS = 4


def down_kernel(
    x_in, c_in, hid_in, slope_in, gw_in, uw_in, dw_in, row_out, wgt_out,
    ext_ref, c_ref, hid_ref, slope_ref, gu_ref, dw_ref, wgt_ref,
    slot, own, seat, low1, high1, low2, high2, send, recv, local,
):
    at = Place()
    at.greet()
    tokens = x_in.shape[2]
    width = c_ref.shape[3]
    hid = dw_ref.shape[0]
    part = tokens // PARTS
    rows = 4 * part
    copy = pltpu.make_async_copy
    cut = 7 * 128
    red = []
    for k in range(PARTS):
        red.append(
            PlaneReduce(
                at, slot.at[k], own.at[k], seat.at[k], low1.at[k], high1.at[k], high2.at[k],
                low2.at[k], cut, lambda s, k=k: send.at[k, s], lambda s, k=k: recv.at[k, s],
            )
        )

    def place(j):
        core = 1 - at.core if j % 2 == 0 else at.core
        return (slice(None), core, pl.ds(j // 2 * part, part))

    count = 2 * PARTS
    ext = (pl.ds(width, 128),)
    loads = [
        [
            copy(hid_in.at[place(j)], hid_ref.at[j], local.at[0, j]),
            copy(c_in.at[place(j)], c_ref.at[j], local.at[1, j]),
            copy(x_in.at[place(j) + ext], ext_ref.at[j], local.at[2, j]),
            copy(slope_in.at[place(j)], slope_ref.at[j], local.at[3, j]),
        ]
        for j in range(count)
    ]
    saves = [copy(wgt_ref.at[j], wgt_out.at[place(j)], local.at[4, j]) for j in range(count)]
    gates_w = copy(gw_in, gu_ref.at[:, pl.ds(0, hid)], local.at[5, 0])
    ups_w = copy(uw_in, gu_ref.at[:, pl.ds(hid, hid)], local.at[5, 1])
    downs_w = copy(dw_in, dw_ref, local.at[5, 2])
    for load in loads[0]:
        load.start()
    gates_w.start()
    ups_w.start()
    downs_w.start()
    for j in range(1, count):
        for load in loads[j]:
            load.start()
    e, lane, mine = expert_lanes(rows)

    def block(j, row_dst):
        for load in loads[j]:
            load.wait()
        if j == 0:
            gates_w.wait()
            ups_w.wait()
        pair = slope_ref[j].reshape(rows, 2 * hid)
        row_dst[:, :, :width] = dot_bt(pair, gu_ref[...]).astype(BF).reshape(4, part, width)
        if j == 0:
            downs_w.wait()
        gate = gate_of(ext_ref[j].reshape(rows, 128))
        returned = dot_nn(hid_ref[j].reshape(rows, hid), dw_ref[...]).astype(BF).astype(F32)
        cot = c_ref[j].reshape(rows, width).astype(F32)
        grad_gates = jnp.sum(cot * returned, axis=1, keepdims=True)
        wgt_ref[j] = (gate * returned).astype(BF).reshape(4, part, width)
        saves[j].start()
        high = grad_gates.astype(BF).astype(F32)
        row_dst[:, :, width:] = (
            jnp.where(lane == e, high, jnp.where(lane == e + 32, grad_gates - high, 0.0))
            .astype(BF)
            .reshape(4, part, 128)
        )

    def settle(k):
        low, high = red[k].finish()
        row_out[k * part : (k + 1) * part, :cut] = low
        row_out[k * part : (k + 1) * part, cut:] = high

    for k in range(PARTS):
        block(2 * k, slot.at[k])
        red[k].start()
        if k >= 1:
            red[k - 1].on_xy()
        if k >= 2:
            settle(k - 2)
        block(2 * k + 1, own.at[k])
        red[k].on_s()
    red[PARTS - 1].on_xy()
    settle(PARTS - 2)
    settle(PARTS - 1)
    for item in red:
        item.drain()
    for save in saves:
        save.wait()


def expert_down(x_all, c_all, hidden, slope, gw, uw, dw):
    group, tokens, width = c_all.shape
    hid = gw.shape[1]
    part = tokens // PARTS
    cut = 7 * 128
    wide = width + 128
    sds = jax.ShapeDtypeStruct
    hbm = pl.BlockSpec(memory_space=ANY)

    def low(*shape):
        return pltpu.VMEM(shape, BF)

    return pl.pallas_call(
        down_kernel,
        in_specs=[hbm] * 7,
        out_specs=(pl.BlockSpec(memory_space=pltpu.VMEM), hbm),
        out_shape=(sds((tokens, wide), F32), sds((4, 2, tokens, width), BF)),
        scratch_shapes=[
            low(2 * PARTS, 4, part, 128),
            low(2 * PARTS, 4, part, width),
            low(2 * PARTS, 4, part, hid),
            low(2 * PARTS, 4, part, 2 * hid),
            low(width, 2 * hid),
            low(hid, width),
            low(2 * PARTS, 4, part, width),
            low(PARTS, 4, part, wide),
            low(PARTS, 4, part, wide),
            low(PARTS, 4, part, wide),
            low(PARTS, 2, part, cut),
            low(PARTS, 2, part, wide - cut),
            low(PARTS, part, cut),
            low(PARTS, part, wide - cut),
            pltpu.SemaphoreType.DMA((PARTS, 7)),
            pltpu.SemaphoreType.DMA((PARTS, 7)),
            pltpu.SemaphoreType.DMA((6, 2 * PARTS)),
        ],
        compiler_params=pltpu.CompilerParams(
            collective_id=4, has_side_effects=True, vmem_limit_bytes=63 * 2**20
        ),
        cost_estimate=pl.CostEstimate(
            flops=5 * 10**10, bytes_accessed=5 * 10**7, transcendentals=10**6
        ),
    )(
        x_all.reshape(4, 2, tokens, wide),
        c_all.reshape(4, 2, tokens, width),
        hidden.reshape(4, 2, tokens, hid),
        slope.reshape(4, 2, tokens, 2 * hid),
        gw,
        uw,
        dw,
    )


def pack_weights(w_router, norm_attn, norm_moe, w_query, key_projection, value_projection):
    rows, n_experts = w_router.shape
    small = jnp.concatenate(
        [
            w_router,
            norm_attn[:, None],
            norm_moe[:, None],
            jnp.zeros((rows, 128 - n_experts - 2), BF),
        ],
        axis=1,
    )
    return jnp.concatenate([w_query, key_projection, value_projection, small], axis=1)


N_BACK = 16


def back_kernel(
    n_experts,
    lens_ref,
    order_ref,
    row_in,
    wgt_in,
    tok_in,
    q_in,
    att_in,
    lse_in,
    mid_in,
    cot_in,
    kv_in,
    pay_in,
    pack_in,
    wo_in,
    output_ref,
    tokens_grad_ref,
    aq_out,
    ak_out,
    b_out,
    w_own,
    w_seat,
    w_half1,
    w_half2,
    row_ref,
    tok_ref,
    q_ref,
    att_ref,
    lse_ref,
    mid_ref,
    cot_ref,
    kv_ref,
    pay_ref,
    pack_ref,
    wo_ref,
    do_ref,
    dkv_ref,
    kseat,
    klow1,
    khigh1,
    klow2,
    khigh2,
    bseat,
    bhalf1,
    bhalf2,
    aseat,
    ahalf1,
    ahalf2,
    cseat,
    clow1,
    chigh1,
    clow2,
    chigh2,
    n1_ref,
    dqkv_ref,
    small_ref,
    grad_middle_ref,
    bz,
    bnear,
    bfar,
    az,
    anear,
    afar,
    cz,
    cnear,
    cfar,
    r_send,
    r_recv,
    l_send,
    l_recv,
    local,
):
    at = Place()
    at.greet()
    tokens, width = tok_ref.shape
    group = 8
    kv_width = KEY_VALUE_HEADS * HEAD_SIZE
    q_width = QUERY_HEADS * HEAD_SIZE
    qkv = q_width + 2 * kv_width
    per_kv = QUERY_HEADS // KEY_VALUE_HEADS
    chunk = width // 4
    shard = chunk // group
    part = tokens // 2
    red = {}

    def sems(n):
        return (lambda k: r_send.at[n, k]), (lambda k: r_recv.at[n, k])

    own_loads = []
    for k in range(2):
        send, recv = sems(len(red))
        mine = wgt_in.at[:, :, pl.ds(k * part, part)]
        own_loads.append(
            pltpu.make_async_copy(mine.at[:, at.core], w_own.at[k], local.at[12 + k])
        )
        red["w", k] = PlaneReduce(
            at, mine.at[:, 1 - at.core], w_own.at[k], w_seat.at[k], w_half1.at[k, 0],
            w_half1.at[k, 1], w_half2.at[k, 0], w_half2.at[k, 1], width // 2, send, recv,
        )
    for k in range(2):
        send, recv = sems(len(red))
        rows = pl.ds(k * part, part)
        mine = dkv_ref.at[:, :, rows]
        red["k", k] = PlaneReduce(
            at, mine.at[:, 1 - at.core], mine.at[:, at.core], kseat.at[k], klow1.at[k], khigh1.at[k],
            khigh2.at[k], klow2.at[k], kv_width, send, recv,
        )
    for z in range(4):
        send, recv = sems(len(red))
        red["b", z] = PlaneReduce(
            at, wo_ref.at[z, :, 1 - at.core], wo_ref.at[z, :, at.core], bseat.at[z], bhalf1.at[z, 0],
            bhalf1.at[z, 1], bhalf2.at[z, 0], bhalf2.at[z, 1], width // 2, send, recv,
        )
    cols_q, cols_k = pl.ds(0, q_width), pl.ds(q_width, 2 * kv_width + 128)
    for k in range(4):
        send, recv = sems(len(red))
        z = at.order[k]
        red["q", k] = PlaneReduce(
            at, pack_ref.at[z, :, 1 - at.core, :, cols_q], pack_ref.at[z, :, at.core, :, cols_q],
            aseat.at[k], ahalf1.at[k, 0], ahalf1.at[k, 1], ahalf2.at[k, 0], ahalf2.at[k, 1],
            q_width // 2, send, recv,
        )
    for k in range(4):
        send, recv = sems(len(red))
        z = at.order[k]
        red["s", k] = PlaneReduce(
            at, pack_ref.at[z, :, 1 - at.core, :, cols_k], pack_ref.at[z, :, at.core, :, cols_k],
            cseat.at[k], clow1.at[k], chigh1.at[k], chigh2.at[k], clow2.at[k],
            3 * 128, send, recv,
        )
    lines = {}
    for n, (name, blocks, near, far) in enumerate(
        (("b", bz, bnear, bfar), ("q", az, anear, afar), ("s", cz, cnear, cfar))
    ):
        lines[name] = LineReduce(
            at, blocks, near, far, lambda k, n=n: l_send.at[n, k], lambda k, n=n: l_recv.at[n, k]
        )

    loads = {}
    cols_small = pl.ds(qkv, 128)
    cols_main = pl.ds(0, qkv)
    for n, (name, src, dst) in enumerate(
        (
            ("row", row_in, row_ref),
            ("small", pack_in.at[:, :, :, :, cols_small], pack_ref.at[:, :, :, :, cols_small]),
            ("pay", pay_in, pay_ref),
            ("mid", mid_in, mid_ref),
            ("cot", cot_in, cot_ref),
            ("wo", wo_in, wo_ref),
            ("att", att_in, att_ref),
            ("lse", lse_in, lse_ref),
            ("q", q_in, q_ref),
            ("kv", kv_in, kv_ref),
            ("tok", tok_in, tok_ref),
            ("main", pack_in.at[:, :, :, :, cols_main], pack_ref.at[:, :, :, :, cols_main]),
        )
    ):
        loads[name] = pltpu.make_async_copy(src, dst, local.at[n])
    early = ("row", "small", "pay", "mid", "cot")
    for name in early:
        loads[name].start()
    red["w", 0].start()
    loads["wo"].start()
    own_loads[0].start()
    stream, begin, relative = stream_facts(lens_ref, order_ref, tokens, group, at.e)
    for name in early:
        loads[name].wait()
    for name in ("att", "lse", "q", "kv", "tok", "main"):
        loads[name].start()

    def tok_unit():
        tok = tok_ref[...].astype(F32)
        scale = lax.rsqrt(jnp.mean(tok * tok, axis=1, keepdims=True) + EPSILON)
        return tok * scale, scale

    small = pack_ref[..., qkv:].reshape(width, 128)
    gain_one = column_as_row(small, n_experts)
    gain_two = column_as_row(small, n_experts + 1)
    lane = lax.broadcasted_iota(jnp.int32, (tokens, 128), 1)
    ext = pay_ref[:, width:].astype(F32)
    gates = jnp.where(
        lane < n_experts, ext + pltpu.roll(ext, 96, 1) + pltpu.roll(ext, 64, 1), 0.0
    )
    ext = row_ref[:, width:]
    grad_gates = jnp.where(lane < n_experts, ext + pltpu.roll(ext, 96, 1), 0.0)
    weighted_sum = jnp.sum(gates * grad_gates, axis=1, keepdims=True)
    grad_logits = (gates * (grad_gates - weighted_sum)).astype(BF)
    grad_normed = dot_bt(grad_logits, small) + row_ref[:, :width]
    middle = mid_ref[...]
    scale_two = lax.rsqrt(jnp.mean(middle * middle, axis=1, keepdims=True) + EPSILON)
    unit_two = middle * scale_two
    inner_sum = jnp.mean(grad_normed * gain_two * unit_two, axis=1, keepdims=True)
    grad_middle = cot_ref[...].astype(F32) + scale_two * (
        grad_normed * gain_two - unit_two * inner_sum
    )
    products = grad_normed * unit_two
    loads["wo"].wait()
    own_loads[0].wait()
    red["w", 0].on_s()
    red["w", 1].start()
    own_loads[1].start()
    grad_middle_ref[...] = grad_middle
    mixed = grad_middle.astype(BF)
    for z in range(4):
        heads = dot_bt(mixed, wo_ref[z].reshape(chunk, width)).astype(BF)
        for j in range(chunk // HEAD_SIZE):
            do_ref[z * (chunk // HEAD_SIZE) + j] = heads[:, j * HEAD_SIZE : (j + 1) * HEAD_SIZE]
    loads["att"].wait()
    for z in range(4):
        left = att_ref[:, z * chunk : (z + 1) * chunk].astype(BF)
        wo_ref[z] = dot_at(left, mixed).astype(BF).reshape(4, 2, shard, width)
        red["b", z].start()
    lane_small = lax.broadcasted_iota(jnp.int32, (width, 128), 1)
    small_ref[...] = dot_at(pay_ref[:, :width], grad_logits) + jnp.where(
        lane_small == n_experts + 1, column_sums(products), 0.0
    )
    for name in ("lse", "q", "kv"):
        loads[name].wait()
    row_ref[:, :width] = jnp.zeros((tokens, width), F32)
    n_tiles = tokens // TILE
    wide = TILE * group
    for g in range(KEY_VALUE_HEADS):
        for i in range(n_tiles):
            here = slice(i * TILE, (i + 1) * TILE)
            dots = []
            for h in range(per_kv):
                col = (g * per_kv + h) * HEAD_SIZE
                dots.append(
                    jnp.sum(
                        do_ref[g * per_kv + h, here, :].astype(F32)
                        * att_ref[here, col : col + HEAD_SIZE],
                        axis=1,
                        keepdims=True,
                    )
                )
            dots = jnp.concatenate(dots, axis=0)
            lse_ref[g, i, :, 64:] = jnp.broadcast_to(dots, (per_kv * TILE, 64))
    for z in range(4):
        red["b", z].on_s()
    cosine, sine = rotary(relative)
    loads["tok"].wait()
    n1_ref[...] = (tok_unit()[0] * gain_one).astype(BF)

    factor = LOG2E / math.sqrt(HEAD_SIZE)
    score_scale = 1.0 / math.sqrt(HEAD_SIZE)

    def attend_back(r):
        queries_of = [i for i in range(n_tiles) if r in tiles_of(i)]
        biases = {i: tile_bias(i, r, stream, begin, group) for i in queries_of}
        there = slice(r * TILE, (r + 1) * TILE)
        for g in range(KEY_VALUE_HEADS):
            key_cols = slice(g * HEAD_SIZE, (g + 1) * HEAD_SIZE)
            value_cols = slice(kv_width + g * HEAD_SIZE, kv_width + (g + 1) * HEAD_SIZE)
            heads = slice(g * per_kv, (g + 1) * per_kv)
            keys = kv_ref[:, there, key_cols].reshape(wide, HEAD_SIZE)
            values = kv_ref[:, there, value_cols].reshape(wide, HEAD_SIZE)
            grad_keys = None
            grad_values = None
            for i in queries_of:
                here = slice(i * TILE, (i + 1) * TILE)
                queries = q_ref[heads, here, :].reshape(per_kv * TILE, HEAD_SIZE)
                grads = do_ref[heads, here, :].reshape(per_kv * TILE, HEAD_SIZE)
                s = dot_bt(queries, keys) * factor
                s = (s.reshape(per_kv, TILE, wide) + biases[i][None]).reshape(per_kv * TILE, wide)
                p = jnp.exp2(s - lse_ref[g, i, :, :1])
                ds = (p * (dot_bt(grads, values) - lse_ref[g, i, :, 64:65])).astype(BF)
                term_k = dot_at(ds, queries)
                term_v = dot_at(p.astype(BF), grads)
                grad_keys = term_k if grad_keys is None else grad_keys + term_k
                grad_values = term_v if grad_values is None else grad_values + term_v
                grad_queries = dot_nn(ds, keys)
                for h in range(per_kv):
                    col = (g * per_kv + h) * HEAD_SIZE
                    row_ref[here, col : col + HEAD_SIZE] += grad_queries[
                        h * TILE : (h + 1) * TILE
                    ]
            dkv_ref[:, :, there, key_cols] = (
                (grad_keys * score_scale).astype(BF).reshape(4, 2, TILE, HEAD_SIZE)
            )
            dkv_ref[:, :, there, value_cols] = grad_values.astype(BF).reshape(4, 2, TILE, HEAD_SIZE)

    def settle(name, z, blocks, cut):
        low, high = red[name, z].finish()
        blocks[z, :, :cut] = low.astype(BF)
        blocks[z, :, cut:] = high.astype(BF)

    red["w", 0].on_xy()
    attend_back(0)
    for z in range(4):
        red["b", z].on_xy()
    attend_back(1)
    red["k", 0].start()
    attend_back(2)
    red["k", 0].on_s()
    for z in range(4):
        settle("b", z, bz, width // 2)
    lines["b"].start()
    own_loads[1].wait()
    red["w", 1].on_s()
    attend_back(3)
    red["k", 1].start()
    red["k", 0].on_xy()

    def output_part(k):
        rows = slice(k * part, (k + 1) * part)
        low, high = red["w", k].finish()
        output_ref[rows, : width // 2] = (mid_ref[rows, : width // 2] + low).astype(BF)
        output_ref[rows, width // 2 :] = (mid_ref[rows, width // 2 :] + high).astype(BF)

    def turned_back(v):
        return (v * cosine - swap_halves(v) * sine).astype(BF)

    for h in range(QUERY_HEADS):
        cols = slice(h * HEAD_SIZE, (h + 1) * HEAD_SIZE)
        dqkv_ref[:, cols] = turned_back(row_ref[:, cols] * score_scale)
    red["k", 1].on_s()
    loads["main"].wait()
    grad_q = dqkv_ref[:, :q_width]
    far_first = (3, 2, 1, 0)

    def span(k):
        return pl.ds(pl.multiple_of(at.order[k] * chunk, 128), chunk)

    for k in far_first:
        z = at.order[k]
        att_ref[:, span(k)] = dot_bt(
            grad_q, pack_ref[z, :, :, :, :q_width].reshape(chunk, q_width)
        )
        pack_ref[z, :, :, :, :q_width] = (
            dot_at(n1_ref[:, span(k)], grad_q).astype(BF).reshape(4, 2, shard, q_width)
        )
        red["q", k].start()
        if k == 3:
            red["k", 1].on_xy()
    for k in range(2):
        rows = slice(k * part, (k + 1) * part)
        low, high = red["k", k].finish()
        row_ref[rows, :kv_width] = low
        row_ref[rows, kv_width : 2 * kv_width] = high
    lines["b"].middle()
    red["w", 1].on_xy()
    for k in far_first:
        red["q", k].on_s()
    for h in range(KEY_VALUE_HEADS):
        v = row_ref[:, h * HEAD_SIZE : (h + 1) * HEAD_SIZE]
        dqkv_ref[:, q_width + h * HEAD_SIZE : q_width + (h + 1) * HEAD_SIZE] = turned_back(v)
    dqkv_ref[:, q_width + kv_width :] = row_ref[:, kv_width : 2 * kv_width].astype(BF)
    grad_kv = dqkv_ref[:, q_width:]
    for z in range(4):
        cols = slice(z * chunk, (z + 1) * chunk)
        att_ref[:, cols] += dot_bt(
            grad_kv, pack_ref[z, :, :, :, q_width:qkv].reshape(chunk, 2 * kv_width)
        )
        pack_ref[z, :, :, :, q_width:qkv] = (
            dot_at(n1_ref[:, cols], grad_kv).astype(BF).reshape(4, 2, shard, 2 * kv_width)
        )
    unit_one, scale_one = tok_unit()
    grad_one = att_ref[...]
    small_ref[...] += jnp.where(lane_small == n_experts, column_sums(grad_one * unit_one), 0.0)
    pack_ref[..., qkv:] = small_ref[...].astype(BF).reshape(4, 4, 2, shard, 128)
    for k in far_first:
        red["s", k].start()
    lines["b"].last()
    for k in far_first:
        red["q", k].on_xy()
    for k in far_first:
        red["s", k].on_s()
    inner_sum = jnp.mean(grad_one * gain_one * unit_one, axis=1, keepdims=True)
    back_one = scale_one * (grad_one * gain_one - unit_one * inner_sum)
    tokens_grad_ref[...] = (grad_middle_ref[...] + back_one).astype(BF)

    def settle_in_order(name, blocks, cut):
        def one(k):
            low, high = red[name, k].finish()
            blocks[at.order[k], :, :cut] = low.astype(BF)
            blocks[at.order[k], :, cut:] = high.astype(BF)

        one(3)
        lines[name].leave(3)
        one(2)
        lines[name].leave(2)
        lines[name].hand(3)
        one(1)
        lines[name].leave(1)
        lines[name].hand(2)
        one(0)

    settle_in_order("q", az, q_width // 2)
    for k in far_first:
        red["s", k].on_xy()
    settle_in_order("s", cz, 3 * 128)
    output_part(0)
    lines["q"].hand(1)
    lines["s"].hand(1)
    lines["b"].finish(b_out)
    output_part(1)
    lines["q"].finish(aq_out)
    lines["s"].finish(ak_out)
    for item in red.values():
        item.drain()


def back(
    lengths, seq_order, row, weighted, tokens, q_rot, att, lse, middle, cot, kv, pay, pack, wo, n_experts
):
    count, width = tokens.shape
    group = 8
    shard = width // 32
    kv_width = KEY_VALUE_HEADS * HEAD_SIZE
    part = count // 2
    wide_r = width + 128
    wide_s, cut_s = 2 * kv_width + 128, 3 * 128
    half = width // 2
    sds = jax.ShapeDtypeStruct
    smem = pl.BlockSpec(memory_space=pltpu.SMEM)
    vmem = pl.BlockSpec(memory_space=pltpu.VMEM)
    hbm = pl.BlockSpec(memory_space=ANY)
    pack = pack.reshape(4, 4, 2, shard, pack.shape[1])
    wo = wo.reshape(4, 4, 2, shard, width)

    def low(*shape):
        return pltpu.VMEM(shape, BF)

    def like(a):
        return pltpu.VMEM(a.shape, a.dtype)

    return pl.pallas_call(
        functools.partial(back_kernel, n_experts),
        in_specs=[smem, smem] + [hbm] * 12,
        out_specs=(vmem,) * 5,
        out_shape=(
            sds((count, width), BF),
            sds((count, width), BF),
            sds((shard, width), F32),
            sds((shard, wide_s), F32),
            sds((shard, width), F32),
        ),
        scratch_shapes=[
            low(2, 4, part, width),
            low(2, 4, part, width),
            low(2, 2, 2, part, half),
            low(2, 2, part, half),
            pltpu.VMEM((count, wide_r), F32),
            like(tokens),
            like(q_rot),
            like(att),
            like(lse),
            like(middle),
            like(cot),
            like(kv),
            like(pay),
            like(pack),
            like(wo),
            like(q_rot),
            low(4, 2, count, 2 * kv_width),
            low(2, 4, part, 2 * kv_width),
            low(2, 2, part, kv_width),
            low(2, 2, part, kv_width),
            low(2, part, kv_width),
            low(2, part, kv_width),
            low(4, 4, shard, width),
            low(4, 2, 2, shard, half),
            low(4, 2, shard, half),
            low(4, 4, shard, width),
            low(4, 2, 2, shard, half),
            low(4, 2, shard, half),
            low(4, 4, shard, wide_s),
            low(4, 2, shard, cut_s),
            low(4, 2, shard, wide_s - cut_s),
            low(4, shard, cut_s),
            low(4, shard, wide_s - cut_s),
            low(count, width),
            low(count, width + 2 * kv_width),
            pltpu.VMEM((width, 128), F32),
            pltpu.VMEM((count, width), F32),
            low(4, shard, width),
            low(3, shard, width),
            low(2, shard, width),
            low(4, shard, width),
            low(3, shard, width),
            low(2, shard, width),
            low(4, shard, wide_s),
            low(3, shard, wide_s),
            low(2, shard, wide_s),
            pltpu.SemaphoreType.DMA((N_BACK, 7)),
            pltpu.SemaphoreType.DMA((N_BACK, 7)),
            pltpu.SemaphoreType.DMA((3, 5)),
            pltpu.SemaphoreType.DMA((3, 5)),
            pltpu.SemaphoreType.DMA((14,)),
        ],
        compiler_params=pltpu.CompilerParams(
            collective_id=2, has_side_effects=True, vmem_limit_bytes=63 * 2**20
        ),
        cost_estimate=pl.CostEstimate(
            flops=15 * 10**10, bytes_accessed=5 * 10**7, transcendentals=10**7
        ),
    )(lengths, seq_order, row, weighted, tokens, q_rot, att, lse, middle, cot, kv, pay, pack, wo)


def last_kernel(
    n_experts, mine_hbm, out_hbm, grad_hbm, q_hbm, s_hbm, b_hbm,
    gate_ref, up_ref, down_ref, out_ref, grad_ref, q_ref, k_ref, v_ref, b_ref, router_ref, one_ref,
    two_ref, mine_ref, s_in, sems,
):
    pairs = (
        (mine_hbm, mine_ref), (s_hbm, s_in), (out_hbm, out_ref), (grad_hbm, grad_ref),
        (q_hbm, q_ref), (b_hbm, b_ref),
    )
    loads = [pltpu.make_async_copy(a, b, sems.at[n]) for n, (a, b) in enumerate(pairs)]
    for load in loads:
        load.start()
    loads[0].wait()
    loads[1].wait()
    depth = gate_ref.shape[0]
    tall, wide = down_ref.shape
    kv_width = k_ref.shape[1]
    k_ref[...] = s_in[:, :kv_width]
    v_ref[...] = s_in[:, kv_width : 2 * kv_width]
    small = s_in[:, 2 * kv_width :]
    high = small.astype(BF)
    rest = small - high.astype(F32)
    mid = rest.astype(BF)
    low = (rest - mid.astype(F32)).astype(BF)
    row = lax.broadcasted_iota(jnp.int32, (16, 128), 0)
    pick = (row == lax.broadcasted_iota(jnp.int32, (16, 128), 1)).astype(F32).astype(BF)
    turned = dot_bt(pick, high) + dot_bt(pick, mid) + dot_bt(pick, low)
    router_ref[...] = turned[:n_experts]
    one_ref[...] = turned[n_experts : n_experts + 1]
    two_ref[...] = turned[n_experts + 1 : n_experts + 2]
    gate_ref[...] = mine_ref[:depth].astype(F32)
    up_ref[...] = mine_ref[depth : 2 * depth].astype(F32)
    down_ref[:, : wide // 2] = mine_ref[2 * depth : 2 * depth + tall].astype(F32)
    down_ref[:, wide // 2 :] = mine_ref[2 * depth + tall :].astype(F32)
    for load in loads[2:]:
        load.wait()


def last(mine, output, tokens_grad, query_mine, rest_mine, out_mine, n_experts):
    shard, wide_s = rest_mine.shape
    kv_width = KEY_VALUE_HEADS * HEAD_SIZE
    hid = mine.shape[1]
    tall = mine.shape[0] // 6
    sds = jax.ShapeDtypeStruct
    vmem = pl.BlockSpec(memory_space=pltpu.VMEM)
    return pl.pallas_call(
        functools.partial(last_kernel, n_experts),
        in_specs=[pl.BlockSpec(memory_space=ANY)] * 6,
        out_specs=(vmem,) * 12,
        out_shape=(
            sds((2 * tall, hid), F32),
            sds((2 * tall, hid), F32),
            sds((tall, 2 * hid), F32),
            sds(output.shape, output.dtype),
            sds(tokens_grad.shape, tokens_grad.dtype),
            sds(query_mine.shape, F32),
            sds((shard, kv_width), F32),
            sds((shard, kv_width), F32),
            sds(out_mine.shape, F32),
            sds((n_experts, shard), F32),
            sds((1, shard), F32),
            sds((1, shard), F32),
        ),
        scratch_shapes=[
            pltpu.VMEM(mine.shape, BF),
            pltpu.VMEM(rest_mine.shape, F32),
            pltpu.SemaphoreType.DMA((6,)),
        ],
        compiler_params=pltpu.CompilerParams(vmem_limit_bytes=60 * 2**20),
    )(mine, output, tokens_grad, query_mine, rest_mine, out_mine)


def on_device_fast(
    tokens,
    lengths,
    seq_order,
    routes,
    norm_attn,
    w_query,
    key_projection,
    value_projection,
    w_out,
    norm_moe,
    w_router,
    w_gate,
    w_up,
    w_down,
    cotangent,
):
    token_count, width = tokens.shape
    n_experts = w_router.shape[1]
    group_tokens = token_count * lax.axis_size("expert")
    pack = pack_weights(w_router, norm_attn, norm_moe, w_query, key_projection, value_projection)
    x_all, gw, uw, pack, wo, kv_all, q_rot, attended, lse, middle, pay = front(
        lengths, seq_order, tokens, routes, pack, w_out, w_gate[0], w_up[0], n_experts
    )
    x_all = x_all.reshape(group_tokens, width + 128)
    c_all, dw, hidden, slope, expert_grads = expert_up(x_all, cotangent, gw, uw, w_down[0])
    grad_row, weighted = expert_down(x_all, c_all, hidden, slope, gw, uw, dw)
    expert_mine = lax.psum_scatter(
        expert_grads.reshape(-1, expert_grads.shape[2]), "dp", scatter_dimension=0, tiled=True
    )
    output, tokens_grad, query_mine, mine, out_mine = back(
        lengths,
        seq_order,
        grad_row,
        weighted,
        tokens,
        q_rot,
        attended,
        lse,
        middle,
        cotangent,
        kv_all,
        pay,
        pack,
        wo,
        n_experts,
    )
    gate, up, down, output, tokens_grad, query, key, value, out, router, one, two = last(
        expert_mine, output, tokens_grad, query_mine, mine, out_mine, n_experts
    )
    return (
        output,
        tokens_grad,
        one.reshape(-1),
        query,
        key,
        value,
        out,
        two.reshape(-1),
        router.T,
        gate[None],
        up[None],
        down[None],
    )


def solution(mesh):
    both = ("dp", "expert")
    small = mesh.shape["dp"] == 4 and mesh.shape["expert"] == 8
    return jax.shard_map(
        on_device_fast if small else on_device,
        mesh=mesh,
        in_specs=(
            P(both, None),
            P("dp", None),
            P("dp", None),
            P(both, None),
            P(both),
            P(both, None),
            P(both, None),
            P(both, None),
            P(both, None),
            P(both),
            P(both, None),
            P("expert", "dp", None),
            P("expert", "dp", None),
            P("expert", "dp", None),
            P(both, None),
        ),
        out_specs=(
            P(both, None),
            P(both, None),
            P(both),
            P(both, None),
            P(both, None),
            P(both, None),
            P(both, None),
            P(both),
            P(both, None),
            P("expert", "dp", None),
            P("expert", "dp", None),
            P("expert", "dp", None),
        ),
        check_vma=False,
    )
```

```python
import functools
import math

import jax
import jax.numpy as jnp
from jax import lax
from jax.experimental import pallas as pl
from jax.experimental.pallas import tpu as pltpu
from jax.sharding import PartitionSpec as P

QUERY_HEADS = 12
KEY_VALUE_HEADS = 2
HEAD_SIZE = 128


EPSILON = 1e-06
ROPE_BASE = 10000.0
MASKED_SCORE = -1e30
BF = jnp.bfloat16
F32 = jnp.float32


def rms_scale(values):
    return lax.rsqrt(jnp.mean(values * values, axis=-1, keepdims=True) + EPSILON)


def rope_tables(positions, half_size):
    angle_steps = lax.broadcasted_iota(F32, (half_size,), 0)
    frequency = jnp.exp(angle_steps * (-math.log(ROPE_BASE) / half_size))
    angles = positions.astype(F32)[:, None] * frequency
    return (jnp.cos(angles)[:, None, :], jnp.sin(angles)[:, None, :])


def apply_rotation(values, cosine_table, sine_table):
    half_size = values.shape[-1] // 2
    first = values[..., :half_size]
    second = values[..., half_size:]
    return jnp.concatenate(
        [first * cosine_table - second * sine_table, second * cosine_table + first * sine_table],
        axis=-1,
    )


def reverse_rotation(grads_in, cosine_table, sine_table):
    return apply_rotation(grads_in, cosine_table, -sine_table)


def seq_layout(lengths, seq_order):
    count_seq = lengths.shape[1]
    picked = seq_order[0][:, None] == lax.broadcasted_iota(jnp.int32, (count_seq, count_seq), 1)
    ordered = jnp.sum(jnp.where(picked, lengths[0][None, :], 0), axis=1)
    return (ordered, jnp.cumsum(ordered))


def seq_place(positions, ordered, seq_ends):
    passed = seq_ends[None, :] <= positions[:, None]
    sequence_index = jnp.sum(passed.astype(jnp.int32), axis=1)
    starts = jnp.sum(jnp.where(passed, ordered[None, :], 0), axis=1)
    return (sequence_index, positions - starts)


def block_scores(
    query_rows, key_portion, query_seq, query_stream, key_seq, key_stream, score_scale
):
    raw_scores = (
        jnp.einsum("tkrd,skd->krts", query_rows, key_portion, preferred_element_type=F32)
        * score_scale
    )
    allowed = (query_seq[:, None] == key_seq[None, :]) & (
        key_stream[None, :] <= query_stream[:, None]
    )
    return jnp.where(allowed, raw_scores, MASKED_SCORE)


def norm_backward(grad_normed, unit_values, inv_scale, gain_float):
    scaled = grad_normed * gain_float
    gain_grad = jnp.sum(grad_normed * unit_values, axis=0)
    input_grad = inv_scale * (
        scaled - unit_values * jnp.mean(scaled * unit_values, axis=-1, keepdims=True)
    )
    return (gain_grad, input_grad)


def dot(a, b):
    return jnp.dot(a, b, preferred_element_type=F32)


def dot_nt(a, b):
    return jnp.einsum("ac,bc->ab", a, b, preferred_element_type=F32)


def dot_tn(a, b):
    return jnp.einsum("ta,tb->ab", a, b, preferred_element_type=F32)


def on_device(
    tokens,
    lengths,
    seq_order,
    routes,
    norm_attn,
    w_query,
    key_projection,
    value_projection,
    w_out,
    norm_moe,
    w_router,
    w_gate,
    w_up,
    w_down,
    cotangent,
):
    token_count, width = tokens.shape
    n_experts = w_router.shape[1]
    rows = w_query.shape[0]
    group_size = lax.axis_size("expert")
    my_index = lax.axis_index("expert")
    query_per_key_heads = QUERY_HEADS // KEY_VALUE_HEADS
    kv_width = KEY_VALUE_HEADS * HEAD_SIZE
    q_width = QUERY_HEADS * HEAD_SIZE
    score_scale = 1.0 / math.sqrt(HEAD_SIZE)
    group_tokens = token_count * group_size

    small = jnp.concatenate(
        [
            w_router,
            norm_attn[:, None],
            norm_moe[:, None],
            jnp.zeros((rows, 128 - n_experts - 2), BF),
        ],
        axis=1,
    )
    pack = jnp.concatenate([w_query, key_projection, value_projection, small, w_out], axis=1)
    gate_w = lax.all_gather(w_gate[0], "dp", axis=0, tiled=True)
    up_w = lax.all_gather(w_up[0], "dp", axis=0, tiled=True)
    down_w = lax.all_gather(w_down[0], "dp", axis=0, tiled=True)
    pack = lax.all_gather(pack, ("dp", "expert"), axis=0, tiled=True)
    cot_all = lax.all_gather(cotangent, "expert", axis=0, tiled=True)
    c_k = q_width
    c_v = c_k + kv_width
    c_s = c_v + kv_width
    c_o = c_s + 128
    query_w = pack[:, :c_k]
    key_w = pack[:, c_k:c_v]
    value_w = pack[:, c_v:c_s]
    router_w = pack[:, c_s : c_s + n_experts]
    gain_one = pack[:, c_s + n_experts].astype(F32)
    gain_two = pack[:, c_s + n_experts + 1].astype(F32)
    out_w = pack[:, c_o:]

    seq_lens, seq_ends = seq_layout(lengths, seq_order)
    my_stream = lax.broadcasted_iota(jnp.int32, (token_count,), 0) * group_size + my_index
    query_seq, query_rel = seq_place(my_stream, seq_lens, seq_ends)
    all_rows = lax.broadcasted_iota(jnp.int32, (group_tokens,), 0)
    key_stream = all_rows % token_count * group_size + all_rows // token_count
    key_seq = seq_place(key_stream, seq_lens, seq_ends)[0]
    block_row_count = math.gcd(group_tokens, 512)
    block_count = group_tokens // block_row_count
    cosine_table, sine_table = rope_tables(query_rel, HEAD_SIZE // 2)
    inputs_float = tokens.astype(F32)
    inv_one = rms_scale(inputs_float)
    unit_one = inputs_float * inv_one
    normed_one = (unit_one * gain_one).astype(BF)
    query_pre = dot(normed_one, query_w)
    key_pre = dot(normed_one, key_w)
    value_pre = dot(normed_one, value_w)
    rotated_queries = (
        apply_rotation(
            query_pre.reshape(token_count, QUERY_HEADS, HEAD_SIZE), cosine_table, sine_table
        )
        .astype(BF)
        .reshape(token_count, KEY_VALUE_HEADS, query_per_key_heads, HEAD_SIZE)
    )
    rotated_keys = apply_rotation(
        key_pre.reshape(token_count, KEY_VALUE_HEADS, HEAD_SIZE),
        cosine_table,
        sine_table,
    ).astype(BF)
    key_value = jnp.concatenate(
        [rotated_keys.reshape(token_count, kv_width), value_pre.astype(BF)],
        axis=1,
    )
    gathered = lax.all_gather(key_value, "expert", axis=0, tiled=True)
    key_blocks = (
        gathered.reshape(block_count, block_row_count, 2 * kv_width),
        key_seq.reshape(block_count, block_row_count),
        key_stream.reshape(block_count, block_row_count),
    )

    def stats_step(carry, blocks):
        run_max, run_sum = carry
        key_value_block, seq_block, stream_block = blocks
        key_portion = key_value_block[:, :kv_width].reshape(-1, KEY_VALUE_HEADS, HEAD_SIZE)
        scores = block_scores(
            rotated_queries, key_portion, query_seq, my_stream, seq_block, stream_block, score_scale
        )
        new_max = jnp.maximum(run_max, jnp.max(scores, axis=-1))
        run_sum = run_sum * jnp.exp(run_max - new_max) + jnp.sum(
            jnp.exp(scores - new_max[..., None]), axis=-1
        )
        return ((new_max, run_sum), None)

    initial_maximum = jnp.full(
        (KEY_VALUE_HEADS, query_per_key_heads, token_count), MASKED_SCORE, F32
    )
    (row_max, row_sum), unused = lax.scan(
        stats_step, (initial_maximum, jnp.zeros_like(initial_maximum)), key_blocks
    )
    log_total = row_max + jnp.log(row_sum)

    def value_step(summed, blocks):
        key_value_block, seq_block, stream_block = blocks
        key_portion = key_value_block[:, :kv_width].reshape(-1, KEY_VALUE_HEADS, HEAD_SIZE)
        value_portion = key_value_block[:, kv_width:].reshape(-1, KEY_VALUE_HEADS, HEAD_SIZE)
        scores = block_scores(
            rotated_queries, key_portion, query_seq, my_stream, seq_block, stream_block, score_scale
        )
        low_chances = jnp.exp(scores - log_total[..., None]).astype(BF)
        summed = summed + jnp.einsum(
            "krts,skd->tkrd", low_chances, value_portion, preferred_element_type=F32
        )
        return (summed, None)

    empty_head_state = jnp.zeros(
        (token_count, KEY_VALUE_HEADS, query_per_key_heads, HEAD_SIZE), F32
    )
    attended, unused = lax.scan(value_step, empty_head_state, key_blocks)
    attended_low = attended.reshape(token_count, q_width).astype(BF)
    middle = inputs_float + dot(attended_low, out_w)
    inv_two = rms_scale(middle)
    unit_two = middle * inv_two
    normed_two = (unit_two * gain_two).astype(BF)

    logits = dot(normed_two, router_w)
    choose = jnp.any(
        routes[:, :, None] == lax.broadcasted_iota(jnp.int32, (1, 1, n_experts), 2), axis=1
    )
    top_logit = jnp.max(jnp.where(choose, logits, -jnp.inf), axis=1, keepdims=True)
    spread = jnp.where(choose, jnp.exp(jnp.minimum(logits - top_logit, 0.0)), 0.0)
    gates = spread / jnp.sum(spread, axis=1, keepdims=True)

    normed_all = lax.all_gather(normed_two, "expert", axis=0, tiled=True)
    gates_all = lax.all_to_all(
        gates.T.reshape(n_experts, 1, token_count), "expert", split_axis=0, concat_axis=1, tiled=True
    )
    gate_col = gates_all.reshape(group_tokens, 1)

    gate_pre = dot(normed_all, gate_w)
    up_pre = dot(normed_all, up_w)
    sig = jax.nn.sigmoid(gate_pre)
    silu = gate_pre * sig
    hidden = (silu * up_pre).astype(BF)
    returned = dot(hidden, down_w).astype(BF).astype(F32)
    cot_float = cot_all.astype(F32)
    grad_gates = jnp.sum(cot_float * returned, axis=1)
    weighted = (gate_col * returned).astype(BF)
    grad_returned = (gate_col * cot_float).astype(BF)
    grad_hidden = dot_nt(grad_returned, down_w)
    grad_gate_pre = (grad_hidden * up_pre * sig * (1.0 + gate_pre * (1.0 - sig))).astype(BF)
    grad_up_pre = (grad_hidden * silu).astype(BF)
    grad_row = (dot_nt(grad_gate_pre, gate_w) + dot_nt(grad_up_pre, up_w)).astype(BF)
    down_grad = dot_tn(hidden, grad_returned).astype(BF)
    gate_grad = dot_tn(normed_all, grad_gate_pre).astype(BF)
    up_grad = dot_tn(normed_all, grad_up_pre).astype(BF)

    grad_gates = lax.all_to_all(
        grad_gates.reshape(group_size, 1, token_count), "expert", split_axis=0, concat_axis=1, tiled=True
    ).reshape(n_experts, token_count).T
    row_sum_grad = lax.psum_scatter(grad_row, "expert", scatter_dimension=0, tiled=True)
    output = (
        middle + lax.psum_scatter(weighted, "expert", scatter_dimension=0, tiled=True).astype(F32)
    ).astype(BF)

    grad_out = cotangent.astype(F32)
    grad_logits = (
        gates * (grad_gates - jnp.sum(gates * grad_gates, axis=1, keepdims=True))
    ).astype(BF)
    router_grad = dot_tn(normed_two, grad_logits)
    grad_normed_two = dot_nt(grad_logits, router_w) + row_sum_grad.astype(F32)
    gain_two_grad, grad_middle = norm_backward(grad_normed_two, unit_two, inv_two, gain_two)
    grad_middle = grad_out + grad_middle
    grad_mixed = grad_middle.astype(BF)
    out_grad = dot_tn(attended_low, grad_mixed)
    grad_attended = dot_nt(grad_mixed, out_w).astype(BF)
    head_gradient = grad_attended.reshape(
        token_count, KEY_VALUE_HEADS, query_per_key_heads, HEAD_SIZE
    )
    row_dot = jnp.transpose(jnp.sum(head_gradient.astype(F32) * attended, axis=-1), (1, 2, 0))

    def grad_step(query_grad, blocks):
        key_value_block, seq_block, stream_block = blocks
        key_portion = key_value_block[:, :kv_width].reshape(-1, KEY_VALUE_HEADS, HEAD_SIZE)
        value_portion = key_value_block[:, kv_width:].reshape(-1, KEY_VALUE_HEADS, HEAD_SIZE)
        scores = block_scores(
            rotated_queries, key_portion, query_seq, my_stream, seq_block, stream_block, score_scale
        )
        chances = jnp.exp(scores - log_total[..., None])
        low_chances = chances.astype(BF)
        grad_chances = jnp.einsum(
            "tkrd,skd->krts", head_gradient, value_portion, preferred_element_type=F32
        )
        grad_scores = (chances * (grad_chances - row_dot[..., None])).astype(BF)
        query_grad = query_grad + jnp.einsum(
            "krts,skd->tkrd", grad_scores, key_portion, preferred_element_type=F32
        )
        key_terms = (
            jnp.einsum("krts,tkrd->skd", grad_scores, rotated_queries, preferred_element_type=F32)
            * score_scale
        )
        value_terms = jnp.einsum(
            "krts,tkrd->skd", low_chances, head_gradient, preferred_element_type=F32
        )
        return (query_grad, (key_terms.astype(BF), value_terms.astype(BF)))

    query_grad, (key_terms, value_terms) = lax.scan(grad_step, empty_head_state, key_blocks)
    query_grad = query_grad * score_scale
    kv_terms = jnp.concatenate(
        [key_terms.reshape(group_tokens, kv_width), value_terms.reshape(group_tokens, kv_width)],
        axis=1,
    )
    kv_mine = lax.psum_scatter(kv_terms, "expert", scatter_dimension=0, tiled=True)
    grad_query_pre = (
        reverse_rotation(
            query_grad.reshape(token_count, QUERY_HEADS, HEAD_SIZE), cosine_table, sine_table
        )
        .reshape(token_count, q_width)
        .astype(BF)
    )
    grad_key_pre = (
        reverse_rotation(
            kv_mine[:, :kv_width].astype(F32).reshape(token_count, KEY_VALUE_HEADS, HEAD_SIZE),
            cosine_table,
            sine_table,
        )
        .reshape(token_count, kv_width)
        .astype(BF)
    )
    grad_qkv = jnp.concatenate([grad_query_pre, grad_key_pre, kv_mine[:, kv_width:]], axis=1)
    grad_normed_one = dot_nt(grad_qkv, pack[:, :c_s])
    qkv_grad = dot_tn(normed_one, grad_qkv)
    gain_one_grad, grad_input = norm_backward(grad_normed_one, unit_one, inv_one, gain_one)
    tokens_grad = (grad_middle + grad_input).astype(BF)
    small_grad = jnp.concatenate(
        [
            router_grad,
            gain_one_grad[:, None],
            gain_two_grad[:, None],
            jnp.zeros((width, 128 - n_experts - 2), F32),
        ],
        axis=1,
    )
    pack_grad = jnp.concatenate(
        [qkv_grad.astype(BF), small_grad.astype(BF), out_grad.astype(BF)], axis=1
    )
    mine = lax.psum_scatter(pack_grad, ("dp", "expert"), scatter_dimension=0, tiled=True)
    mine = mine.astype(F32)
    gate_mine, up_mine, down_mine = (
        lax.psum_scatter(grad, "dp", scatter_dimension=0, tiled=True).astype(F32)[None]
        for grad in (gate_grad, up_grad, down_grad)
    )
    return (
        output,
        tokens_grad,
        mine[:, c_s + n_experts],
        mine[:, :c_k],
        mine[:, c_k:c_v],
        mine[:, c_v:c_s],
        mine[:, c_o:],
        mine[:, c_s + n_experts + 1],
        mine[:, c_s : c_s + n_experts],
        gate_mine,
        up_mine,
        down_mine,
    )


MESH_ID = pl.DeviceIdType.MESH
ANY = pl.ANY
LOG2E = math.log2(math.e)


class Place:
    def __init__(self):
        d = lax.axis_index("dp")
        e = lax.axis_index("expert")
        core = lax.rem(e, 2)
        x = lax.rem(lax.div(e, 2), 2)
        y = lax.div(e, 4)
        self.d, self.e, self.core = d, e, core
        self.chip = lax.div(e, 2)
        self.e_s = e + 1 - 2 * core
        self.e_x = e + 2 - 4 * x
        self.e_y = e + 4 - 8 * y
        self.e_d = self.e_x + 4 - 8 * y
        self.chip_x = self.chip + 1 - 2 * x
        self.chip_y = self.chip + 2 - 4 * y
        self.chip_d = self.chip_x + 2 - 4 * y
        self.sib = (d, self.e_s)
        self.nx = (d, self.e_x)
        self.ny = (d, self.e_y)
        half = lax.div(d, 2)
        odd = lax.rem(d, 2)
        self.pair = (2 * half + 1 - odd, e)
        self.cross = (3 - d, e)
        self.inner = (d == 1) | (d == 2)
        self.order = (d, 2 * half + 1 - odd, 2 - half, 3 - 3 * half)

    def greet(self):
        barrier = pltpu.get_barrier_semaphore()
        for other in (self.sib, self.nx, self.ny, self.pair):
            pl.semaphore_signal(barrier, inc=1, device_id=other, device_id_type=MESH_ID)

        @pl.when(self.inner)
        def _():
            pl.semaphore_signal(barrier, inc=1, device_id=self.cross, device_id_type=MESH_ID)
            pl.semaphore_wait(barrier, 5)

        @pl.when(jnp.logical_not(self.inner))
        def _():
            pl.semaphore_wait(barrier, 4)


def rcopy(src, dst, send_sem, recv_sem, device):
    return pltpu.make_async_remote_copy(
        src_ref=src,
        dst_ref=dst,
        send_sem=send_sem,
        recv_sem=recv_sem,
        device_id=device,
        device_id_type=MESH_ID,
    )


class PlaneGather:
    def __init__(self, at, blk, half, send, recv):
        self.at, self.blk, self.half, self.send, self.recv = at, blk, half, send, recv

    def push(self, ref, target, slot_send, slot_recv, src=None):
        rcopy(
            ref if src is None else src, ref, self.send(slot_send), self.recv(slot_recv), target
        ).start()

    def await_(self, ref, slot):
        rcopy(ref, ref, self.send(0), self.recv(slot), self.at.sib).wait_recv()

    def sent(self, ref, slot):
        rcopy(ref, ref, self.send(slot), self.recv(0), self.at.sib).wait_send()

    def start(self, src=None):
        at = self.at
        own = self.blk(at.e)
        self.push(own, at.nx, 0, 0, src)
        self.push(own, at.ny, 1, 1, src)
        self.push(own, at.sib, 2, 4, src)

    def on_x(self):
        at = self.at
        got = self.blk(at.e_x)
        self.await_(got, 0)
        self.push(self.half(at.e_x, 0), at.ny, 3, 3)
        self.push(got, at.sib, 4, 5)

    def on_y(self):
        at = self.at
        got = self.blk(at.e_y)
        self.await_(got, 1)
        self.push(self.half(at.e_y, 1), at.nx, 5, 2)
        self.push(got, at.sib, 6, 6)

    def on_d(self):
        at = self.at
        self.await_(self.half(at.e_d, 1), 2)
        self.await_(self.half(at.e_d, 0), 3)
        self.push(self.blk(at.e_d), at.sib, 7, 7)

    def on_s(self):
        at = self.at
        turn = at.e_s - at.e
        self.await_(self.blk(at.e_s), 4)
        self.await_(self.blk(at.e_x + turn), 5)
        self.await_(self.blk(at.e_y + turn), 6)
        self.await_(self.blk(at.e_d + turn), 7)

    def drain(self):
        at = self.at
        whole = self.blk(at.e)
        for slot in (0, 1, 2, 4, 6, 7):
            self.sent(whole, slot)
        self.sent(self.half(at.e, 0), 3)
        self.sent(self.half(at.e, 1), 5)


class LineGather:
    def __init__(self, at, blk, send, recv):
        self.at, self.blk, self.send, self.recv = at, blk, send, recv

    def start(self, src=None):
        at = self.at
        own = self.blk(at.d)
        from_ = own if src is None else src
        rcopy(from_, own, self.send(0), self.recv(1), at.pair).start()

        @pl.when(at.inner)
        def _():
            rcopy(from_, own, self.send(1), self.recv(2), at.cross).start()

    def on(self, k):
        at = self.at
        got = self.blk(at.order[k])
        rcopy(got, got, self.send(0), self.recv(k), at.pair).wait_recv()

        @pl.when(at.inner)
        def _():
            if k == 1:
                rcopy(got, got, self.send(2), self.recv(3), at.cross).start()
            else:
                rcopy(got, got, self.send(k + 1), self.recv(k), at.pair).start()

    def relay(self, k):
        @pl.when(self.at.inner)
        def _():
            self.on(k)

    def land(self):
        at = self.at

        @pl.when(jnp.logical_not(at.inner))
        def _():
            for k in (1, 2, 3):
                got = self.blk(at.order[k])
                rcopy(got, got, self.send(0), self.recv(k), at.pair).wait_recv()

    def drain(self):
        at = self.at
        own = self.blk(at.d)
        rcopy(own, own, self.send(0), self.recv(0), at.pair).wait_send()

        @pl.when(at.inner)
        def _():
            for slot in (1, 2, 3, 4):
                rcopy(own, own, self.send(slot), self.recv(0), at.pair).wait_send()


def rows_of(ref, start, size):
    return ref.at[pl.ds(pl.multiple_of(start, 16), size)]


def stream_facts(lens_ref, order_ref, token_count, group_size, e):
    count = lens_ref.shape[1]
    stream = lax.broadcasted_iota(jnp.int32, (token_count, 128), 0) * group_size + e
    begin = jnp.zeros_like(stream)
    end = jnp.int32(0)
    for j in range(count):
        size = jnp.int32(0)
        for i in range(count):
            size = size + jnp.where(order_ref[0, j] == i, lens_ref[0, i], 0)
        end = end + size
        begin = begin + jnp.where(stream >= end, size, 0)
    return stream, begin, stream - begin


def rotary(relative):
    lane = lax.rem(lax.broadcasted_iota(jnp.int32, relative.shape, 1), HEAD_SIZE // 2)
    frequency = jnp.exp(lane.astype(F32) * (-math.log(ROPE_BASE) / (HEAD_SIZE // 2)))
    angles = relative.astype(F32) * frequency
    first = lax.broadcasted_iota(jnp.int32, relative.shape, 1) < HEAD_SIZE // 2
    sine = jnp.sin(angles)
    return jnp.cos(angles), jnp.where(first, -sine, sine)


def swap_halves(values):
    return pltpu.roll(values, HEAD_SIZE // 2, 1)


TILE = 64


def tiles_of(i):
    return range(max(0, i - 2), i + 1)


def tile_bias(i, r, stream, begin, group_size):
    wide = TILE * group_size
    j = lax.broadcasted_iota(jnp.int32, (TILE, wide), 1)
    key = (r * TILE + lax.rem(j, TILE)) * group_size + lax.div(j, TILE)
    ok = key >= begin[i * TILE : (i + 1) * TILE, :1]
    if r == i:
        ok = ok & (key <= stream[i * TILE : (i + 1) * TILE, :1])
    return jnp.where(ok, 0.0, MASKED_SCORE)


def dot_nn(a, b):
    return lax.dot_general(a, b, (((1,), (0,)), ((), ())), preferred_element_type=F32)


def dot_bt(a, b):
    return lax.dot_general(a, b, (((1,), (1,)), ((), ())), preferred_element_type=F32)


def dot_at(a, b):
    return lax.dot_general(a, b, (((0,), (0,)), ((), ())), preferred_element_type=F32)


def column_as_row(small, lane):
    pick = (lax.broadcasted_iota(jnp.int32, (8, 128), 1) == lane).astype(F32).astype(BF)
    return dot_bt(pick, small)[:1]


def front_kernel(
    n_experts,
    lens_ref,
    order_ref,
    tok_ref,
    routes_ref,
    pack_ref,
    wo_ref,
    gw_ref,
    uw_ref,
    x_all,
    gw_all,
    uw_all,
    pack_out,
    wo_out,
    kv_out,
    q_out,
    att_out,
    lse_out,
    mid_out,
    pay_ref,
    pack_all,
    wo_all,
    kv_all,
    unit_ref,
    acc_ref,
    s_ref,
    ag_send,
    ag_recv,
    z_send,
    z_recv,
    local,
):
    at = Place()
    at.greet()
    tokens, width = tok_ref.shape
    shard = pack_ref.shape[0]
    group = 8
    kv_width = KEY_VALUE_HEADS * HEAD_SIZE
    q_width = QUERY_HEADS * HEAD_SIZE
    qkv = q_width + 2 * kv_width
    per_kv = QUERY_HEADS // KEY_VALUE_HEADS
    chunk = shard * group
    cut_a = 9 * 128
    cut_b = wo_ref.shape[1] // 2
    items = {}

    def add_item(name, blk, half):
        n = len(items)
        items[name] = PlaneGather(
            at, blk, half, lambda k, n=n: ag_send.at[n, k], lambda k, n=n: ag_recv.at[n, k]
        )

    def add_weight(name, ref, z, cut):
        wide = ref.shape[1]

        def place(e):
            return pl.ds(pl.multiple_of(z * chunk + e * shard, 16), shard)

        def half(e, h):
            return ref.at[place(e), pl.ds(0, cut) if h == 0 else pl.ds(cut, wide - cut)]

        add_item(name, lambda e: ref.at[place(e)], half)

    for k in range(4):
        add_weight(("a", k), pack_all, at.order[k], cut_a)
    for k in range(4):
        add_weight(("b", k), wo_all, at.order[k], cut_b)
    add_item("kv", lambda e: kv_all.at[e], lambda e, h: kv_all.at[e, :, pl.ds(h * kv_width, kv_width)])
    part = tokens // 2
    for name, ref, cut in (("x", x_all, 7 * 128),):
        wide = ref.shape[2]
        for k in range(2):
            rows = pl.ds(k * part, part)

            def half(e, h, ref=ref, rows=rows, cut=cut, wide=wide):
                return ref.at[e, rows, pl.ds(0, cut) if h == 0 else pl.ds(cut, wide - cut)]

            add_item((name, k), lambda e, ref=ref, rows=rows: ref.at[e, rows], half)

    lines = {}

    def add_line(name, ref, size, start):
        n = len(lines)
        lines[name] = LineGather(
            at,
            lambda z: rows_of(ref, start(z), size),
            lambda k, n=n: z_send.at[n, k],
            lambda k, n=n: z_recv.at[n, k],
        )

    add_line("a", pack_all, shard, lambda z: z * chunk + at.e * shard)
    add_line("b", wo_all, shard, lambda z: z * chunk + at.e * shard)
    for name, ref, src in (("g", gw_all, gw_ref), ("u", uw_all, uw_ref)):
        size = src.shape[0]
        add_line(name, ref, size, lambda z, size=size: z * size)

    own_a = rows_of(pack_all, at.d * chunk + at.e * shard, shard)
    own_b = rows_of(wo_all, at.d * chunk + at.e * shard, shard)
    copies = [
        pltpu.make_async_copy(pack_ref, own_a, local.at[0]),
        pltpu.make_async_copy(wo_ref, own_b, local.at[1]),
    ]
    for n, (name, src) in enumerate((("g", gw_ref), ("u", uw_ref))):
        copies.append(pltpu.make_async_copy(src, lines[name].blk(at.d), local.at[2 + n]))

    lines["a"].start(pack_ref)
    items["a", 0].start(pack_ref)
    lines["b"].start(wo_ref)
    for copy in copies:
        copy.start()

    tok = tok_ref[...].astype(F32)
    scale_one = lax.rsqrt(jnp.mean(tok * tok, axis=1, keepdims=True) + EPSILON)
    unit_ref[...] = tok * scale_one
    stream, begin, relative = stream_facts(lens_ref, order_ref, tokens, group, at.e)
    cosine, sine = rotary(relative)
    acc_ref[...] = jnp.zeros_like(acc_ref)
    copies[0].wait()
    copies[1].wait()

    def consume(k):
        z = at.order[k]
        place = pl.ds(pl.multiple_of(z * chunk, 128), chunk)
        gain = column_as_row(pack_all[place, qkv:], n_experts)
        normed = (unit_ref[:, place] * gain).astype(BF)
        acc_ref[...] += dot_nn(normed, pack_all[place, :qkv])

    lines["a"].on(1)
    items["a", 1].start()
    items["a", 0].on_x()
    items["a", 0].on_y()
    lines["g"].start(gw_ref)
    items["a", 0].on_d()
    lines["a"].on(2)
    items["a", 2].start()
    items["a", 1].on_x()
    items["a", 1].on_y()
    items["a", 0].on_s()
    consume(0)
    lines["a"].on(3)
    items["a", 3].start()
    lines["b"].on(1)
    lines["u"].start(uw_ref)
    items["a", 1].on_d()
    items["a", 2].on_x()
    items["a", 2].on_y()
    items["a", 1].on_s()
    consume(1)
    lines["b"].on(2)
    items["a", 2].on_d()
    items["a", 3].on_x()
    items["a", 3].on_y()
    items["b", 0].start()
    items["a", 2].on_s()
    consume(2)
    lines["b"].on(3)
    items["a", 3].on_d()
    items["a", 3].on_s()
    consume(3)
    lines["g"].relay(1)
    keep = [
        pltpu.make_async_copy(pack_all, pack_out, local.at[7]),
    ]
    keep[0].start()

    def turned(col):
        v = acc_ref[:, col : col + HEAD_SIZE]
        return (v * cosine + swap_halves(v) * sine).astype(BF)

    for h in range(KEY_VALUE_HEADS):
        kv_all[at.e, :, h * HEAD_SIZE : (h + 1) * HEAD_SIZE] = turned(q_width + h * HEAD_SIZE)
    kv_all[at.e, :, kv_width:] = acc_ref[:, q_width + kv_width :].astype(BF)
    items["kv"].start()
    for h in range(QUERY_HEADS):
        q_out[h] = turned(h * HEAD_SIZE)
    items["b", 0].on_x()
    items["b", 0].on_y()
    items["b", 1].start()
    items["kv"].on_x()
    items["kv"].on_y()
    items["b", 0].on_d()
    items["b", 2].start()
    items["kv"].on_d()
    items["kv"].on_s()
    keep.append(pltpu.make_async_copy(kv_all, kv_out, local.at[8]))
    keep[1].start()

    def step_b(n):
        if n == 0:
            items["b", 1].on_x()
            items["b", 1].on_y()
            items["b", 3].start()
        elif n == 1:
            lines["g"].relay(2)
            items["b", 1].on_d()
            items["b", 2].on_x()
            items["b", 2].on_y()
        elif n == 2:
            lines["u"].relay(1)
            items["b", 2].on_d()
            items["b", 3].on_x()
            items["b", 3].on_y()
        elif n == 3:
            items["b", 3].on_d()
            lines["u"].relay(2)

    factor = LOG2E / math.sqrt(HEAD_SIZE)
    wide = TILE * group
    for i in range(tokens // TILE):
        step_b(i)
        first = tiles_of(i)[0]
        biases = [tile_bias(i, r, stream, begin, group) for r in tiles_of(i)]
        here = slice(i * TILE, (i + 1) * TILE)
        for g in range(KEY_VALUE_HEADS):
            queries = q_out[g * per_kv : (g + 1) * per_kv, here, :].reshape(per_kv * TILE, HEAD_SIZE)
            top = None
            for r in tiles_of(i):
                keys = kv_all[:, r * TILE : (r + 1) * TILE, g * HEAD_SIZE : (g + 1) * HEAD_SIZE]
                s = dot_bt(queries, keys.reshape(wide, HEAD_SIZE)) * factor
                s = s.reshape(per_kv, TILE, wide) + biases[r - first][None]
                s = s.reshape(per_kv * TILE, wide)
                s_ref[:, (r - first) * wide : (r - first + 1) * wide] = s
                high = jnp.max(s, axis=1, keepdims=True)
                top = high if top is None else jnp.maximum(top, high)
            total = None
            mixed = None
            for r in tiles_of(i):
                p = jnp.exp2(s_ref[:, (r - first) * wide : (r - first + 1) * wide] - top)
                values = kv_all[
                    :, r * TILE : (r + 1) * TILE, kv_width + g * HEAD_SIZE : kv_width + (g + 1) * HEAD_SIZE
                ].reshape(wide, HEAD_SIZE)
                row = jnp.sum(p, axis=1, keepdims=True)
                term = dot_nn(p.astype(BF), values)
                total = row if total is None else total + row
                mixed = term if mixed is None else mixed + term
            mixed = mixed / total
            lse_out[g, i] = jnp.broadcast_to(top + jnp.log2(total), (per_kv * TILE, 128))
            for h in range(per_kv):
                col = (g * per_kv + h) * HEAD_SIZE
                att_out[here, col : col + HEAD_SIZE] = mixed[h * TILE : (h + 1) * TILE]

    for k in range(4):
        items["b", k].on_s()
    keep.append(pltpu.make_async_copy(wo_all, wo_out, local.at[9]))
    keep[2].start()
    lines["g"].relay(3)
    attended = att_out[...].astype(BF)
    step = 256
    for n in range(width // step):
        cols = slice(n * step, (n + 1) * step)
        mid_out[:, cols] = tok_ref[:, cols].astype(F32) + dot_nn(attended, wo_all[:, cols])
    middle = mid_out[...]
    scale_two = lax.rsqrt(jnp.mean(middle * middle, axis=1, keepdims=True) + EPSILON)
    small = pack_all[:, qkv:]
    normed_two = (middle * scale_two * column_as_row(small, n_experts + 1)).astype(BF)
    pay_ref[:, :width] = normed_two
    logits = dot_nn(normed_two, small)
    lane = lax.broadcasted_iota(jnp.int32, (tokens, 128), 1)
    number = lax.broadcasted_iota(jnp.int32, (16, tokens), 0)
    named = number == routes_ref[:1, :]
    for k in range(1, routes_ref.shape[0]):
        named = named | (number == routes_ref[k : k + 1, :])
    turn = lax.broadcasted_iota(jnp.int32, (16, 128), 0) == lax.broadcasted_iota(
        jnp.int32, (16, 128), 1
    )
    choose = dot_at(named.astype(F32).astype(BF), turn.astype(F32).astype(BF)) > 0.5
    top = jnp.max(jnp.where(choose, logits, MASKED_SCORE), axis=1, keepdims=True)
    spread = jnp.where(choose, jnp.exp(jnp.minimum(logits - top, 0.0)), 0.0)
    gates = spread / jnp.sum(spread, axis=1, keepdims=True)
    pay_ref[:, width:] = split_three(gates)
    own_x = [
        pltpu.make_async_copy(
            pay_ref.at[pl.ds(k * part, part)], x_all.at[at.e, pl.ds(k * part, part)], local.at[10 + k]
        )
        for k in range(2)
    ]
    for k in range(2):
        items["x", k].start(pay_ref.at[pl.ds(k * part, part)])
        own_x[k].start()
    lines["u"].relay(3)
    for k in range(2):
        items["x", k].on_x()
        items["x", k].on_y()
    for k in range(2):
        items["x", k].on_d()
    for k in range(2):
        items["x", k].on_s()
    lines["g"].land()
    lines["u"].land()
    for item in items.values():
        item.drain()
    for line in lines.values():
        line.drain()
    for copy in copies[2:] + keep + own_x:
        copy.wait()


def split_three(values):
    high = values.astype(BF).astype(F32)
    mid = (values - high).astype(BF).astype(F32)
    low = values - high - mid
    return (high + pltpu.roll(mid, 32, 1) + pltpu.roll(low, 64, 1)).astype(BF)


def front(lengths, seq_order, tokens, routes, pack, wo, gw, uw, n_experts):
    count, width = tokens.shape
    group, line = 8, 4
    kv_width = KEY_VALUE_HEADS * HEAD_SIZE
    per_kv = QUERY_HEADS // KEY_VALUE_HEADS
    sds = jax.ShapeDtypeStruct
    smem = pl.BlockSpec(memory_space=pltpu.SMEM)
    vmem = pl.BlockSpec(memory_space=pltpu.VMEM)
    hbm = pl.BlockSpec(memory_space=ANY)
    n_items = 11
    return pl.pallas_call(
        functools.partial(front_kernel, n_experts),
        in_specs=[smem, smem] + [vmem] * 6,
        out_specs=(hbm,) * 6 + (vmem,) * 5,
        out_shape=(
            sds((group, count, width + 128), BF),
            sds((line * gw.shape[0], gw.shape[1]), BF),
            sds((line * uw.shape[0], uw.shape[1]), BF),
            sds((width, pack.shape[1]), BF),
            sds((width, wo.shape[1]), BF),
            sds((group, count, 2 * kv_width), BF),
            sds((QUERY_HEADS, count, HEAD_SIZE), BF),
            sds((count, QUERY_HEADS * HEAD_SIZE), F32),
            sds((KEY_VALUE_HEADS, count // TILE, per_kv * TILE, 128), F32),
            sds((count, width), F32),
            sds((count, width + 128), BF),
        ),
        scratch_shapes=[
            pltpu.VMEM((width, pack.shape[1]), BF),
            pltpu.VMEM((width, wo.shape[1]), BF),
            pltpu.VMEM((group, count, 2 * kv_width), BF),
            pltpu.VMEM((count, width), F32),
            pltpu.VMEM((count, pack.shape[1] - 128), F32),
            pltpu.VMEM((per_kv * TILE, 3 * TILE * group), F32),
            pltpu.SemaphoreType.DMA((n_items, 8)),
            pltpu.SemaphoreType.DMA((n_items, 8)),
            pltpu.SemaphoreType.DMA((4, 5)),
            pltpu.SemaphoreType.DMA((4, 4)),
            pltpu.SemaphoreType.DMA((12,)),
        ],
        compiler_params=pltpu.CompilerParams(
            collective_id=1, has_side_effects=True, vmem_limit_bytes=60 * 2**20
        ),
    )(lengths, seq_order, tokens, routes, pack, wo, gw, uw)


class PlaneReduce:
    def __init__(self, at, first, own, seat, xs, ys, x2, y2, cut, send, recv):
        self.at, self.first, self.own = at, first, own
        self.seat, self.xs, self.ys, self.x2, self.y2 = seat, xs, ys, x2, y2
        self.cut, self.send, self.recv = cut, send, recv

    def copy(self, slot, src, dst, target):
        return rcopy(src, dst, self.send(slot), self.recv(slot), target)

    def moves(self):
        at, own, cut = self.at, self.own, self.cut
        low, high = pl.ds(0, cut), pl.ds(cut, self.seat.shape[-1] - cut)
        return {
            0: lambda: self.copy(0, self.first, self.seat, at.sib),
            1: lambda: self.copy(1, own.at[at.chip_x, :, low], self.xs.at[0], at.nx),
            2: lambda: self.copy(2, own.at[at.chip_d, :, low], self.xs.at[1], at.nx),
            3: lambda: self.copy(3, own.at[at.chip_y, :, high], self.ys.at[0], at.ny),
            4: lambda: self.copy(4, own.at[at.chip_d, :, high], self.ys.at[1], at.ny),
            5: lambda: self.copy(5, own.at[at.chip_y, :, low], self.y2, at.ny),
            6: lambda: self.copy(6, own.at[at.chip_x, :, high], self.x2, at.nx),
        }

    def begin(self, slot):
        self.moves()[slot]().start()

    def got(self, slot):
        self.moves()[slot]().wait_recv()

    def start(self):
        self.begin(0)

    def on_s(self):
        self.got(0)

        def add(q, none):
            self.own[q] = (self.own[q].astype(F32) + self.seat[q].astype(F32)).astype(BF)
            return none

        lax.fori_loop(0, 4, add, 0)
        for slot in (1, 2, 3, 4):
            self.begin(slot)

    def on_xy(self):
        at, own, cut = self.at, self.own, self.cut
        self.got(1)
        self.got(2)
        own[at.chip_y, :, :cut] = (
            own[at.chip_y, :, :cut].astype(F32) + self.xs[1].astype(F32)
        ).astype(BF)
        self.begin(5)
        self.got(3)
        self.got(4)
        own[at.chip_x, :, cut:] = (
            own[at.chip_x, :, cut:].astype(F32) + self.ys[1].astype(F32)
        ).astype(BF)
        self.begin(6)

    def finish(self):
        at, own, cut = self.at, self.own, self.cut
        self.got(5)
        low = own[at.chip, :, :cut].astype(F32) + self.xs[0].astype(F32) + self.y2[...].astype(F32)
        self.got(6)
        high = own[at.chip, :, cut:].astype(F32) + self.ys[0].astype(F32) + self.x2[...].astype(F32)
        return low, high

    def sent(self, slot):
        self.moves()[slot]().wait_send()

    def drain(self, slots=range(7)):
        for slot in slots:
            self.sent(slot)


class LineReduce:
    def __init__(self, at, blocks, near, far, send, recv):
        self.at, self.blocks, self.near, self.far = at, blocks, near, far
        self.send, self.recv = send, recv

    def copy(self, slot, src, dst, target):
        return rcopy(src, dst, self.send(slot), self.recv(slot), target)

    def outer_moves(self):
        at = self.at
        return [
            self.copy(n, self.blocks.at[at.order[n + 1]], self.near.at[n], at.pair)
            for n in range(3)
        ]

    def cross_moves(self):
        at = self.at
        return [
            self.copy(3 + n, self.blocks.at[at.order[n + 2]], self.far.at[n], at.cross)
            for n in range(2)
        ]

    def back_move(self):
        at = self.at
        return self.copy(0, self.blocks.at[at.order[1]], self.near.at[0], at.pair)

    def start(self):
        at = self.at

        @pl.when(jnp.logical_not(at.inner))
        def _():
            for move in self.outer_moves():
                move.start()

    def middle(self):
        at, blocks = self.at, self.blocks

        @pl.when(at.inner)
        def _():
            for n in range(2):
                rcopy(
                    self.near.at[n + 1], self.near.at[n + 1], self.send(0), self.recv(n + 1), at.pair
                ).wait_recv()
                blocks[at.order[n + 2]] = (
                    blocks[at.order[n + 2]].astype(F32) + self.near[n + 1].astype(F32)
                ).astype(BF)
                self.cross_moves()[n].start()

    def last(self):
        at, blocks = self.at, self.blocks

        @pl.when(at.inner)
        def _():
            self.cross_moves()[1].wait_recv()
            blocks[at.order[1]] = (
                blocks[at.order[1]].astype(F32) + self.far[1].astype(F32)
            ).astype(BF)
            self.back_move().start()

    def leave(self, k):
        @pl.when(jnp.logical_not(self.at.inner))
        def _():
            self.outer_moves()[k - 1].start()

    def hand(self, k):
        at, blocks = self.at, self.blocks

        @pl.when(at.inner)
        def _():
            if k == 1:
                self.cross_moves()[1].wait_recv()
                come = self.far[1]
            else:
                rcopy(
                    self.near.at[k - 1], self.near.at[k - 1], self.send(0), self.recv(k - 1), at.pair
                ).wait_recv()
                come = self.near[k - 1]
            blocks[at.order[k]] = (blocks[at.order[k]].astype(F32) + come.astype(F32)).astype(BF)
            if k == 1:
                self.back_move().start()
            else:
                self.cross_moves()[k - 2].start()

    def finish(self, out):
        at = self.at
        self.back_move().wait_recv()
        total = self.blocks[at.d].astype(F32) + self.near[0].astype(F32)

        @pl.when(at.inner)
        def _():
            self.cross_moves()[0].wait_recv()
            out[...] = total + self.far[0].astype(F32)
            for move in self.cross_moves():
                move.wait_send()
            self.back_move().wait_send()

        @pl.when(jnp.logical_not(at.inner))
        def _():
            out[...] = total
            for move in self.outer_moves():
                move.wait_send()


def column_sums(values):
    high = values.astype(BF)
    low = (values - high.astype(F32)).astype(BF)
    ones = jnp.ones((values.shape[0], 128), BF)
    return dot_at(high, ones) + dot_at(low, ones)


def expert_lanes(rows):
    e = lax.axis_index("expert")
    lane = lax.broadcasted_iota(jnp.int32, (rows, 128), 1)
    return e, lane, (lane == e) | (lane == e + 32) | (lane == e + 64)


def gate_of(ext):
    mine = expert_lanes(ext.shape[0])[2]
    return jnp.sum(jnp.where(mine, ext.astype(F32), 0.0), axis=1, keepdims=True)


EXPERT_ROWS = 512


def up_kernel(
    x_in, cot_ref, gw_in, uw_in, dw_in, c_out, dw_all, hid_out, slope_out, grad_ref,
    x_ref, c_ref, gu_ref, dw_ref, hid_ref, slope_ref, back_ref, g_send, g_recv, z_send, z_recv, local,
):
    at = Place()
    at.greet()
    rows = x_ref.shape[0]
    tokens, width = cot_ref.shape
    hid = hid_ref.shape[1]
    part = tokens // 2
    copy = pltpu.make_async_copy
    tall = dw_in.shape[0]
    line = LineGather(
        at, lambda z: rows_of(dw_all, z * tall, tall), lambda k: z_send.at[k], lambda k: z_recv.at[k]
    )
    cots = []
    for k in range(2):
        span = pl.ds(k * part, part)

        def half(e, h, span=span):
            return c_ref.at[e, span, pl.ds(h * (width // 2), width // 2)]

        cots.append(
            PlaneGather(
                at,
                lambda e, span=span: c_ref.at[e, span],
                half,
                lambda s, k=k: g_send.at[k, s],
                lambda s, k=k: g_recv.at[k, s],
            )
        )
    line.start(dw_in)
    for k in range(2):
        cots[k].start(cot_ref.at[pl.ds(k * part, part)])
    gates_w = copy(gw_in, gu_ref.at[:, pl.ds(0, hid)], local.at[0])
    ups_w = copy(uw_in, gu_ref.at[:, pl.ds(hid, hid)], local.at[1])
    own_c = copy(cot_ref, c_ref.at[at.e], local.at[2])
    own_d = copy(dw_in, line.blk(at.d), local.at[3])
    count = rows // EXPERT_ROWS
    spans = [pl.ds(b * EXPERT_ROWS, EXPERT_ROWS) for b in range(count)]
    loads = [copy(x_in.at[spans[b]], x_ref.at[spans[b]], local.at[4 + b]) for b in range(count)]
    saves = []
    gates_w.start()
    loads[0].start()
    ups_w.start()
    for b in range(1, count):
        loads[b].start()
    own_c.start()
    own_d.start()
    gates_w.wait()
    ups_w.wait()
    step = 256
    for b in range(count):
        loads[b].wait()

        def work(h, none, b=b):
            here = pl.ds(pl.multiple_of(b * EXPERT_ROWS + h * step, step), step)
            x = x_ref[here, :width]
            for f in range(hid // 256):
                cols = slice(f * 256, (f + 1) * 256)
                after = slice(hid + f * 256, hid + (f + 1) * 256)
                gate_pre = dot_nn(x, gu_ref[:, cols])
                up_pre = dot_nn(x, gu_ref[:, after])
                sig = 1.0 / (1.0 + jnp.exp(-gate_pre))
                silu = gate_pre * sig
                hid_ref[here, cols] = (silu * up_pre).astype(BF)
                slope_ref[here, after] = silu.astype(BF)
                slope_ref[here, cols] = (up_pre * sig * (1.0 + gate_pre * (1.0 - sig))).astype(BF)
            return none

        lax.fori_loop(0, EXPERT_ROWS // step, work, 0)
        saves.append(copy(hid_ref.at[spans[b]], hid_out.at[spans[b]], local.at[8 + b]))
        saves[-1].start()
        if b == 1:
            line.relay(1)
            line.relay(2)
            for cot in cots:
                cot.on_x()
                cot.on_y()
        if b == 3:
            line.relay(3)
    for cot in cots:
        cot.on_d()
    own_c.wait()
    for cot in cots:
        cot.on_s()
    saves.append(copy(c_ref, c_out, local.at[16]))
    saves[-1].start()

    def weigh(e, none):
        here = pl.ds(pl.multiple_of(e * tokens, tokens), tokens)
        back_ref[here, :] = (gate_of(x_ref[here, width:]) * c_ref[e].astype(F32)).astype(BF)
        return none

    lax.fori_loop(0, c_ref.shape[0], weigh, 0)
    deep = gw_in.shape[0] // 4
    for t in range(2):
        down = dot_at(hid_ref[:, 2 * t * tall : 2 * (t + 1) * tall], back_ref[...]).astype(BF)
        for j in range(2):
            piece = down[j * tall : (j + 1) * tall]
            grad_ref[2 * t + j, 2 * deep : 2 * deep + tall] = piece[:, : width // 2]
            grad_ref[2 * t + j, 2 * deep + tall :] = piece[:, width // 2 :]
    line.land()
    own_d.wait()
    load_d = copy(dw_all, dw_ref, local.at[17])
    load_d.start()
    load_d.wait()

    def slopes(h, none):
        here = pl.ds(pl.multiple_of(h * step, step), step)
        rows_back = back_ref[here, :]
        for f in range(hid // 256):
            cols = slice(f * 256, (f + 1) * 256)
            after = slice(hid + f * 256, hid + (f + 1) * 256)
            grad_hidden = dot_bt(rows_back, dw_ref[cols, :])
            for span in (cols, after):
                slope_ref[here, span] = (grad_hidden * slope_ref[here, span].astype(F32)).astype(BF)
        return none

    lax.fori_loop(0, rows // step, slopes, 0)
    saves.append(copy(slope_ref, slope_out, local.at[12]))
    saves[-1].start()
    for z in range(4):
        both = dot_at(x_ref[:, z * deep : (z + 1) * deep], slope_ref[...]).astype(BF)
        grad_ref[z, :deep] = both[:, :hid]
        grad_ref[z, deep : 2 * deep] = both[:, hid:]
    for cot in cots:
        cot.drain()
    line.drain()
    for save in saves:
        save.wait()


def expert_up(x_all, cot, gw, uw, dw):
    rows = x_all.shape[0]
    tokens, width = cot.shape
    hid = gw.shape[1]
    sds = jax.ShapeDtypeStruct
    vmem = pl.BlockSpec(memory_space=pltpu.VMEM)
    hbm = pl.BlockSpec(memory_space=ANY)

    def low(*shape):
        return pltpu.VMEM(shape, BF)

    return pl.pallas_call(
        up_kernel,
        in_specs=[hbm, vmem, hbm, hbm, vmem],
        out_specs=(hbm, hbm, hbm, hbm, vmem),
        out_shape=(
            sds((rows // tokens, tokens, width), BF),
            sds((hid, width), BF),
            sds((rows, hid), BF),
            sds((rows, 2 * hid), BF),
            sds((4, 3 * width // 4, hid), BF),
        ),
        scratch_shapes=[
            low(rows, width + 128),
            low(rows // tokens, tokens, width),
            low(width, 2 * hid),
            low(hid, width),
            low(rows, hid),
            low(rows, 2 * hid),
            low(rows, width),
            pltpu.SemaphoreType.DMA((2, 8)),
            pltpu.SemaphoreType.DMA((2, 8)),
            pltpu.SemaphoreType.DMA((5,)),
            pltpu.SemaphoreType.DMA((4,)),
            pltpu.SemaphoreType.DMA((18,)),
        ],
        compiler_params=pltpu.CompilerParams(
            collective_id=3, has_side_effects=True, vmem_limit_bytes=62 * 2**20
        ),
        cost_estimate=pl.CostEstimate(
            flops=8 * 10**10, bytes_accessed=5 * 10**7, transcendentals=10**6
        ),
    )(x_all, cot, gw, uw, dw)


PARTS = 4


def down_kernel(
    x_in, c_in, hid_in, slope_in, gw_in, uw_in, dw_in, row_out, wgt_out,
    ext_ref, c_ref, hid_ref, slope_ref, gu_ref, dw_ref, wgt_ref,
    slot, own, seat, low1, high1, low2, high2, send, recv, local,
):
    at = Place()
    at.greet()
    tokens = x_in.shape[2]
    width = c_ref.shape[3]
    hid = dw_ref.shape[0]
    part = tokens // PARTS
    rows = 4 * part
    copy = pltpu.make_async_copy
    cut = 7 * 128
    red = []
    for k in range(PARTS):
        red.append(
            PlaneReduce(
                at, slot.at[k], own.at[k], seat.at[k], low1.at[k], high1.at[k], high2.at[k],
                low2.at[k], cut, lambda s, k=k: send.at[k, s], lambda s, k=k: recv.at[k, s],
            )
        )

    def place(j):
        core = 1 - at.core if j % 2 == 0 else at.core
        return (slice(None), core, pl.ds(j // 2 * part, part))

    count = 2 * PARTS
    ext = (pl.ds(width, 128),)
    loads = [
        [
            copy(hid_in.at[place(j)], hid_ref.at[j], local.at[0, j]),
            copy(c_in.at[place(j)], c_ref.at[j], local.at[1, j]),
            copy(x_in.at[place(j) + ext], ext_ref.at[j], local.at[2, j]),
            copy(slope_in.at[place(j)], slope_ref.at[j], local.at[3, j]),
        ]
        for j in range(count)
    ]
    saves = [copy(wgt_ref.at[j], wgt_out.at[place(j)], local.at[4, j]) for j in range(count)]
    gates_w = copy(gw_in, gu_ref.at[:, pl.ds(0, hid)], local.at[5, 0])
    ups_w = copy(uw_in, gu_ref.at[:, pl.ds(hid, hid)], local.at[5, 1])
    downs_w = copy(dw_in, dw_ref, local.at[5, 2])
    for load in loads[0]:
        load.start()
    gates_w.start()
    ups_w.start()
    downs_w.start()
    for j in range(1, count):
        for load in loads[j]:
            load.start()
    e, lane, mine = expert_lanes(rows)

    def block(j, row_dst):
        for load in loads[j]:
            load.wait()
        if j == 0:
            gates_w.wait()
            ups_w.wait()
        pair = slope_ref[j].reshape(rows, 2 * hid)
        row_dst[:, :, :width] = dot_bt(pair, gu_ref[...]).astype(BF).reshape(4, part, width)
        if j == 0:
            downs_w.wait()
        gate = gate_of(ext_ref[j].reshape(rows, 128))
        returned = dot_nn(hid_ref[j].reshape(rows, hid), dw_ref[...]).astype(BF).astype(F32)
        cot = c_ref[j].reshape(rows, width).astype(F32)
        grad_gates = jnp.sum(cot * returned, axis=1, keepdims=True)
        wgt_ref[j] = (gate * returned).astype(BF).reshape(4, part, width)
        saves[j].start()
        high = grad_gates.astype(BF).astype(F32)
        row_dst[:, :, width:] = (
            jnp.where(lane == e, high, jnp.where(lane == e + 32, grad_gates - high, 0.0))
            .astype(BF)
            .reshape(4, part, 128)
        )

    def settle(k):
        low, high = red[k].finish()
        row_out[k * part : (k + 1) * part, :cut] = low
        row_out[k * part : (k + 1) * part, cut:] = high

    for k in range(PARTS):
        block(2 * k, slot.at[k])
        red[k].start()
        if k >= 1:
            red[k - 1].on_xy()
        if k >= 2:
            settle(k - 2)
        block(2 * k + 1, own.at[k])
        red[k].on_s()
    red[PARTS - 1].on_xy()
    settle(PARTS - 2)
    settle(PARTS - 1)
    for item in red:
        item.drain()
    for save in saves:
        save.wait()


def expert_down(x_all, c_all, hidden, slope, gw, uw, dw):
    group, tokens, width = c_all.shape
    hid = gw.shape[1]
    part = tokens // PARTS
    cut = 7 * 128
    wide = width + 128
    sds = jax.ShapeDtypeStruct
    hbm = pl.BlockSpec(memory_space=ANY)

    def low(*shape):
        return pltpu.VMEM(shape, BF)

    return pl.pallas_call(
        down_kernel,
        in_specs=[hbm] * 7,
        out_specs=(pl.BlockSpec(memory_space=pltpu.VMEM), hbm),
        out_shape=(sds((tokens, wide), F32), sds((4, 2, tokens, width), BF)),
        scratch_shapes=[
            low(2 * PARTS, 4, part, 128),
            low(2 * PARTS, 4, part, width),
            low(2 * PARTS, 4, part, hid),
            low(2 * PARTS, 4, part, 2 * hid),
            low(width, 2 * hid),
            low(hid, width),
            low(2 * PARTS, 4, part, width),
            low(PARTS, 4, part, wide),
            low(PARTS, 4, part, wide),
            low(PARTS, 4, part, wide),
            low(PARTS, 2, part, cut),
            low(PARTS, 2, part, wide - cut),
            low(PARTS, part, cut),
            low(PARTS, part, wide - cut),
            pltpu.SemaphoreType.DMA((PARTS, 7)),
            pltpu.SemaphoreType.DMA((PARTS, 7)),
            pltpu.SemaphoreType.DMA((6, 2 * PARTS)),
        ],
        compiler_params=pltpu.CompilerParams(
            collective_id=4, has_side_effects=True, vmem_limit_bytes=63 * 2**20
        ),
        cost_estimate=pl.CostEstimate(
            flops=5 * 10**10, bytes_accessed=5 * 10**7, transcendentals=10**6
        ),
    )(
        x_all.reshape(4, 2, tokens, wide),
        c_all.reshape(4, 2, tokens, width),
        hidden.reshape(4, 2, tokens, hid),
        slope.reshape(4, 2, tokens, 2 * hid),
        gw,
        uw,
        dw,
    )


def pack_weights(w_router, norm_attn, norm_moe, w_query, key_projection, value_projection):
    rows, n_experts = w_router.shape
    small = jnp.concatenate(
        [
            w_router.T,
            norm_attn[None, :],
            norm_moe[None, :],
            jnp.zeros((128 - n_experts - 2, rows), BF),
        ],
        axis=0,
    ).T
    return jnp.concatenate([w_query, key_projection, value_projection, small], axis=1)


N_BACK = 16


def back_kernel(
    n_experts,
    lens_ref,
    order_ref,
    row_in,
    wgt_in,
    tok_in,
    q_in,
    att_in,
    lse_in,
    mid_in,
    cot_in,
    kv_in,
    pay_in,
    pack_in,
    wo_in,
    output_ref,
    tokens_grad_ref,
    aq_out,
    ak_out,
    b_out,
    w_own,
    w_seat,
    w_half1,
    w_half2,
    row_ref,
    tok_ref,
    q_ref,
    att_ref,
    lse_ref,
    mid_ref,
    cot_ref,
    kv_ref,
    pay_ref,
    pack_ref,
    wo_ref,
    do_ref,
    dkv_ref,
    kseat,
    klow1,
    khigh1,
    klow2,
    khigh2,
    bseat,
    bhalf1,
    bhalf2,
    aseat,
    ahalf1,
    ahalf2,
    cseat,
    clow1,
    chigh1,
    clow2,
    chigh2,
    n1_ref,
    dqkv_ref,
    small_ref,
    grad_middle_ref,
    bz,
    bnear,
    bfar,
    az,
    anear,
    afar,
    cz,
    cnear,
    cfar,
    r_send,
    r_recv,
    l_send,
    l_recv,
    local,
):
    at = Place()
    at.greet()
    tokens, width = tok_ref.shape
    group = 8
    kv_width = KEY_VALUE_HEADS * HEAD_SIZE
    q_width = QUERY_HEADS * HEAD_SIZE
    qkv = q_width + 2 * kv_width
    per_kv = QUERY_HEADS // KEY_VALUE_HEADS
    chunk = width // 4
    shard = chunk // group
    part = tokens // 2
    red = {}

    def sems(n):
        return (lambda k: r_send.at[n, k]), (lambda k: r_recv.at[n, k])

    own_loads = []
    for k in range(2):
        send, recv = sems(len(red))
        mine = wgt_in.at[:, :, pl.ds(k * part, part)]
        own_loads.append(
            pltpu.make_async_copy(mine.at[:, at.core], w_own.at[k], local.at[12 + k])
        )
        red["w", k] = PlaneReduce(
            at, mine.at[:, 1 - at.core], w_own.at[k], w_seat.at[k], w_half1.at[k, 0],
            w_half1.at[k, 1], w_half2.at[k, 0], w_half2.at[k, 1], width // 2, send, recv,
        )
    for k in range(2):
        send, recv = sems(len(red))
        rows = pl.ds(k * part, part)
        mine = dkv_ref.at[:, :, rows]
        red["k", k] = PlaneReduce(
            at, mine.at[:, 1 - at.core], mine.at[:, at.core], kseat.at[k], klow1.at[k], khigh1.at[k],
            khigh2.at[k], klow2.at[k], kv_width, send, recv,
        )
    for z in range(4):
        send, recv = sems(len(red))
        red["b", z] = PlaneReduce(
            at, wo_ref.at[z, :, 1 - at.core], wo_ref.at[z, :, at.core], bseat.at[z], bhalf1.at[z, 0],
            bhalf1.at[z, 1], bhalf2.at[z, 0], bhalf2.at[z, 1], width // 2, send, recv,
        )
    cols_q, cols_k = pl.ds(0, q_width), pl.ds(q_width, 2 * kv_width + 128)
    for k in range(4):
        send, recv = sems(len(red))
        z = at.order[k]
        red["q", k] = PlaneReduce(
            at, pack_ref.at[z, :, 1 - at.core, :, cols_q], pack_ref.at[z, :, at.core, :, cols_q],
            aseat.at[k], ahalf1.at[k, 0], ahalf1.at[k, 1], ahalf2.at[k, 0], ahalf2.at[k, 1],
            q_width // 2, send, recv,
        )
    for k in range(4):
        send, recv = sems(len(red))
        z = at.order[k]
        red["s", k] = PlaneReduce(
            at, pack_ref.at[z, :, 1 - at.core, :, cols_k], pack_ref.at[z, :, at.core, :, cols_k],
            cseat.at[k], clow1.at[k], chigh1.at[k], chigh2.at[k], clow2.at[k],
            3 * 128, send, recv,
        )
    lines = {}
    for n, (name, blocks, near, far) in enumerate(
        (("b", bz, bnear, bfar), ("q", az, anear, afar), ("s", cz, cnear, cfar))
    ):
        lines[name] = LineReduce(
            at, blocks, near, far, lambda k, n=n: l_send.at[n, k], lambda k, n=n: l_recv.at[n, k]
        )

    loads = {}
    cols_small = pl.ds(qkv, 128)
    cols_main = pl.ds(0, qkv)
    for n, (name, src, dst) in enumerate(
        (
            ("row", row_in, row_ref),
            ("small", pack_in.at[:, :, :, :, cols_small], pack_ref.at[:, :, :, :, cols_small]),
            ("pay", pay_in, pay_ref),
            ("mid", mid_in, mid_ref),
            ("cot", cot_in, cot_ref),
            ("wo", wo_in, wo_ref),
            ("att", att_in, att_ref),
            ("lse", lse_in, lse_ref),
            ("q", q_in, q_ref),
            ("kv", kv_in, kv_ref),
            ("tok", tok_in, tok_ref),
            ("main", pack_in.at[:, :, :, :, cols_main], pack_ref.at[:, :, :, :, cols_main]),
        )
    ):
        loads[name] = pltpu.make_async_copy(src, dst, local.at[n])
    early = ("row", "small", "pay", "mid", "cot")
    for name in early:
        loads[name].start()
    red["w", 0].start()
    loads["wo"].start()
    own_loads[0].start()
    stream, begin, relative = stream_facts(lens_ref, order_ref, tokens, group, at.e)
    for name in early:
        loads[name].wait()
    for name in ("att", "lse", "q", "kv", "tok", "main"):
        loads[name].start()

    def tok_unit():
        tok = tok_ref[...].astype(F32)
        scale = lax.rsqrt(jnp.mean(tok * tok, axis=1, keepdims=True) + EPSILON)
        return tok * scale, scale

    small = pack_ref[..., qkv:].reshape(width, 128)
    gain_one = column_as_row(small, n_experts)
    gain_two = column_as_row(small, n_experts + 1)
    lane = lax.broadcasted_iota(jnp.int32, (tokens, 128), 1)
    ext = pay_ref[:, width:].astype(F32)
    gates = jnp.where(
        lane < n_experts, ext + pltpu.roll(ext, 96, 1) + pltpu.roll(ext, 64, 1), 0.0
    )
    ext = row_ref[:, width:]
    grad_gates = jnp.where(lane < n_experts, ext + pltpu.roll(ext, 96, 1), 0.0)
    weighted_sum = jnp.sum(gates * grad_gates, axis=1, keepdims=True)
    grad_logits = (gates * (grad_gates - weighted_sum)).astype(BF)
    grad_normed = dot_bt(grad_logits, small) + row_ref[:, :width]
    middle = mid_ref[...]
    scale_two = lax.rsqrt(jnp.mean(middle * middle, axis=1, keepdims=True) + EPSILON)
    unit_two = middle * scale_two
    inner_sum = jnp.mean(grad_normed * gain_two * unit_two, axis=1, keepdims=True)
    grad_middle = cot_ref[...].astype(F32) + scale_two * (
        grad_normed * gain_two - unit_two * inner_sum
    )
    products = grad_normed * unit_two
    loads["wo"].wait()
    own_loads[0].wait()
    red["w", 0].on_s()
    red["w", 1].start()
    own_loads[1].start()
    grad_middle_ref[...] = grad_middle
    mixed = grad_middle.astype(BF)
    for z in range(4):
        heads = dot_bt(mixed, wo_ref[z].reshape(chunk, width)).astype(BF)
        for j in range(chunk // HEAD_SIZE):
            do_ref[z * (chunk // HEAD_SIZE) + j] = heads[:, j * HEAD_SIZE : (j + 1) * HEAD_SIZE]
    loads["att"].wait()
    for z in range(4):
        left = att_ref[:, z * chunk : (z + 1) * chunk].astype(BF)
        wo_ref[z] = dot_at(left, mixed).astype(BF).reshape(4, 2, shard, width)
        red["b", z].start()
    lane_small = lax.broadcasted_iota(jnp.int32, (width, 128), 1)
    small_ref[...] = dot_at(pay_ref[:, :width], grad_logits) + jnp.where(
        lane_small == n_experts + 1, column_sums(products), 0.0
    )
    for name in ("lse", "q", "kv"):
        loads[name].wait()
    row_ref[:, :width] = jnp.zeros((tokens, width), F32)
    n_tiles = tokens // TILE
    wide = TILE * group
    for g in range(KEY_VALUE_HEADS):
        for i in range(n_tiles):
            here = slice(i * TILE, (i + 1) * TILE)
            dots = []
            for h in range(per_kv):
                col = (g * per_kv + h) * HEAD_SIZE
                dots.append(
                    jnp.sum(
                        do_ref[g * per_kv + h, here, :].astype(F32)
                        * att_ref[here, col : col + HEAD_SIZE],
                        axis=1,
                        keepdims=True,
                    )
                )
            dots = jnp.concatenate(dots, axis=0)
            lse_ref[g, i, :, 64:] = jnp.broadcast_to(dots, (per_kv * TILE, 64))
    for z in range(4):
        red["b", z].on_s()
    cosine, sine = rotary(relative)
    loads["tok"].wait()
    n1_ref[...] = (tok_unit()[0] * gain_one).astype(BF)

    factor = LOG2E / math.sqrt(HEAD_SIZE)
    score_scale = 1.0 / math.sqrt(HEAD_SIZE)

    def attend_back(r):
        queries_of = [i for i in range(n_tiles) if r in tiles_of(i)]
        biases = {i: tile_bias(i, r, stream, begin, group) for i in queries_of}
        there = slice(r * TILE, (r + 1) * TILE)
        for g in range(KEY_VALUE_HEADS):
            key_cols = slice(g * HEAD_SIZE, (g + 1) * HEAD_SIZE)
            value_cols = slice(kv_width + g * HEAD_SIZE, kv_width + (g + 1) * HEAD_SIZE)
            heads = slice(g * per_kv, (g + 1) * per_kv)
            keys = kv_ref[:, there, key_cols].reshape(wide, HEAD_SIZE)
            values = kv_ref[:, there, value_cols].reshape(wide, HEAD_SIZE)
            grad_keys = None
            grad_values = None
            for i in queries_of:
                here = slice(i * TILE, (i + 1) * TILE)
                queries = q_ref[heads, here, :].reshape(per_kv * TILE, HEAD_SIZE)
                grads = do_ref[heads, here, :].reshape(per_kv * TILE, HEAD_SIZE)
                s = dot_bt(queries, keys) * factor
                s = (s.reshape(per_kv, TILE, wide) + biases[i][None]).reshape(per_kv * TILE, wide)
                p = jnp.exp2(s - lse_ref[g, i, :, :1])
                ds = (p * (dot_bt(grads, values) - lse_ref[g, i, :, 64:65])).astype(BF)
                term_k = dot_at(ds, queries)
                term_v = dot_at(p.astype(BF), grads)
                grad_keys = term_k if grad_keys is None else grad_keys + term_k
                grad_values = term_v if grad_values is None else grad_values + term_v
                grad_queries = dot_nn(ds, keys)
                for h in range(per_kv):
                    col = (g * per_kv + h) * HEAD_SIZE
                    row_ref[here, col : col + HEAD_SIZE] += grad_queries[
                        h * TILE : (h + 1) * TILE
                    ]
            dkv_ref[:, :, there, key_cols] = (
                (grad_keys * score_scale).astype(BF).reshape(4, 2, TILE, HEAD_SIZE)
            )
            dkv_ref[:, :, there, value_cols] = grad_values.astype(BF).reshape(4, 2, TILE, HEAD_SIZE)

    def settle(name, z, blocks, cut):
        low, high = red[name, z].finish()
        blocks[z, :, :cut] = low.astype(BF)
        blocks[z, :, cut:] = high.astype(BF)

    red["w", 0].on_xy()
    attend_back(0)
    for z in range(4):
        red["b", z].on_xy()
    attend_back(1)
    red["k", 0].start()
    attend_back(2)
    red["k", 0].on_s()
    for z in range(4):
        settle("b", z, bz, width // 2)
    lines["b"].start()
    own_loads[1].wait()
    red["w", 1].on_s()
    attend_back(3)
    red["k", 1].start()
    red["k", 0].on_xy()

    def output_part(k):
        rows = slice(k * part, (k + 1) * part)
        low, high = red["w", k].finish()
        output_ref[rows, : width // 2] = (mid_ref[rows, : width // 2] + low).astype(BF)
        output_ref[rows, width // 2 :] = (mid_ref[rows, width // 2 :] + high).astype(BF)

    def turned_back(v):
        return (v * cosine - swap_halves(v) * sine).astype(BF)

    for h in range(QUERY_HEADS):
        cols = slice(h * HEAD_SIZE, (h + 1) * HEAD_SIZE)
        dqkv_ref[:, cols] = turned_back(row_ref[:, cols] * score_scale)
    red["k", 1].on_s()
    loads["main"].wait()
    grad_q = dqkv_ref[:, :q_width]
    far_first = (3, 2, 1, 0)

    def span(k):
        return pl.ds(pl.multiple_of(at.order[k] * chunk, 128), chunk)

    for k in far_first:
        z = at.order[k]
        att_ref[:, span(k)] = dot_bt(
            grad_q, pack_ref[z, :, :, :, :q_width].reshape(chunk, q_width)
        )
        pack_ref[z, :, :, :, :q_width] = (
            dot_at(n1_ref[:, span(k)], grad_q).astype(BF).reshape(4, 2, shard, q_width)
        )
        red["q", k].start()
        if k == 3:
            red["k", 1].on_xy()
    for k in range(2):
        rows = slice(k * part, (k + 1) * part)
        low, high = red["k", k].finish()
        row_ref[rows, :kv_width] = low
        row_ref[rows, kv_width : 2 * kv_width] = high
    lines["b"].middle()
    red["w", 1].on_xy()
    for k in far_first:
        red["q", k].on_s()
    for h in range(KEY_VALUE_HEADS):
        v = row_ref[:, h * HEAD_SIZE : (h + 1) * HEAD_SIZE]
        dqkv_ref[:, q_width + h * HEAD_SIZE : q_width + (h + 1) * HEAD_SIZE] = turned_back(v)
    dqkv_ref[:, q_width + kv_width :] = row_ref[:, kv_width : 2 * kv_width].astype(BF)
    grad_kv = dqkv_ref[:, q_width:]
    for z in range(4):
        cols = slice(z * chunk, (z + 1) * chunk)
        att_ref[:, cols] += dot_bt(
            grad_kv, pack_ref[z, :, :, :, q_width:qkv].reshape(chunk, 2 * kv_width)
        )
        pack_ref[z, :, :, :, q_width:qkv] = (
            dot_at(n1_ref[:, cols], grad_kv).astype(BF).reshape(4, 2, shard, 2 * kv_width)
        )
    unit_one, scale_one = tok_unit()
    grad_one = att_ref[...]
    small_ref[...] += jnp.where(lane_small == n_experts, column_sums(grad_one * unit_one), 0.0)
    pack_ref[..., qkv:] = small_ref[...].astype(BF).reshape(4, 4, 2, shard, 128)
    for k in far_first:
        red["s", k].start()
    lines["b"].last()
    for k in far_first:
        red["q", k].on_xy()
    for k in far_first:
        red["s", k].on_s()
    inner_sum = jnp.mean(grad_one * gain_one * unit_one, axis=1, keepdims=True)
    back_one = scale_one * (grad_one * gain_one - unit_one * inner_sum)
    tokens_grad_ref[...] = (grad_middle_ref[...] + back_one).astype(BF)

    def settle_in_order(name, blocks, cut):
        def one(k):
            low, high = red[name, k].finish()
            blocks[at.order[k], :, :cut] = low.astype(BF)
            blocks[at.order[k], :, cut:] = high.astype(BF)

        one(3)
        lines[name].leave(3)
        one(2)
        lines[name].leave(2)
        lines[name].hand(3)
        one(1)
        lines[name].leave(1)
        lines[name].hand(2)
        one(0)

    settle_in_order("q", az, q_width // 2)
    for k in far_first:
        red["s", k].on_xy()
    settle_in_order("s", cz, 3 * 128)
    output_part(0)
    lines["q"].hand(1)
    lines["s"].hand(1)
    lines["b"].finish(b_out)
    output_part(1)
    lines["q"].finish(aq_out)
    lines["s"].finish(ak_out)
    for item in red.values():
        item.drain()


def back(
    lengths, seq_order, row, weighted, tokens, q_rot, att, lse, middle, cot, kv, pay, pack, wo, n_experts
):
    count, width = tokens.shape
    group = 8
    shard = width // 32
    kv_width = KEY_VALUE_HEADS * HEAD_SIZE
    part = count // 2
    wide_r = width + 128
    wide_s, cut_s = 2 * kv_width + 128, 3 * 128
    half = width // 2
    sds = jax.ShapeDtypeStruct
    smem = pl.BlockSpec(memory_space=pltpu.SMEM)
    vmem = pl.BlockSpec(memory_space=pltpu.VMEM)
    hbm = pl.BlockSpec(memory_space=ANY)
    pack = pack.reshape(4, 4, 2, shard, pack.shape[1])
    wo = wo.reshape(4, 4, 2, shard, width)

    def low(*shape):
        return pltpu.VMEM(shape, BF)

    def like(a):
        return pltpu.VMEM(a.shape, a.dtype)

    return pl.pallas_call(
        functools.partial(back_kernel, n_experts),
        in_specs=[smem, smem] + [hbm] * 12,
        out_specs=(vmem,) * 5,
        out_shape=(
            sds((count, width), BF),
            sds((count, width), BF),
            sds((shard, width), F32),
            sds((shard, wide_s), F32),
            sds((shard, width), F32),
        ),
        scratch_shapes=[
            low(2, 4, part, width),
            low(2, 4, part, width),
            low(2, 2, 2, part, half),
            low(2, 2, part, half),
            pltpu.VMEM((count, wide_r), F32),
            like(tokens),
            like(q_rot),
            like(att),
            like(lse),
            like(middle),
            like(cot),
            like(kv),
            like(pay),
            like(pack),
            like(wo),
            like(q_rot),
            low(4, 2, count, 2 * kv_width),
            low(2, 4, part, 2 * kv_width),
            low(2, 2, part, kv_width),
            low(2, 2, part, kv_width),
            low(2, part, kv_width),
            low(2, part, kv_width),
            low(4, 4, shard, width),
            low(4, 2, 2, shard, half),
            low(4, 2, shard, half),
            low(4, 4, shard, width),
            low(4, 2, 2, shard, half),
            low(4, 2, shard, half),
            low(4, 4, shard, wide_s),
            low(4, 2, shard, cut_s),
            low(4, 2, shard, wide_s - cut_s),
            low(4, shard, cut_s),
            low(4, shard, wide_s - cut_s),
            low(count, width),
            low(count, width + 2 * kv_width),
            pltpu.VMEM((width, 128), F32),
            pltpu.VMEM((count, width), F32),
            low(4, shard, width),
            low(3, shard, width),
            low(2, shard, width),
            low(4, shard, width),
            low(3, shard, width),
            low(2, shard, width),
            low(4, shard, wide_s),
            low(3, shard, wide_s),
            low(2, shard, wide_s),
            pltpu.SemaphoreType.DMA((N_BACK, 7)),
            pltpu.SemaphoreType.DMA((N_BACK, 7)),
            pltpu.SemaphoreType.DMA((3, 5)),
            pltpu.SemaphoreType.DMA((3, 5)),
            pltpu.SemaphoreType.DMA((14,)),
        ],
        compiler_params=pltpu.CompilerParams(
            collective_id=2, has_side_effects=True, vmem_limit_bytes=63 * 2**20
        ),
        cost_estimate=pl.CostEstimate(
            flops=15 * 10**10, bytes_accessed=5 * 10**7, transcendentals=10**7
        ),
    )(lengths, seq_order, row, weighted, tokens, q_rot, att, lse, middle, cot, kv, pay, pack, wo)


def last_kernel(
    n_experts, mine_hbm, out_hbm, grad_hbm, q_hbm, s_hbm, b_hbm,
    gate_ref, up_ref, down_ref, out_ref, grad_ref, q_ref, k_ref, v_ref, b_ref, router_ref, one_ref,
    two_ref, mine_ref, s_in, sems,
):
    pairs = (
        (mine_hbm, mine_ref), (s_hbm, s_in), (out_hbm, out_ref), (grad_hbm, grad_ref),
        (q_hbm, q_ref), (b_hbm, b_ref),
    )
    loads = [pltpu.make_async_copy(a, b, sems.at[n]) for n, (a, b) in enumerate(pairs)]
    for load in loads:
        load.start()
    loads[0].wait()
    loads[1].wait()
    depth = gate_ref.shape[0]
    tall, wide = down_ref.shape
    kv_width = k_ref.shape[1]
    k_ref[...] = s_in[:, :kv_width]
    v_ref[...] = s_in[:, kv_width : 2 * kv_width]
    small = s_in[:, 2 * kv_width :]
    high = small.astype(BF)
    rest = small - high.astype(F32)
    mid = rest.astype(BF)
    low = (rest - mid.astype(F32)).astype(BF)
    row = lax.broadcasted_iota(jnp.int32, (16, 128), 0)
    pick = (row == lax.broadcasted_iota(jnp.int32, (16, 128), 1)).astype(F32).astype(BF)
    turned = dot_bt(pick, high) + dot_bt(pick, mid) + dot_bt(pick, low)
    router_ref[...] = turned[:n_experts]
    one_ref[...] = turned[n_experts : n_experts + 1]
    two_ref[...] = turned[n_experts + 1 : n_experts + 2]
    gate_ref[...] = mine_ref[:depth].astype(F32)
    up_ref[...] = mine_ref[depth : 2 * depth].astype(F32)
    down_ref[:, : wide // 2] = mine_ref[2 * depth : 2 * depth + tall].astype(F32)
    down_ref[:, wide // 2 :] = mine_ref[2 * depth + tall :].astype(F32)
    for load in loads[2:]:
        load.wait()


def last(mine, output, tokens_grad, query_mine, rest_mine, out_mine, n_experts):
    shard, wide_s = rest_mine.shape
    kv_width = KEY_VALUE_HEADS * HEAD_SIZE
    hid = mine.shape[1]
    tall = mine.shape[0] // 6
    sds = jax.ShapeDtypeStruct
    vmem = pl.BlockSpec(memory_space=pltpu.VMEM)
    return pl.pallas_call(
        functools.partial(last_kernel, n_experts),
        in_specs=[pl.BlockSpec(memory_space=ANY)] * 6,
        out_specs=(vmem,) * 12,
        out_shape=(
            sds((2 * tall, hid), F32),
            sds((2 * tall, hid), F32),
            sds((tall, 2 * hid), F32),
            sds(output.shape, output.dtype),
            sds(tokens_grad.shape, tokens_grad.dtype),
            sds(query_mine.shape, F32),
            sds((shard, kv_width), F32),
            sds((shard, kv_width), F32),
            sds(out_mine.shape, F32),
            sds((n_experts, shard), F32),
            sds((1, shard), F32),
            sds((1, shard), F32),
        ),
        scratch_shapes=[
            pltpu.VMEM(mine.shape, BF),
            pltpu.VMEM(rest_mine.shape, F32),
            pltpu.SemaphoreType.DMA((6,)),
        ],
        compiler_params=pltpu.CompilerParams(vmem_limit_bytes=60 * 2**20),
    )(mine, output, tokens_grad, query_mine, rest_mine, out_mine)


def on_device_fast(
    tokens,
    lengths,
    seq_order,
    routes,
    norm_attn,
    w_query,
    key_projection,
    value_projection,
    w_out,
    norm_moe,
    w_router,
    w_gate,
    w_up,
    w_down,
    cotangent,
):
    token_count, width = tokens.shape
    n_experts = w_router.shape[1]
    group_tokens = token_count * lax.axis_size("expert")
    pack = pack_weights(w_router, norm_attn, norm_moe, w_query, key_projection, value_projection)
    x_all, gw, uw, pack, wo, kv_all, q_rot, attended, lse, middle, pay = front(
        lengths, seq_order, tokens, routes.T, pack, w_out, w_gate[0], w_up[0], n_experts
    )
    x_all = x_all.reshape(group_tokens, width + 128)
    c_all, dw, hidden, slope, expert_grads = expert_up(x_all, cotangent, gw, uw, w_down[0])
    grad_row, weighted = expert_down(x_all, c_all, hidden, slope, gw, uw, dw)
    expert_mine = lax.psum_scatter(
        expert_grads.reshape(-1, expert_grads.shape[2]), "dp", scatter_dimension=0, tiled=True
    )
    output, tokens_grad, query_mine, mine, out_mine = back(
        lengths,
        seq_order,
        grad_row,
        weighted,
        tokens,
        q_rot,
        attended,
        lse,
        middle,
        cotangent,
        kv_all,
        pay,
        pack,
        wo,
        n_experts,
    )
    gate, up, down, output, tokens_grad, query, key, value, out, router, one, two = last(
        expert_mine, output, tokens_grad, query_mine, mine, out_mine, n_experts
    )
    return (
        output,
        tokens_grad,
        one.reshape(-1),
        query,
        key,
        value,
        out,
        two.reshape(-1),
        router.T,
        gate[None],
        up[None],
        down[None],
    )


def solution(mesh):
    both = ("dp", "expert")
    small = mesh.shape["dp"] == 4 and mesh.shape["expert"] == 8
    return jax.shard_map(
        on_device_fast if small else on_device,
        mesh=mesh,
        in_specs=(
            P(both, None),
            P("dp", None),
            P("dp", None),
            P(both, None),
            P(both),
            P(both, None),
            P(both, None),
            P(both, None),
            P(both, None),
            P(both),
            P(both, None),
            P("expert", "dp", None),
            P("expert", "dp", None),
            P("expert", "dp", None),
            P(both, None),
        ),
        out_specs=(
            P(both, None),
            P(both, None),
            P(both),
            P(both, None),
            P(both, None),
            P(both, None),
            P(both, None),
            P(both),
            P(both, None),
            P("expert", "dp", None),
            P("expert", "dp", None),
            P("expert", "dp", None),
        ),
        check_vma=False,
    )
```
